32 devices in a mesh: tm: 8 (over y, x, core), sky: 4 (over z).
Axes of the slice: x: 2, y: 2, z: 4, core: 2. Of those that a mesh axis runs over, the one named last changes fastest.
Arguments:
- residuals: bfloat16 [32, 512, 1024], P('tm', None, 'sky')
- seg_counts: int32 [32], P('tm'), may hold values from 256 to 512, as said below
- attitude: bfloat16 [32, 512, 512], P('tm', 'sky')
- sched_seg: int32 [256, 256], P(('tm', 'sky')), may hold values from 0 to 31, as said below
- sched_slot: int32 [256, 256], P(('tm', 'sky')), may hold values from 0 to 511, as said below
- periods: int32 [1024], replicated, may hold values from 16 to 16383
Outputs:
- cleaned: float32 [32, 512, 1024], P('tm', None, 'sky')
- log_evidence: float32 [256, 128], P(('tm', 'sky'))
The draws below stay inside these ranges and needn't reach their ends.
Inputs may be any that keep to these rules, and one draw needn't show every extreme that they name: `seg_counts`: every segment has between 256 and 512 observed slots; some segment has all 512. `sched_seg`: in each aligned block of 8 rows (the plans of one device) at most 512 entries fall in the segments of one index of tm, and in every block some index receives exactly 512. `sched_slot`: each slot is below the observed count of its segment.
All inputs are finite; a program needn't handle non-finite values.
Results may differ from the reference program's by a relative error of at most 0.035.
Values may be sent and summed in bfloat16 or wider, within the bound.
No kernel may reach another device: no remote copies, remote signals or barrier semaphores. Data moves between devices by JAX's collectives and lax.ppermute only.
A program may use at most 128 MiB of HBM per device.

```python
import jax
import jax.numpy as jnp
from jax import lax

SLOTS = 512
NPER = 1024
OBS = 256
SRC_GROUP = 128
NCB = 2
ITERS = 2
SEG_DEV = 4
SCHED_DEV = 8
SEGMENTS = 32
COLS = 1024
PLANS = 256
N_SKY = 4


def count_table(key):
    first, second = jax.random.split(key)
    values = jax.random.randint(first, (SEGMENTS,), SLOTS // 2, SLOTS + 1)
    spot = jax.random.randint(second, (), 0, SEGMENTS)
    return jnp.where(jnp.arange(SEGMENTS) == spot, SLOTS, values).astype(jnp.int32)


def period_table(key):
    return jax.random.randint(key, (NPER,), 16, 16384).astype(jnp.int32)


def plan_table(key):
    counts = count_table(jax.random.fold_in(key, 11))
    owners = SEGMENTS // SEG_DEV
    blocks = PLANS // SCHED_DEV
    wanted = SCHED_DEV * OBS
    mean = wanted // owners
    rank = jnp.arange(owners)
    profile = jnp.where(rank < owners // 4, 2 * mean, jnp.where(rank < owners // 2, mean, mean // 2))

    def single(block_key):
        key_a, key_b, key_c, key_d = jax.random.split(block_key, 4)
        loads = profile[jax.random.permutation(key_a, owners)]
        bounds = jnp.cumsum(loads)
        target = jnp.searchsorted(bounds, jnp.arange(wanted), side='right').astype(jnp.int32)
        target = jax.random.permutation(key_b, target)
        segment = target * SEG_DEV + jax.random.randint(key_c, (wanted,), 0, SEG_DEV)
        raw = jax.random.randint(key_d, (wanted,), 0, 1 << 20)
        slot = raw * counts[segment] // (1 << 20)
        return (segment.reshape(SCHED_DEV, OBS), slot.reshape(SCHED_DEV, OBS))
    segs, slots = jax.vmap(single)(jax.random.split(jax.random.fold_in(key, 23), blocks))
    return (segs.reshape(PLANS, OBS).astype(jnp.int32), slots.reshape(PLANS, OBS).astype(jnp.int32))


def draw_seg_counts(key, part):
    return count_table(jax.random.fold_in(key, 11))


def draw_periods(key, part):
    return period_table(jax.random.fold_in(key, 31))


def draw_sched_seg(key, part):
    return plan_table(key)[0]


def draw_sched_slot(key, part):
    return plan_table(key)[1]


def draw_attitude(key, part):
    first = jax.random.fold_in(jax.random.fold_in(key, 53), 0)
    ident = (jnp.arange(SLOTS)[:, None] == jnp.arange(SLOTS)[None, :]).astype(jnp.float32)
    noise = 0.5 * jax.random.normal(first, (SEGMENTS, SLOTS, SLOTS)) / SLOTS ** 0.5
    return (ident[None] + noise).astype(jnp.bfloat16)


def draw_residuals(key, part):
    base = jax.random.normal(jax.random.fold_in(key, 41), (SEGMENTS, SLOTS, COLS))
    return base.astype(jnp.bfloat16)


def setup_inputs(seed: int = 0) -> dict:
    splits = jax.random.split(jax.random.key(seed), 7)
    residuals = draw_residuals(jax.random.fold_in(splits[6], 71), 0)
    seg_counts = draw_seg_counts(jax.random.fold_in(splits[6], 71), 0)
    attitude = draw_attitude(jax.random.fold_in(splits[6], 71), 0)
    sched_seg = draw_sched_seg(jax.random.fold_in(splits[6], 71), 0)
    sched_slot = draw_sched_slot(jax.random.fold_in(splits[6], 71), 0)
    periods = draw_periods(jax.random.fold_in(splits[6], 71), 0)
    return {"residuals": residuals, "seg_counts": seg_counts, "attitude": attitude, "sched_seg": sched_seg, "sched_slot": sched_slot, "periods": periods}


TWO_PI = 6.283185307179586
BETA = 2.0
RIDGE = 1.0


def make_basis(times, periods):
    period_float = periods.astype(jnp.float32)
    phase = (times[:, None] % periods[None, :]).astype(jnp.float32) * (TWO_PI / period_float)[None, :]
    return jnp.concatenate([jnp.cos(phase), jnp.sin(phase)], axis=1).astype(jnp.bfloat16)


def fit_group(basis, observed):
    squares = basis.astype(jnp.float32) ** 2
    norm_cos = jnp.sum(squares[:, :NPER], axis=0) + RIDGE
    norm_sin = jnp.sum(squares[:, NPER:], axis=0) + RIDGE
    corr = jnp.dot(basis.T, observed, preferred_element_type=jnp.float32)
    cosine = corr[:NPER]
    sine = corr[NPER:]
    amp_c = cosine / norm_cos[:, None]
    amp_s = sine / norm_sin[:, None]
    power = cosine * amp_c + sine * amp_s
    logits = BETA * power
    highest = jnp.max(logits, axis=0)
    expo = jnp.exp(logits - highest[None, :])
    total = jnp.sum(expo, axis=0)
    share = expo / total[None, :]
    coeff = jnp.concatenate([share * amp_c, share * amp_s], axis=0).astype(jnp.bfloat16)
    model = jnp.dot(basis, coeff, preferred_element_type=jnp.float32)
    return model, highest + jnp.log(total)


def reference(residuals, seg_counts, attitude, sched_seg, sched_slot, periods):
    valid = jnp.arange(SLOTS, dtype=jnp.int32)[None, :] < seg_counts[:, None]
    index = jnp.arange(PLANS, dtype=jnp.int32)
    region = (index // SCHED_DEV) % N_SKY
    block = (index % SCHED_DEV) % NCB
    first = ((region * NCB + block) * SRC_GROUP).astype(jnp.int32)
    columns = jnp.arange(SRC_GROUP, dtype=jnp.int32)
    current = residuals.astype(jnp.float32)
    evidence = jnp.zeros((PLANS, SRC_GROUP), jnp.float32)
    for iteration in range(ITERS):
        masked = jnp.where(valid[:, :, None], current, 0.0).astype(jnp.bfloat16)
        white = lax.map(lambda pair: jnp.dot(pair[0], pair[1], preferred_element_type=jnp.float32).astype(jnp.bfloat16), (attitude, masked))

        def visit(placed, item):
            seg_row, slot_row, start = item
            cols = start + columns
            observed = white[seg_row[:, None], slot_row[:, None], cols[None, :]]
            basis = make_basis(seg_row * SLOTS + slot_row, periods)
            model, score = fit_group(basis, observed)
            placed = placed.at[seg_row[:, None], slot_row[:, None], cols[None, :]].add(model.astype(jnp.float32))
            return placed, score

        placed, evidence = lax.scan(visit, jnp.zeros(current.shape, jnp.float32), (sched_seg, sched_slot, first))
        current = current - placed
    return current, evidence
```

```python
import functools

import jax
import jax.numpy as jnp
from jax import lax
from jax.experimental import pallas as pl
from jax.experimental.pallas import tpu as pltpu
from jax.sharding import PartitionSpec as P

SRC_GROUP = 128
ITERS = 2
STREAMS = 8
BETA = 2.0
RIDGE = 1.0
VMEM_LIMIT = 60 * 1024 * 1024

COS_POLY = (1.0, -19.73920440673828, 64.9391098022461, -85.4500503540039, 60.16689682006836,
            -25.96480369567871, 6.52468729019165)
SIN_POLY = (6.283185005187988, -41.34158706665039, 81.59986114501953, -76.61351013183594,
            41.33811950683594, -12.463061332702637)

VMEM = pl.BlockSpec(memory_space=pltpu.VMEM)
SMEM = pl.BlockSpec(memory_space=pltpu.SMEM)


def horner(poly, v):
    acc = jnp.full_like(v, poly[-1])
    for term in poly[-2::-1]:
        acc = acc * v + term
    return acc


def basis_kernel(time_ref, period_ref, inverse_ref, basis_ref, norm_ref):
    obs = time_ref.shape[0]
    nper = period_ref.shape[1]
    rows = 32
    for chunk in range(nper // 128):
        lanes = pl.ds(chunk * 128, 128)
        sines = pl.ds(nper + chunk * 128, 128)
        period = period_ref[:, lanes]
        inverse = inverse_ref[:, lanes]

        def step(index, sums):
            at = pl.ds(pl.multiple_of(index * rows, rows), rows)
            time = time_ref[at, :]
            turns = jnp.round(time * inverse)
            part = (time - turns * period) * inverse
            square = part * part
            cosine = horner(COS_POLY, square).astype(jnp.bfloat16)
            sine = (horner(SIN_POLY, square) * part).astype(jnp.bfloat16)
            basis_ref[0, at, lanes] = cosine
            basis_ref[0, at, sines] = sine
            cosine = cosine.astype(jnp.float32)
            sine = sine.astype(jnp.float32)
            return (
                sums[0] + jnp.sum((cosine * cosine).reshape(rows // 8, 8, 128), axis=0),
                sums[1] + jnp.sum((sine * sine).reshape(rows // 8, 8, 128), axis=0),
            )

        zero = jnp.zeros((8, 128), jnp.float32)
        total_c, total_s = lax.fori_loop(0, obs // rows, step, (zero, zero))
        norm_ref[0, :, lanes] = 1.0 / (jnp.sum(total_c, axis=0, keepdims=True) + RIDGE)
        norm_ref[0, :, sines] = 1.0 / (jnp.sum(total_s, axis=0, keepdims=True) + RIDGE)


def make_basis(times, periods):
    sched_dev, obs = times.shape
    nper = periods.shape[0]
    wide = jnp.broadcast_to(
        times.astype(jnp.float32).reshape(-1, 1), (sched_dev * obs, SRC_GROUP)
    )
    period = periods.astype(jnp.float32)[None, :]
    return pl.pallas_call(
        basis_kernel,
        grid=(sched_dev,),
        in_specs=[
            pl.BlockSpec((obs, SRC_GROUP), lambda j: (j, 0)),
            pl.BlockSpec((1, nper), lambda j: (0, 0)),
            pl.BlockSpec((1, nper), lambda j: (0, 0)),
        ],
        out_specs=[
            pl.BlockSpec((1, obs, 2 * nper), lambda j: (j, 0, 0)),
            pl.BlockSpec((1, 1, 2 * nper), lambda j: (j, 0, 0)),
        ],
        out_shape=[
            jax.ShapeDtypeStruct((sched_dev, obs, 2 * nper), jnp.bfloat16),
            jax.ShapeDtypeStruct((sched_dev, 1, 2 * nper), jnp.float32),
        ],
        compiler_params=pltpu.CompilerParams(vmem_limit_bytes=VMEM_LIMIT),
        cost_estimate=pl.CostEstimate(
            flops=sched_dev * obs * nper * 300, bytes_accessed=sched_dev * obs * nper * 4, transcendentals=0
        ),
    )(wide, period, 1.0 / period)


def copy_rows(count, out_ref, out_at, in_ref, in_at, unroll=8):
    def step(index, carry):
        for lane in range(unroll):
            row = index * unroll + lane
            out_ref[pl.ds(out_at(row), 1), :] = in_ref[pl.ds(in_at(row), 1), :]
        return carry

    lax.fori_loop(0, count // unroll, step, 0)


def fit_kernel(place_ref, arrived_ref, basis_ref, norm_ref, out_ref, score_ref,
               rows_ref, obs_ref, corr_ref, coeff_ref, model_ref, back_ref):
    plan = pl.program_id(0)
    plans = pl.num_programs(0)
    obs, width = obs_ref.shape
    nper = basis_ref.shape[2] // 2

    @pl.when(plan == 0)
    def _():
        rows_ref[...] = arrived_ref[...].astype(jnp.float32)

    first = plan * obs
    copy_rows(obs, obs_ref, lambda row: row, rows_ref, lambda row: place_ref[first + row])
    corr_ref[...] = lax.dot_general(
        obs_ref[...].astype(jnp.bfloat16), basis_ref[0], (((0,), (0,)), ((), ())),
        preferred_element_type=jnp.float32,
    )
    group = 16
    for start in range(0, width, group):
        at = pl.ds(start, group)
        power = []
        for chunk in range(nper // 128):
            lanes = pl.ds(chunk * 128, 128)
            sines = pl.ds(nper + chunk * 128, 128)
            cosine = corr_ref[at, lanes]
            sine = corr_ref[at, sines]
            power.append(
                cosine * (cosine * norm_ref[0, :, lanes]) + sine * (sine * norm_ref[0, :, sines])
            )
        highest = functools.reduce(jnp.maximum, power)
        highest = jnp.max(highest, axis=1, keepdims=True)
        expo = [jnp.exp(BETA * (value - highest)) for value in power]
        total = jnp.sum(functools.reduce(jnp.add, expo), axis=1, keepdims=True)
        scale = 1.0 / total
        for chunk in range(nper // 128):
            lanes = pl.ds(chunk * 128, 128)
            sines = pl.ds(nper + chunk * 128, 128)
            share = expo[chunk] * scale
            coeff_ref[at, lanes] = (share * (corr_ref[at, lanes] * norm_ref[0, :, lanes])).astype(jnp.bfloat16)
            coeff_ref[at, sines] = (share * (corr_ref[at, sines] * norm_ref[0, :, sines])).astype(jnp.bfloat16)
        score_ref[0, at, :] = BETA * highest + jnp.log(total)
    model_ref[...] = lax.dot_general(
        basis_ref[0], coeff_ref[...], (((1,), (1,)), ((), ())), preferred_element_type=jnp.float32
    )
    copy_rows(obs, back_ref, lambda row: place_ref[first + row], model_ref, lambda row: row)

    @pl.when(plan == plans - 1)
    def _():
        out_ref[...] = back_ref[...].astype(jnp.bfloat16)


def fit_plans(place, arrived, basis, norms):
    sched_dev, obs, twice = basis.shape
    slots, width = arrived.shape
    work = sched_dev * obs * twice * width
    return pl.pallas_call(
        fit_kernel,
        grid=(sched_dev,),
        in_specs=[
            SMEM,
            VMEM,
            pl.BlockSpec((1, obs, twice), lambda j: (j, 0, 0)),
            pl.BlockSpec((1, 1, twice), lambda j: (j, 0, 0)),
        ],
        out_specs=[VMEM, pl.BlockSpec((1, width, 1), lambda j: (j, 0, 0))],
        out_shape=[
            jax.ShapeDtypeStruct((slots, width), jnp.bfloat16),
            jax.ShapeDtypeStruct((sched_dev, width, 1), jnp.float32),
        ],
        scratch_shapes=[
            pltpu.VMEM((slots, width), jnp.float32),
            pltpu.VMEM((obs, width), jnp.float32),
            pltpu.VMEM((width, twice), jnp.float32),
            pltpu.VMEM((width, twice), jnp.bfloat16),
            pltpu.VMEM((obs, width), jnp.float32),
            pltpu.VMEM((slots, width), jnp.float32),
        ],
        compiler_params=pltpu.CompilerParams(vmem_limit_bytes=VMEM_LIMIT),
        cost_estimate=pl.CostEstimate(flops=4 * work, bytes_accessed=2 * basis.size, transcendentals=0),
    )(place, arrived, basis, norms)


def whiten_and_pick(asked_ref, count_ref, attitude_ref, load, picked_ref, white_ref, gather_ref):
    segs, slots, _ = attitude_ref.shape
    requests, width = picked_ref.shape
    blocks = white_ref.shape[0] // (segs * slots)
    row = lax.broadcasted_iota(jnp.int32, (slots, width * blocks), 0)
    for seg in range(segs):
        masked = jnp.where(row < count_ref[seg], load(seg).astype(jnp.float32), 0.0).astype(jnp.bfloat16)
        white = jnp.dot(attitude_ref[seg], masked, preferred_element_type=jnp.float32)
        for block in range(blocks):
            white_ref[pl.ds((block * segs + seg) * slots, slots), :] = white[:, block * width:(block + 1) * width]
    copy_rows(requests, gather_ref, lambda row: row, white_ref, lambda row: asked_ref[row])
    picked_ref[...] = gather_ref[...].astype(jnp.bfloat16)


def pick_kernel(asked_ref, count_ref, attitude_ref, residual_ref, picked_ref, white_ref, gather_ref):
    whiten_and_pick(
        asked_ref, count_ref, attitude_ref, lambda seg: residual_ref[seg], picked_ref, white_ref, gather_ref
    )


def place_rows(asked_ref, returned_ref, current_ref, out_ref, rows_ref, sums):
    segs, slots, _ = current_ref.shape
    requests, width = returned_ref.shape
    blocks = current_ref.shape[2] // width
    part = requests // len(sums)
    rows_ref[...] = returned_ref[...].astype(jnp.float32)
    for total in sums:
        total[...] = jnp.zeros_like(total)

    def step(index, carry):
        rows = [stream * part + index for stream in range(len(sums))]
        places = [asked_ref[row] for row in rows]
        values = [
            total[pl.ds(place, 1), :] + rows_ref[pl.ds(row, 1), :]
            for total, place, row in zip(sums, places, rows)
        ]
        for total, place, value in zip(sums, places, values):
            total[pl.ds(place, 1), :] = value
        return carry

    lax.fori_loop(0, part, step, 0, unroll=2)
    for seg in range(segs):
        for block in range(blocks):
            at = pl.ds((block * segs + seg) * slots, slots)
            lanes = slice(block * width, (block + 1) * width)
            placed = functools.reduce(jnp.add, [total[at, :] for total in sums])
            out_ref[seg, :, lanes] = current_ref[seg, :, lanes].astype(jnp.float32) - placed


def place_pick_kernel(asked_ref, count_ref, attitude_ref, returned_ref, current_ref, out_ref, picked_ref,
                      white_ref, gather_ref, rows_ref, *sums):
    place_rows(asked_ref, returned_ref, current_ref, out_ref, rows_ref, sums)
    whiten_and_pick(
        asked_ref, count_ref, attitude_ref, lambda seg: out_ref[seg], picked_ref, white_ref, gather_ref
    )


def place_kernel(asked_ref, returned_ref, current_ref, out_ref, rows_ref, *sums):
    place_rows(asked_ref, returned_ref, current_ref, out_ref, rows_ref, sums)


def on_device(residuals, seg_counts, attitude, sched_seg, sched_slot, periods):
    tm_count = lax.axis_size("tm")
    sched_dev, obs = sched_seg.shape
    seg_dev, slots, width = residuals.shape
    column_blocks = width // SRC_GROUP
    capacity = 2 * sched_dev * obs // tm_count
    requests = tm_count * capacity
    whole = lax.all_gather(attitude, "sky", axis=1, tiled=True)

    seg_flat = sched_seg.reshape(-1)
    slot_flat = sched_slot.reshape(-1)
    block_of = jnp.repeat(jnp.arange(sched_dev, dtype=jnp.int32) % column_blocks, obs)
    target = seg_flat // seg_dev
    local_row = (block_of * seg_dev + seg_flat % seg_dev) * slots + slot_flat
    onehot = (target[:, None] == jnp.arange(tm_count, dtype=jnp.int32)[None, :]).astype(jnp.int32)
    position = jnp.sum(jnp.cumsum(onehot, axis=0) * onehot, axis=1) - 1
    place = target * capacity + position
    rows = seg_dev * slots * column_blocks
    wanted = jnp.full((requests,), rows, jnp.int32).at[place].set(local_row, unique_indices=True)
    asked = lax.all_to_all(
        wanted.reshape(tm_count, capacity), "tm", split_axis=0, concat_axis=0, tiled=True
    ).reshape(-1)
    basis, norms = make_basis(sched_seg * slots + sched_slot, periods)

    def exchange(values):
        shaped = values.reshape(tm_count, capacity, SRC_GROUP)
        return lax.all_to_all(shaped, "tm", split_axis=0, concat_axis=0, tiled=True).reshape(
            requests, SRC_GROUP
        )

    table = pltpu.VMEM((rows + 8, SRC_GROUP), jnp.float32)
    list_rows = pltpu.VMEM((requests, SRC_GROUP), jnp.float32)
    picked_shape = jax.ShapeDtypeStruct((requests, SRC_GROUP), jnp.bfloat16)
    current_shape = jax.ShapeDtypeStruct(residuals.shape, jnp.float32)
    params = pltpu.CompilerParams(vmem_limit_bytes=VMEM_LIMIT)
    white_flops = 2 * seg_dev * slots * slots * width

    current = residuals
    for iteration in range(ITERS):
        if iteration == 0:
            picked = pl.pallas_call(
                pick_kernel,
                in_specs=[SMEM, SMEM, VMEM, VMEM],
                out_specs=VMEM,
                out_shape=picked_shape,
                scratch_shapes=[table, list_rows],
                compiler_params=params,
                cost_estimate=pl.CostEstimate(flops=white_flops, bytes_accessed=8 << 20, transcendentals=0),
            )(asked, seg_counts, whole, current)
        else:
            current, picked = pl.pallas_call(
                place_pick_kernel,
                in_specs=[SMEM, SMEM, VMEM, VMEM, VMEM],
                out_specs=[VMEM, VMEM],
                out_shape=[current_shape, picked_shape],
                scratch_shapes=[table, list_rows, list_rows] + [table] * STREAMS,
                compiler_params=params,
                cost_estimate=pl.CostEstimate(flops=white_flops, bytes_accessed=16 << 20, transcendentals=0),
            )(asked, seg_counts, whole, returned, current)
        model, score = fit_plans(place, exchange(picked), basis, norms)
        returned = exchange(model)
    current = pl.pallas_call(
        place_kernel,
        in_specs=[SMEM, VMEM, VMEM],
        out_specs=VMEM,
        out_shape=current_shape,
        scratch_shapes=[list_rows] + [table] * STREAMS,
        compiler_params=params,
        cost_estimate=pl.CostEstimate(flops=1 << 20, bytes_accessed=16 << 20, transcendentals=0),
    )(asked, returned, current)
    return (current, score.reshape(sched_dev, SRC_GROUP))


def solution(mesh):
    in_specs = (
        P("tm", None, "sky"),
        P("tm"),
        P("tm", "sky", None),
        P(("tm", "sky"), None),
        P(("tm", "sky"), None),
        P(),
    )
    out_specs = (P("tm", None, "sky"), P(("tm", "sky"), None))
    return jax.shard_map(
        on_device, mesh=mesh, in_specs=in_specs, out_specs=out_specs, check_vma=False
    )
```

```python
import functools

import jax
import jax.numpy as jnp
from jax import lax
from jax.experimental import pallas as pl
from jax.experimental.pallas import tpu as pltpu
from jax.sharding import PartitionSpec as P

SRC_GROUP = 128
ITERS = 2
STREAMS = 4
STEP = 16
BETA = 2.0
RIDGE = 1.0
VMEM_LIMIT = 60 * 1024 * 1024

COS_POLY = (1.0, -19.73920440673828, 64.9391098022461, -85.4500503540039, 60.16689682006836,
            -25.96480369567871, 6.52468729019165)
SIN_POLY = (6.283185005187988, -41.34158706665039, 81.59986114501953, -76.61351013183594,
            41.33811950683594, -12.463061332702637)

VMEM = pl.BlockSpec(memory_space=pltpu.VMEM)
SMEM = pl.BlockSpec(memory_space=pltpu.SMEM)


def horner(poly, v):
    acc = jnp.full_like(v, poly[-1])
    for term in poly[-2::-1]:
        acc = acc * v + term
    return acc


def basis_kernel(time_ref, period_ref, inverse_ref, basis_ref, norm_ref):
    obs = time_ref.shape[0]
    nper = period_ref.shape[1]
    rows = 32
    for chunk in range(nper // 128):
        lanes = pl.ds(chunk * 128, 128)
        sines = pl.ds(nper + chunk * 128, 128)
        period = period_ref[:, lanes]
        inverse = inverse_ref[:, lanes]

        def step(index, sums):
            at = pl.ds(pl.multiple_of(index * rows, rows), rows)
            time = time_ref[at, :]
            turns = jnp.round(time * inverse)
            part = (time - turns * period) * inverse
            square = part * part
            cosine = horner(COS_POLY, square).astype(jnp.bfloat16)
            sine = (horner(SIN_POLY, square) * part).astype(jnp.bfloat16)
            basis_ref[0, at, lanes] = cosine
            basis_ref[0, at, sines] = sine
            cosine = cosine.astype(jnp.float32)
            sine = sine.astype(jnp.float32)
            return (
                sums[0] + jnp.sum((cosine * cosine).reshape(rows // 8, 8, 128), axis=0),
                sums[1] + jnp.sum((sine * sine).reshape(rows // 8, 8, 128), axis=0),
            )

        zero = jnp.zeros((8, 128), jnp.float32)
        total_c, total_s = lax.fori_loop(0, obs // rows, step, (zero, zero))
        norm_ref[0, :, lanes] = 1.0 / (jnp.sum(total_c, axis=0, keepdims=True) + RIDGE)
        norm_ref[0, :, sines] = 1.0 / (jnp.sum(total_s, axis=0, keepdims=True) + RIDGE)


def make_basis(times, periods):
    sched_dev, obs = times.shape
    nper = periods.shape[0]
    wide = jnp.broadcast_to(
        times.astype(jnp.float32).reshape(-1, 1), (sched_dev * obs, SRC_GROUP)
    )
    period = periods.astype(jnp.float32)[None, :]
    return pl.pallas_call(
        basis_kernel,
        grid=(sched_dev,),
        in_specs=[
            pl.BlockSpec((obs, SRC_GROUP), lambda j: (j, 0)),
            pl.BlockSpec((1, nper), lambda j: (0, 0)),
            pl.BlockSpec((1, nper), lambda j: (0, 0)),
        ],
        out_specs=[
            pl.BlockSpec((1, obs, 2 * nper), lambda j: (j, 0, 0)),
            pl.BlockSpec((1, 1, 2 * nper), lambda j: (j, 0, 0)),
        ],
        out_shape=[
            jax.ShapeDtypeStruct((sched_dev, obs, 2 * nper), jnp.bfloat16),
            jax.ShapeDtypeStruct((sched_dev, 1, 2 * nper), jnp.float32),
        ],
        compiler_params=pltpu.CompilerParams(vmem_limit_bytes=VMEM_LIMIT),
        cost_estimate=pl.CostEstimate(
            flops=sched_dev * obs * nper * 300, bytes_accessed=sched_dev * obs * nper * 4, transcendentals=0
        ),
    )(wide, period, 1.0 / period)


def fit_kernel(tm_count, cnt_ref, src_ref, dst_ref, *refs):
    arrived = refs[:tm_count]
    basis_ref, norm_ref = refs[tm_count:tm_count + 2]
    outs = refs[tm_count + 2:2 * tm_count + 2]
    score_ref, rows_ref, obs_ref, corr_ref, coeff_ref, model_ref, back_ref = refs[2 * tm_count + 2:]
    plan = pl.program_id(0)
    plans = pl.num_programs(0)
    capacity, width = arrived[0].shape
    obs = basis_ref.shape[1]
    nper = basis_ref.shape[2] // 2
    spaced = capacity + STEP

    @pl.when(plan == 0)
    def _():
        for owner in range(tm_count):
            rows_ref[pl.ds(owner * spaced, capacity), :] = arrived[owner][...].astype(jnp.float32)

    def ranges(move):
        for owner in range(tm_count):
            first = owner * spaced + src_ref[plan, owner]
            target = dst_ref[plan, owner]

            def step(index, carry):
                move(first + index * STEP, target + index * STEP)
                return carry

            lax.fori_loop(0, (cnt_ref[plan, owner] + STEP - 1) // STEP, step, 0)

    def collect(first, target):
        obs_ref[pl.ds(target, STEP), :] = rows_ref[pl.ds(first, STEP), :]

    def put_back(first, target):
        back_ref[pl.ds(first, STEP), :] = model_ref[pl.ds(target, STEP), :]

    ranges(collect)
    corr_ref[...] = lax.dot_general(
        obs_ref[:obs, :].astype(jnp.bfloat16), basis_ref[0], (((0,), (0,)), ((), ())),
        preferred_element_type=jnp.float32,
    )
    group = 16
    for start in range(0, width, group):
        at = pl.ds(start, group)
        power = []
        for chunk in range(nper // 128):
            lanes = pl.ds(chunk * 128, 128)
            sines = pl.ds(nper + chunk * 128, 128)
            cosine = corr_ref[at, lanes]
            sine = corr_ref[at, sines]
            power.append(
                cosine * (cosine * norm_ref[0, :, lanes]) + sine * (sine * norm_ref[0, :, sines])
            )
        highest = functools.reduce(jnp.maximum, power)
        highest = jnp.max(highest, axis=1, keepdims=True)
        expo = [jnp.exp(BETA * (value - highest)) for value in power]
        total = jnp.sum(functools.reduce(jnp.add, expo), axis=1, keepdims=True)
        scale = 1.0 / total
        for chunk in range(nper // 128):
            lanes = pl.ds(chunk * 128, 128)
            sines = pl.ds(nper + chunk * 128, 128)
            share = expo[chunk] * scale
            coeff_ref[at, lanes] = (share * (corr_ref[at, lanes] * norm_ref[0, :, lanes])).astype(jnp.bfloat16)
            coeff_ref[at, sines] = (share * (corr_ref[at, sines] * norm_ref[0, :, sines])).astype(jnp.bfloat16)
        score_ref[0, at, :] = BETA * highest + jnp.log(total)
    model_ref[:obs, :] = lax.dot_general(
        basis_ref[0], coeff_ref[...], (((1,), (1,)), ((), ())), preferred_element_type=jnp.float32
    )
    ranges(put_back)

    @pl.when(plan == plans - 1)
    def _():
        for owner in range(tm_count):
            outs[owner][...] = back_ref[pl.ds(owner * spaced, capacity), :].astype(jnp.bfloat16)


def fit_plans(tables, arrived, basis, norms):
    tm_count = len(arrived)
    sched_dev, obs, twice = basis.shape
    capacity, width = arrived[0].shape
    work = sched_dev * obs * twice * width
    spaced = tm_count * (capacity + STEP)
    *models, score = pl.pallas_call(
        functools.partial(fit_kernel, tm_count),
        grid=(sched_dev,),
        in_specs=[SMEM, SMEM, SMEM] + [VMEM] * tm_count + [
            pl.BlockSpec((1, obs, twice), lambda j: (j, 0, 0)),
            pl.BlockSpec((1, 1, twice), lambda j: (j, 0, 0)),
        ],
        out_specs=[VMEM] * tm_count + [pl.BlockSpec((1, width, 1), lambda j: (j, 0, 0))],
        out_shape=[jax.ShapeDtypeStruct((capacity, width), jnp.bfloat16)] * tm_count
        + [jax.ShapeDtypeStruct((sched_dev, width, 1), jnp.float32)],
        scratch_shapes=[
            pltpu.VMEM((spaced, width), jnp.float32),
            pltpu.VMEM((obs + STEP, width), jnp.float32),
            pltpu.VMEM((width, twice), jnp.float32),
            pltpu.VMEM((width, twice), jnp.bfloat16),
            pltpu.VMEM((obs + STEP, width), jnp.float32),
            pltpu.VMEM((spaced, width), jnp.float32),
        ],
        compiler_params=pltpu.CompilerParams(vmem_limit_bytes=VMEM_LIMIT),
        cost_estimate=pl.CostEstimate(flops=4 * work, bytes_accessed=2 * basis.size, transcendentals=0),
    )(*tables, *arrived, basis, norms)
    return models, score


def load_attitude(where_ref, own_ref, passed, whole_ref, sems):
    sky = where_ref[0]
    count = len(passed) // 2 + 1
    rows = own_ref.shape[1]
    copies = [(True, sky, own_ref)]
    for hop in range(1, count):
        copies.append((sky >= hop, sky - hop, passed[2 * hop - 2]))
        copies.append((sky + hop < count, sky + hop, passed[2 * hop - 1]))

    def each(act):
        for index, (valid, quarter, ref) in enumerate(copies):
            def run(index=index, quarter=quarter, ref=ref):
                at = pl.ds(pl.multiple_of(quarter * rows, rows), rows)
                act(pltpu.make_async_copy(ref, whole_ref.at[:, at, :], sems.at[index]))

            if valid is True:
                run()
            else:
                pl.when(valid)(run)

    each(lambda copy: copy.start())
    return lambda: each(lambda copy: copy.wait())


def whiten_and_pick(asked_ref, cnt_ref, count_ref, whole_ref, load, picked, white_ref, gather_ref):
    segs, slots, _ = whole_ref.shape
    capacity, width = picked[0].shape
    blocks = white_ref.shape[0] // (segs * slots)
    row = lax.broadcasted_iota(jnp.int32, (slots, width * blocks), 0)
    for seg in range(segs):
        masked = jnp.where(row < count_ref[seg], load(seg).astype(jnp.float32), 0.0).astype(jnp.bfloat16)
        white = jnp.dot(whole_ref[seg], masked, preferred_element_type=jnp.float32)
        for block in range(blocks):
            white_ref[pl.ds((block * segs + seg) * slots, slots), :] = white[:, block * width:(block + 1) * width]
    for owner, out_ref in enumerate(picked):
        def step(index, carry):
            at = owner * capacity + index * 8
            for lane in range(8):
                gather_ref[pl.ds(at + lane, 1), :] = white_ref[pl.ds(asked_ref[at + lane], 1), :]
            return carry

        lax.fori_loop(0, (cnt_ref[owner] + 7) // 8, step, 0)
        out_ref[...] = gather_ref[pl.ds(owner * capacity, capacity), :].astype(jnp.bfloat16)


def place_rows(asked_ref, cnt_ref, returned, current_ref, out_ref, rows_ref, sums):
    segs, slots, _ = current_ref.shape
    capacity, width = returned[0].shape
    blocks = current_ref.shape[2] // width
    streams = len(sums)
    for total in sums:
        total[...] = jnp.zeros_like(total)
    for owner, ref in enumerate(returned):
        rows_ref[pl.ds(owner * capacity, capacity), :] = ref[...].astype(jnp.float32)

        def step(index, carry):
            first = owner * capacity + index * 8
            for start in range(0, 8, streams):
                rows = [first + start + lane for lane in range(streams)]
                places = [asked_ref[row] for row in rows]
                values = [
                    total[pl.ds(place, 1), :] + rows_ref[pl.ds(row, 1), :]
                    for total, place, row in zip(sums, places, rows)
                ]
                for total, place, value in zip(sums, places, values):
                    total[pl.ds(place, 1), :] = value
            return carry

        lax.fori_loop(0, (cnt_ref[owner] + 7) // 8, step, 0)
    for seg in range(segs):
        for block in range(blocks):
            at = pl.ds((block * segs + seg) * slots, slots)
            lanes = slice(block * width, (block + 1) * width)
            placed = functools.reduce(jnp.add, [total[at, :] for total in sums])
            out_ref[seg, :, lanes] = current_ref[seg, :, lanes].astype(jnp.float32) - placed


def owner_kernel(tm_count, passed_count, placing, picking, *refs):
    refs = list(refs)

    def take(count):
        taken = refs[:count]
        del refs[:count]
        return taken

    asked_ref, cnt_ref, count_ref, where_ref = take(4)
    (current_ref,) = take(1)
    attitude = take(passed_count + 1) if picking else None
    returned = take(tm_count) if placing else None
    out_ref = take(1)[0] if placing else None
    picked = take(tm_count) if picking else None
    wait = None
    if picking:
        whole_ref, sems, white_ref = take(3)
        wait = load_attitude(where_ref, attitude[0], attitude[1:], whole_ref, sems)
    (rows_ref,) = take(1)
    if placing:
        place_rows(asked_ref, cnt_ref, returned, current_ref, out_ref, rows_ref, refs)
    if picking:
        wait()
        source = out_ref if placing else current_ref
        whiten_and_pick(
            asked_ref, cnt_ref, count_ref, whole_ref, lambda seg: source[seg], picked, white_ref, rows_ref
        )


def owner_step(scalars, current, attitude, returned):
    asked, cnt, seg_counts, where = scalars
    seg_dev, slots, width = current.shape
    placing, picking = returned is not None, attitude is not None
    tm_count = cnt.shape[0]
    capacity = asked.shape[0] // tm_count
    table = pltpu.VMEM((seg_dev * slots * width // SRC_GROUP + 8, SRC_GROUP), jnp.float32)
    in_specs = [SMEM] * 4 + [VMEM]
    args = [asked, cnt, seg_counts, where, current]
    out_shape = []
    scratch = []
    if picking:
        in_specs += [pl.BlockSpec(memory_space=pl.ANY)] * len(attitude)
        args += attitude
        scratch += [
            pltpu.VMEM((seg_dev, slots, slots), jnp.bfloat16),
            pltpu.SemaphoreType.DMA((len(attitude),)),
            table,
        ]
    scratch.append(pltpu.VMEM((tm_count * capacity, SRC_GROUP), jnp.float32))
    if placing:
        in_specs += [VMEM] * tm_count
        args += returned
        out_shape.append(jax.ShapeDtypeStruct(current.shape, jnp.float32))
        scratch += [table] * STREAMS
    if picking:
        out_shape += [jax.ShapeDtypeStruct((capacity, SRC_GROUP), jnp.bfloat16)] * tm_count
    passed = len(attitude) - 1 if picking else 0
    out = pl.pallas_call(
        functools.partial(owner_kernel, tm_count, passed, placing, picking),
        in_specs=in_specs,
        out_specs=[VMEM] * len(out_shape),
        out_shape=out_shape,
        scratch_shapes=scratch,
        compiler_params=pltpu.CompilerParams(vmem_limit_bytes=VMEM_LIMIT),
        cost_estimate=pl.CostEstimate(
            flops=2 * seg_dev * slots * slots * width, bytes_accessed=16 << 20, transcendentals=0
        ),
    )(*args)
    if placing:
        return out[0], list(out[1:])
    return current, list(out)


def make_lists(sched_seg, sched_slot, seg_dev, slots, column_blocks, tm_count, capacity):
    sched_dev, obs = sched_seg.shape
    partner = (sched_seg // seg_dev) ^ lax.axis_index("tm")
    block_of = (jnp.arange(sched_dev, dtype=jnp.int32) % column_blocks)[:, None]
    local_row = (block_of * seg_dev + sched_seg % seg_dev) * slots + sched_slot
    hot = (partner[:, :, None] == jnp.arange(tm_count, dtype=jnp.int32)).astype(jnp.int32)
    cnt = jnp.sum(hot, axis=1)
    plans = jnp.arange(sched_dev)
    before = (plans[None, :] < plans[:, None]).astype(jnp.int32)
    src = jnp.sum(before[:, :, None] * cnt[None, :, :], axis=1)
    owners = jnp.arange(tm_count)
    ahead = (owners[None, :] < owners[:, None]).astype(jnp.int32)
    dst = jnp.sum(ahead[None, :, :] * cnt[:, None, :], axis=2)
    entry = jnp.arange(obs)
    rank = jnp.sum(
        ((partner[:, None, :] == partner[:, :, None]) & (entry[None, :] < entry[:, None])).astype(jnp.int32),
        axis=2,
    )
    place = partner * capacity + jnp.sum(hot * src[:, None, :], axis=2) + rank
    order = jnp.sum(hot * dst[:, None, :], axis=2) + rank
    time = sched_seg * slots + sched_slot
    times = jnp.sum(jnp.where(order[:, None, :] == entry[None, :, None], time[:, None, :], 0), axis=2)
    rows = seg_dev * slots * column_blocks
    wanted = rows + jnp.sum(
        jnp.where(
            place.reshape(1, -1) == jnp.arange(tm_count * capacity, dtype=jnp.int32)[:, None],
            local_row.reshape(1, -1) - rows,
            0,
        ),
        axis=1,
    )
    return (cnt, src, dst), times, wanted


def exchange(blocks):
    count = len(blocks)
    return [blocks[0]] + [
        lax.ppermute(blocks[step], "tm", [(i, i ^ step) for i in range(count)]) for step in range(1, count)
    ]


def pass_along(shard):
    count = lax.axis_size("sky")
    right = left = shard
    passed = []
    for hop in range(1, count):
        right = lax.ppermute(right, "sky", [(i, i + 1) for i in range(hop - 1, count - 1)])
        left = lax.ppermute(left, "sky", [(i, i - 1) for i in range(1, count - hop + 1)])
        passed += [right, left]
    return [shard] + passed


def on_device(residuals, seg_counts, attitude, sched_seg, sched_slot, periods):
    tm_count = lax.axis_size("tm")
    sched_dev, obs = sched_seg.shape
    seg_dev, slots, width = residuals.shape
    column_blocks = width // SRC_GROUP
    capacity = 2 * sched_dev * obs // tm_count
    pieces = pass_along(attitude)
    tables, times, wanted = make_lists(
        sched_seg, sched_slot, seg_dev, slots, column_blocks, tm_count, capacity
    )
    wanted = wanted.reshape(tm_count, capacity)
    asked = jnp.concatenate(exchange([wanted[owner] for owner in range(tm_count)]))
    cnt = jnp.sum((asked.reshape(tm_count, capacity) < seg_dev * slots * column_blocks).astype(jnp.int32), axis=1)
    basis, norms = make_basis(times, periods)
    scalars = (asked, cnt, seg_counts, lax.axis_index("sky").reshape(1))

    current, returned = residuals, None
    for iteration in range(ITERS):
        current, picked = owner_step(scalars, current, pieces, returned)
        models, score = fit_plans(tables, exchange(picked), basis, norms)
        returned = exchange(models)
    current, _ = owner_step(scalars, current, None, returned)
    return (current, score.reshape(sched_dev, SRC_GROUP))


def solution(mesh):
    in_specs = (
        P("tm", None, "sky"),
        P("tm"),
        P("tm", "sky", None),
        P(("tm", "sky"), None),
        P(("tm", "sky"), None),
        P(),
    )
    out_specs = (P("tm", None, "sky"), P(("tm", "sky"), None))
    return jax.shard_map(
        on_device, mesh=mesh, in_specs=in_specs, out_specs=out_specs, check_vma=False
    )
```

```python
import functools

import jax
import jax.numpy as jnp
from jax import lax
from jax.experimental import pallas as pl
from jax.experimental.pallas import tpu as pltpu
from jax.sharding import PartitionSpec as P

SRC_GROUP = 128
ITERS = 2
STREAMS = 4
STEP = 16
BETA = 2.0
RIDGE = 1.0
VMEM_LIMIT = 36 * 1024 * 1024
BASIS_CALLS = 4
CHUNKS = 2
UNROLL = 16

COS_POLY = (1.0, -19.73920440673828, 64.9391098022461, -85.4500503540039, 60.16689682006836,
            -25.96480369567871, 6.52468729019165)
SIN_POLY = (6.283185005187988, -41.34158706665039, 81.59986114501953, -76.61351013183594,
            41.33811950683594, -12.463061332702637)

VMEM = pl.BlockSpec(memory_space=pltpu.VMEM)
SMEM = pl.BlockSpec(memory_space=pltpu.SMEM)


def horner(poly, v):
    acc = jnp.full_like(v, poly[-1])
    for term in poly[-2::-1]:
        acc = acc * v + term
    return acc


def basis_kernel(time_ref, period_ref, inverse_ref, basis_ref, norm_ref):
    obs = time_ref.shape[0]
    nper = period_ref.shape[1]
    rows = 32
    for chunk in range(nper // 128):
        lanes = pl.ds(chunk * 128, 128)
        sines = pl.ds(nper + chunk * 128, 128)
        period = period_ref[:, lanes]
        inverse = inverse_ref[:, lanes]

        def step(index, sums):
            at = pl.ds(pl.multiple_of(index * rows, rows), rows)
            time = time_ref[at, :]
            turns = jnp.round(time * inverse)
            part = (time - turns * period) * inverse
            square = part * part
            cosine = horner(COS_POLY, square).astype(jnp.bfloat16)
            sine = (horner(SIN_POLY, square) * part).astype(jnp.bfloat16)
            basis_ref[0, at, lanes] = cosine
            basis_ref[0, at, sines] = sine
            cosine = cosine.astype(jnp.float32)
            sine = sine.astype(jnp.float32)
            return (
                sums[0] + jnp.sum((cosine * cosine).reshape(rows // 8, 8, 128), axis=0),
                sums[1] + jnp.sum((sine * sine).reshape(rows // 8, 8, 128), axis=0),
            )

        zero = jnp.zeros((8, 128), jnp.float32)
        total_c, total_s = lax.fori_loop(0, obs // rows, step, (zero, zero))
        norm_ref[0, :, lanes] = 1.0 / (jnp.sum(total_c, axis=0, keepdims=True) + RIDGE)
        norm_ref[0, :, sines] = 1.0 / (jnp.sum(total_s, axis=0, keepdims=True) + RIDGE)


def make_basis(times, periods):
    sched_dev, obs = times.shape
    nper = periods.shape[0]
    wide = jnp.broadcast_to(
        times.astype(jnp.float32).reshape(-1, 1), (sched_dev * obs, SRC_GROUP)
    )
    period = periods.astype(jnp.float32)[None, :]
    return pl.pallas_call(
        basis_kernel,
        grid=(sched_dev,),
        in_specs=[
            pl.BlockSpec((obs, SRC_GROUP), lambda j: (j, 0)),
            pl.BlockSpec((1, nper), lambda j: (0, 0)),
            pl.BlockSpec((1, nper), lambda j: (0, 0)),
        ],
        out_specs=[
            pl.BlockSpec((1, obs, 2 * nper), lambda j: (j, 0, 0)),
            pl.BlockSpec((1, 1, 2 * nper), lambda j: (j, 0, 0)),
        ],
        out_shape=[
            jax.ShapeDtypeStruct((sched_dev, obs, 2 * nper), jnp.bfloat16),
            jax.ShapeDtypeStruct((sched_dev, 1, 2 * nper), jnp.float32),
        ],
        compiler_params=pltpu.CompilerParams(vmem_limit_bytes=VMEM_LIMIT),
        cost_estimate=pl.CostEstimate(
            flops=sched_dev * obs * nper * 10000, bytes_accessed=sched_dev * obs * nper * 4, transcendentals=0
        ),
    )(wide, period, 1.0 / period)


def fit_kernel(tm_count, src_ref, dst_ref, *refs):
    refs = list(refs)

    def take(count):
        taken = refs[:count]
        del refs[:count]
        return taken

    arrived = take(tm_count)
    parts = take(BASIS_CALLS)
    (norm_ref,) = take(1)
    outs = take(tm_count)
    score_ref, basis_ref, sems, rows_ref, back_ref = take(5)
    slots = [take(4), take(4)]
    plans, obs, twice = basis_ref.shape
    nper = twice // 2
    capacity, width = arrived[0].shape
    spaced = capacity + STEP
    steps = src_ref.shape[1]
    each = plans // len(parts)

    def basis_copy(plan):
        return pltpu.make_async_copy(parts[plan // each].at[plan % each], basis_ref.at[plan], sems.at[plan])

    for plan in range(plans):
        basis_copy(plan).start()
    for owner in range(tm_count):
        rows_ref[pl.ds(owner * spaced, capacity), :] = arrived[owner][...].astype(jnp.float32)

    def correlate(plan, obs_ref, corr_ref):
        for step in range(steps):
            obs_ref[pl.ds(dst_ref[plan, step], STEP), :] = rows_ref[pl.ds(src_ref[plan, step], STEP), :]
        corr_ref[...] = lax.dot_general(
            obs_ref[:obs, :].astype(jnp.bfloat16), basis_ref[plan], (((0,), (0,)), ((), ())),
            preferred_element_type=jnp.float32,
        )

    def finish(plan, corr_ref, coeff_ref, model_ref):
        group = 16
        for start in range(0, width, group):
            at = pl.ds(start, group)
            power = []
            for chunk in range(nper // 128):
                lanes = pl.ds(chunk * 128, 128)
                sines = pl.ds(nper + chunk * 128, 128)
                cosine = corr_ref[at, lanes]
                sine = corr_ref[at, sines]
                power.append(
                    cosine * (cosine * norm_ref[plan, :, lanes]) + sine * (sine * norm_ref[plan, :, sines])
                )
            highest = functools.reduce(jnp.maximum, power)
            highest = jnp.max(highest, axis=1, keepdims=True)
            expo = [jnp.exp(BETA * (value - highest)) for value in power]
            total = jnp.sum(functools.reduce(jnp.add, expo), axis=1, keepdims=True)
            scale = 1.0 / total
            for chunk in range(nper // 128):
                lanes = pl.ds(chunk * 128, 128)
                sines = pl.ds(nper + chunk * 128, 128)
                share = expo[chunk] * scale
                coeff_ref[at, lanes] = (share * (corr_ref[at, lanes] * norm_ref[plan, :, lanes])).astype(jnp.bfloat16)
                coeff_ref[at, sines] = (share * (corr_ref[at, sines] * norm_ref[plan, :, sines])).astype(jnp.bfloat16)
            score_ref[plan, at, :] = BETA * highest + jnp.log(total)
        model_ref[:obs, :] = lax.dot_general(
            basis_ref[plan], coeff_ref[...], (((1,), (1,)), ((), ())), preferred_element_type=jnp.float32
        )
        for step in range(steps):
            back_ref[pl.ds(src_ref[plan, step], STEP), :] = model_ref[pl.ds(dst_ref[plan, step], STEP), :]

    basis_copy(0).wait()
    correlate(0, slots[0][0], slots[0][1])

    def pair(index, carry):
        plan = index * 2
        for ahead in (1, 2):
            for known in range(ahead, plans, 2):
                pl.when(plan + ahead == known)(basis_copy(known).wait)
        correlate(plan + 1, slots[1][0], slots[1][1])
        finish(plan, *slots[0][1:])
        correlate(jnp.minimum(plan + 2, plans - 1), slots[0][0], slots[0][1])
        finish(plan + 1, *slots[1][1:])
        return carry

    lax.fori_loop(0, plans // 2, pair, 0)
    for owner in range(tm_count):
        outs[owner][...] = back_ref[pl.ds(owner * spaced, capacity), :].astype(jnp.bfloat16)


def fit_plans(tables, arrived, parts, norms):
    tm_count = len(arrived)
    each, obs, twice = parts[0].shape
    sched_dev = each * len(parts)
    capacity, width = arrived[0].shape
    work = sched_dev * obs * twice * width
    spaced = tm_count * (capacity + STEP) + STEP
    slot = [
        pltpu.VMEM((obs + STEP, width), jnp.float32),
        pltpu.VMEM((width, twice), jnp.float32),
        pltpu.VMEM((width, twice), jnp.bfloat16),
        pltpu.VMEM((obs + STEP, width), jnp.float32),
    ]
    *models, score = pl.pallas_call(
        functools.partial(fit_kernel, tm_count),
        in_specs=[SMEM, SMEM] + [VMEM] * tm_count + [pl.BlockSpec(memory_space=pl.ANY)] * len(parts) + [VMEM],
        out_specs=[VMEM] * (tm_count + 1),
        out_shape=[jax.ShapeDtypeStruct((capacity, width), jnp.bfloat16)] * tm_count
        + [jax.ShapeDtypeStruct((sched_dev, width, 1), jnp.float32)],
        scratch_shapes=[
            pltpu.VMEM((sched_dev, obs, twice), jnp.bfloat16),
            pltpu.SemaphoreType.DMA((sched_dev,)),
            pltpu.VMEM((spaced, width), jnp.float32),
            pltpu.VMEM((spaced, width), jnp.float32),
        ] + slot + slot,
        compiler_params=pltpu.CompilerParams(vmem_limit_bytes=VMEM_LIMIT),
        cost_estimate=pl.CostEstimate(flops=20 * work, bytes_accessed=sched_dev * obs * twice * 2, transcendentals=0),
    )(*tables, *arrived, *parts, norms)
    return models, score


def load_attitude(sky, own_ref, chunks, whole_ref, sems):
    rows = own_ref.shape[1]
    copies = [(None, sky, slice(None), own_ref)]
    for index, passed in enumerate(chunks):
        count = len(passed) // 2 + 1
        segs = passed[0].shape[0]
        held = pl.ds(index * segs, segs)
        for hop in range(1, count):
            copies.append((sky >= hop, sky - hop, held, passed[2 * hop - 2]))
            copies.append((sky + hop < count, sky + hop, held, passed[2 * hop - 1]))

    def each(act):
        for index, (valid, quarter, held, ref) in enumerate(copies):
            def run(index=index, quarter=quarter, held=held, ref=ref):
                at = pl.ds(pl.multiple_of(quarter * rows, rows), rows)
                act(pltpu.make_async_copy(ref, whole_ref.at[held, at, :], sems.at[index]))

            if valid is None:
                run()
            else:
                pl.when(valid)(run)

    each(lambda copy: copy.start())
    return lambda: each(lambda copy: copy.wait())


def whiten_and_pick(me, asked_ref, cnt_ref, count_ref, whole_ref, load, picked, white_ref, gather_ref):
    segs, slots, _ = whole_ref.shape
    capacity, width = picked[0].shape
    blocks = white_ref.shape[0] // (segs * slots)
    row = lax.broadcasted_iota(jnp.int32, (slots, width * blocks), 0)
    for seg in range(segs):
        masked = jnp.where(row < count_ref[seg], load(seg).astype(jnp.float32), 0.0).astype(jnp.bfloat16)
        white = jnp.dot(whole_ref[seg], masked, preferred_element_type=jnp.float32)
        for block in range(blocks):
            white_ref[pl.ds((block * segs + seg) * slots, slots), :] = white[:, block * width:(block + 1) * width]
    for owner, out_ref in enumerate(picked):
        asker = owner ^ me

        def step(index, carry):
            first = index * UNROLL
            for lane in range(UNROLL):
                gather_ref[pl.ds(owner * capacity + first + lane, 1), :] = white_ref[
                    pl.ds(asked_ref[asker * capacity + first + lane], 1), :
                ]
            return carry

        lax.fori_loop(0, (cnt_ref[asker] + UNROLL - 1) // UNROLL, step, 0)
        out_ref[...] = gather_ref[pl.ds(owner * capacity, capacity), :].astype(jnp.bfloat16)


def place_rows(me, asked_ref, cnt_ref, returned, current_ref, out_ref, rows_ref, sums):
    segs, slots, _ = current_ref.shape
    capacity, width = returned[0].shape
    blocks = current_ref.shape[2] // width
    streams = len(sums)
    for total in sums:
        total[...] = jnp.zeros_like(total)
    for owner, ref in enumerate(returned):
        rows_ref[pl.ds(owner * capacity, capacity), :] = ref[...].astype(jnp.float32)

        asker = owner ^ me

        def step(index, carry):
            first = index * UNROLL
            for start in range(0, UNROLL, streams):
                lanes = [first + start + lane for lane in range(streams)]
                places = [asked_ref[asker * capacity + lane] for lane in lanes]
                values = [
                    total[pl.ds(place, 1), :] + rows_ref[pl.ds(owner * capacity + lane, 1), :]
                    for total, place, lane in zip(sums, places, lanes)
                ]
                for total, place, value in zip(sums, places, values):
                    total[pl.ds(place, 1), :] = value
            return carry

        lax.fori_loop(0, (cnt_ref[asker] + UNROLL - 1) // UNROLL, step, 0)
    for seg in range(segs):
        for block in range(blocks):
            at = pl.ds((block * segs + seg) * slots, slots)
            lanes = slice(block * width, (block + 1) * width)
            placed = functools.reduce(jnp.add, [total[at, :] for total in sums])
            out_ref[seg, :, lanes] = current_ref[seg, :, lanes].astype(jnp.float32) - placed


def owner_kernel(tm_count, chunk_counts, placing, *refs):
    refs = list(refs)

    def take(count):
        taken = refs[:count]
        del refs[:count]
        return taken

    asked_ref, cnt_ref, count_ref, where_ref, _, current_ref = take(6)
    me, sky = where_ref[0], where_ref[1]
    picking = chunk_counts is not None
    if picking:
        (own_ref,) = take(1)
        chunks = [take(count) for count in chunk_counts]
    returned = take(tm_count) if placing else None
    out_ref = take(1)[0] if placing else None
    picked = take(tm_count) if picking else None
    if picking:
        whole_ref, sems, white_ref = take(3)
        wait = load_attitude(sky, own_ref, chunks, whole_ref, sems)
    (rows_ref,) = take(1)
    if placing:
        place_rows(me, asked_ref, cnt_ref, returned, current_ref, out_ref, rows_ref, refs)
    if picking:
        wait()
        source = out_ref if placing else current_ref
        whiten_and_pick(
            me, asked_ref, cnt_ref, count_ref, whole_ref, lambda seg: source[seg], picked, white_ref, rows_ref
        )


def owner_step(scalars, norms, current, attitude, returned):
    asked, cnt, seg_counts, where = scalars
    seg_dev, slots, width = current.shape
    placing, picking = returned is not None, attitude is not None
    tm_count = cnt.shape[0]
    capacity = asked.shape[0] // tm_count
    table = pltpu.VMEM((seg_dev * slots * width // SRC_GROUP + 8, SRC_GROUP), jnp.float32)
    anywhere = pl.BlockSpec(memory_space=pl.ANY)
    in_specs = [SMEM] * 4 + [anywhere, VMEM]
    args = [asked, cnt, seg_counts, where, norms, current]
    out_shape = []
    scratch = []
    counts = None
    if picking:
        own, chunks = attitude
        counts = [len(chunk) for chunk in chunks]
        args += [own] + [piece for chunk in chunks for piece in chunk]
        in_specs += [anywhere] * (1 + sum(counts))
        scratch += [
            pltpu.VMEM((seg_dev, slots, slots), jnp.bfloat16),
            pltpu.SemaphoreType.DMA((1 + sum(counts),)),
            table,
        ]
    scratch.append(pltpu.VMEM((tm_count * capacity, SRC_GROUP), jnp.float32))
    if placing:
        in_specs += [VMEM] * tm_count
        args += returned
        out_shape.append(jax.ShapeDtypeStruct(current.shape, jnp.float32))
        scratch += [table] * STREAMS
    if picking:
        out_shape += [jax.ShapeDtypeStruct((capacity, SRC_GROUP), jnp.bfloat16)] * tm_count
    out = pl.pallas_call(
        functools.partial(owner_kernel, tm_count, counts, placing),
        in_specs=in_specs,
        out_specs=[VMEM] * len(out_shape),
        out_shape=out_shape,
        scratch_shapes=scratch,
        compiler_params=pltpu.CompilerParams(vmem_limit_bytes=VMEM_LIMIT),
        cost_estimate=pl.CostEstimate(
            flops=16 * seg_dev * slots * slots * width, bytes_accessed=16 << 20, transcendentals=0
        ),
    )(*args)
    if placing:
        return out[0], list(out[1:])
    return current, list(out)


def make_lists(sched_seg, sched_slot, seg_dev, slots, column_blocks, tm_count, capacity):
    sched_dev, obs = sched_seg.shape
    me = lax.axis_index("tm")
    owner = sched_seg // seg_dev
    partner = owner ^ me
    block_of = (jnp.arange(sched_dev, dtype=jnp.int32) % column_blocks)[:, None]
    local_row = (block_of * seg_dev + sched_seg % seg_dev) * slots + sched_slot
    hot = (partner[:, :, None] == jnp.arange(tm_count, dtype=jnp.int32)).astype(jnp.int32)
    cnt = jnp.sum(hot, axis=1)
    plans = jnp.arange(sched_dev)
    before = (plans[None, :] < plans[:, None]).astype(jnp.int32)
    src = jnp.sum(before[:, :, None] * cnt[None, :, :], axis=1)
    owners = jnp.arange(tm_count)
    ahead = (owners[None, :] < owners[:, None]).astype(jnp.int32)
    dst = jnp.sum(ahead[None, :, :] * cnt[:, None, :], axis=2)
    entry = jnp.arange(obs)
    rank = jnp.sum(
        ((partner[:, None, :] == partner[:, :, None]) & (entry[None, :] < entry[:, None])).astype(jnp.int32),
        axis=2,
    )
    place = owner * capacity + jnp.sum(hot * src[:, None, :], axis=2) + rank
    order = jnp.sum(hot * dst[:, None, :], axis=2) + rank
    time = sched_seg * slots + sched_slot
    times = jnp.sum(jnp.where(order[:, None, :] == entry[None, :, None], time[:, None, :], 0), axis=2)
    rows = seg_dev * slots * column_blocks
    wanted = rows + jnp.sum(
        jnp.where(
            place.reshape(1, -1) == jnp.arange(tm_count * capacity, dtype=jnp.int32)[:, None],
            local_row.reshape(1, -1) - rows,
            0,
        ),
        axis=1,
    )
    step_count = (cnt + STEP - 1) // STEP
    step_first = jnp.sum(ahead[None, :, :] * step_count[:, None, :], axis=2)
    step = jnp.arange(obs // STEP + tm_count)[None, :, None] - step_first[:, None, :]
    inside = (step >= 0) & (step < step_count[:, None, :])
    spaced = capacity + STEP
    end = tm_count * spaced
    step_src = end + jnp.sum(
        jnp.where(inside, owners * spaced - end + src[:, None, :] + step * STEP, 0), axis=2
    )
    step_dst = obs + jnp.sum(jnp.where(inside, dst[:, None, :] + step * STEP - obs, 0), axis=2)
    return (step_src, step_dst), times, wanted


def exchange(blocks):
    count = len(blocks)
    out = list(blocks)
    for step in sorted(range(1, count), key=lambda step: -bin(step // 2).count("1")):
        out[step] = lax.ppermute(blocks[step], "tm", [(i, i ^ step) for i in range(count)])
    return out


def pass_along(attitude):
    count = lax.axis_size("sky")
    part = attitude.shape[0] // CHUNKS
    right = [attitude[index * part:(index + 1) * part] for index in range(CHUNKS)]
    left = list(right)
    chunks = [[] for _ in range(CHUNKS)]
    for hop in range(1, count):
        for index in range(CHUNKS):
            right[index] = lax.ppermute(right[index], "sky", [(i, i + 1) for i in range(hop - 1, count - 1)])
            left[index] = lax.ppermute(left[index], "sky", [(i, i - 1) for i in range(1, count - hop + 1)])
            chunks[index] += [right[index], left[index]]
    return attitude, chunks


def on_device(residuals, seg_counts, attitude, sched_seg, sched_slot, periods):
    tm_count = lax.axis_size("tm")
    sched_dev, obs = sched_seg.shape
    seg_dev, slots, width = residuals.shape
    column_blocks = width // SRC_GROUP
    capacity = 2 * sched_dev * obs // tm_count
    pieces = pass_along(attitude)
    tables, times, wanted = make_lists(
        sched_seg, sched_slot, seg_dev, slots, column_blocks, tm_count, capacity
    )
    asked = lax.all_to_all(wanted.reshape(tm_count, capacity), "tm", split_axis=0, concat_axis=0, tiled=True)
    cnt = jnp.sum((asked < seg_dev * slots * column_blocks).astype(jnp.int32), axis=1)
    part = sched_dev // BASIS_CALLS
    parts, norms = zip(
        *[make_basis(times[index * part:(index + 1) * part], periods) for index in range(BASIS_CALLS)]
    )
    norms = jnp.concatenate(norms)
    where = jnp.stack([lax.axis_index("tm"), lax.axis_index("sky")])
    scalars = (asked.reshape(-1), cnt, seg_counts, where)

    current, returned = residuals, None
    for iteration in range(ITERS):
        current, picked = owner_step(scalars, norms, current, pieces, returned)
        models, score = fit_plans(tables, exchange(picked), parts, norms)
        returned = exchange(models)
    current, _ = owner_step(scalars, norms, current, None, returned)
    return (current, score.reshape(sched_dev, SRC_GROUP))


def solution(mesh):
    in_specs = (
        P("tm", None, "sky"),
        P("tm"),
        P("tm", "sky", None),
        P(("tm", "sky"), None),
        P(("tm", "sky"), None),
        P(),
    )
    out_specs = (P("tm", None, "sky"), P(("tm", "sky"), None))
    return jax.shard_map(
        on_device, mesh=mesh, in_specs=in_specs, out_specs=out_specs, check_vma=False
    )
```

```python
import functools

import jax
import jax.numpy as jnp
from jax import lax
from jax.experimental import pallas as pl
from jax.experimental.pallas import tpu as pltpu
from jax.sharding import PartitionSpec as P

SRC_GROUP = 128
ITERS = 2
STREAMS = 4
STEP = 16
BETA = 2.0
RIDGE = 1.0
VMEM_LIMIT = 24 * 1024 * 1024
BASIS_CALLS = 2
UNROLL = 16

COS_POLY = (1.0, -19.73920440673828, 64.9391098022461, -85.4500503540039, 60.16689682006836,
            -25.96480369567871, 6.52468729019165)
SIN_POLY = (6.283185005187988, -41.34158706665039, 81.59986114501953, -76.61351013183594,
            41.33811950683594, -12.463061332702637)

VMEM = pl.BlockSpec(memory_space=pltpu.VMEM)
SMEM = pl.BlockSpec(memory_space=pltpu.SMEM)


def horner(poly, v):
    acc = jnp.full_like(v, poly[-1])
    for term in poly[-2::-1]:
        acc = acc * v + term
    return acc


def basis_kernel(after, time_ref, period_ref, inverse_ref, *refs):
    basis_ref, norm_ref = refs[after:]
    obs = time_ref.shape[0]
    nper = period_ref.shape[1]
    rows = 32
    for chunk in range(nper // 128):
        lanes = pl.ds(chunk * 128, 128)
        sines = pl.ds(nper + chunk * 128, 128)
        period = period_ref[:, lanes]
        inverse = inverse_ref[:, lanes]

        def step(index, sums):
            at = pl.ds(pl.multiple_of(index * rows, rows), rows)
            time = time_ref[at, :]
            turns = jnp.round(time * inverse)
            part = (time - turns * period) * inverse
            square = part * part
            cosine = horner(COS_POLY, square).astype(jnp.bfloat16)
            sine = (horner(SIN_POLY, square) * part).astype(jnp.bfloat16)
            basis_ref[0, at, lanes] = cosine
            basis_ref[0, at, sines] = sine
            cosine = cosine.astype(jnp.float32)
            sine = sine.astype(jnp.float32)
            return (
                sums[0] + jnp.sum((cosine * cosine).reshape(rows // 8, 8, 128), axis=0),
                sums[1] + jnp.sum((sine * sine).reshape(rows // 8, 8, 128), axis=0),
            )

        zero = jnp.zeros((8, 128), jnp.float32)
        total_c, total_s = lax.fori_loop(0, obs // rows, step, (zero, zero))
        norm_ref[0, :, lanes] = 1.0 / (jnp.sum(total_c, axis=0, keepdims=True) + RIDGE)
        norm_ref[0, :, sines] = 1.0 / (jnp.sum(total_s, axis=0, keepdims=True) + RIDGE)


def make_basis(times, periods, after):
    sched_dev, obs = times.shape
    nper = periods.shape[0]
    wide = jnp.broadcast_to(
        times.astype(jnp.float32).reshape(-1, 1), (sched_dev * obs, SRC_GROUP)
    )
    period = periods.astype(jnp.float32)[None, :]
    return pl.pallas_call(
        functools.partial(basis_kernel, len(after)),
        grid=(sched_dev,),
        in_specs=[
            pl.BlockSpec((obs, SRC_GROUP), lambda j: (j, 0)),
            pl.BlockSpec((1, nper), lambda j: (0, 0)),
            pl.BlockSpec((1, nper), lambda j: (0, 0)),
        ] + [pl.BlockSpec(memory_space=pl.ANY)] * len(after),
        out_specs=[
            pl.BlockSpec((1, obs, 2 * nper), lambda j: (j, 0, 0)),
            pl.BlockSpec((1, 1, 2 * nper), lambda j: (j, 0, 0)),
        ],
        out_shape=[
            jax.ShapeDtypeStruct((sched_dev, obs, 2 * nper), jnp.bfloat16),
            jax.ShapeDtypeStruct((sched_dev, 1, 2 * nper), jnp.float32),
        ],
        compiler_params=pltpu.CompilerParams(vmem_limit_bytes=VMEM_LIMIT),
        cost_estimate=pl.CostEstimate(
            flops=sched_dev * obs * nper * 10000, bytes_accessed=sched_dev * obs * nper * 4, transcendentals=0
        ),
    )(wide, period, 1.0 / period, *after)


def fit_kernel(tm_count, src_ref, dst_ref, *refs):
    refs = list(refs)

    def take(count):
        taken = refs[:count]
        del refs[:count]
        return taken

    arrived = take(tm_count)
    parts = take(BASIS_CALLS)
    (norm_ref,) = take(1)
    outs = take(tm_count)
    score_ref, basis_ref, sems, rows_ref, back_ref = take(5)
    slots = [take(4), take(4)]
    plans, obs, twice = basis_ref.shape
    nper = twice // 2
    capacity, width = arrived[0].shape
    spaced = capacity + STEP
    steps = src_ref.shape[1]
    each = plans // len(parts)

    def basis_copy(plan):
        return pltpu.make_async_copy(parts[plan // each].at[plan % each], basis_ref.at[plan], sems.at[plan])

    for plan in range(plans):
        basis_copy(plan).start()
    for owner in range(tm_count):
        rows_ref[pl.ds(owner * spaced, capacity), :] = arrived[owner][...].astype(jnp.float32)

    def correlate(plan, obs_ref, corr_ref):
        for step in range(steps):
            obs_ref[pl.ds(dst_ref[plan, step], STEP), :] = rows_ref[pl.ds(src_ref[plan, step], STEP), :]
        corr_ref[...] = lax.dot_general(
            obs_ref[:obs, :].astype(jnp.bfloat16), basis_ref[plan], (((0,), (0,)), ((), ())),
            preferred_element_type=jnp.float32,
        )

    def finish(plan, corr_ref, coeff_ref, model_ref):
        group = 16
        for start in range(0, width, group):
            at = pl.ds(start, group)
            power = []
            for chunk in range(nper // 128):
                lanes = pl.ds(chunk * 128, 128)
                sines = pl.ds(nper + chunk * 128, 128)
                cosine = corr_ref[at, lanes]
                sine = corr_ref[at, sines]
                power.append(
                    cosine * (cosine * norm_ref[plan, :, lanes]) + sine * (sine * norm_ref[plan, :, sines])
                )
            highest = functools.reduce(jnp.maximum, power)
            highest = jnp.max(highest, axis=1, keepdims=True)
            expo = [jnp.exp(BETA * (value - highest)) for value in power]
            total = jnp.sum(functools.reduce(jnp.add, expo), axis=1, keepdims=True)
            scale = 1.0 / total
            for chunk in range(nper // 128):
                lanes = pl.ds(chunk * 128, 128)
                sines = pl.ds(nper + chunk * 128, 128)
                share = expo[chunk] * scale
                coeff_ref[at, lanes] = (share * (corr_ref[at, lanes] * norm_ref[plan, :, lanes])).astype(jnp.bfloat16)
                coeff_ref[at, sines] = (share * (corr_ref[at, sines] * norm_ref[plan, :, sines])).astype(jnp.bfloat16)
            score_ref[plan, at, :] = BETA * highest + jnp.log(total)
        model_ref[:obs, :] = lax.dot_general(
            basis_ref[plan], coeff_ref[...], (((1,), (1,)), ((), ())), preferred_element_type=jnp.float32
        )
        for step in range(steps):
            back_ref[pl.ds(src_ref[plan, step], STEP), :] = model_ref[pl.ds(dst_ref[plan, step], STEP), :]

    basis_copy(0).wait()
    correlate(0, slots[0][0], slots[0][1])

    def pair(index, carry):
        plan = index * 2
        for ahead in (1, 2):
            for known in range(ahead, plans, 2):
                pl.when(plan + ahead == known)(basis_copy(known).wait)
        correlate(plan + 1, slots[1][0], slots[1][1])
        finish(plan, *slots[0][1:])
        correlate(jnp.minimum(plan + 2, plans - 1), slots[0][0], slots[0][1])
        finish(plan + 1, *slots[1][1:])
        return carry

    lax.fori_loop(0, plans // 2, pair, 0)
    for owner in range(tm_count):
        outs[owner][...] = back_ref[pl.ds(owner * spaced, capacity), :].astype(jnp.bfloat16)


def fit_plans(tables, arrived, parts, norms):
    tm_count = len(arrived)
    each, obs, twice = parts[0].shape
    sched_dev = each * len(parts)
    capacity, width = arrived[0].shape
    work = sched_dev * obs * twice * width
    spaced = tm_count * (capacity + STEP) + STEP
    slot = [
        pltpu.VMEM((obs + STEP, width), jnp.float32),
        pltpu.VMEM((width, twice), jnp.float32),
        pltpu.VMEM((width, twice), jnp.bfloat16),
        pltpu.VMEM((obs + STEP, width), jnp.float32),
    ]
    *models, score = pl.pallas_call(
        functools.partial(fit_kernel, tm_count),
        in_specs=[SMEM, SMEM] + [VMEM] * tm_count + [pl.BlockSpec(memory_space=pl.ANY)] * len(parts) + [VMEM],
        out_specs=[VMEM] * (tm_count + 1),
        out_shape=[jax.ShapeDtypeStruct((capacity, width), jnp.bfloat16)] * tm_count
        + [jax.ShapeDtypeStruct((sched_dev, width, 1), jnp.float32)],
        scratch_shapes=[
            pltpu.VMEM((sched_dev, obs, twice), jnp.bfloat16),
            pltpu.SemaphoreType.DMA((sched_dev,)),
            pltpu.VMEM((spaced, width), jnp.float32),
            pltpu.VMEM((spaced, width), jnp.float32),
        ] + slot + slot,
        compiler_params=pltpu.CompilerParams(vmem_limit_bytes=VMEM_LIMIT),
        cost_estimate=pl.CostEstimate(flops=20 * work, bytes_accessed=sched_dev * obs * twice * 2, transcendentals=0),
    )(*tables, *arrived, *parts, norms)
    return models, score


def load_attitude(sky, own_ref, passed, whole_ref, sems):
    rows = own_ref.shape[1]
    count = len(passed) // 2 + 1
    copies = [(None, sky, own_ref)]
    for hop in range(1, count):
        copies.append((sky >= hop, sky - hop, passed[2 * hop - 2]))
        copies.append((sky + hop < count, sky + hop, passed[2 * hop - 1]))

    def each(act):
        for index, (valid, quarter, ref) in enumerate(copies):
            def run(index=index, quarter=quarter, ref=ref):
                at = pl.ds(pl.multiple_of(quarter * rows, rows), rows)
                act(pltpu.make_async_copy(ref, whole_ref.at[:, at, :], sems.at[index]))

            if valid is None:
                run()
            else:
                pl.when(valid)(run)

    each(lambda copy: copy.start())
    return lambda: each(lambda copy: copy.wait())


def whiten_and_pick(me, asked_ref, cnt_ref, count_ref, whole_ref, load, picked, white_ref, gather_ref):
    segs, slots, _ = whole_ref.shape
    capacity, width = picked[0].shape
    blocks = white_ref.shape[0] // (segs * slots)
    row = lax.broadcasted_iota(jnp.int32, (slots, width * blocks), 0)
    for seg in range(segs):
        masked = jnp.where(row < count_ref[seg], load(seg).astype(jnp.float32), 0.0).astype(jnp.bfloat16)
        white = jnp.dot(whole_ref[seg], masked, preferred_element_type=jnp.float32)
        for block in range(blocks):
            white_ref[pl.ds((block * segs + seg) * slots, slots), :] = white[:, block * width:(block + 1) * width]
    for owner, out_ref in enumerate(picked):
        asker = owner ^ me

        def step(index, carry):
            first = index * UNROLL
            for lane in range(UNROLL):
                gather_ref[pl.ds(owner * capacity + first + lane, 1), :] = white_ref[
                    pl.ds(asked_ref[asker * capacity + first + lane], 1), :
                ]
            return carry

        lax.fori_loop(0, (cnt_ref[asker] + UNROLL - 1) // UNROLL, step, 0)
        out_ref[...] = gather_ref[pl.ds(owner * capacity, capacity), :].astype(jnp.bfloat16)


def place_rows(me, asked_ref, cnt_ref, returned, current_ref, out_ref, rows_ref, sums):
    segs, slots, _ = current_ref.shape
    capacity, width = returned[0].shape
    blocks = current_ref.shape[2] // width
    streams = len(sums)
    for total in sums:
        total[...] = jnp.zeros_like(total)
    for owner, ref in enumerate(returned):
        rows_ref[pl.ds(owner * capacity, capacity), :] = ref[...].astype(jnp.float32)

        asker = owner ^ me

        def step(index, carry):
            first = index * UNROLL
            for start in range(0, UNROLL, streams):
                lanes = [first + start + lane for lane in range(streams)]
                places = [asked_ref[asker * capacity + lane] for lane in lanes]
                values = [
                    total[pl.ds(place, 1), :] + rows_ref[pl.ds(owner * capacity + lane, 1), :]
                    for total, place, lane in zip(sums, places, lanes)
                ]
                for total, place, value in zip(sums, places, values):
                    total[pl.ds(place, 1), :] = value
            return carry

        lax.fori_loop(0, (cnt_ref[asker] + UNROLL - 1) // UNROLL, step, 0)
    for seg in range(segs):
        for block in range(blocks):
            at = pl.ds((block * segs + seg) * slots, slots)
            lanes = slice(block * width, (block + 1) * width)
            placed = functools.reduce(jnp.add, [total[at, :] for total in sums])
            out_ref[seg, :, lanes] = current_ref[seg, :, lanes].astype(jnp.float32) - placed


def owner_kernel(tm_count, passed_count, placing, *refs):
    refs = list(refs)

    def take(count):
        taken = refs[:count]
        del refs[:count]
        return taken

    asked_ref, cnt_ref, count_ref, where_ref, _, current_ref = take(6)
    me, sky = where_ref[0], where_ref[1]
    picking = passed_count > 0
    if picking:
        (own_ref,) = take(1)
        passed = take(passed_count)
    returned = take(tm_count) if placing else None
    out_ref = take(1)[0] if placing else None
    picked = take(tm_count) if picking else None
    if picking:
        whole_ref, sems, white_ref = take(3)
        wait = load_attitude(sky, own_ref, passed, whole_ref, sems)
    (rows_ref,) = take(1)
    if placing:
        place_rows(me, asked_ref, cnt_ref, returned, current_ref, out_ref, rows_ref, refs)
    if picking:
        wait()
        source = out_ref if placing else current_ref
        whiten_and_pick(
            me, asked_ref, cnt_ref, count_ref, whole_ref, lambda seg: source[seg], picked, white_ref, rows_ref
        )


def owner_step(scalars, norms, current, attitude, returned):
    asked, cnt, seg_counts, where = scalars
    seg_dev, slots, width = current.shape
    placing, picking = returned is not None, attitude is not None
    tm_count = cnt.shape[0]
    capacity = asked.shape[0] // tm_count
    table = pltpu.VMEM((seg_dev * slots * width // SRC_GROUP + 8, SRC_GROUP), jnp.float32)
    anywhere = pl.BlockSpec(memory_space=pl.ANY)
    in_specs = [SMEM] * 4 + [anywhere, VMEM]
    args = [asked, cnt, seg_counts, where, norms, current]
    out_shape = []
    scratch = []
    if picking:
        args += attitude
        in_specs += [anywhere] * len(attitude)
        scratch += [
            pltpu.VMEM((seg_dev, slots, slots), jnp.bfloat16),
            pltpu.SemaphoreType.DMA((len(attitude),)),
            table,
        ]
    scratch.append(pltpu.VMEM((tm_count * capacity, SRC_GROUP), jnp.float32))
    if placing:
        in_specs += [VMEM] * tm_count
        args += returned
        out_shape.append(jax.ShapeDtypeStruct(current.shape, jnp.float32))
        scratch += [table] * STREAMS
    if picking:
        out_shape += [jax.ShapeDtypeStruct((capacity, SRC_GROUP), jnp.bfloat16)] * tm_count
    out = pl.pallas_call(
        functools.partial(owner_kernel, tm_count, len(attitude) - 1 if picking else 0, placing),
        in_specs=in_specs,
        out_specs=[VMEM] * len(out_shape),
        out_shape=out_shape,
        scratch_shapes=scratch,
        compiler_params=pltpu.CompilerParams(vmem_limit_bytes=VMEM_LIMIT),
        cost_estimate=pl.CostEstimate(
            flops=16 * seg_dev * slots * slots * width, bytes_accessed=16 << 20, transcendentals=0
        ),
    )(*args)
    if placing:
        return out[0], list(out[1:])
    return current, list(out)


def make_lists(sched_seg, sched_slot, seg_dev, slots, column_blocks, tm_count, capacity):
    sched_dev, obs = sched_seg.shape
    me = lax.axis_index("tm")
    owner = sched_seg // seg_dev
    partner = owner ^ me
    block_of = (jnp.arange(sched_dev, dtype=jnp.int32) % column_blocks)[:, None]
    local_row = (block_of * seg_dev + sched_seg % seg_dev) * slots + sched_slot
    hot = (partner[:, :, None] == jnp.arange(tm_count, dtype=jnp.int32)).astype(jnp.int32)
    cnt = jnp.sum(hot, axis=1)
    plans = jnp.arange(sched_dev)
    before = (plans[None, :] < plans[:, None]).astype(jnp.int32)
    src = jnp.sum(before[:, :, None] * cnt[None, :, :], axis=1)
    owners = jnp.arange(tm_count)
    ahead = (owners[None, :] < owners[:, None]).astype(jnp.int32)
    dst = jnp.sum(ahead[None, :, :] * cnt[:, None, :], axis=2)
    entry = jnp.arange(obs)
    rank = jnp.sum(
        ((partner[:, None, :] == partner[:, :, None]) & (entry[None, :] < entry[:, None])).astype(jnp.int32),
        axis=2,
    )
    place = owner * capacity + jnp.sum(hot * src[:, None, :], axis=2) + rank
    order = jnp.sum(hot * dst[:, None, :], axis=2) + rank
    time = sched_seg * slots + sched_slot
    times = jnp.sum(jnp.where(order[:, None, :] == entry[None, :, None], time[:, None, :], 0), axis=2)
    rows = seg_dev * slots * column_blocks
    wanted = rows + jnp.sum(
        jnp.where(
            place.reshape(1, -1) == jnp.arange(tm_count * capacity, dtype=jnp.int32)[:, None],
            local_row.reshape(1, -1) - rows,
            0,
        ),
        axis=1,
    )
    step_count = (cnt + STEP - 1) // STEP
    step_first = jnp.sum(ahead[None, :, :] * step_count[:, None, :], axis=2)
    step = jnp.arange(obs // STEP + tm_count)[None, :, None] - step_first[:, None, :]
    inside = (step >= 0) & (step < step_count[:, None, :])
    spaced = capacity + STEP
    end = tm_count * spaced
    step_src = end + jnp.sum(
        jnp.where(inside, owners * spaced - end + src[:, None, :] + step * STEP, 0), axis=2
    )
    step_dst = obs + jnp.sum(jnp.where(inside, dst[:, None, :] + step * STEP - obs, 0), axis=2)
    return (step_src, step_dst), times, wanted


def exchange(blocks):
    count = len(blocks)
    out = list(blocks)
    for step in sorted(range(1, count), key=lambda step: -bin(step // 2).count("1")):
        out[step] = lax.ppermute(blocks[step], "tm", [(i, i ^ step) for i in range(count)])
    return out


def pass_along(attitude, work):
    count = lax.axis_size("sky")
    right = left = attitude
    pieces = [attitude]
    done = []
    for hop in range(1, count):
        right = lax.ppermute(right, "sky", [(i, i + 1) for i in range(hop - 1, count - 1)])
        left = lax.ppermute(left, "sky", [(i, i - 1) for i in range(1, count - hop + 1)])
        pieces += [right, left]
        if hop < count - 1 and work:
            done.append(work.pop(0)([right, left]))
    return pieces, done


def on_device(residuals, seg_counts, attitude, sched_seg, sched_slot, periods):
    tm_count = lax.axis_size("tm")
    sched_dev, obs = sched_seg.shape
    seg_dev, slots, width = residuals.shape
    column_blocks = width // SRC_GROUP
    capacity = 2 * sched_dev * obs // tm_count
    tables, times, wanted = make_lists(
        sched_seg, sched_slot, seg_dev, slots, column_blocks, tm_count, capacity
    )
    asked = lax.all_to_all(wanted.reshape(tm_count, capacity), "tm", split_axis=0, concat_axis=0, tiled=True)
    cnt = jnp.sum((asked < seg_dev * slots * column_blocks).astype(jnp.int32), axis=1)
    part = sched_dev // BASIS_CALLS
    work = [
        functools.partial(make_basis, times[index * part:(index + 1) * part], periods)
        for index in range(BASIS_CALLS)
    ]
    pieces, made = pass_along(attitude, work)
    parts, norms = zip(*made)
    norms = jnp.concatenate(norms)
    where = jnp.stack([lax.axis_index("tm"), lax.axis_index("sky")])
    scalars = (asked.reshape(-1), cnt, seg_counts, where)

    current, returned = residuals, None
    for iteration in range(ITERS):
        current, picked = owner_step(scalars, norms, current, pieces, returned)
        models, score = fit_plans(tables, exchange(picked), parts, norms)
        returned = exchange(models)
    current, _ = owner_step(scalars, norms, current, None, returned)
    return (current, score.reshape(sched_dev, SRC_GROUP))


def solution(mesh):
    in_specs = (
        P("tm", None, "sky"),
        P("tm"),
        P("tm", "sky", None),
        P(("tm", "sky"), None),
        P(("tm", "sky"), None),
        P(),
    )
    out_specs = (P("tm", None, "sky"), P(("tm", "sky"), None))
    return jax.shard_map(
        on_device, mesh=mesh, in_specs=in_specs, out_specs=out_specs, check_vma=False
    )
```

```python
import functools

import jax
import jax.numpy as jnp
from jax import lax
from jax.experimental import pallas as pl
from jax.experimental.pallas import tpu as pltpu
from jax.sharding import PartitionSpec as P

SRC_GROUP = 128
ITERS = 2
STREAMS = 4
LATE_STREAMS = 2
STEP = 16
BETA = 2.0
RIDGE = 1.0
VMEM_LIMIT = 24 * 1024 * 1024
BASIS_CALLS = 4
UNROLL = 16
COST_US = 10 ** 9

COS_POLY = (1.0, -19.73920440673828, 64.9391098022461, -85.4500503540039, 60.16689682006836,
            -25.96480369567871, 6.52468729019165)
SIN_POLY = (6.283185005187988, -41.34158706665039, 81.59986114501953, -76.61351013183594,
            41.33811950683594, -12.463061332702637)

VMEM = pl.BlockSpec(memory_space=pltpu.VMEM)
HBM = pl.BlockSpec(memory_space=pltpu.HBM)
ANY = pl.BlockSpec(memory_space=pl.ANY)
SMEM = pl.BlockSpec(memory_space=pltpu.SMEM)


def horner(poly, v):
    acc = jnp.full_like(v, poly[-1])
    for term in poly[-2::-1]:
        acc = acc * v + term
    return acc


def basis_kernel(after, time_ref, period_ref, inverse_ref, *refs):
    basis_ref, norm_ref = refs[after:]
    obs = time_ref.shape[0]
    nper = period_ref.shape[1]
    rows = 32
    for chunk in range(nper // 128):
        lanes = pl.ds(chunk * 128, 128)
        sines = pl.ds(nper + chunk * 128, 128)
        period = period_ref[:, lanes]
        inverse = inverse_ref[:, lanes]

        def step(index, sums):
            at = pl.ds(pl.multiple_of(index * rows, rows), rows)
            time = time_ref[at, :]
            turns = jnp.round(time * inverse)
            part = (time - turns * period) * inverse
            square = part * part
            cosine = horner(COS_POLY, square).astype(jnp.bfloat16)
            sine = (horner(SIN_POLY, square) * part).astype(jnp.bfloat16)
            basis_ref[0, at, lanes] = cosine
            basis_ref[0, at, sines] = sine
            cosine = cosine.astype(jnp.float32)
            sine = sine.astype(jnp.float32)
            return (
                sums[0] + jnp.sum((cosine * cosine).reshape(rows // 8, 8, 128), axis=0),
                sums[1] + jnp.sum((sine * sine).reshape(rows // 8, 8, 128), axis=0),
            )

        zero = jnp.zeros((8, 128), jnp.float32)
        total_c, total_s = lax.fori_loop(0, obs // rows, step, (zero, zero))
        norm_ref[0, :, lanes] = 1.0 / (jnp.sum(total_c, axis=0, keepdims=True) + RIDGE)
        norm_ref[0, :, sines] = 1.0 / (jnp.sum(total_s, axis=0, keepdims=True) + RIDGE)


def make_basis(times, periods, after):
    sched_dev, obs = times.shape
    nper = periods.shape[0]
    wide = jnp.broadcast_to(
        times.astype(jnp.float32).reshape(-1, 1), (sched_dev * obs, SRC_GROUP)
    )
    period = periods.astype(jnp.float32)[None, :]
    return pl.pallas_call(
        functools.partial(basis_kernel, len(after)),
        grid=(sched_dev,),
        in_specs=[
            pl.BlockSpec((obs, SRC_GROUP), lambda j: (j, 0)),
            pl.BlockSpec((1, nper), lambda j: (0, 0)),
            pl.BlockSpec((1, nper), lambda j: (0, 0)),
        ] + [ANY] * len(after),
        out_specs=[
            pl.BlockSpec((1, obs, 2 * nper), lambda j: (j, 0, 0)),
            pl.BlockSpec((1, 1, 2 * nper), lambda j: (j, 0, 0)),
        ],
        out_shape=[
            jax.ShapeDtypeStruct((sched_dev, obs, 2 * nper), jnp.bfloat16),
            jax.ShapeDtypeStruct((sched_dev, 1, 2 * nper), jnp.float32),
        ],
        compiler_params=pltpu.CompilerParams(vmem_limit_bytes=VMEM_LIMIT),
        cost_estimate=pl.CostEstimate(
            flops=sched_dev * obs * nper * 10000, bytes_accessed=sched_dev * obs * nper * 4, transcendentals=0
        ),
    )(wide, period, 1.0 / period, *after)


def fit_kernel(tm_count, src_ref, dst_ref, *refs):
    refs = list(refs)

    def take(count):
        taken = refs[:count]
        del refs[:count]
        return taken

    arrived = take(tm_count)
    parts = take(BASIS_CALLS)
    (norm_ref,) = take(1)
    outs = take(tm_count)
    score_ref, basis_ref, sems, rows_ref, back_ref = take(5)
    slots = [take(4), take(4)]
    plans, obs, twice = basis_ref.shape
    nper = twice // 2
    capacity, width = arrived[0].shape
    spaced = capacity + STEP
    steps = src_ref.shape[1]
    each = plans // len(parts)

    def basis_copy(plan):
        return pltpu.make_async_copy(parts[plan // each].at[plan % each], basis_ref.at[plan], sems.at[plan])

    for plan in range(plans):
        basis_copy(plan).start()
    for owner in range(tm_count):
        rows_ref[pl.ds(owner * spaced, capacity), :] = arrived[owner][...].astype(jnp.float32)

    def correlate(plan, obs_ref, corr_ref):
        for step in range(steps):
            obs_ref[pl.ds(dst_ref[plan, step], STEP), :] = rows_ref[pl.ds(src_ref[plan, step], STEP), :]
        corr_ref[...] = lax.dot_general(
            obs_ref[:obs, :].astype(jnp.bfloat16), basis_ref[plan], (((0,), (0,)), ((), ())),
            preferred_element_type=jnp.float32,
        )

    def finish(plan, corr_ref, coeff_ref, model_ref):
        group = 16
        for start in range(0, width, group):
            at = pl.ds(start, group)
            power = []
            for chunk in range(nper // 128):
                lanes = pl.ds(chunk * 128, 128)
                sines = pl.ds(nper + chunk * 128, 128)
                cosine = corr_ref[at, lanes]
                sine = corr_ref[at, sines]
                power.append(
                    cosine * (cosine * norm_ref[plan, :, lanes]) + sine * (sine * norm_ref[plan, :, sines])
                )
            highest = functools.reduce(jnp.maximum, power)
            highest = jnp.max(highest, axis=1, keepdims=True)
            expo = [jnp.exp(BETA * (value - highest)) for value in power]
            total = jnp.sum(functools.reduce(jnp.add, expo), axis=1, keepdims=True)
            scale = 1.0 / total
            for chunk in range(nper // 128):
                lanes = pl.ds(chunk * 128, 128)
                sines = pl.ds(nper + chunk * 128, 128)
                share = expo[chunk] * scale
                coeff_ref[at, lanes] = (share * (corr_ref[at, lanes] * norm_ref[plan, :, lanes])).astype(jnp.bfloat16)
                coeff_ref[at, sines] = (share * (corr_ref[at, sines] * norm_ref[plan, :, sines])).astype(jnp.bfloat16)
            score_ref[plan, at, :] = BETA * highest + jnp.log(total)
        model_ref[:obs, :] = lax.dot_general(
            basis_ref[plan], coeff_ref[...], (((1,), (1,)), ((), ())), preferred_element_type=jnp.float32
        )
        for step in range(steps):
            back_ref[pl.ds(src_ref[plan, step], STEP), :] = model_ref[pl.ds(dst_ref[plan, step], STEP), :]

    basis_copy(0).wait()
    correlate(0, slots[0][0], slots[0][1])

    def pair(index, carry):
        plan = index * 2
        for ahead in (1, 2):
            for known in range(ahead, plans, 2):
                pl.when(plan + ahead == known)(basis_copy(known).wait)
        correlate(plan + 1, slots[1][0], slots[1][1])
        finish(plan, *slots[0][1:])
        correlate(jnp.minimum(plan + 2, plans - 1), slots[0][0], slots[0][1])
        finish(plan + 1, *slots[1][1:])
        return carry

    lax.fori_loop(0, plans // 2, pair, 0)
    for owner in range(tm_count):
        outs[owner][...] = back_ref[pl.ds(owner * spaced, capacity), :].astype(jnp.bfloat16)


def fit_plans(tables, arrived, parts, norms):
    tm_count = len(arrived)
    each, obs, twice = parts[0].shape
    sched_dev = each * len(parts)
    capacity, width = arrived[0].shape
    work = sched_dev * obs * twice * width
    spaced = tm_count * (capacity + STEP) + STEP
    slot = [
        pltpu.VMEM((obs + STEP, width), jnp.float32),
        pltpu.VMEM((width, twice), jnp.float32),
        pltpu.VMEM((width, twice), jnp.bfloat16),
        pltpu.VMEM((obs + STEP, width), jnp.float32),
    ]
    *models, score = pl.pallas_call(
        functools.partial(fit_kernel, tm_count),
        in_specs=[SMEM, SMEM] + [VMEM] * tm_count + [ANY] * len(parts) + [VMEM],
        out_specs=[VMEM] * (tm_count + 1),
        out_shape=[jax.ShapeDtypeStruct((capacity, width), jnp.bfloat16)] * tm_count
        + [jax.ShapeDtypeStruct((sched_dev, width, 1), jnp.float32)],
        scratch_shapes=[
            pltpu.VMEM((sched_dev, obs, twice), jnp.bfloat16),
            pltpu.SemaphoreType.DMA((sched_dev,)),
            pltpu.VMEM((spaced, width), jnp.float32),
            pltpu.VMEM((spaced, width), jnp.float32),
        ] + slot + slot,
        compiler_params=pltpu.CompilerParams(vmem_limit_bytes=VMEM_LIMIT),
        cost_estimate=pl.CostEstimate(flops=20 * work, bytes_accessed=sched_dev * obs * twice * 2, transcendentals=0),
    )(*tables, *arrived, *parts, norms)
    return models, score


def load_attitude(sky, own_ref, passed, whole_ref, sems):
    rows = own_ref.shape[1]
    count = len(passed) // 2 + 1
    copies = [(None, sky, own_ref)]
    for hop in range(1, count):
        copies.append((sky >= hop, sky - hop, passed[2 * hop - 2]))
        copies.append((sky + hop < count, sky + hop, passed[2 * hop - 1]))

    def each(act):
        for index, (valid, quarter, ref) in enumerate(copies):
            def run(index=index, quarter=quarter, ref=ref):
                at = pl.ds(pl.multiple_of(quarter * rows, rows), rows)
                act(pltpu.make_async_copy(ref, whole_ref.at[:, at, :], sems.at[index]))

            if valid is None:
                run()
            else:
                pl.when(valid)(run)

    each(lambda copy: copy.start())
    return lambda: each(lambda copy: copy.wait())


def whiten_and_pick(me, asked_ref, cnt_ref, count_ref, whole_ref, load, picked, white_ref, gather_ref):
    segs, slots, _ = whole_ref.shape
    capacity, width = picked[0].shape
    blocks = white_ref.shape[0] // (segs * slots)
    row = lax.broadcasted_iota(jnp.int32, (slots, width * blocks), 0)
    for seg in range(segs):
        masked = jnp.where(row < count_ref[seg], load(seg).astype(jnp.float32), 0.0).astype(jnp.bfloat16)
        white = jnp.dot(whole_ref[seg], masked, preferred_element_type=jnp.float32)
        for block in range(blocks):
            white_ref[pl.ds((block * segs + seg) * slots, slots), :] = white[:, block * width:(block + 1) * width]
    for owner, out_ref in enumerate(picked):
        asker = owner ^ me

        def step(index, carry):
            first = index * UNROLL
            for lane in range(UNROLL):
                gather_ref[pl.ds(owner * capacity + first + lane, 1), :] = white_ref[
                    pl.ds(asked_ref[asker * capacity + first + lane], 1), :
                ]
            return carry

        lax.fori_loop(0, (cnt_ref[asker] + UNROLL - 1) // UNROLL, step, 0)
        out_ref[...] = gather_ref[pl.ds(owner * capacity, capacity), :].astype(jnp.bfloat16)


def add_rows(me, asked_ref, cnt_ref, owners, returned, rows_ref, sums):
    capacity = returned[0].shape[0]
    streams = len(sums)
    for total in sums:
        total[...] = jnp.zeros_like(total)
    for number, (owner, ref) in enumerate(zip(owners, returned)):
        rows_ref[pl.ds(number * capacity, capacity), :] = ref[...].astype(jnp.float32)
        asker = owner ^ me

        def step(index, carry):
            first = index * UNROLL
            for start in range(0, UNROLL, streams):
                lanes = [first + start + lane for lane in range(streams)]
                places = [asked_ref[asker * capacity + lane] for lane in lanes]
                values = [
                    total[pl.ds(place, 1), :] + rows_ref[pl.ds(number * capacity + lane, 1), :]
                    for total, place, lane in zip(sums, places, lanes)
                ]
                for total, place, value in zip(sums, places, values):
                    total[pl.ds(place, 1), :] = value
            return carry

        lax.fori_loop(0, (cnt_ref[asker] + UNROLL - 1) // UNROLL, step, 0)


def placed_at(sums, at):
    return functools.reduce(jnp.add, [total[at, :] for total in sums])


def early_kernel(owners, table_base, asked_ref, cnt_ref, where_ref, base_ref, *refs):
    refs = list(refs)
    returned = [refs.pop(0) for _ in owners]
    out_ref, rows_ref = refs.pop(0), refs.pop(0)
    if table_base:
        held_ref, sem = refs.pop(0), refs.pop(0)
        copy = pltpu.make_async_copy(base_ref, held_ref, sem)
        copy.start()
    add_rows(where_ref[0], asked_ref, cnt_ref, owners, returned, rows_ref, refs)
    if table_base:
        copy.wait()
        out_ref[...] = held_ref[...] - placed_at(refs, pl.ds(0, out_ref.shape[0]))
        return
    segs, slots, total_width = base_ref.shape
    width = out_ref.shape[1]
    for block in range(total_width // width):
        for seg in range(segs):
            at = pl.ds((block * segs + seg) * slots, slots)
            base = base_ref[seg, :, block * width:(block + 1) * width].astype(jnp.float32)
            out_ref[at, :] = base - placed_at(refs, at)


def place_early(scalars, owners, base, returned, rows):
    asked, cnt, _, where = scalars
    table_base = base.ndim == 2
    capacity = returned[0].shape[0]
    sums = [pltpu.VMEM((rows + 8, SRC_GROUP), jnp.float32)] * STREAMS
    held = [pltpu.VMEM((rows, SRC_GROUP), jnp.float32), pltpu.SemaphoreType.DMA(())] if table_base else []
    return pl.pallas_call(
        functools.partial(early_kernel, owners, table_base),
        in_specs=[SMEM] * 3 + [HBM if table_base else VMEM] + [VMEM] * len(owners),
        out_specs=VMEM,
        out_shape=jax.ShapeDtypeStruct((rows, SRC_GROUP), jnp.float32),
        scratch_shapes=[pltpu.VMEM((len(owners) * capacity, SRC_GROUP), jnp.float32)] + held + sums,
        compiler_params=pltpu.CompilerParams(vmem_limit_bytes=VMEM_LIMIT),
        cost_estimate=pl.CostEstimate(flops=6 * COST_US, bytes_accessed=1 << 20, transcendentals=0),
    )(asked, cnt, where, base, *[returned[owner] for owner in owners])


def pick_kernel(tm_count, passed_count, asked_ref, cnt_ref, count_ref, where_ref, base_ref, own_ref, *refs):
    refs = list(refs)
    passed = [refs.pop(0) for _ in range(passed_count)]
    picked = [refs.pop(0) for _ in range(tm_count)]
    whole_ref, sems, white_ref, gather_ref = refs
    load_attitude(where_ref[1], own_ref, passed, whole_ref, sems)()
    whiten_and_pick(
        where_ref[0], asked_ref, cnt_ref, count_ref, whole_ref, lambda seg: base_ref[seg], picked, white_ref,
        gather_ref,
    )


def pick_rows(scalars, base, attitude, rows):
    asked, cnt, seg_counts, where = scalars
    tm_count, = cnt.shape
    seg_dev, slots, _ = base.shape
    capacity = asked.shape[0] // tm_count
    return pl.pallas_call(
        functools.partial(pick_kernel, tm_count, len(attitude) - 1),
        in_specs=[SMEM] * 4 + [VMEM] + [ANY] * len(attitude),
        out_specs=[VMEM] * tm_count,
        out_shape=[jax.ShapeDtypeStruct((capacity, SRC_GROUP), jnp.bfloat16)] * tm_count,
        scratch_shapes=[
            pltpu.VMEM((seg_dev, slots, slots), jnp.bfloat16),
            pltpu.SemaphoreType.DMA((len(attitude),)),
            pltpu.VMEM((rows + 8, SRC_GROUP), jnp.float32),
            pltpu.VMEM((tm_count * capacity, SRC_GROUP), jnp.float32),
        ],
        compiler_params=pltpu.CompilerParams(vmem_limit_bytes=VMEM_LIMIT),
        cost_estimate=pl.CostEstimate(flops=5 * COST_US, bytes_accessed=1 << 20, transcendentals=0),
    )(asked, cnt, seg_counts, where, base, *attitude)


def late_pick_kernel(tm_count, passed_count, owners, asked_ref, cnt_ref, count_ref, where_ref, part_ref, own_ref,
                     *refs):
    refs = list(refs)

    def take(count):
        taken = refs[:count]
        del refs[:count]
        return taken

    passed = take(passed_count)
    returned = take(len(owners))
    (out_ref,) = take(1)
    picked = take(tm_count)
    whole_ref, sems, white_ref, gather_ref, table_ref, sem = take(6)
    segs, slots, _ = whole_ref.shape
    blocks = table_ref.shape[0] // (segs * slots)
    wait = load_attitude(where_ref[1], own_ref, passed, whole_ref, sems)
    add_rows(where_ref[0], asked_ref, cnt_ref, owners, returned, gather_ref, refs)
    table_ref[...] = part_ref[...] - placed_at(refs, pl.ds(0, table_ref.shape[0]))
    copy = pltpu.make_async_copy(table_ref, out_ref, sem)
    copy.start()
    wait()

    def load(seg):
        return jnp.concatenate(
            [table_ref[pl.ds((block * segs + seg) * slots, slots), :] for block in range(blocks)], axis=1
        )

    whiten_and_pick(
        where_ref[0], asked_ref, cnt_ref, count_ref, whole_ref, load, picked, white_ref, gather_ref
    )
    copy.wait()


def place_late_and_pick(scalars, owners, part, returned, attitude):
    asked, cnt, seg_counts, where = scalars
    tm_count, = cnt.shape
    seg_dev = seg_counts.shape[0]
    slots = attitude[0].shape[2]
    capacity = asked.shape[0] // tm_count
    rows = part.shape[0]
    table = pltpu.VMEM((rows + 8, SRC_GROUP), jnp.float32)
    out = pl.pallas_call(
        functools.partial(late_pick_kernel, tm_count, len(attitude) - 1, owners),
        in_specs=[SMEM] * 4 + [VMEM] + [ANY] * len(attitude) + [VMEM] * len(owners),
        out_specs=[HBM] + [VMEM] * tm_count,
        out_shape=[jax.ShapeDtypeStruct(part.shape, jnp.float32)]
        + [jax.ShapeDtypeStruct((capacity, SRC_GROUP), jnp.bfloat16)] * tm_count,
        scratch_shapes=[
            pltpu.VMEM((seg_dev, slots, slots), jnp.bfloat16),
            pltpu.SemaphoreType.DMA((len(attitude),)),
            table,
            pltpu.VMEM((tm_count * capacity, SRC_GROUP), jnp.float32),
            pltpu.VMEM((rows, SRC_GROUP), jnp.float32),
            pltpu.SemaphoreType.DMA(()),
        ] + [table] * LATE_STREAMS,
        compiler_params=pltpu.CompilerParams(vmem_limit_bytes=VMEM_LIMIT),
        cost_estimate=pl.CostEstimate(flops=7 * COST_US, bytes_accessed=1 << 20, transcendentals=0),
    )(asked, cnt, seg_counts, where, part, *attitude, *[returned[owner] for owner in owners])
    return out[0], list(out[1:])


def late_kernel(owners, asked_ref, cnt_ref, where_ref, part_ref, *refs):
    refs = list(refs)
    returned = [refs.pop(0) for _ in owners]
    out_ref, rows_ref, held_ref, sems = refs[:4]
    sums = refs[4:]
    segs, slots, total_width = out_ref.shape
    width = part_ref.shape[1]
    add_rows(where_ref[0], asked_ref, cnt_ref, owners, returned, rows_ref, sums)
    copies = []
    for seg in range(segs):
        for block in range(total_width // width):
            at = pl.ds((block * segs + seg) * slots, slots)
            held_ref[seg, :, block * width:(block + 1) * width] = part_ref[at, :] - placed_at(sums, at)
        copies.append(pltpu.make_async_copy(held_ref.at[seg], out_ref.at[seg], sems.at[seg]))
        copies[-1].start()
    for copy in copies:
        copy.wait()


def place_late(scalars, owners, part, returned, shape):
    asked, cnt, _, where = scalars
    capacity = returned[0].shape[0]
    return pl.pallas_call(
        functools.partial(late_kernel, owners),
        in_specs=[SMEM] * 3 + [VMEM] * (1 + len(owners)),
        out_specs=HBM,
        out_shape=jax.ShapeDtypeStruct(shape, jnp.float32),
        scratch_shapes=[
            pltpu.VMEM((len(owners) * capacity, SRC_GROUP), jnp.float32),
            pltpu.VMEM(shape, jnp.float32),
            pltpu.SemaphoreType.DMA((shape[0],)),
        ] + [pltpu.VMEM((part.shape[0] + 8, SRC_GROUP), jnp.float32)] * LATE_STREAMS,
        compiler_params=pltpu.CompilerParams(vmem_limit_bytes=VMEM_LIMIT),
        cost_estimate=pl.CostEstimate(flops=4 * COST_US, bytes_accessed=1 << 20, transcendentals=0),
    )(asked, cnt, where, part, *[returned[owner] for owner in owners])


def make_lists(sched_seg, sched_slot, seg_dev, slots, column_blocks, tm_count, capacity):
    sched_dev, obs = sched_seg.shape
    me = lax.axis_index("tm")
    owner = sched_seg // seg_dev
    partner = owner ^ me
    block_of = (jnp.arange(sched_dev, dtype=jnp.int32) % column_blocks)[:, None]
    local_row = (block_of * seg_dev + sched_seg % seg_dev) * slots + sched_slot
    hot = (partner[:, :, None] == jnp.arange(tm_count, dtype=jnp.int32)).astype(jnp.int32)
    cnt = jnp.sum(hot, axis=1)
    plans = jnp.arange(sched_dev)
    before = (plans[None, :] < plans[:, None]).astype(jnp.int32)
    src = jnp.sum(before[:, :, None] * cnt[None, :, :], axis=1)
    owners = jnp.arange(tm_count)
    ahead = (owners[None, :] < owners[:, None]).astype(jnp.int32)
    dst = jnp.sum(ahead[None, :, :] * cnt[:, None, :], axis=2)
    entry = jnp.arange(obs)
    rank = jnp.sum(
        ((partner[:, None, :] == partner[:, :, None]) & (entry[None, :] < entry[:, None])).astype(jnp.int32),
        axis=2,
    )
    place = owner * capacity + jnp.sum(hot * src[:, None, :], axis=2) + rank
    order = jnp.sum(hot * dst[:, None, :], axis=2) + rank
    time = sched_seg * slots + sched_slot
    times = jnp.sum(jnp.where(order[:, None, :] == entry[None, :, None], time[:, None, :], 0), axis=2)
    rows = seg_dev * slots * column_blocks
    wanted = rows + jnp.sum(
        jnp.where(
            place.reshape(1, -1) == jnp.arange(tm_count * capacity, dtype=jnp.int32)[:, None],
            local_row.reshape(1, -1) - rows,
            0,
        ),
        axis=1,
    )
    step_count = (cnt + STEP - 1) // STEP
    step_first = jnp.sum(ahead[None, :, :] * step_count[:, None, :], axis=2)
    step = jnp.arange(obs // STEP + tm_count)[None, :, None] - step_first[:, None, :]
    inside = (step >= 0) & (step < step_count[:, None, :])
    spaced = capacity + STEP
    end = tm_count * spaced
    step_src = end + jnp.sum(
        jnp.where(inside, owners * spaced - end + src[:, None, :] + step * STEP, 0), axis=2
    )
    step_dst = obs + jnp.sum(jnp.where(inside, dst[:, None, :] + step * STEP - obs, 0), axis=2)
    return (step_src, step_dst), times, wanted


def send_order(count):
    return sorted(range(1, count), key=lambda step: (bin(step // 2).count("1"), step % 2, -step))


def exchange(blocks):
    count = len(blocks)
    out = list(blocks)
    for step in send_order(count):
        out[step] = lax.ppermute(blocks[step], "tm", [(i, i ^ step) for i in range(count)])
    return out


def pass_along(attitude, beside):
    count = lax.axis_size("sky")
    right = left = attitude
    pieces = [attitude]
    for hop in range(1, count):
        right = lax.ppermute(right, "sky", [(i, i + 1) for i in range(hop - 1, count - 1)])
        left = lax.ppermute(left, "sky", [(i, i - 1) for i in range(1, count - hop + 1)])
        if hop in beside:
            right, left = beside[hop](right, left)
        pieces += [right, left]
    return pieces


def on_device(residuals, seg_counts, attitude, sched_seg, sched_slot, periods):
    tm_count = lax.axis_size("tm")
    sched_dev, obs = sched_seg.shape
    seg_dev, slots, width = residuals.shape
    column_blocks = width // SRC_GROUP
    capacity = 2 * sched_dev * obs // tm_count
    tables, times, wanted = make_lists(
        sched_seg, sched_slot, seg_dev, slots, column_blocks, tm_count, capacity
    )
    wanted = wanted.reshape(tm_count, capacity)
    part = sched_dev // BASIS_CALLS
    made = []
    asked = None

    def basis_part(after):
        first = len(made) * part
        made.append(make_basis(times[first:first + part], periods, after))

    def first_hop(right, left):
        nonlocal asked
        held, right, left = lax.optimization_barrier((wanted, right, left))
        asked = lax.all_to_all(held, "tm", split_axis=0, concat_axis=0, tiled=True)
        basis_part([right, left])
        return right, left

    def second_hop(right, left):
        basis_part([right, left])
        basis_part([right, left])
        return right, left

    pieces = pass_along(attitude, {1: first_hop, 2: second_hop})
    cnt = jnp.sum((asked < seg_dev * slots * column_blocks).astype(jnp.int32), axis=1)
    where = jnp.stack([lax.axis_index("tm"), lax.axis_index("sky")])
    scalars = (asked.reshape(-1), cnt, seg_counts, where)
    rows = seg_dev * slots * column_blocks
    order = [0] + send_order(tm_count)
    near, far = order[:3 * tm_count // 4], order[3 * tm_count // 4:]

    base = residuals
    picked = pick_rows(scalars, base, pieces, rows)
    basis_part([picked[0]])
    parts, norms = zip(*made)
    norms = jnp.concatenate(norms)
    for iteration in range(ITERS):
        models, score = fit_plans(tables, exchange(picked), parts, norms)
        returned = exchange(models)
        base = place_early(scalars, near, base, returned, rows)
        if iteration < ITERS - 1:
            base, picked = place_late_and_pick(scalars, far, base, returned, pieces)
    cleaned = place_late(scalars, far, base, returned, residuals.shape)
    return (cleaned, score.reshape(sched_dev, SRC_GROUP))


def solution(mesh):
    in_specs = (
        P("tm", None, "sky"),
        P("tm"),
        P("tm", "sky", None),
        P(("tm", "sky"), None),
        P(("tm", "sky"), None),
        P(),
    )
    out_specs = (P("tm", None, "sky"), P(("tm", "sky"), None))
    return jax.shard_map(
        on_device, mesh=mesh, in_specs=in_specs, out_specs=out_specs, check_vma=False
    )
```

```python
import functools

import jax
import jax.numpy as jnp
from jax import lax
from jax.experimental import pallas as pl
from jax.experimental.pallas import tpu as pltpu
from jax.sharding import PartitionSpec as P

SRC_GROUP = 128
ITERS = 2
STREAMS = 4
LATE_STREAMS = 2
STEP = 16
BETA = 2.0
RIDGE = 1.0
MIB = 1024 * 1024
BASIS_VMEM = 8 * MIB
FIT_VMEM = 22 * MIB
EARLY_VMEM = 20 * MIB
PICK_VMEM = 12 * MIB
LATE_PICK_VMEM = 18 * MIB
LATE_VMEM = 12 * MIB
BASIS_CALLS = 4
UNROLL = 16
COST_US = 10 ** 9

COS_POLY = (1.0, -19.73920440673828, 64.9391098022461, -85.4500503540039, 60.16689682006836,
            -25.96480369567871, 6.52468729019165)
SIN_POLY = (6.283185005187988, -41.34158706665039, 81.59986114501953, -76.61351013183594,
            41.33811950683594, -12.463061332702637)

VMEM = pl.BlockSpec(memory_space=pltpu.VMEM)
HBM = pl.BlockSpec(memory_space=pltpu.HBM)
ANY = pl.BlockSpec(memory_space=pl.ANY)
SMEM = pl.BlockSpec(memory_space=pltpu.SMEM)


def horner(poly, v):
    acc = jnp.full_like(v, poly[-1])
    for term in poly[-2::-1]:
        acc = acc * v + term
    return acc


def basis_kernel(after, time_ref, period_ref, inverse_ref, *refs):
    basis_ref, norm_ref = refs[after:]
    obs = time_ref.shape[0]
    nper = period_ref.shape[1]
    rows = 32
    for chunk in range(nper // 128):
        lanes = pl.ds(chunk * 128, 128)
        sines = pl.ds(nper + chunk * 128, 128)
        period = period_ref[:, lanes]
        inverse = inverse_ref[:, lanes]

        def step(index, sums):
            at = pl.ds(pl.multiple_of(index * rows, rows), rows)
            time = time_ref[at, :]
            turns = jnp.round(time * inverse)
            part = (time - turns * period) * inverse
            square = part * part
            cosine = horner(COS_POLY, square).astype(jnp.bfloat16)
            sine = (horner(SIN_POLY, square) * part).astype(jnp.bfloat16)
            basis_ref[0, at, lanes] = cosine
            basis_ref[0, at, sines] = sine
            cosine = cosine.astype(jnp.float32)
            sine = sine.astype(jnp.float32)
            return (
                sums[0] + jnp.sum((cosine * cosine).reshape(rows // 8, 8, 128), axis=0),
                sums[1] + jnp.sum((sine * sine).reshape(rows // 8, 8, 128), axis=0),
            )

        zero = jnp.zeros((8, 128), jnp.float32)
        total_c, total_s = lax.fori_loop(0, obs // rows, step, (zero, zero))
        norm_ref[0, :, lanes] = 1.0 / (jnp.sum(total_c, axis=0, keepdims=True) + RIDGE)
        norm_ref[0, :, sines] = 1.0 / (jnp.sum(total_s, axis=0, keepdims=True) + RIDGE)


def make_basis(times, periods, after):
    sched_dev, obs = times.shape
    nper = periods.shape[0]
    wide = jnp.broadcast_to(
        times.astype(jnp.float32).reshape(-1, 1), (sched_dev * obs, SRC_GROUP)
    )
    period = periods.astype(jnp.float32)[None, :]
    return pl.pallas_call(
        functools.partial(basis_kernel, len(after)),
        grid=(sched_dev,),
        in_specs=[
            pl.BlockSpec((obs, SRC_GROUP), lambda j: (j, 0)),
            pl.BlockSpec((1, nper), lambda j: (0, 0)),
            pl.BlockSpec((1, nper), lambda j: (0, 0)),
        ] + [ANY] * len(after),
        out_specs=[
            pl.BlockSpec((1, obs, 2 * nper), lambda j: (j, 0, 0)),
            pl.BlockSpec((1, 1, 2 * nper), lambda j: (j, 0, 0)),
        ],
        out_shape=[
            jax.ShapeDtypeStruct((sched_dev, obs, 2 * nper), jnp.bfloat16),
            jax.ShapeDtypeStruct((sched_dev, 1, 2 * nper), jnp.float32),
        ],
        compiler_params=pltpu.CompilerParams(vmem_limit_bytes=BASIS_VMEM),
        cost_estimate=pl.CostEstimate(
            flops=sched_dev * obs * nper * 10000, bytes_accessed=sched_dev * obs * nper * 4, transcendentals=0
        ),
    )(wide, period, 1.0 / period, *after)


def fit_kernel(tm_count, src_ref, dst_ref, *refs):
    refs = list(refs)

    def take(count):
        taken = refs[:count]
        del refs[:count]
        return taken

    arrived = take(tm_count)
    parts = take(BASIS_CALLS)
    (norm_ref,) = take(1)
    outs = take(tm_count)
    score_ref, basis_ref, sems, rows_ref, back_ref = take(5)
    slots = [take(4), take(4)]
    plans, obs, twice = basis_ref.shape
    nper = twice // 2
    capacity, width = arrived[0].shape
    spaced = capacity + STEP
    steps = src_ref.shape[1]
    each = plans // len(parts)

    def basis_copy(plan):
        return pltpu.make_async_copy(parts[plan // each].at[plan % each], basis_ref.at[plan], sems.at[plan])

    for plan in range(plans):
        basis_copy(plan).start()
    for owner in range(tm_count):
        rows_ref[pl.ds(owner * spaced, capacity), :] = arrived[owner][...].astype(jnp.float32)

    def correlate(plan, obs_ref, corr_ref):
        for step in range(steps):
            obs_ref[pl.ds(dst_ref[plan, step], STEP), :] = rows_ref[pl.ds(src_ref[plan, step], STEP), :]
        corr_ref[...] = lax.dot_general(
            obs_ref[:obs, :].astype(jnp.bfloat16), basis_ref[plan], (((0,), (0,)), ((), ())),
            preferred_element_type=jnp.float32,
        )

    def finish(plan, corr_ref, coeff_ref, model_ref):
        group = 16
        for start in range(0, width, group):
            at = pl.ds(start, group)
            power = []
            for chunk in range(nper // 128):
                lanes = pl.ds(chunk * 128, 128)
                sines = pl.ds(nper + chunk * 128, 128)
                cosine = corr_ref[at, lanes]
                sine = corr_ref[at, sines]
                power.append(
                    cosine * (cosine * norm_ref[plan, :, lanes]) + sine * (sine * norm_ref[plan, :, sines])
                )
            highest = functools.reduce(jnp.maximum, power)
            highest = jnp.max(highest, axis=1, keepdims=True)
            expo = [jnp.exp(BETA * (value - highest)) for value in power]
            total = jnp.sum(functools.reduce(jnp.add, expo), axis=1, keepdims=True)
            scale = 1.0 / total
            for chunk in range(nper // 128):
                lanes = pl.ds(chunk * 128, 128)
                sines = pl.ds(nper + chunk * 128, 128)
                share = expo[chunk] * scale
                coeff_ref[at, lanes] = (share * (corr_ref[at, lanes] * norm_ref[plan, :, lanes])).astype(jnp.bfloat16)
                coeff_ref[at, sines] = (share * (corr_ref[at, sines] * norm_ref[plan, :, sines])).astype(jnp.bfloat16)
            score_ref[plan, at, :] = BETA * highest + jnp.log(total)
        model_ref[:obs, :] = lax.dot_general(
            basis_ref[plan], coeff_ref[...], (((1,), (1,)), ((), ())), preferred_element_type=jnp.float32
        )
        for step in range(steps):
            back_ref[pl.ds(src_ref[plan, step], STEP), :] = model_ref[pl.ds(dst_ref[plan, step], STEP), :]

    basis_copy(0).wait()
    correlate(0, slots[0][0], slots[0][1])

    def pair(index, carry):
        plan = index * 2
        for ahead in (1, 2):
            for known in range(ahead, plans, 2):
                pl.when(plan + ahead == known)(basis_copy(known).wait)
        correlate(plan + 1, slots[1][0], slots[1][1])
        finish(plan, *slots[0][1:])
        correlate(jnp.minimum(plan + 2, plans - 1), slots[0][0], slots[0][1])
        finish(plan + 1, *slots[1][1:])
        return carry

    lax.fori_loop(0, plans // 2, pair, 0)
    for owner in range(tm_count):
        outs[owner][...] = back_ref[pl.ds(owner * spaced, capacity), :].astype(jnp.bfloat16)


def fit_plans(tables, arrived, parts, norms):
    tm_count = len(arrived)
    each, obs, twice = parts[0].shape
    sched_dev = each * len(parts)
    capacity, width = arrived[0].shape
    work = sched_dev * obs * twice * width
    spaced = tm_count * (capacity + STEP) + STEP
    slot = [
        pltpu.VMEM((obs + STEP, width), jnp.float32),
        pltpu.VMEM((width, twice), jnp.float32),
        pltpu.VMEM((width, twice), jnp.bfloat16),
        pltpu.VMEM((obs + STEP, width), jnp.float32),
    ]
    *models, score = pl.pallas_call(
        functools.partial(fit_kernel, tm_count),
        in_specs=[SMEM, SMEM] + [VMEM] * tm_count + [ANY] * len(parts) + [VMEM],
        out_specs=[VMEM] * (tm_count + 1),
        out_shape=[jax.ShapeDtypeStruct((capacity, width), jnp.bfloat16)] * tm_count
        + [jax.ShapeDtypeStruct((sched_dev, width, 1), jnp.float32)],
        scratch_shapes=[
            pltpu.VMEM((sched_dev, obs, twice), jnp.bfloat16),
            pltpu.SemaphoreType.DMA((sched_dev,)),
            pltpu.VMEM((spaced, width), jnp.float32),
            pltpu.VMEM((spaced, width), jnp.float32),
        ] + slot + slot,
        compiler_params=pltpu.CompilerParams(vmem_limit_bytes=FIT_VMEM),
        cost_estimate=pl.CostEstimate(flops=20 * work, bytes_accessed=sched_dev * obs * twice * 2, transcendentals=0),
    )(*tables, *arrived, *parts, norms)
    return models, score


def load_attitude(sky, own_ref, passed, whole_ref, sems):
    rows = own_ref.shape[1]
    count = len(passed) // 2 + 1
    copies = [(None, sky, own_ref)]
    for hop in range(1, count):
        copies.append((sky >= hop, sky - hop, passed[2 * hop - 2]))
        copies.append((sky + hop < count, sky + hop, passed[2 * hop - 1]))

    def each(act):
        for index, (valid, quarter, ref) in enumerate(copies):
            def run(index=index, quarter=quarter, ref=ref):
                at = pl.ds(pl.multiple_of(quarter * rows, rows), rows)
                act(pltpu.make_async_copy(ref, whole_ref.at[:, at, :], sems.at[index]))

            if valid is None:
                run()
            else:
                pl.when(valid)(run)

    each(lambda copy: copy.start())
    return lambda: each(lambda copy: copy.wait())


def whiten_and_pick(me, asked_ref, cnt_ref, count_ref, whole_ref, load, picked, white_ref, gather_ref):
    segs, slots, _ = whole_ref.shape
    capacity, width = picked[0].shape
    blocks = white_ref.shape[0] // (segs * slots)
    row = lax.broadcasted_iota(jnp.int32, (slots, width * blocks), 0)
    for seg in range(segs):
        masked = jnp.where(row < count_ref[seg], load(seg).astype(jnp.float32), 0.0).astype(jnp.bfloat16)
        white = jnp.dot(whole_ref[seg], masked, preferred_element_type=jnp.float32)
        for block in range(blocks):
            white_ref[pl.ds((block * segs + seg) * slots, slots), :] = white[:, block * width:(block + 1) * width]
    for owner, out_ref in enumerate(picked):
        asker = owner ^ me

        def step(index, carry):
            first = index * UNROLL
            for lane in range(UNROLL):
                gather_ref[pl.ds(owner * capacity + first + lane, 1), :] = white_ref[
                    pl.ds(asked_ref[asker * capacity + first + lane], 1), :
                ]
            return carry

        lax.fori_loop(0, (cnt_ref[asker] + UNROLL - 1) // UNROLL, step, 0)
        out_ref[...] = gather_ref[pl.ds(owner * capacity, capacity), :].astype(jnp.bfloat16)


def add_rows(me, asked_ref, cnt_ref, owners, returned, rows_ref, sums):
    capacity = returned[0].shape[0]
    streams = len(sums)
    for total in sums:
        total[...] = jnp.zeros_like(total)
    for number, (owner, ref) in enumerate(zip(owners, returned)):
        rows_ref[pl.ds(number * capacity, capacity), :] = ref[...].astype(jnp.float32)
        asker = owner ^ me

        def step(index, carry):
            first = index * UNROLL
            for start in range(0, UNROLL, streams):
                lanes = [first + start + lane for lane in range(streams)]
                places = [asked_ref[asker * capacity + lane] for lane in lanes]
                values = [
                    total[pl.ds(place, 1), :] + rows_ref[pl.ds(number * capacity + lane, 1), :]
                    for total, place, lane in zip(sums, places, lanes)
                ]
                for total, place, value in zip(sums, places, values):
                    total[pl.ds(place, 1), :] = value
            return carry

        lax.fori_loop(0, (cnt_ref[asker] + UNROLL - 1) // UNROLL, step, 0)


def placed_at(sums, at):
    return functools.reduce(jnp.add, [total[at, :] for total in sums])


def early_kernel(owners, table_base, asked_ref, cnt_ref, where_ref, base_ref, *refs):
    refs = list(refs)
    returned = [refs.pop(0) for _ in owners]
    out_ref, rows_ref = refs.pop(0), refs.pop(0)
    if table_base:
        held_ref, sem = refs.pop(0), refs.pop(0)
        copy = pltpu.make_async_copy(base_ref, held_ref, sem)
        copy.start()
    add_rows(where_ref[0], asked_ref, cnt_ref, owners, returned, rows_ref, refs)
    if table_base:
        copy.wait()
        out_ref[...] = held_ref[...] - placed_at(refs, pl.ds(0, out_ref.shape[0]))
        return
    segs, slots, total_width = base_ref.shape
    width = out_ref.shape[1]
    for block in range(total_width // width):
        for seg in range(segs):
            at = pl.ds((block * segs + seg) * slots, slots)
            base = base_ref[seg, :, block * width:(block + 1) * width].astype(jnp.float32)
            out_ref[at, :] = base - placed_at(refs, at)


def place_early(scalars, owners, base, returned, rows):
    asked, cnt, _, where = scalars
    table_base = base.ndim == 2
    capacity = returned[0].shape[0]
    sums = [pltpu.VMEM((rows + 8, SRC_GROUP), jnp.float32)] * STREAMS
    held = [pltpu.VMEM((rows, SRC_GROUP), jnp.float32), pltpu.SemaphoreType.DMA(())] if table_base else []
    return pl.pallas_call(
        functools.partial(early_kernel, owners, table_base),
        in_specs=[SMEM] * 3 + [HBM if table_base else VMEM] + [VMEM] * len(owners),
        out_specs=VMEM,
        out_shape=jax.ShapeDtypeStruct((rows, SRC_GROUP), jnp.float32),
        scratch_shapes=[pltpu.VMEM((len(owners) * capacity, SRC_GROUP), jnp.float32)] + held + sums,
        compiler_params=pltpu.CompilerParams(vmem_limit_bytes=EARLY_VMEM),
        cost_estimate=pl.CostEstimate(flops=6 * COST_US, bytes_accessed=1 << 20, transcendentals=0),
    )(asked, cnt, where, base, *[returned[owner] for owner in owners])


def pick_kernel(tm_count, passed_count, asked_ref, cnt_ref, count_ref, where_ref, base_ref, own_ref, *refs):
    refs = list(refs)
    passed = [refs.pop(0) for _ in range(passed_count)]
    picked = [refs.pop(0) for _ in range(tm_count)]
    whole_ref, sems, white_ref, gather_ref = refs
    load_attitude(where_ref[1], own_ref, passed, whole_ref, sems)()
    whiten_and_pick(
        where_ref[0], asked_ref, cnt_ref, count_ref, whole_ref, lambda seg: base_ref[seg], picked, white_ref,
        gather_ref,
    )


def pick_rows(scalars, base, attitude, rows):
    asked, cnt, seg_counts, where = scalars
    tm_count, = cnt.shape
    seg_dev, slots, _ = base.shape
    capacity = asked.shape[0] // tm_count
    return pl.pallas_call(
        functools.partial(pick_kernel, tm_count, len(attitude) - 1),
        in_specs=[SMEM] * 4 + [VMEM] + [ANY] * len(attitude),
        out_specs=[VMEM] * tm_count,
        out_shape=[jax.ShapeDtypeStruct((capacity, SRC_GROUP), jnp.bfloat16)] * tm_count,
        scratch_shapes=[
            pltpu.VMEM((seg_dev, slots, slots), jnp.bfloat16),
            pltpu.SemaphoreType.DMA((len(attitude),)),
            pltpu.VMEM((rows + 8, SRC_GROUP), jnp.float32),
            pltpu.VMEM((tm_count * capacity, SRC_GROUP), jnp.float32),
        ],
        compiler_params=pltpu.CompilerParams(vmem_limit_bytes=PICK_VMEM),
        cost_estimate=pl.CostEstimate(flops=5 * COST_US, bytes_accessed=1 << 20, transcendentals=0),
    )(asked, cnt, seg_counts, where, base, *attitude)


def late_pick_kernel(tm_count, passed_count, owners, asked_ref, cnt_ref, count_ref, where_ref, part_ref, own_ref,
                     *refs):
    refs = list(refs)

    def take(count):
        taken = refs[:count]
        del refs[:count]
        return taken

    passed = take(passed_count)
    returned = take(len(owners))
    (out_ref,) = take(1)
    picked = take(tm_count)
    whole_ref, sems, white_ref, gather_ref, table_ref, sem = take(6)
    segs, slots, _ = whole_ref.shape
    blocks = table_ref.shape[0] // (segs * slots)
    wait = load_attitude(where_ref[1], own_ref, passed, whole_ref, sems)
    add_rows(where_ref[0], asked_ref, cnt_ref, owners, returned, gather_ref, refs)
    table_ref[...] = part_ref[...] - placed_at(refs, pl.ds(0, table_ref.shape[0]))
    copy = pltpu.make_async_copy(table_ref, out_ref, sem)
    copy.start()
    wait()

    def load(seg):
        return jnp.concatenate(
            [table_ref[pl.ds((block * segs + seg) * slots, slots), :] for block in range(blocks)], axis=1
        )

    whiten_and_pick(
        where_ref[0], asked_ref, cnt_ref, count_ref, whole_ref, load, picked, white_ref, gather_ref
    )
    copy.wait()


def place_late_and_pick(scalars, owners, part, returned, attitude):
    asked, cnt, seg_counts, where = scalars
    tm_count, = cnt.shape
    seg_dev = seg_counts.shape[0]
    slots = attitude[0].shape[2]
    capacity = asked.shape[0] // tm_count
    rows = part.shape[0]
    table = pltpu.VMEM((rows + 8, SRC_GROUP), jnp.float32)
    out = pl.pallas_call(
        functools.partial(late_pick_kernel, tm_count, len(attitude) - 1, owners),
        in_specs=[SMEM] * 4 + [VMEM] + [ANY] * len(attitude) + [VMEM] * len(owners),
        out_specs=[HBM] + [VMEM] * tm_count,
        out_shape=[jax.ShapeDtypeStruct(part.shape, jnp.float32)]
        + [jax.ShapeDtypeStruct((capacity, SRC_GROUP), jnp.bfloat16)] * tm_count,
        scratch_shapes=[
            pltpu.VMEM((seg_dev, slots, slots), jnp.bfloat16),
            pltpu.SemaphoreType.DMA((len(attitude),)),
            table,
            pltpu.VMEM((tm_count * capacity, SRC_GROUP), jnp.float32),
            pltpu.VMEM((rows, SRC_GROUP), jnp.float32),
            pltpu.SemaphoreType.DMA(()),
        ] + [table] * LATE_STREAMS,
        compiler_params=pltpu.CompilerParams(vmem_limit_bytes=LATE_PICK_VMEM),
        cost_estimate=pl.CostEstimate(flops=7 * COST_US, bytes_accessed=1 << 20, transcendentals=0),
    )(asked, cnt, seg_counts, where, part, *attitude, *[returned[owner] for owner in owners])
    return out[0], list(out[1:])


def late_kernel(owners, asked_ref, cnt_ref, where_ref, part_ref, *refs):
    refs = list(refs)
    returned = [refs.pop(0) for _ in owners]
    out_ref, rows_ref, held_ref, sems = refs[:4]
    sums = refs[4:]
    segs, slots, total_width = out_ref.shape
    width = part_ref.shape[1]
    add_rows(where_ref[0], asked_ref, cnt_ref, owners, returned, rows_ref, sums)
    copies = []
    for seg in range(segs):
        for block in range(total_width // width):
            at = pl.ds((block * segs + seg) * slots, slots)
            held_ref[seg, :, block * width:(block + 1) * width] = part_ref[at, :] - placed_at(sums, at)
        copies.append(pltpu.make_async_copy(held_ref.at[seg], out_ref.at[seg], sems.at[seg]))
        copies[-1].start()
    for copy in copies:
        copy.wait()


def place_late(scalars, owners, part, returned, shape):
    asked, cnt, _, where = scalars
    capacity = returned[0].shape[0]
    return pl.pallas_call(
        functools.partial(late_kernel, owners),
        in_specs=[SMEM] * 3 + [VMEM] * (1 + len(owners)),
        out_specs=HBM,
        out_shape=jax.ShapeDtypeStruct(shape, jnp.float32),
        scratch_shapes=[
            pltpu.VMEM((len(owners) * capacity, SRC_GROUP), jnp.float32),
            pltpu.VMEM(shape, jnp.float32),
            pltpu.SemaphoreType.DMA((shape[0],)),
        ] + [pltpu.VMEM((part.shape[0] + 8, SRC_GROUP), jnp.float32)] * LATE_STREAMS,
        compiler_params=pltpu.CompilerParams(vmem_limit_bytes=LATE_VMEM),
        cost_estimate=pl.CostEstimate(flops=4 * COST_US, bytes_accessed=1 << 20, transcendentals=0),
    )(asked, cnt, where, part, *[returned[owner] for owner in owners])


def make_lists(sched_seg, sched_slot, seg_dev, slots, column_blocks, tm_count, capacity):
    sched_dev, obs = sched_seg.shape
    me = lax.axis_index("tm")
    owner = sched_seg // seg_dev
    partner = owner ^ me
    block_of = (jnp.arange(sched_dev, dtype=jnp.int32) % column_blocks)[:, None]
    local_row = (block_of * seg_dev + sched_seg % seg_dev) * slots + sched_slot
    hot = (partner[:, :, None] == jnp.arange(tm_count, dtype=jnp.int32)).astype(jnp.int32)
    cnt = jnp.sum(hot, axis=1)
    plans = jnp.arange(sched_dev)
    before = (plans[None, :] < plans[:, None]).astype(jnp.int32)
    src = jnp.sum(before[:, :, None] * cnt[None, :, :], axis=1)
    owners = jnp.arange(tm_count)
    ahead = (owners[None, :] < owners[:, None]).astype(jnp.int32)
    dst = jnp.sum(ahead[None, :, :] * cnt[:, None, :], axis=2)
    entry = jnp.arange(obs)
    rank = jnp.sum(
        ((partner[:, None, :] == partner[:, :, None]) & (entry[None, :] < entry[:, None])).astype(jnp.int32),
        axis=2,
    )
    place = owner * capacity + jnp.sum(hot * src[:, None, :], axis=2) + rank
    order = jnp.sum(hot * dst[:, None, :], axis=2) + rank
    time = sched_seg * slots + sched_slot
    times = jnp.sum(jnp.where(order[:, None, :] == entry[None, :, None], time[:, None, :], 0), axis=2)
    rows = seg_dev * slots * column_blocks
    wanted = rows + jnp.sum(
        jnp.where(
            place.reshape(1, -1) == jnp.arange(tm_count * capacity, dtype=jnp.int32)[:, None],
            local_row.reshape(1, -1) - rows,
            0,
        ),
        axis=1,
    )
    step_count = (cnt + STEP - 1) // STEP
    step_first = jnp.sum(ahead[None, :, :] * step_count[:, None, :], axis=2)
    step = jnp.arange(obs // STEP + tm_count)[None, :, None] - step_first[:, None, :]
    inside = (step >= 0) & (step < step_count[:, None, :])
    spaced = capacity + STEP
    end = tm_count * spaced
    step_src = end + jnp.sum(
        jnp.where(inside, owners * spaced - end + src[:, None, :] + step * STEP, 0), axis=2
    )
    step_dst = obs + jnp.sum(jnp.where(inside, dst[:, None, :] + step * STEP - obs, 0), axis=2)
    return (step_src, step_dst), times, wanted


def send_order(count):
    return sorted(range(1, count), key=lambda step: (bin(step // 2).count("1"), step % 2, -step))


def exchange(blocks):
    count = len(blocks)
    out = list(blocks)
    for step in send_order(count):
        out[step] = lax.ppermute(blocks[step], "tm", [(i, i ^ step) for i in range(count)])
    return out


def pass_along(attitude, beside):
    count = lax.axis_size("sky")
    right = left = attitude
    pieces = [attitude]
    for hop in range(1, count):
        right = lax.ppermute(right, "sky", [(i, i + 1) for i in range(hop - 1, count - 1)])
        left = lax.ppermute(left, "sky", [(i, i - 1) for i in range(1, count - hop + 1)])
        if hop in beside:
            right, left = beside[hop](right, left)
        pieces += [right, left]
    return pieces


def on_device(residuals, seg_counts, attitude, sched_seg, sched_slot, periods):
    tm_count = lax.axis_size("tm")
    sched_dev, obs = sched_seg.shape
    seg_dev, slots, width = residuals.shape
    column_blocks = width // SRC_GROUP
    capacity = 2 * sched_dev * obs // tm_count
    tables, times, wanted = make_lists(
        sched_seg, sched_slot, seg_dev, slots, column_blocks, tm_count, capacity
    )
    wanted = wanted.reshape(tm_count, capacity)
    part = sched_dev // BASIS_CALLS
    made = []
    asked = None

    def basis_part(after):
        first = len(made) * part
        made.append(make_basis(times[first:first + part], periods, after))

    def first_hop(right, left):
        nonlocal asked
        basis_part([right, left])
        held, _ = lax.optimization_barrier((wanted, made[0][1]))
        asked = lax.all_to_all(held, "tm", split_axis=0, concat_axis=0, tiled=True)
        return right, left

    def second_hop(right, left):
        basis_part([right, left])
        basis_part([right, left])
        return right, left

    pieces = pass_along(attitude, {1: first_hop, 2: second_hop})
    cnt = jnp.sum((asked < seg_dev * slots * column_blocks).astype(jnp.int32), axis=1)
    where = jnp.stack([lax.axis_index("tm"), lax.axis_index("sky")])
    scalars = (asked.reshape(-1), cnt, seg_counts, where)
    rows = seg_dev * slots * column_blocks
    order = [0] + send_order(tm_count)
    near, far = order[:3 * tm_count // 4], order[3 * tm_count // 4:]

    base = residuals
    picked = pick_rows(scalars, base, pieces, rows)
    basis_part([picked[0]])
    parts, norms = zip(*made)
    norms = jnp.concatenate(norms)
    for iteration in range(ITERS):
        models, score = fit_plans(tables, exchange(picked), parts, norms)
        returned = exchange(models)
        base = place_early(scalars, near, base, returned, rows)
        if iteration < ITERS - 1:
            base, picked = place_late_and_pick(scalars, far, base, returned, pieces)
    cleaned = place_late(scalars, far, base, returned, residuals.shape)
    return (cleaned, score.reshape(sched_dev, SRC_GROUP))


def solution(mesh):
    in_specs = (
        P("tm", None, "sky"),
        P("tm"),
        P("tm", "sky", None),
        P(("tm", "sky"), None),
        P(("tm", "sky"), None),
        P(),
    )
    out_specs = (P("tm", None, "sky"), P(("tm", "sky"), None))
    return jax.shard_map(
        on_device, mesh=mesh, in_specs=in_specs, out_specs=out_specs, check_vma=False
    )
```

```python
import functools

import jax
import jax.numpy as jnp
from jax import lax
from jax.experimental import pallas as pl
from jax.experimental.pallas import tpu as pltpu
from jax.sharding import PartitionSpec as P

SRC_GROUP = 128
ITERS = 2
STREAMS = 4
LATE_STREAMS = 2
STEP = 16
BETA = 2.0
RIDGE = 1.0
MIB = 1024 * 1024
BASIS_VMEM = 8 * MIB
FIT_VMEM = 22 * MIB
EARLY_VMEM = 20 * MIB
PICK_VMEM = 12 * MIB
LATE_PICK_VMEM = 18 * MIB
LATE_VMEM = 12 * MIB
BASIS_CALLS = 4
UNROLL = 32
SUB = 8
HBM_SPARE = 32
COST_US = 10 ** 9

COS_POLY = (1.0, -19.73920440673828, 64.9391098022461, -85.4500503540039, 60.16689682006836,
            -25.96480369567871, 6.52468729019165)
SIN_POLY = (6.283185005187988, -41.34158706665039, 81.59986114501953, -76.61351013183594,
            41.33811950683594, -12.463061332702637)

VMEM = pl.BlockSpec(memory_space=pltpu.VMEM)
HBM = pl.BlockSpec(memory_space=pltpu.HBM)
ANY = pl.BlockSpec(memory_space=pl.ANY)
SMEM = pl.BlockSpec(memory_space=pltpu.SMEM)


def horner(poly, v):
    acc = jnp.full_like(v, poly[-1])
    for term in poly[-2::-1]:
        acc = acc * v + term
    return acc


def basis_kernel(after, time_ref, period_ref, inverse_ref, *refs):
    basis_ref, norm_ref = refs[after:]
    obs = time_ref.shape[0]
    nper = period_ref.shape[1]
    rows = 32
    for chunk in range(nper // 128):
        lanes = pl.ds(chunk * 128, 128)
        sines = pl.ds(nper + chunk * 128, 128)
        period = period_ref[:, lanes]
        inverse = inverse_ref[:, lanes]

        def step(index, sums):
            at = pl.ds(pl.multiple_of(index * rows, rows), rows)
            time = time_ref[at, :]
            turns = jnp.round(time * inverse)
            part = (time - turns * period) * inverse
            square = part * part
            cosine = horner(COS_POLY, square).astype(jnp.bfloat16)
            sine = (horner(SIN_POLY, square) * part).astype(jnp.bfloat16)
            basis_ref[0, at, lanes] = cosine
            basis_ref[0, at, sines] = sine
            cosine = cosine.astype(jnp.float32)
            sine = sine.astype(jnp.float32)
            return (
                sums[0] + jnp.sum((cosine * cosine).reshape(rows // 8, 8, 128), axis=0),
                sums[1] + jnp.sum((sine * sine).reshape(rows // 8, 8, 128), axis=0),
            )

        zero = jnp.zeros((8, 128), jnp.float32)
        total_c, total_s = lax.fori_loop(0, obs // rows, step, (zero, zero))
        norm_ref[0, :, lanes] = 1.0 / (jnp.sum(total_c, axis=0, keepdims=True) + RIDGE)
        norm_ref[0, :, sines] = 1.0 / (jnp.sum(total_s, axis=0, keepdims=True) + RIDGE)


def make_basis(times, periods, after):
    sched_dev, obs = times.shape
    nper = periods.shape[0]
    wide = jnp.broadcast_to(
        times.astype(jnp.float32).reshape(-1, 1), (sched_dev * obs, SRC_GROUP)
    )
    period = periods.astype(jnp.float32)[None, :]
    return pl.pallas_call(
        functools.partial(basis_kernel, len(after)),
        grid=(sched_dev,),
        in_specs=[
            pl.BlockSpec((obs, SRC_GROUP), lambda j: (j, 0)),
            pl.BlockSpec((1, nper), lambda j: (0, 0)),
            pl.BlockSpec((1, nper), lambda j: (0, 0)),
        ] + [ANY] * len(after),
        out_specs=[
            pl.BlockSpec((1, obs, 2 * nper), lambda j: (j, 0, 0)),
            pl.BlockSpec((1, 1, 2 * nper), lambda j: (j, 0, 0)),
        ],
        out_shape=[
            jax.ShapeDtypeStruct((sched_dev, obs, 2 * nper), jnp.bfloat16),
            jax.ShapeDtypeStruct((sched_dev, 1, 2 * nper), jnp.float32),
        ],
        compiler_params=pltpu.CompilerParams(vmem_limit_bytes=BASIS_VMEM),
        cost_estimate=pl.CostEstimate(
            flops=sched_dev * obs * nper * 10000, bytes_accessed=sched_dev * obs * nper * 4, transcendentals=0
        ),
    )(wide, period, 1.0 / period, *after)


def fit_kernel(order, src_ref, dst_ref, *refs):
    refs = list(refs)

    def take(count):
        taken = refs[:count]
        del refs[:count]
        return taken

    tm_count = len(order)
    arrived = dict(zip(order, take(tm_count)))
    parts = take(BASIS_CALLS)
    (norm_ref,) = take(1)
    outs = take(tm_count)
    score_ref, basis_ref, sems, rows_ref, back_ref = take(5)
    slots = [take(4), take(4)]
    plans, obs, twice = basis_ref.shape
    nper = twice // 2
    capacity, width = arrived[0].shape
    spaced = capacity + STEP
    steps = src_ref.shape[1]
    each = plans // len(parts)

    def basis_copy(plan):
        return pltpu.make_async_copy(parts[plan // each].at[plan % each], basis_ref.at[plan], sems.at[plan])

    for plan in range(plans):
        basis_copy(plan).start()
    for owner in range(tm_count):
        rows_ref[pl.ds(owner * spaced, capacity), :] = arrived[owner][...].astype(jnp.float32)

    def correlate(plan, obs_ref, corr_ref):
        for step in range(steps):
            obs_ref[pl.ds(dst_ref[plan, step], STEP), :] = rows_ref[pl.ds(src_ref[plan, step], STEP), :]
        corr_ref[...] = lax.dot_general(
            obs_ref[:obs, :].astype(jnp.bfloat16), basis_ref[plan], (((0,), (0,)), ((), ())),
            preferred_element_type=jnp.float32,
        )

    def finish(plan, corr_ref, coeff_ref, model_ref):
        group = 16
        for start in range(0, width, group):
            at = pl.ds(start, group)
            power = []
            for chunk in range(nper // 128):
                lanes = pl.ds(chunk * 128, 128)
                sines = pl.ds(nper + chunk * 128, 128)
                cosine = corr_ref[at, lanes]
                sine = corr_ref[at, sines]
                power.append(
                    cosine * (cosine * norm_ref[plan, :, lanes]) + sine * (sine * norm_ref[plan, :, sines])
                )
            highest = functools.reduce(jnp.maximum, power)
            highest = jnp.max(highest, axis=1, keepdims=True)
            expo = [jnp.exp(BETA * (value - highest)) for value in power]
            total = jnp.sum(functools.reduce(jnp.add, expo), axis=1, keepdims=True)
            scale = 1.0 / total
            for chunk in range(nper // 128):
                lanes = pl.ds(chunk * 128, 128)
                sines = pl.ds(nper + chunk * 128, 128)
                share = expo[chunk] * scale
                coeff_ref[at, lanes] = (share * (corr_ref[at, lanes] * norm_ref[plan, :, lanes])).astype(jnp.bfloat16)
                coeff_ref[at, sines] = (share * (corr_ref[at, sines] * norm_ref[plan, :, sines])).astype(jnp.bfloat16)
            score_ref[plan, at, :] = BETA * highest + jnp.log(total)
        model_ref[:obs, :] = lax.dot_general(
            basis_ref[plan], coeff_ref[...], (((1,), (1,)), ((), ())), preferred_element_type=jnp.float32
        )
        for step in range(steps):
            back_ref[pl.ds(src_ref[plan, step], STEP), :] = model_ref[pl.ds(dst_ref[plan, step], STEP), :]

    basis_copy(0).wait()
    correlate(0, slots[0][0], slots[0][1])

    def pair(index, carry):
        plan = index * 2
        for ahead in (1, 2):
            for known in range(ahead, plans, 2):
                pl.when(plan + ahead == known)(basis_copy(known).wait)
        correlate(plan + 1, slots[1][0], slots[1][1])
        finish(plan, *slots[0][1:])
        correlate(jnp.minimum(plan + 2, plans - 1), slots[0][0], slots[0][1])
        finish(plan + 1, *slots[1][1:])
        return carry

    lax.fori_loop(0, plans // 2, pair, 0)
    for owner in range(tm_count):
        outs[owner][...] = back_ref[pl.ds(owner * spaced, capacity), :].astype(jnp.bfloat16)


def fit_plans(tables, arrived, parts, norms):
    tm_count = len(arrived)
    order = [0] + ask_order(tm_count)
    each, obs, twice = parts[0].shape
    sched_dev = each * len(parts)
    capacity, width = arrived[0].shape
    work = sched_dev * obs * twice * width
    spaced = tm_count * (capacity + STEP) + STEP
    slot = [
        pltpu.VMEM((obs + STEP, width), jnp.float32),
        pltpu.VMEM((width, twice), jnp.float32),
        pltpu.VMEM((width, twice), jnp.bfloat16),
        pltpu.VMEM((obs + STEP, width), jnp.float32),
    ]
    *models, score = pl.pallas_call(
        functools.partial(fit_kernel, order),
        in_specs=[SMEM, SMEM] + [VMEM] * tm_count + [ANY] * len(parts) + [VMEM],
        out_specs=[VMEM] * (tm_count + 1),
        out_shape=[jax.ShapeDtypeStruct((capacity, width), jnp.bfloat16)] * tm_count
        + [jax.ShapeDtypeStruct((sched_dev, width, 1), jnp.float32)],
        scratch_shapes=[
            pltpu.VMEM((sched_dev, obs, twice), jnp.bfloat16),
            pltpu.SemaphoreType.DMA((sched_dev,)),
            pltpu.VMEM((spaced, width), jnp.float32),
            pltpu.VMEM((spaced, width), jnp.float32),
        ] + slot + slot,
        compiler_params=pltpu.CompilerParams(vmem_limit_bytes=FIT_VMEM),
        cost_estimate=pl.CostEstimate(flops=20 * work, bytes_accessed=sched_dev * obs * twice * 2, transcendentals=0),
    )(*tables, *[arrived[owner] for owner in order], *parts, norms)
    return models, score


def load_attitude(sky, own_ref, passed, whole_ref, sems):
    rows = own_ref.shape[1]
    count = len(passed) // 2 + 1
    copies = [(None, sky, own_ref)]
    for hop in range(1, count):
        copies.append((sky >= hop, sky - hop, passed[2 * hop - 2]))
        copies.append((sky + hop < count, sky + hop, passed[2 * hop - 1]))

    def each(act, segs):
        for index, (valid, quarter, ref) in enumerate(copies):
            def run(index=index, quarter=quarter, ref=ref):
                at = pl.ds(pl.multiple_of(quarter * rows, rows), rows)
                for seg in segs:
                    act(pltpu.make_async_copy(ref.at[seg], whole_ref.at[seg, at, :], sems.at[index, seg]))

            if valid is None:
                run()
            else:
                pl.when(valid)(run)

    each(lambda copy: copy.start(), range(own_ref.shape[0]))
    return lambda seg: each(lambda copy: copy.wait(), [seg])


def whiten_and_pick(me, asked_ref, cnt_ref, count_ref, whole_ref, wait, load, picked, white_ref, gather_ref):
    segs, slots, _ = whole_ref.shape
    capacity, width = picked[0].shape
    blocks = white_ref.shape[0] // (segs * slots)
    row = lax.broadcasted_iota(jnp.int32, (slots, width * blocks), 0)
    for seg in range(segs):
        wait(seg)
        masked = jnp.where(row < count_ref[seg], load(seg).astype(jnp.float32), 0.0).astype(jnp.bfloat16)
        white = jnp.dot(whole_ref[seg], masked, preferred_element_type=jnp.float32)
        for block in range(blocks):
            white_ref[pl.ds((block * segs + seg) * slots, slots), :] = white[:, block * width:(block + 1) * width]
    for owner, out_ref in enumerate(picked):
        asker = owner ^ me

        def step(index, carry):
            first = asker * capacity + index * UNROLL
            tile = (owner * capacity) // SUB + index * (UNROLL // SUB)
            for lane in range(UNROLL):
                gather_ref[tile + lane // SUB, pl.ds(lane % SUB, 1), :] = white_ref[
                    pl.ds(asked_ref[first + lane], 1), :
                ]
            return carry

        lax.fori_loop(0, (cnt_ref[asker] + UNROLL - 1) // UNROLL, step, 0)
        block = gather_ref[pl.ds(owner * capacity // SUB, capacity // SUB)]
        out_ref[...] = block.reshape(capacity, width).astype(jnp.bfloat16)


def add_rows(me, asked_ref, cnt_ref, owners, returned, rows_ref, sums):
    capacity = returned[0].shape[0]
    streams = len(sums)
    for total in sums:
        total[...] = jnp.zeros_like(total)
    for number, (owner, ref) in enumerate(zip(owners, returned)):
        tiles = capacity // SUB
        rows_ref[pl.ds(number * tiles, tiles)] = ref[...].astype(jnp.float32).reshape(tiles, SUB, -1)
        asker = owner ^ me

        def step(index, carry):
            first = asker * capacity + index * UNROLL
            tile = number * tiles + index * (UNROLL // SUB)
            for start in range(0, UNROLL, streams):
                lanes = [start + lane for lane in range(streams)]
                places = [asked_ref[first + lane] for lane in lanes]
                values = [
                    total[pl.ds(place, 1), :] + rows_ref[tile + lane // SUB, pl.ds(lane % SUB, 1), :]
                    for total, place, lane in zip(sums, places, lanes)
                ]
                for total, place, value in zip(sums, places, values):
                    total[pl.ds(place, 1), :] = value
            return carry

        lax.fori_loop(0, (cnt_ref[asker] + UNROLL - 1) // UNROLL, step, 0)


def placed_at(sums, at):
    return functools.reduce(jnp.add, [total[at, :] for total in sums])


def early_kernel(owners, table_base, asked_ref, cnt_ref, where_ref, base_ref, *refs):
    refs = list(refs)
    returned = [refs.pop(0) for _ in owners]
    out_ref, rows_ref = refs.pop(0), refs.pop(0)
    if table_base:
        held_ref, sem = refs.pop(0), refs.pop(0)
        copy = pltpu.make_async_copy(base_ref.at[pl.ds(0, held_ref.shape[0]), :], held_ref, sem)
        copy.start()
    add_rows(where_ref[0], asked_ref, cnt_ref, owners, returned, rows_ref, refs)
    if table_base:
        copy.wait()
        out_ref[...] = held_ref[...] - placed_at(refs, pl.ds(0, out_ref.shape[0]))
        return
    segs, slots, total_width = base_ref.shape
    width = out_ref.shape[1]
    for block in range(total_width // width):
        for seg in range(segs):
            at = pl.ds((block * segs + seg) * slots, slots)
            base = base_ref[seg, :, block * width:(block + 1) * width].astype(jnp.float32)
            out_ref[at, :] = base - placed_at(refs, at)


def place_early(scalars, owners, base, returned, rows):
    asked, cnt, _, where = scalars
    table_base = base.ndim == 2
    capacity = returned[0].shape[0]
    sums = [pltpu.VMEM((rows + 8, SRC_GROUP), jnp.float32)] * STREAMS
    held = [pltpu.VMEM((rows, SRC_GROUP), jnp.float32), pltpu.SemaphoreType.DMA(())] if table_base else []
    return pl.pallas_call(
        functools.partial(early_kernel, owners, table_base),
        in_specs=[SMEM] * 3 + [HBM if table_base else VMEM] + [VMEM] * len(owners),
        out_specs=VMEM,
        out_shape=jax.ShapeDtypeStruct((rows, SRC_GROUP), jnp.float32),
        scratch_shapes=[pltpu.VMEM((len(owners) * capacity // SUB, SUB, SRC_GROUP), jnp.float32)] + held + sums,
        compiler_params=pltpu.CompilerParams(vmem_limit_bytes=EARLY_VMEM),
        cost_estimate=pl.CostEstimate(flops=6 * COST_US, bytes_accessed=1 << 20, transcendentals=0),
    )(asked, cnt, where, base, *[returned[owner] for owner in owners])


def pick_kernel(tm_count, passed_count, asked_ref, cnt_ref, count_ref, where_ref, base_ref, own_ref, *refs):
    refs = list(refs)
    passed = [refs.pop(0) for _ in range(passed_count)]
    picked = [refs.pop(0) for _ in range(tm_count)]
    whole_ref, sems, white_ref, gather_ref = refs
    wait = load_attitude(where_ref[1], own_ref, passed, whole_ref, sems)
    whiten_and_pick(
        where_ref[0], asked_ref, cnt_ref, count_ref, whole_ref, wait, lambda seg: base_ref[seg], picked, white_ref,
        gather_ref,
    )


def pick_rows(scalars, base, attitude, rows):
    asked, cnt, seg_counts, where = scalars
    tm_count, = cnt.shape
    seg_dev, slots, _ = base.shape
    capacity = asked.shape[0] // tm_count
    return pl.pallas_call(
        functools.partial(pick_kernel, tm_count, len(attitude) - 1),
        in_specs=[SMEM] * 4 + [VMEM] + [ANY] * len(attitude),
        out_specs=[VMEM] * tm_count,
        out_shape=[jax.ShapeDtypeStruct((capacity, SRC_GROUP), jnp.bfloat16)] * tm_count,
        scratch_shapes=[
            pltpu.VMEM((seg_dev, slots, slots), jnp.bfloat16),
            pltpu.SemaphoreType.DMA((len(attitude), seg_dev)),
            pltpu.VMEM((rows + 8, SRC_GROUP), jnp.float32),
            pltpu.VMEM((tm_count * capacity // SUB, SUB, SRC_GROUP), jnp.float32),
        ],
        compiler_params=pltpu.CompilerParams(vmem_limit_bytes=PICK_VMEM),
        cost_estimate=pl.CostEstimate(flops=5 * COST_US, bytes_accessed=1 << 20, transcendentals=0),
    )(asked, cnt, seg_counts, where, base, *attitude)


def late_pick_kernel(tm_count, passed_count, owners, asked_ref, cnt_ref, count_ref, where_ref, part_ref, own_ref,
                     *refs):
    refs = list(refs)

    def take(count):
        taken = refs[:count]
        del refs[:count]
        return taken

    passed = take(passed_count)
    returned = take(len(owners))
    (out_ref,) = take(1)
    picked = take(tm_count)
    whole_ref, sems, white_ref, gather_ref, table_ref, sem = take(6)
    segs, slots, _ = whole_ref.shape
    blocks = table_ref.shape[0] // (segs * slots)
    wait = load_attitude(where_ref[1], own_ref, passed, whole_ref, sems)
    add_rows(where_ref[0], asked_ref, cnt_ref, owners, returned, gather_ref, refs)
    table_ref[...] = part_ref[...] - placed_at(refs, pl.ds(0, table_ref.shape[0]))
    copy = pltpu.make_async_copy(table_ref, out_ref.at[pl.ds(0, table_ref.shape[0]), :], sem)
    copy.start()

    def load(seg):
        return jnp.concatenate(
            [table_ref[pl.ds((block * segs + seg) * slots, slots), :] for block in range(blocks)], axis=1
        )

    whiten_and_pick(
        where_ref[0], asked_ref, cnt_ref, count_ref, whole_ref, wait, load, picked, white_ref, gather_ref
    )
    copy.wait()


def place_late_and_pick(scalars, owners, part, returned, attitude):
    asked, cnt, seg_counts, where = scalars
    tm_count, = cnt.shape
    seg_dev = seg_counts.shape[0]
    slots = attitude[0].shape[2]
    capacity = asked.shape[0] // tm_count
    rows = part.shape[0]
    table = pltpu.VMEM((rows + 8, SRC_GROUP), jnp.float32)
    out = pl.pallas_call(
        functools.partial(late_pick_kernel, tm_count, len(attitude) - 1, owners),
        in_specs=[SMEM] * 4 + [VMEM] + [ANY] * len(attitude) + [VMEM] * len(owners),
        out_specs=[HBM] + [VMEM] * tm_count,
        out_shape=[jax.ShapeDtypeStruct((HBM_SPARE * rows, SRC_GROUP), jnp.float32)]
        + [jax.ShapeDtypeStruct((capacity, SRC_GROUP), jnp.bfloat16)] * tm_count,
        scratch_shapes=[
            pltpu.VMEM((seg_dev, slots, slots), jnp.bfloat16),
            pltpu.SemaphoreType.DMA((len(attitude), seg_dev)),
            table,
            pltpu.VMEM((tm_count * capacity // SUB, SUB, SRC_GROUP), jnp.float32),
            pltpu.VMEM((rows, SRC_GROUP), jnp.float32),
            pltpu.SemaphoreType.DMA(()),
        ] + [table] * LATE_STREAMS,
        compiler_params=pltpu.CompilerParams(vmem_limit_bytes=LATE_PICK_VMEM),
        cost_estimate=pl.CostEstimate(flops=7 * COST_US, bytes_accessed=1 << 20, transcendentals=0),
    )(asked, cnt, seg_counts, where, part, *attitude, *[returned[owner] for owner in owners])
    return out[0], list(out[1:])


def late_kernel(owners, asked_ref, cnt_ref, where_ref, part_ref, *refs):
    refs = list(refs)
    returned = [refs.pop(0) for _ in owners]
    out_ref, rows_ref, held_ref, sems = refs[:4]
    sums = refs[4:]
    segs, slots, total_width = out_ref.shape
    width = part_ref.shape[1]
    add_rows(where_ref[0], asked_ref, cnt_ref, owners, returned, rows_ref, sums)
    copies = []
    for seg in range(segs):
        for block in range(total_width // width):
            at = pl.ds((block * segs + seg) * slots, slots)
            held_ref[seg, :, block * width:(block + 1) * width] = part_ref[at, :] - placed_at(sums, at)
        copies.append(pltpu.make_async_copy(held_ref.at[seg], out_ref.at[seg], sems.at[seg]))
        copies[-1].start()
    for copy in copies:
        copy.wait()


def place_late(scalars, owners, part, returned, shape):
    asked, cnt, _, where = scalars
    capacity = returned[0].shape[0]
    return pl.pallas_call(
        functools.partial(late_kernel, owners),
        in_specs=[SMEM] * 3 + [VMEM] * (1 + len(owners)),
        out_specs=HBM,
        out_shape=jax.ShapeDtypeStruct(shape, jnp.float32),
        scratch_shapes=[
            pltpu.VMEM((len(owners) * capacity // SUB, SUB, SRC_GROUP), jnp.float32),
            pltpu.VMEM(shape, jnp.float32),
            pltpu.SemaphoreType.DMA((shape[0],)),
        ] + [pltpu.VMEM((part.shape[0] + 8, SRC_GROUP), jnp.float32)] * LATE_STREAMS,
        compiler_params=pltpu.CompilerParams(vmem_limit_bytes=LATE_VMEM),
        cost_estimate=pl.CostEstimate(flops=4 * COST_US, bytes_accessed=1 << 20, transcendentals=0),
    )(asked, cnt, where, part, *[returned[owner] for owner in owners])


def make_lists(sched_seg, sched_slot, seg_dev, slots, column_blocks, tm_count, capacity):
    sched_dev, obs = sched_seg.shape
    me = lax.axis_index("tm")
    owner = sched_seg // seg_dev
    partner = owner ^ me
    block_of = (jnp.arange(sched_dev, dtype=jnp.int32) % column_blocks)[:, None]
    local_row = (block_of * seg_dev + sched_seg % seg_dev) * slots + sched_slot
    hot = (partner[:, :, None] == jnp.arange(tm_count, dtype=jnp.int32)).astype(jnp.int32)
    cnt = jnp.sum(hot, axis=1)
    plans = jnp.arange(sched_dev)
    before = (plans[None, :] < plans[:, None]).astype(jnp.int32)
    src = jnp.sum(before[:, :, None] * cnt[None, :, :], axis=1)
    owners = jnp.arange(tm_count)
    ahead = (owners[None, :] < owners[:, None]).astype(jnp.int32)
    dst = jnp.sum(ahead[None, :, :] * cnt[:, None, :], axis=2)
    entry = jnp.arange(obs)
    rank = jnp.sum(
        ((partner[:, None, :] == partner[:, :, None]) & (entry[None, :] < entry[:, None])).astype(jnp.int32),
        axis=2,
    )
    place = owner * capacity + jnp.sum(hot * src[:, None, :], axis=2) + rank
    order = jnp.sum(hot * dst[:, None, :], axis=2) + rank
    time = sched_seg * slots + sched_slot
    times = jnp.sum(jnp.where(order[:, None, :] == entry[None, :, None], time[:, None, :], 0), axis=2)
    rows = seg_dev * slots * column_blocks
    wanted = rows + jnp.sum(
        jnp.where(
            place.reshape(1, -1) == jnp.arange(tm_count * capacity, dtype=jnp.int32)[:, None],
            local_row.reshape(1, -1) - rows,
            0,
        ),
        axis=1,
    )
    step_count = (cnt + STEP - 1) // STEP
    step_first = jnp.sum(ahead[None, :, :] * step_count[:, None, :], axis=2)
    step = jnp.arange(obs // STEP + tm_count)[None, :, None] - step_first[:, None, :]
    inside = (step >= 0) & (step < step_count[:, None, :])
    spaced = capacity + STEP
    end = tm_count * spaced
    step_src = end + jnp.sum(
        jnp.where(inside, owners * spaced - end + src[:, None, :] + step * STEP, 0), axis=2
    )
    step_dst = obs + jnp.sum(jnp.where(inside, dst[:, None, :] + step * STEP - obs, 0), axis=2)
    return (step_src, step_dst), times, wanted


def send_order(count):
    return sorted(range(1, count), key=lambda step: (bin(step // 2).count("1"), step % 2, -step))


def ask_order(count):
    first = [1, count // 2]
    return first + sorted(
        (step for step in range(2, count) if step not in first), key=lambda step: -bin(step // 2).count("1")
    )


def exchange(blocks):
    count = len(blocks)
    out = list(blocks)
    for step in range(1, count):
        out[step] = lax.ppermute(blocks[step], "tm", [(i, i ^ step) for i in range(count)])
    return out


def pass_along(attitude, beside):
    count = lax.axis_size("sky")
    right = left = attitude
    pieces = [attitude]
    for hop in range(1, count):
        right = lax.ppermute(right, "sky", [(i, i + 1) for i in range(hop - 1, count - 1)])
        left = lax.ppermute(left, "sky", [(i, i - 1) for i in range(1, count - hop + 1)])
        if hop in beside:
            right, left = beside[hop](right, left)
        pieces += [right, left]
    return pieces


def on_device(residuals, seg_counts, attitude, sched_seg, sched_slot, periods):
    tm_count = lax.axis_size("tm")
    sched_dev, obs = sched_seg.shape
    seg_dev, slots, width = residuals.shape
    column_blocks = width // SRC_GROUP
    capacity = 2 * sched_dev * obs // tm_count
    tables, times, wanted = make_lists(
        sched_seg, sched_slot, seg_dev, slots, column_blocks, tm_count, capacity
    )
    wanted = wanted.reshape(tm_count, capacity)
    part = sched_dev // BASIS_CALLS
    made = []
    asked = None

    def basis_part(after):
        first = len(made) * part
        made.append(make_basis(times[first:first + part], periods, after))

    def first_hop(right, left):
        basis_part([right, left])
        basis_part([right, left])
        return right, left

    def second_hop(right, left):
        nonlocal asked
        basis_part([right, left])
        held, _ = lax.optimization_barrier((wanted, made[-1][1]))
        asked = lax.all_to_all(held, "tm", split_axis=0, concat_axis=0, tiled=True)
        return right, left

    pieces = pass_along(attitude, {1: first_hop, 2: second_hop})
    cnt = jnp.sum((asked < seg_dev * slots * column_blocks).astype(jnp.int32), axis=1)
    where = jnp.stack([lax.axis_index("tm"), lax.axis_index("sky")])
    scalars = (asked.reshape(-1), cnt, seg_counts, where)
    rows = seg_dev * slots * column_blocks
    order = [0] + send_order(tm_count)
    near, far = order[:3 * tm_count // 4], order[3 * tm_count // 4:]

    base = residuals
    picked = pick_rows(scalars, base, pieces, rows)
    basis_part([picked[0]])
    parts, norms = zip(*made)
    norms = jnp.concatenate(norms)
    for iteration in range(ITERS):
        models, score = fit_plans(tables, exchange(picked), parts, norms)
        returned = exchange(models)
        base = place_early(scalars, near, base, returned, rows)
        if iteration < ITERS - 1:
            base, picked = place_late_and_pick(scalars, far, base, returned, pieces)
    cleaned = place_late(scalars, far, base, returned, residuals.shape)
    return (cleaned, score.reshape(sched_dev, SRC_GROUP))


def solution(mesh):
    in_specs = (
        P("tm", None, "sky"),
        P("tm"),
        P("tm", "sky", None),
        P(("tm", "sky"), None),
        P(("tm", "sky"), None),
        P(),
    )
    out_specs = (P("tm", None, "sky"), P(("tm", "sky"), None))
    return jax.shard_map(
        on_device, mesh=mesh, in_specs=in_specs, out_specs=out_specs, check_vma=False
    )
```

```python
import functools

import jax
import jax.numpy as jnp
from jax import lax
from jax.experimental import pallas as pl
from jax.experimental.pallas import tpu as pltpu
from jax.sharding import PartitionSpec as P

SRC_GROUP = 128
ITERS = 2
STREAMS = 4
LATE_STREAMS = 2
STEP = 16
BETA = 2.0
RIDGE = 1.0
MIB = 1024 * 1024
BASIS_VMEM = 8 * MIB
FIT_VMEM = 22 * MIB
EARLY_VMEM = 20 * MIB
PICK_VMEM = 12 * MIB
LATE_PICK_VMEM = 18 * MIB
LATE_VMEM = 12 * MIB
BASIS_CALLS = (1, 2, 3, 2)
UNROLL = 32
PICK_UNROLL = 16
SUB = 8
HBM_ROWS = 24 * 1024 * 1024 // 512
HBM_PLANS = 48
COST_US = 10 ** 9

COS_POLY = (1.0, -19.73920440673828, 64.9391098022461, -85.4500503540039, 60.16689682006836,
            -25.96480369567871, 6.52468729019165)
SIN_POLY = (6.283185005187988, -41.34158706665039, 81.59986114501953, -76.61351013183594,
            41.33811950683594, -12.463061332702637)

VMEM = pl.BlockSpec(memory_space=pltpu.VMEM)
HBM = pl.BlockSpec(memory_space=pltpu.HBM)
ANY = pl.BlockSpec(memory_space=pl.ANY)
SMEM = pl.BlockSpec(memory_space=pltpu.SMEM)


def horner(poly, v):
    acc = jnp.full_like(v, poly[-1])
    for term in poly[-2::-1]:
        acc = acc * v + term
    return acc


def basis_kernel(time_ref, period_ref, inverse_ref, *refs):
    basis_ref, norm_ref = refs[-2:]
    obs = time_ref.shape[0]
    nper = period_ref.shape[1]
    rows = 32
    for chunk in range(nper // 128):
        lanes = pl.ds(chunk * 128, 128)
        sines = pl.ds(nper + chunk * 128, 128)
        period = period_ref[:, lanes]
        inverse = inverse_ref[:, lanes]

        def step(index, sums):
            at = pl.ds(pl.multiple_of(index * rows, rows), rows)
            time = time_ref[at, :]
            turns = jnp.round(time * inverse)
            part = (time - turns * period) * inverse
            square = part * part
            cosine = horner(COS_POLY, square).astype(jnp.bfloat16)
            sine = (horner(SIN_POLY, square) * part).astype(jnp.bfloat16)
            basis_ref[0, at, lanes] = cosine
            basis_ref[0, at, sines] = sine
            cosine = cosine.astype(jnp.float32)
            sine = sine.astype(jnp.float32)
            return (
                sums[0] + jnp.sum((cosine * cosine).reshape(rows // 8, 8, 128), axis=0),
                sums[1] + jnp.sum((sine * sine).reshape(rows // 8, 8, 128), axis=0),
            )

        zero = jnp.zeros((8, 128), jnp.float32)
        total_c, total_s = lax.fori_loop(0, obs // rows, step, (zero, zero))
        norm_ref[0, :, lanes] = 1.0 / (jnp.sum(total_c, axis=0, keepdims=True) + RIDGE)
        norm_ref[0, :, sines] = 1.0 / (jnp.sum(total_s, axis=0, keepdims=True) + RIDGE)


def make_basis(times, periods, first, count, held, after):
    sched_dev, obs = times.shape
    nper = periods.shape[0]
    wide = jnp.broadcast_to(
        times[first:first + count].astype(jnp.float32).reshape(-1, 1), (count * obs, SRC_GROUP)
    )
    period = periods.astype(jnp.float32)[None, :]
    others = after + ([] if held is None else [held])
    return pl.pallas_call(
        basis_kernel,
        grid=(count,),
        in_specs=[
            pl.BlockSpec((obs, SRC_GROUP), lambda j: (j, 0)),
            pl.BlockSpec((1, nper), lambda j: (0, 0)),
            pl.BlockSpec((1, nper), lambda j: (0, 0)),
        ] + [ANY] * len(others),
        out_specs=[
            pl.BlockSpec((1, obs, 2 * nper), lambda j: (first + j, 0, 0)),
            pl.BlockSpec((1, 1, 2 * nper), lambda j: (j, 0, 0)),
        ],
        out_shape=[
            jax.ShapeDtypeStruct((max(HBM_PLANS, sched_dev), obs, 2 * nper), jnp.bfloat16),
            jax.ShapeDtypeStruct((count, 1, 2 * nper), jnp.float32),
        ],
        input_output_aliases={} if held is None else {2 + len(others): 0},
        compiler_params=pltpu.CompilerParams(vmem_limit_bytes=BASIS_VMEM),
        cost_estimate=pl.CostEstimate(
            flops=count * obs * nper * 2500, bytes_accessed=count * obs * nper * 4, transcendentals=0
        ),
    )(wide, period, 1.0 / period, *others)


def fit_kernel(order, src_ref, dst_ref, *refs):
    refs = list(refs)

    def take(count):
        taken = refs[:count]
        del refs[:count]
        return taken

    tm_count = len(order)
    arrived = dict(zip(order, take(tm_count)))
    all_ref, norm_ref = take(2)
    outs = take(tm_count)
    score_ref, basis_ref, sems, rows_ref, back_ref = take(5)
    slots = [take(4), take(4)]
    plans, obs, twice = basis_ref.shape
    nper = twice // 2
    capacity, width = arrived[0].shape
    spaced = capacity + STEP
    steps = src_ref.shape[1]

    def basis_copy(plan):
        return pltpu.make_async_copy(all_ref.at[plan], basis_ref.at[plan], sems.at[plan])

    for plan in range(plans):
        basis_copy(plan).start()
    for owner in range(tm_count):
        rows_ref[pl.ds(owner * spaced, capacity), :] = arrived[owner][...].astype(jnp.float32)

    def correlate(plan, obs_ref, corr_ref):
        for step in range(steps):
            obs_ref[pl.ds(dst_ref[plan, step], STEP), :] = rows_ref[pl.ds(src_ref[plan, step], STEP), :]
        corr_ref[...] = lax.dot_general(
            obs_ref[:obs, :].astype(jnp.bfloat16), basis_ref[plan], (((0,), (0,)), ((), ())),
            preferred_element_type=jnp.float32,
        )

    def finish(plan, corr_ref, coeff_ref, model_ref):
        group = 16
        for start in range(0, width, group):
            at = pl.ds(start, group)
            power = []
            for chunk in range(nper // 128):
                lanes = pl.ds(chunk * 128, 128)
                sines = pl.ds(nper + chunk * 128, 128)
                cosine = corr_ref[at, lanes]
                sine = corr_ref[at, sines]
                power.append(
                    cosine * (cosine * norm_ref[plan, :, lanes]) + sine * (sine * norm_ref[plan, :, sines])
                )
            highest = functools.reduce(jnp.maximum, power)
            highest = jnp.max(highest, axis=1, keepdims=True)
            expo = [jnp.exp(BETA * (value - highest)) for value in power]
            total = jnp.sum(functools.reduce(jnp.add, expo), axis=1, keepdims=True)
            scale = 1.0 / total
            for chunk in range(nper // 128):
                lanes = pl.ds(chunk * 128, 128)
                sines = pl.ds(nper + chunk * 128, 128)
                share = expo[chunk] * scale
                coeff_ref[at, lanes] = (share * (corr_ref[at, lanes] * norm_ref[plan, :, lanes])).astype(jnp.bfloat16)
                coeff_ref[at, sines] = (share * (corr_ref[at, sines] * norm_ref[plan, :, sines])).astype(jnp.bfloat16)
            score_ref[plan, at, :] = BETA * highest + jnp.log(total)
        model_ref[:obs, :] = lax.dot_general(
            basis_ref[plan], coeff_ref[...], (((1,), (1,)), ((), ())), preferred_element_type=jnp.float32
        )
        for step in range(steps):
            back_ref[pl.ds(src_ref[plan, step], STEP), :] = model_ref[pl.ds(dst_ref[plan, step], STEP), :]

    basis_copy(0).wait()
    correlate(0, slots[0][0], slots[0][1])

    def pair(index, carry):
        plan = index * 2
        for ahead in (1, 2):
            for known in range(ahead, plans, 2):
                pl.when(plan + ahead == known)(basis_copy(known).wait)
        correlate(plan + 1, slots[1][0], slots[1][1])
        finish(plan, *slots[0][1:])
        correlate(jnp.minimum(plan + 2, plans - 1), slots[0][0], slots[0][1])
        finish(plan + 1, *slots[1][1:])
        return carry

    lax.fori_loop(0, plans // 2, pair, 0)
    for owner in range(tm_count):
        outs[owner][...] = back_ref[pl.ds(owner * spaced, capacity), :].astype(jnp.bfloat16)


def fit_plans(tables, arrived, basis, norms):
    tm_count = len(arrived)
    order = [0] + ask_order(tm_count)
    _, obs, twice = basis.shape
    sched_dev = norms.shape[0]
    capacity, width = arrived[0].shape
    work = sched_dev * obs * twice * width
    spaced = tm_count * (capacity + STEP) + STEP
    slot = [
        pltpu.VMEM((obs + STEP, width), jnp.float32),
        pltpu.VMEM((width, twice), jnp.float32),
        pltpu.VMEM((width, twice), jnp.bfloat16),
        pltpu.VMEM((obs + STEP, width), jnp.float32),
    ]
    *models, score = pl.pallas_call(
        functools.partial(fit_kernel, order),
        in_specs=[SMEM, SMEM] + [VMEM] * tm_count + [ANY, VMEM],
        out_specs=[VMEM] * (tm_count + 1),
        out_shape=[jax.ShapeDtypeStruct((capacity, width), jnp.bfloat16)] * tm_count
        + [jax.ShapeDtypeStruct((sched_dev, width, 1), jnp.float32)],
        scratch_shapes=[
            pltpu.VMEM((sched_dev, obs, twice), jnp.bfloat16),
            pltpu.SemaphoreType.DMA((sched_dev,)),
            pltpu.VMEM((spaced, width), jnp.float32),
            pltpu.VMEM((spaced, width), jnp.float32),
        ] + slot + slot,
        compiler_params=pltpu.CompilerParams(vmem_limit_bytes=FIT_VMEM),
        cost_estimate=pl.CostEstimate(flops=20 * work, bytes_accessed=sched_dev * obs * twice * 2, transcendentals=0),
    )(*tables, *[arrived[owner] for owner in order], basis, norms)
    return models, score


def load_attitude(sky, own_ref, passed, whole_ref, sems):
    rows = own_ref.shape[1]
    count = len(passed) // 2 + 1
    copies = [(None, sky, own_ref)]
    for hop in range(1, count):
        copies.append((sky >= hop, sky - hop, passed[2 * hop - 2]))
        copies.append((sky + hop < count, sky + hop, passed[2 * hop - 1]))

    def each(act):
        for index, (valid, quarter, ref) in enumerate(copies):
            def run(index=index, quarter=quarter, ref=ref):
                at = pl.ds(pl.multiple_of(quarter * rows, rows), rows)
                act(pltpu.make_async_copy(ref, whole_ref.at[:, at, :], sems.at[index]))

            if valid is None:
                run()
            else:
                pl.when(valid)(run)

    each(lambda copy: copy.start())
    return lambda: each(lambda copy: copy.wait())


def whiten_and_pick(me, asked_ref, cnt_ref, count_ref, whole_ref, wait, load, picked, white_ref, gather_ref):
    segs, slots, _ = whole_ref.shape
    capacity, width = picked[0].shape
    blocks = white_ref.shape[0] // (segs * slots)
    row = lax.broadcasted_iota(jnp.int32, (slots, width * blocks), 0)
    wait()
    for seg in range(segs):
        masked = jnp.where(row < count_ref[seg], load(seg).astype(jnp.float32), 0.0).astype(jnp.bfloat16)
        white = jnp.dot(whole_ref[seg], masked, preferred_element_type=jnp.float32)
        for block in range(blocks):
            white_ref[pl.ds((block * segs + seg) * slots, slots), :] = white[:, block * width:(block + 1) * width]
    for owner, out_ref in enumerate(picked):
        asker = owner ^ me

        def step(index, carry):
            first = index * PICK_UNROLL
            for lane in range(PICK_UNROLL):
                gather_ref[pl.ds(owner * capacity + first + lane, 1), :] = white_ref[
                    pl.ds(asked_ref[asker * capacity + first + lane], 1), :
                ]
            return carry

        lax.fori_loop(0, (cnt_ref[asker] + PICK_UNROLL - 1) // PICK_UNROLL, step, 0)
        out_ref[...] = gather_ref[pl.ds(owner * capacity, capacity), :].astype(jnp.bfloat16)


def add_rows(me, asked_ref, cnt_ref, owners, returned, rows_ref, sums, tiled):
    capacity = returned[0].shape[0]
    streams = len(sums)
    for total in sums:
        total[...] = jnp.zeros_like(total)
    for number, (owner, ref) in enumerate(zip(owners, returned)):
        tiles = capacity // SUB
        block = ref[...].astype(jnp.float32)
        if tiled:
            rows_ref[pl.ds(number * tiles, tiles)] = block.reshape(tiles, SUB, -1)
        else:
            rows_ref[pl.ds(number * capacity, capacity), :] = block
        asker = owner ^ me

        def row_at(index, lane):
            if tiled:
                return rows_ref[number * tiles + index * (UNROLL // SUB) + lane // SUB, pl.ds(lane % SUB, 1), :]
            return rows_ref[pl.ds(number * capacity + index * UNROLL + lane, 1), :]

        def step(index, carry):
            first = asker * capacity + index * UNROLL
            for start in range(0, UNROLL, streams):
                lanes = [start + lane for lane in range(streams)]
                places = [asked_ref[first + lane] for lane in lanes]
                values = [
                    total[pl.ds(place, 1), :] + row_at(index, lane)
                    for total, place, lane in zip(sums, places, lanes)
                ]
                for total, place, value in zip(sums, places, values):
                    total[pl.ds(place, 1), :] = value
            return carry

        lax.fori_loop(0, (cnt_ref[asker] + UNROLL - 1) // UNROLL, step, 0)


def placed_at(sums, at):
    return functools.reduce(jnp.add, [total[at, :] for total in sums])


def early_kernel(owners, table_base, asked_ref, cnt_ref, where_ref, base_ref, *refs):
    refs = list(refs)
    returned = [refs.pop(0) for _ in owners]
    out_ref, rows_ref = refs.pop(0), refs.pop(0)
    if table_base:
        held_ref, sem = refs.pop(0), refs.pop(0)
        copy = pltpu.make_async_copy(base_ref.at[pl.ds(0, held_ref.shape[0]), :], held_ref, sem)
        copy.start()
    add_rows(where_ref[0], asked_ref, cnt_ref, owners, returned, rows_ref, refs, not table_base)
    if table_base:
        copy.wait()
        out_ref[...] = held_ref[...] - placed_at(refs, pl.ds(0, out_ref.shape[0]))
        return
    segs, slots, total_width = base_ref.shape
    width = out_ref.shape[1]
    for block in range(total_width // width):
        for seg in range(segs):
            at = pl.ds((block * segs + seg) * slots, slots)
            base = base_ref[seg, :, block * width:(block + 1) * width].astype(jnp.float32)
            out_ref[at, :] = base - placed_at(refs, at)


def place_early(scalars, owners, base, returned, rows):
    asked, cnt, _, where = scalars
    table_base = base.ndim == 2
    capacity = returned[0].shape[0]
    sums = [pltpu.VMEM((rows + 8, SRC_GROUP), jnp.float32)] * STREAMS
    shape = (len(owners) * capacity, SRC_GROUP)
    if not table_base:
        shape = (shape[0] // SUB, SUB, SRC_GROUP)
    held = [pltpu.VMEM((rows, SRC_GROUP), jnp.float32), pltpu.SemaphoreType.DMA(())] if table_base else []
    return pl.pallas_call(
        functools.partial(early_kernel, owners, table_base),
        in_specs=[SMEM] * 3 + [HBM if table_base else VMEM] + [VMEM] * len(owners),
        out_specs=VMEM,
        out_shape=jax.ShapeDtypeStruct((rows, SRC_GROUP), jnp.float32),
        scratch_shapes=[pltpu.VMEM(shape, jnp.float32)] + held + sums,
        compiler_params=pltpu.CompilerParams(vmem_limit_bytes=EARLY_VMEM),
        cost_estimate=pl.CostEstimate(flops=6 * COST_US, bytes_accessed=1 << 20, transcendentals=0),
    )(asked, cnt, where, base, *[returned[owner] for owner in owners])


def pick_kernel(tm_count, passed_count, asked_ref, cnt_ref, count_ref, where_ref, base_ref, own_ref, *refs):
    refs = list(refs)
    passed = [refs.pop(0) for _ in range(passed_count)]
    picked = [refs.pop(0) for _ in range(tm_count)]
    whole_ref, sems, white_ref, gather_ref = refs
    wait = load_attitude(where_ref[1], own_ref, passed, whole_ref, sems)
    whiten_and_pick(
        where_ref[0], asked_ref, cnt_ref, count_ref, whole_ref, wait, lambda seg: base_ref[seg], picked, white_ref,
        gather_ref,
    )


def pick_rows(scalars, base, attitude, rows):
    asked, cnt, seg_counts, where = scalars
    tm_count, = cnt.shape
    seg_dev, slots, _ = base.shape
    capacity = asked.shape[0] // tm_count
    return pl.pallas_call(
        functools.partial(pick_kernel, tm_count, len(attitude) - 1),
        in_specs=[SMEM] * 4 + [VMEM] + [ANY] * len(attitude),
        out_specs=[VMEM] * tm_count,
        out_shape=[jax.ShapeDtypeStruct((capacity, SRC_GROUP), jnp.bfloat16)] * tm_count,
        scratch_shapes=[
            pltpu.VMEM((seg_dev, slots, slots), jnp.bfloat16),
            pltpu.SemaphoreType.DMA((len(attitude),)),
            pltpu.VMEM((rows + 8, SRC_GROUP), jnp.float32),
            pltpu.VMEM((tm_count * capacity, SRC_GROUP), jnp.float32),
        ],
        compiler_params=pltpu.CompilerParams(vmem_limit_bytes=PICK_VMEM),
        cost_estimate=pl.CostEstimate(flops=5 * COST_US, bytes_accessed=1 << 20, transcendentals=0),
    )(asked, cnt, seg_counts, where, base, *attitude)


def late_pick_kernel(tm_count, passed_count, owners, asked_ref, cnt_ref, count_ref, where_ref, part_ref, own_ref,
                     *refs):
    refs = list(refs)

    def take(count):
        taken = refs[:count]
        del refs[:count]
        return taken

    passed = take(passed_count)
    returned = take(len(owners))
    (out_ref,) = take(1)
    picked = take(tm_count)
    whole_ref, sems, white_ref, gather_ref, table_ref, sem = take(6)
    segs, slots, _ = whole_ref.shape
    blocks = table_ref.shape[0] // (segs * slots)
    wait = load_attitude(where_ref[1], own_ref, passed, whole_ref, sems)
    add_rows(where_ref[0], asked_ref, cnt_ref, owners, returned, gather_ref, refs, False)
    table_ref[...] = part_ref[...] - placed_at(refs, pl.ds(0, table_ref.shape[0]))
    copy = pltpu.make_async_copy(table_ref, out_ref.at[pl.ds(0, table_ref.shape[0]), :], sem)
    copy.start()

    def load(seg):
        return jnp.concatenate(
            [table_ref[pl.ds((block * segs + seg) * slots, slots), :] for block in range(blocks)], axis=1
        )

    whiten_and_pick(
        where_ref[0], asked_ref, cnt_ref, count_ref, whole_ref, wait, load, picked, white_ref, gather_ref
    )
    copy.wait()


def place_late_and_pick(scalars, owners, part, returned, attitude):
    asked, cnt, seg_counts, where = scalars
    tm_count, = cnt.shape
    seg_dev = seg_counts.shape[0]
    slots = attitude[0].shape[2]
    capacity = asked.shape[0] // tm_count
    rows = part.shape[0]
    table = pltpu.VMEM((rows + 8, SRC_GROUP), jnp.float32)
    out = pl.pallas_call(
        functools.partial(late_pick_kernel, tm_count, len(attitude) - 1, owners),
        in_specs=[SMEM] * 4 + [VMEM] + [ANY] * len(attitude) + [VMEM] * len(owners),
        out_specs=[HBM] + [VMEM] * tm_count,
        out_shape=[jax.ShapeDtypeStruct((max(HBM_ROWS, rows), SRC_GROUP), jnp.float32)]
        + [jax.ShapeDtypeStruct((capacity, SRC_GROUP), jnp.bfloat16)] * tm_count,
        scratch_shapes=[
            pltpu.VMEM((seg_dev, slots, slots), jnp.bfloat16),
            pltpu.SemaphoreType.DMA((len(attitude),)),
            table,
            pltpu.VMEM((tm_count * capacity, SRC_GROUP), jnp.float32),
            pltpu.VMEM((rows, SRC_GROUP), jnp.float32),
            pltpu.SemaphoreType.DMA(()),
        ] + [table] * LATE_STREAMS,
        compiler_params=pltpu.CompilerParams(vmem_limit_bytes=LATE_PICK_VMEM),
        cost_estimate=pl.CostEstimate(flops=7 * COST_US, bytes_accessed=1 << 20, transcendentals=0),
    )(asked, cnt, seg_counts, where, part, *attitude, *[returned[owner] for owner in owners])
    return out[0], list(out[1:])


def late_kernel(owners, asked_ref, cnt_ref, where_ref, part_ref, *refs):
    refs = list(refs)
    returned = [refs.pop(0) for _ in owners]
    out_ref, rows_ref, held_ref, sems = refs[:4]
    sums = refs[4:]
    segs, slots, total_width = out_ref.shape
    width = part_ref.shape[1]
    add_rows(where_ref[0], asked_ref, cnt_ref, owners, returned, rows_ref, sums, False)
    copies = []
    for seg in range(segs):
        for block in range(total_width // width):
            at = pl.ds((block * segs + seg) * slots, slots)
            held_ref[seg, :, block * width:(block + 1) * width] = part_ref[at, :] - placed_at(sums, at)
        copies.append(pltpu.make_async_copy(held_ref.at[seg], out_ref.at[seg], sems.at[seg]))
        copies[-1].start()
    for copy in copies:
        copy.wait()


def place_late(scalars, owners, part, returned, shape):
    asked, cnt, _, where = scalars
    capacity = returned[0].shape[0]
    return pl.pallas_call(
        functools.partial(late_kernel, owners),
        in_specs=[SMEM] * 3 + [VMEM] * (1 + len(owners)),
        out_specs=HBM,
        out_shape=jax.ShapeDtypeStruct(shape, jnp.float32),
        scratch_shapes=[
            pltpu.VMEM((len(owners) * capacity, SRC_GROUP), jnp.float32),
            pltpu.VMEM(shape, jnp.float32),
            pltpu.SemaphoreType.DMA((shape[0],)),
        ] + [pltpu.VMEM((part.shape[0] + 8, SRC_GROUP), jnp.float32)] * LATE_STREAMS,
        compiler_params=pltpu.CompilerParams(vmem_limit_bytes=LATE_VMEM),
        cost_estimate=pl.CostEstimate(flops=4 * COST_US, bytes_accessed=1 << 20, transcendentals=0),
    )(asked, cnt, where, part, *[returned[owner] for owner in owners])


def make_lists(sched_seg, sched_slot, seg_dev, slots, column_blocks, tm_count, capacity):
    sched_dev, obs = sched_seg.shape
    me = lax.axis_index("tm")
    owner = sched_seg // seg_dev
    partner = owner ^ me
    block_of = (jnp.arange(sched_dev, dtype=jnp.int32) % column_blocks)[:, None]
    local_row = (block_of * seg_dev + sched_seg % seg_dev) * slots + sched_slot
    hot = (partner[:, :, None] == jnp.arange(tm_count, dtype=jnp.int32)).astype(jnp.int32)
    cnt = jnp.sum(hot, axis=1)
    plans = jnp.arange(sched_dev)
    before = (plans[None, :] < plans[:, None]).astype(jnp.int32)
    src = jnp.sum(before[:, :, None] * cnt[None, :, :], axis=1)
    owners = jnp.arange(tm_count)
    ahead = (owners[None, :] < owners[:, None]).astype(jnp.int32)
    dst = jnp.sum(ahead[None, :, :] * cnt[:, None, :], axis=2)
    entry = jnp.arange(obs)
    rank = jnp.sum(
        ((partner[:, None, :] == partner[:, :, None]) & (entry[None, :] < entry[:, None])).astype(jnp.int32),
        axis=2,
    )
    place = owner * capacity + jnp.sum(hot * src[:, None, :], axis=2) + rank
    order = jnp.sum(hot * dst[:, None, :], axis=2) + rank
    time = sched_seg * slots + sched_slot
    times = jnp.sum(jnp.where(order[:, None, :] == entry[None, :, None], time[:, None, :], 0), axis=2)
    rows = seg_dev * slots * column_blocks
    wanted = rows + jnp.sum(
        jnp.where(
            place.reshape(1, -1) == jnp.arange(tm_count * capacity, dtype=jnp.int32)[:, None],
            local_row.reshape(1, -1) - rows,
            0,
        ),
        axis=1,
    )
    step_count = (cnt + STEP - 1) // STEP
    step_first = jnp.sum(ahead[None, :, :] * step_count[:, None, :], axis=2)
    step = jnp.arange(obs // STEP + tm_count)[None, :, None] - step_first[:, None, :]
    inside = (step >= 0) & (step < step_count[:, None, :])
    spaced = capacity + STEP
    end = tm_count * spaced
    step_src = end + jnp.sum(
        jnp.where(inside, owners * spaced - end + src[:, None, :] + step * STEP, 0), axis=2
    )
    step_dst = obs + jnp.sum(jnp.where(inside, dst[:, None, :] + step * STEP - obs, 0), axis=2)
    return (step_src, step_dst), times, wanted


def send_order(count):
    return sorted(range(1, count), key=lambda step: (bin(step // 2).count("1"), step % 2, -step))


def ask_order(count):
    first = [1, count // 2]
    return first + sorted(
        (step for step in range(2, count) if step not in first), key=lambda step: -bin(step // 2).count("1")
    )


def exchange(blocks):
    count = len(blocks)
    out = list(blocks)
    for step in range(1, count):
        out[step] = lax.ppermute(blocks[step], "tm", [(i, i ^ step) for i in range(count)])
    return out


def pass_along(attitude, beside):
    count = lax.axis_size("sky")
    right = left = attitude
    pieces = [attitude]
    for hop in range(1, count):
        right = lax.ppermute(right, "sky", [(i, i + 1) for i in range(hop - 1, count - 1)])
        left = lax.ppermute(left, "sky", [(i, i - 1) for i in range(1, count - hop + 1)])
        if hop in beside:
            right, left = beside[hop](right, left)
        pieces += [right, left]
    return pieces


def on_device(residuals, seg_counts, attitude, sched_seg, sched_slot, periods):
    tm_count = lax.axis_size("tm")
    sched_dev, obs = sched_seg.shape
    seg_dev, slots, width = residuals.shape
    column_blocks = width // SRC_GROUP
    capacity = 2 * sched_dev * obs // tm_count
    tables, times, wanted = make_lists(
        sched_seg, sched_slot, seg_dev, slots, column_blocks, tm_count, capacity
    )
    wanted = wanted.reshape(tm_count, capacity)
    basis, norms = None, []
    asked = None

    def basis_part(after):
        nonlocal basis
        first, count = sum(BASIS_CALLS[:len(norms)]), BASIS_CALLS[len(norms)]
        basis, norm = make_basis(times, periods, first, count, basis, after)
        norms.append(norm)

    def first_hop(right, left):
        nonlocal asked
        held, right, left = lax.optimization_barrier((wanted, right, left))
        basis_part([right, left])
        held, _ = lax.optimization_barrier((held, norms[0]))
        asked = lax.all_to_all(held, "tm", split_axis=0, concat_axis=0, tiled=True)
        basis_part([])
        return right, left

    def second_hop(right, left):
        basis_part([right, left])
        return right, left

    pieces = pass_along(attitude, {1: first_hop, 2: second_hop})
    cnt = jnp.sum((asked < seg_dev * slots * column_blocks).astype(jnp.int32), axis=1)
    where = jnp.stack([lax.axis_index("tm"), lax.axis_index("sky")])
    scalars = (asked.reshape(-1), cnt, seg_counts, where)
    rows = seg_dev * slots * column_blocks
    order = [0] + send_order(tm_count)
    near, far = order[:3 * tm_count // 4], order[3 * tm_count // 4:]

    base = residuals
    picked = pick_rows(scalars, base, pieces, rows)
    basis_part([picked[0]])
    norms = jnp.concatenate(norms)
    for iteration in range(ITERS):
        models, score = fit_plans(tables, exchange(picked), basis, norms)
        returned = exchange(models)
        base = place_early(scalars, near, base, returned, rows)
        if iteration < ITERS - 1:
            base, picked = place_late_and_pick(scalars, far, base, returned, pieces)
    cleaned = place_late(scalars, far, base, returned, residuals.shape)
    return (cleaned, score.reshape(sched_dev, SRC_GROUP))


def solution(mesh):
    in_specs = (
        P("tm", None, "sky"),
        P("tm"),
        P("tm", "sky", None),
        P(("tm", "sky"), None),
        P(("tm", "sky"), None),
        P(),
    )
    out_specs = (P("tm", None, "sky"), P(("tm", "sky"), None))
    return jax.shard_map(
        on_device, mesh=mesh, in_specs=in_specs, out_specs=out_specs, check_vma=False
    )
```

```python
import functools

import jax
import jax.numpy as jnp
from jax import lax
from jax.experimental import pallas as pl
from jax.experimental.pallas import tpu as pltpu
from jax.sharding import PartitionSpec as P

SRC_GROUP = 128
ITERS = 2
STREAMS = 4
LATE_STREAMS = 2
STEP = 16
BETA = 2.0
ROUND = 1.5 * 2.0 ** 23
RIDGE = 1.0
MIB = 1024 * 1024
BASIS_VMEM = 8 * MIB
FIT_VMEM = 22 * MIB
EARLY_VMEM = 20 * MIB
PICK_VMEM = 12 * MIB
LATE_PICK_VMEM = 18 * MIB
LATE_VMEM = 12 * MIB
BASIS_CALLS = (1, 2, 2, 3)
UNROLL = 32
PICK_UNROLL = 16
SUB = 8
HBM_SPARE = 32
COST_US = 10 ** 9

COS_POLY = (1.0, -19.73920440673828, 64.9391098022461, -85.4500503540039, 60.16689682006836,
            -25.96480369567871, 6.52468729019165)
SIN_POLY = (6.283185005187988, -41.34158706665039, 81.59986114501953, -76.61351013183594,
            41.33811950683594, -12.463061332702637)

VMEM = pl.BlockSpec(memory_space=pltpu.VMEM)
HBM = pl.BlockSpec(memory_space=pltpu.HBM)
ANY = pl.BlockSpec(memory_space=pl.ANY)
SMEM = pl.BlockSpec(memory_space=pltpu.SMEM)


def horner(poly, v):
    acc = jnp.full_like(v, poly[-1])
    for term in poly[-2::-1]:
        acc = acc * v + term
    return acc


def basis_kernel(after, time_ref, period_ref, inverse_ref, *refs):
    basis_ref, norm_ref = refs[after:]
    obs = time_ref.shape[0]
    nper = period_ref.shape[1]
    rows = 64
    for chunk in range(nper // 128):
        lanes = pl.ds(chunk * 128, 128)
        sines = pl.ds(nper + chunk * 128, 128)
        period = period_ref[:, lanes]
        inverse = inverse_ref[:, lanes]

        def step(index, sums):
            at = pl.ds(pl.multiple_of(index * rows, rows), rows)
            time = time_ref[at, :]
            turns = (time * inverse + ROUND) - ROUND
            part = (time - turns * period) * inverse
            square = part * part
            cosine = horner(COS_POLY, square).astype(jnp.bfloat16)
            sine = (horner(SIN_POLY, square) * part).astype(jnp.bfloat16)
            basis_ref[0, at, lanes] = cosine
            basis_ref[0, at, sines] = sine
            cosine = cosine.astype(jnp.float32)
            sine = sine.astype(jnp.float32)
            return (
                sums[0] + jnp.sum((cosine * cosine).reshape(rows // 8, 8, 128), axis=0),
                sums[1] + jnp.sum((sine * sine).reshape(rows // 8, 8, 128), axis=0),
            )

        zero = jnp.zeros((8, 128), jnp.float32)
        total_c, total_s = lax.fori_loop(0, obs // rows, step, (zero, zero))
        norm_ref[0, :, lanes] = 1.0 / (jnp.sum(total_c, axis=0, keepdims=True) + RIDGE)
        norm_ref[0, :, sines] = 1.0 / (jnp.sum(total_s, axis=0, keepdims=True) + RIDGE)


def make_basis(times, periods, after):
    sched_dev, obs = times.shape
    nper = periods.shape[0]
    wide = jnp.broadcast_to(
        times.astype(jnp.float32).reshape(-1, 1), (sched_dev * obs, SRC_GROUP)
    )
    period = periods.astype(jnp.float32)[None, :]
    return pl.pallas_call(
        functools.partial(basis_kernel, len(after)),
        grid=(sched_dev,),
        in_specs=[
            pl.BlockSpec((obs, SRC_GROUP), lambda j: (j, 0)),
            pl.BlockSpec((1, nper), lambda j: (0, 0)),
            pl.BlockSpec((1, nper), lambda j: (0, 0)),
        ] + [ANY] * len(after),
        out_specs=[
            pl.BlockSpec((1, obs, 2 * nper), lambda j: (j, 0, 0)),
            pl.BlockSpec((1, 1, 2 * nper), lambda j: (j, 0, 0)),
        ],
        out_shape=[
            jax.ShapeDtypeStruct((sched_dev, obs, 2 * nper), jnp.bfloat16),
            jax.ShapeDtypeStruct((sched_dev, 1, 2 * nper), jnp.float32),
        ],
        compiler_params=pltpu.CompilerParams(vmem_limit_bytes=BASIS_VMEM),
        cost_estimate=pl.CostEstimate(
            flops=sched_dev * obs * nper * 8000, bytes_accessed=sched_dev * obs * nper * 4, transcendentals=0
        ),
    )(wide, period, 1.0 / period, *after)


def fit_kernel(order, src_ref, dst_ref, *refs):
    refs = list(refs)

    def take(count):
        taken = refs[:count]
        del refs[:count]
        return taken

    tm_count = len(order)
    arrived = dict(zip(order, take(tm_count)))
    parts = take(len(BASIS_CALLS))
    (norm_ref,) = take(1)
    outs = take(tm_count)
    score_ref, basis_ref, sems, rows_ref, back_ref = take(5)
    slots = [take(4), take(4)]
    plans, obs, twice = basis_ref.shape
    nper = twice // 2
    capacity, width = arrived[0].shape
    spaced = capacity + STEP
    steps = src_ref.shape[1]
    held = [(part, plan) for part, count in zip(parts, BASIS_CALLS) for plan in range(count)]

    def basis_copy(plan):
        part, index = held[plan]
        return pltpu.make_async_copy(part.at[index], basis_ref.at[plan], sems.at[plan])

    for plan in range(plans):
        basis_copy(plan).start()
    for owner in range(tm_count):
        rows_ref[pl.ds(owner * spaced, capacity), :] = arrived[owner][...].astype(jnp.float32)

    def correlate(plan, obs_ref, corr_ref):
        for step in range(steps):
            obs_ref[pl.ds(dst_ref[plan, step], STEP), :] = rows_ref[pl.ds(src_ref[plan, step], STEP), :]
        corr_ref[...] = lax.dot_general(
            obs_ref[:obs, :].astype(jnp.bfloat16), basis_ref[plan], (((0,), (0,)), ((), ())),
            preferred_element_type=jnp.float32,
        )

    def finish(plan, corr_ref, coeff_ref, model_ref):
        group = 16
        for start in range(0, width, group):
            at = pl.ds(start, group)
            power = []
            for chunk in range(nper // 128):
                lanes = pl.ds(chunk * 128, 128)
                sines = pl.ds(nper + chunk * 128, 128)
                cosine = corr_ref[at, lanes]
                sine = corr_ref[at, sines]
                power.append(
                    cosine * (cosine * norm_ref[plan, :, lanes]) + sine * (sine * norm_ref[plan, :, sines])
                )
            highest = functools.reduce(jnp.maximum, power)
            highest = jnp.max(highest, axis=1, keepdims=True)
            expo = [jnp.exp(BETA * (value - highest)) for value in power]
            total = jnp.sum(functools.reduce(jnp.add, expo), axis=1, keepdims=True)
            scale = 1.0 / total
            for chunk in range(nper // 128):
                lanes = pl.ds(chunk * 128, 128)
                sines = pl.ds(nper + chunk * 128, 128)
                share = expo[chunk] * scale
                coeff_ref[at, lanes] = (share * (corr_ref[at, lanes] * norm_ref[plan, :, lanes])).astype(jnp.bfloat16)
                coeff_ref[at, sines] = (share * (corr_ref[at, sines] * norm_ref[plan, :, sines])).astype(jnp.bfloat16)
            score_ref[plan, at, :] = BETA * highest + jnp.log(total)
        model_ref[:obs, :] = lax.dot_general(
            basis_ref[plan], coeff_ref[...], (((1,), (1,)), ((), ())), preferred_element_type=jnp.float32
        )
        for step in range(steps):
            back_ref[pl.ds(src_ref[plan, step], STEP), :] = model_ref[pl.ds(dst_ref[plan, step], STEP), :]

    basis_copy(0).wait()
    correlate(0, slots[0][0], slots[0][1])

    def pair(index, carry):
        plan = index * 2
        for ahead in (1, 2):
            for known in range(ahead, plans, 2):
                pl.when(plan + ahead == known)(basis_copy(known).wait)
        correlate(plan + 1, slots[1][0], slots[1][1])
        finish(plan, *slots[0][1:])
        correlate(jnp.minimum(plan + 2, plans - 1), slots[0][0], slots[0][1])
        finish(plan + 1, *slots[1][1:])
        return carry

    lax.fori_loop(0, plans // 2, pair, 0)
    for owner in range(tm_count):
        outs[owner][...] = back_ref[pl.ds(owner * spaced, capacity), :].astype(jnp.bfloat16)


def fit_plans(tables, arrived, parts, norms):
    tm_count = len(arrived)
    order = [0] + ask_order(tm_count)
    _, obs, twice = parts[0].shape
    sched_dev = norms.shape[0]
    capacity, width = arrived[0].shape
    work = sched_dev * obs * twice * width
    spaced = tm_count * (capacity + STEP) + STEP
    slot = [
        pltpu.VMEM((obs + STEP, width), jnp.float32),
        pltpu.VMEM((width, twice), jnp.float32),
        pltpu.VMEM((width, twice), jnp.bfloat16),
        pltpu.VMEM((obs + STEP, width), jnp.float32),
    ]
    *models, score = pl.pallas_call(
        functools.partial(fit_kernel, order),
        in_specs=[SMEM, SMEM] + [VMEM] * tm_count + [ANY] * len(parts) + [VMEM],
        out_specs=[VMEM] * (tm_count + 1),
        out_shape=[jax.ShapeDtypeStruct((capacity, width), jnp.bfloat16)] * tm_count
        + [jax.ShapeDtypeStruct((sched_dev, width, 1), jnp.float32)],
        scratch_shapes=[
            pltpu.VMEM((sched_dev, obs, twice), jnp.bfloat16),
            pltpu.SemaphoreType.DMA((sched_dev,)),
            pltpu.VMEM((spaced, width), jnp.float32),
            pltpu.VMEM((spaced, width), jnp.float32),
        ] + slot + slot,
        compiler_params=pltpu.CompilerParams(vmem_limit_bytes=FIT_VMEM),
        cost_estimate=pl.CostEstimate(flops=20 * work, bytes_accessed=sched_dev * obs * twice * 2, transcendentals=0),
    )(*tables, *[arrived[owner] for owner in order], *parts, norms)
    return models, score


def load_attitude(sky, own_ref, passed, whole_ref, sems):
    rows = own_ref.shape[1]
    count = len(passed) // 2 + 1
    copies = [(None, sky, own_ref)]
    for hop in range(1, count):
        copies.append((sky >= hop, sky - hop, passed[2 * hop - 2]))
        copies.append((sky + hop < count, sky + hop, passed[2 * hop - 1]))

    def each(act):
        for index, (valid, quarter, ref) in enumerate(copies):
            def run(index=index, quarter=quarter, ref=ref):
                at = pl.ds(pl.multiple_of(quarter * rows, rows), rows)
                act(pltpu.make_async_copy(ref, whole_ref.at[:, at, :], sems.at[index]))

            if valid is None:
                run()
            else:
                pl.when(valid)(run)

    each(lambda copy: copy.start())
    return lambda: each(lambda copy: copy.wait())


def whiten_and_pick(me, asked_ref, cnt_ref, count_ref, whole_ref, wait, load, picked, white_ref, gather_ref):
    segs, slots, _ = whole_ref.shape
    capacity, width = picked[0].shape
    blocks = white_ref.shape[0] // (segs * slots)
    row = lax.broadcasted_iota(jnp.int32, (slots, width * blocks), 0)
    wait()
    for seg in range(segs):
        masked = jnp.where(row < count_ref[seg], load(seg).astype(jnp.float32), 0.0).astype(jnp.bfloat16)
        white = jnp.dot(whole_ref[seg], masked, preferred_element_type=jnp.float32)
        for block in range(blocks):
            white_ref[pl.ds((block * segs + seg) * slots, slots), :] = white[:, block * width:(block + 1) * width]
    for owner, out_ref in enumerate(picked):
        asker = owner ^ me

        def step(index, carry):
            first = index * PICK_UNROLL
            for lane in range(PICK_UNROLL):
                gather_ref[pl.ds(owner * capacity + first + lane, 1), :] = white_ref[
                    pl.ds(asked_ref[asker * capacity + first + lane], 1), :
                ]
            return carry

        lax.fori_loop(0, (cnt_ref[asker] + PICK_UNROLL - 1) // PICK_UNROLL, step, 0)
        out_ref[...] = gather_ref[pl.ds(owner * capacity, capacity), :].astype(jnp.bfloat16)


def add_rows(me, asked_ref, cnt_ref, owners, returned, rows_ref, sums, tiled):
    capacity = returned[0].shape[0]
    streams = len(sums)
    for total in sums:
        total[...] = jnp.zeros_like(total)
    for number, (owner, ref) in enumerate(zip(owners, returned)):
        tiles = capacity // SUB
        block = ref[...].astype(jnp.float32)
        if tiled:
            rows_ref[pl.ds(number * tiles, tiles)] = block.reshape(tiles, SUB, -1)
        else:
            rows_ref[pl.ds(number * capacity, capacity), :] = block
        asker = owner ^ me

        def row_at(index, lane):
            if tiled:
                return rows_ref[number * tiles + index * (UNROLL // SUB) + lane // SUB, pl.ds(lane % SUB, 1), :]
            return rows_ref[pl.ds(number * capacity + index * UNROLL + lane, 1), :]

        def step(index, carry):
            first = asker * capacity + index * UNROLL
            for start in range(0, UNROLL, streams):
                lanes = [start + lane for lane in range(streams)]
                places = [asked_ref[first + lane] for lane in lanes]
                values = [
                    total[pl.ds(place, 1), :] + row_at(index, lane)
                    for total, place, lane in zip(sums, places, lanes)
                ]
                for total, place, value in zip(sums, places, values):
                    total[pl.ds(place, 1), :] = value
            return carry

        lax.fori_loop(0, (cnt_ref[asker] + UNROLL - 1) // UNROLL, step, 0)


def placed_at(sums, at):
    return functools.reduce(jnp.add, [total[at, :] for total in sums])


def early_kernel(owners, table_base, asked_ref, cnt_ref, where_ref, base_ref, *refs):
    refs = list(refs)
    returned = [refs.pop(0) for _ in owners]
    out_ref, rows_ref = refs.pop(0), refs.pop(0)
    if table_base:
        held_ref, sem = refs.pop(0), refs.pop(0)
        copy = pltpu.make_async_copy(base_ref.at[pl.ds(0, held_ref.shape[0]), :], held_ref, sem)
        copy.start()
    add_rows(where_ref[0], asked_ref, cnt_ref, owners, returned, rows_ref, refs, True)
    if table_base:
        copy.wait()
        out_ref[...] = held_ref[...] - placed_at(refs, pl.ds(0, out_ref.shape[0]))
        return
    segs, slots, total_width = base_ref.shape
    width = out_ref.shape[1]
    for block in range(total_width // width):
        for seg in range(segs):
            at = pl.ds((block * segs + seg) * slots, slots)
            base = base_ref[seg, :, block * width:(block + 1) * width].astype(jnp.float32)
            out_ref[at, :] = base - placed_at(refs, at)


def place_early(scalars, owners, base, returned, rows):
    asked, cnt, _, where = scalars
    table_base = base.ndim == 2
    capacity = returned[0].shape[0]
    sums = [pltpu.VMEM((rows + 8, SRC_GROUP), jnp.float32)] * STREAMS
    held = [pltpu.VMEM((rows, SRC_GROUP), jnp.float32), pltpu.SemaphoreType.DMA(())] if table_base else []
    return pl.pallas_call(
        functools.partial(early_kernel, owners, table_base),
        in_specs=[SMEM] * 3 + [HBM if table_base else VMEM] + [VMEM] * len(owners),
        out_specs=VMEM,
        out_shape=jax.ShapeDtypeStruct((rows, SRC_GROUP), jnp.float32),
        scratch_shapes=[pltpu.VMEM((len(owners) * capacity // SUB, SUB, SRC_GROUP), jnp.float32)] + held + sums,
        compiler_params=pltpu.CompilerParams(vmem_limit_bytes=EARLY_VMEM),
        cost_estimate=pl.CostEstimate(flops=6 * COST_US, bytes_accessed=1 << 20, transcendentals=0),
    )(asked, cnt, where, base, *[returned[owner] for owner in owners])


def pick_kernel(tm_count, passed_count, asked_ref, cnt_ref, count_ref, where_ref, base_ref, own_ref, *refs):
    refs = list(refs)
    passed = [refs.pop(0) for _ in range(passed_count)]
    picked = [refs.pop(0) for _ in range(tm_count)]
    whole_ref, sems, white_ref, gather_ref = refs
    wait = load_attitude(where_ref[1], own_ref, passed, whole_ref, sems)
    whiten_and_pick(
        where_ref[0], asked_ref, cnt_ref, count_ref, whole_ref, wait, lambda seg: base_ref[seg], picked, white_ref,
        gather_ref,
    )


def pick_rows(scalars, base, attitude, rows):
    asked, cnt, seg_counts, where = scalars
    tm_count, = cnt.shape
    seg_dev, slots, _ = base.shape
    capacity = asked.shape[0] // tm_count
    return pl.pallas_call(
        functools.partial(pick_kernel, tm_count, len(attitude) - 1),
        in_specs=[SMEM] * 4 + [VMEM] + [ANY] * len(attitude),
        out_specs=[VMEM] * tm_count,
        out_shape=[jax.ShapeDtypeStruct((capacity, SRC_GROUP), jnp.bfloat16)] * tm_count,
        scratch_shapes=[
            pltpu.VMEM((seg_dev, slots, slots), jnp.bfloat16),
            pltpu.SemaphoreType.DMA((len(attitude),)),
            pltpu.VMEM((rows + 8, SRC_GROUP), jnp.float32),
            pltpu.VMEM((tm_count * capacity, SRC_GROUP), jnp.float32),
        ],
        compiler_params=pltpu.CompilerParams(vmem_limit_bytes=PICK_VMEM),
        cost_estimate=pl.CostEstimate(flops=5 * COST_US, bytes_accessed=1 << 20, transcendentals=0),
    )(asked, cnt, seg_counts, where, base, *attitude)


def late_pick_kernel(tm_count, passed_count, owners, asked_ref, cnt_ref, count_ref, where_ref, part_ref, own_ref,
                     *refs):
    refs = list(refs)

    def take(count):
        taken = refs[:count]
        del refs[:count]
        return taken

    passed = take(passed_count)
    returned = take(len(owners))
    (out_ref,) = take(1)
    picked = take(tm_count)
    whole_ref, sems, white_ref, gather_ref, table_ref, sem = take(6)
    segs, slots, _ = whole_ref.shape
    blocks = table_ref.shape[0] // (segs * slots)
    wait = load_attitude(where_ref[1], own_ref, passed, whole_ref, sems)
    add_rows(where_ref[0], asked_ref, cnt_ref, owners, returned, gather_ref, refs, False)
    table_ref[...] = part_ref[...] - placed_at(refs, pl.ds(0, table_ref.shape[0]))
    copy = pltpu.make_async_copy(table_ref, out_ref.at[pl.ds(0, table_ref.shape[0]), :], sem)
    copy.start()

    def load(seg):
        return jnp.concatenate(
            [table_ref[pl.ds((block * segs + seg) * slots, slots), :] for block in range(blocks)], axis=1
        )

    whiten_and_pick(
        where_ref[0], asked_ref, cnt_ref, count_ref, whole_ref, wait, load, picked, white_ref, gather_ref
    )
    copy.wait()


def place_late_and_pick(scalars, owners, part, returned, attitude):
    asked, cnt, seg_counts, where = scalars
    tm_count, = cnt.shape
    seg_dev = seg_counts.shape[0]
    slots = attitude[0].shape[2]
    capacity = asked.shape[0] // tm_count
    rows = part.shape[0]
    table = pltpu.VMEM((rows + 8, SRC_GROUP), jnp.float32)
    out = pl.pallas_call(
        functools.partial(late_pick_kernel, tm_count, len(attitude) - 1, owners),
        in_specs=[SMEM] * 4 + [VMEM] + [ANY] * len(attitude) + [VMEM] * len(owners),
        out_specs=[HBM] + [VMEM] * tm_count,
        out_shape=[jax.ShapeDtypeStruct((HBM_SPARE * rows, SRC_GROUP), jnp.float32)]
        + [jax.ShapeDtypeStruct((capacity, SRC_GROUP), jnp.bfloat16)] * tm_count,
        scratch_shapes=[
            pltpu.VMEM((seg_dev, slots, slots), jnp.bfloat16),
            pltpu.SemaphoreType.DMA((len(attitude),)),
            table,
            pltpu.VMEM((tm_count * capacity, SRC_GROUP), jnp.float32),
            pltpu.VMEM((rows, SRC_GROUP), jnp.float32),
            pltpu.SemaphoreType.DMA(()),
        ] + [table] * LATE_STREAMS,
        compiler_params=pltpu.CompilerParams(vmem_limit_bytes=LATE_PICK_VMEM),
        cost_estimate=pl.CostEstimate(flops=7 * COST_US, bytes_accessed=1 << 20, transcendentals=0),
    )(asked, cnt, seg_counts, where, part, *attitude, *[returned[owner] for owner in owners])
    return out[0], list(out[1:])


def late_kernel(owners, asked_ref, cnt_ref, where_ref, part_ref, *refs):
    refs = list(refs)
    returned = [refs.pop(0) for _ in owners]
    out_ref, rows_ref, held_ref, sems = refs[:4]
    sums = refs[4:]
    segs, slots, total_width = out_ref.shape
    width = part_ref.shape[1]
    add_rows(where_ref[0], asked_ref, cnt_ref, owners, returned, rows_ref, sums, False)
    copies = []
    for seg in range(segs):
        for block in range(total_width // width):
            at = pl.ds((block * segs + seg) * slots, slots)
            held_ref[seg, :, block * width:(block + 1) * width] = part_ref[at, :] - placed_at(sums, at)
        copies.append(pltpu.make_async_copy(held_ref.at[seg], out_ref.at[seg], sems.at[seg]))
        copies[-1].start()
    for copy in copies:
        copy.wait()


def place_late(scalars, owners, part, returned, shape):
    asked, cnt, _, where = scalars
    capacity = returned[0].shape[0]
    return pl.pallas_call(
        functools.partial(late_kernel, owners),
        in_specs=[SMEM] * 3 + [VMEM] * (1 + len(owners)),
        out_specs=HBM,
        out_shape=jax.ShapeDtypeStruct(shape, jnp.float32),
        scratch_shapes=[
            pltpu.VMEM((len(owners) * capacity, SRC_GROUP), jnp.float32),
            pltpu.VMEM(shape, jnp.float32),
            pltpu.SemaphoreType.DMA((shape[0],)),
        ] + [pltpu.VMEM((part.shape[0] + 8, SRC_GROUP), jnp.float32)] * LATE_STREAMS,
        compiler_params=pltpu.CompilerParams(vmem_limit_bytes=LATE_VMEM),
        cost_estimate=pl.CostEstimate(flops=4 * COST_US, bytes_accessed=1 << 20, transcendentals=0),
    )(asked, cnt, where, part, *[returned[owner] for owner in owners])


def make_lists(sched_seg, sched_slot, seg_dev, slots, column_blocks, tm_count, capacity):
    sched_dev, obs = sched_seg.shape
    me = lax.axis_index("tm")
    owner = sched_seg // seg_dev
    partner = owner ^ me
    block_of = (jnp.arange(sched_dev, dtype=jnp.int32) % column_blocks)[:, None]
    local_row = (block_of * seg_dev + sched_seg % seg_dev) * slots + sched_slot
    hot = (partner[:, :, None] == jnp.arange(tm_count, dtype=jnp.int32)).astype(jnp.int32)
    cnt = jnp.sum(hot, axis=1)
    plans = jnp.arange(sched_dev)
    before = (plans[None, :] < plans[:, None]).astype(jnp.int32)
    src = jnp.sum(before[:, :, None] * cnt[None, :, :], axis=1)
    owners = jnp.arange(tm_count)
    ahead = (owners[None, :] < owners[:, None]).astype(jnp.int32)
    dst = jnp.sum(ahead[None, :, :] * cnt[:, None, :], axis=2)
    entry = jnp.arange(obs)
    rank = jnp.sum(
        ((partner[:, None, :] == partner[:, :, None]) & (entry[None, :] < entry[:, None])).astype(jnp.int32),
        axis=2,
    )
    place = owner * capacity + jnp.sum(hot * src[:, None, :], axis=2) + rank
    order = jnp.sum(hot * dst[:, None, :], axis=2) + rank
    time = sched_seg * slots + sched_slot
    times = jnp.sum(jnp.where(order[:, None, :] == entry[None, :, None], time[:, None, :], 0), axis=2)
    rows = seg_dev * slots * column_blocks
    wanted = rows + jnp.sum(
        jnp.where(
            place.reshape(1, -1) == jnp.arange(tm_count * capacity, dtype=jnp.int32)[:, None],
            local_row.reshape(1, -1) - rows,
            0,
        ),
        axis=1,
    )
    step_count = (cnt + STEP - 1) // STEP
    step_first = jnp.sum(ahead[None, :, :] * step_count[:, None, :], axis=2)
    step = jnp.arange(obs // STEP + tm_count)[None, :, None] - step_first[:, None, :]
    inside = (step >= 0) & (step < step_count[:, None, :])
    spaced = capacity + STEP
    end = tm_count * spaced
    step_src = end + jnp.sum(
        jnp.where(inside, owners * spaced - end + src[:, None, :] + step * STEP, 0), axis=2
    )
    step_dst = obs + jnp.sum(jnp.where(inside, dst[:, None, :] + step * STEP - obs, 0), axis=2)
    return (step_src, step_dst), times, wanted


def send_order(count):
    return sorted(range(1, count), key=lambda step: (bin(step // 2).count("1"), step % 2, -step))


def ask_order(count):
    first = [1, count // 2]
    return first + sorted(
        (step for step in range(2, count) if step not in first), key=lambda step: -bin(step // 2).count("1")
    )


def exchange(blocks):
    count = len(blocks)
    out = list(blocks)
    for step in range(1, count):
        out[step] = lax.ppermute(blocks[step], "tm", [(i, i ^ step) for i in range(count)])
    return out


def pass_along(attitude, beside):
    count = lax.axis_size("sky")
    right = left = attitude
    pieces = [attitude]
    for hop in range(1, count):
        right = lax.ppermute(right, "sky", [(i, i + 1) for i in range(hop - 1, count - 1)])
        left = lax.ppermute(left, "sky", [(i, i - 1) for i in range(1, count - hop + 1)])
        if hop in beside:
            right, left = beside[hop](right, left)
        pieces += [right, left]
    return pieces


def on_device(residuals, seg_counts, attitude, sched_seg, sched_slot, periods):
    tm_count = lax.axis_size("tm")
    sched_dev, obs = sched_seg.shape
    seg_dev, slots, width = residuals.shape
    column_blocks = width // SRC_GROUP
    capacity = 2 * sched_dev * obs // tm_count
    tables, times, wanted = make_lists(
        sched_seg, sched_slot, seg_dev, slots, column_blocks, tm_count, capacity
    )
    wanted = wanted.reshape(tm_count, capacity)
    made = []
    asked = None

    def basis_part(after):
        first, count = sum(BASIS_CALLS[:len(made)]), BASIS_CALLS[len(made)]
        made.append(make_basis(times[first:first + count], periods, after))

    def first_hop(right, left):
        nonlocal asked
        basis_part([right, left])
        held, _ = lax.optimization_barrier((wanted, made[0][1]))
        asked = lax.all_to_all(held, "tm", split_axis=0, concat_axis=0, tiled=True)
        return right, left

    def second_hop(right, left):
        basis_part([right, left])
        basis_part([right, left])
        return right, left

    pieces = pass_along(attitude, {1: first_hop, 2: second_hop})
    cnt = jnp.sum((asked < seg_dev * slots * column_blocks).astype(jnp.int32), axis=1)
    where = jnp.stack([lax.axis_index("tm"), lax.axis_index("sky")])
    scalars = (asked.reshape(-1), cnt, seg_counts, where)
    rows = seg_dev * slots * column_blocks
    order = [0] + send_order(tm_count)
    near, far = order[:3 * tm_count // 4], order[3 * tm_count // 4:]

    base = residuals
    picked = pick_rows(scalars, base, pieces, rows)
    basis_part([picked[0]])
    parts, norms = zip(*made)
    norms = jnp.concatenate(norms)
    for iteration in range(ITERS):
        models, score = fit_plans(tables, exchange(picked), parts, norms)
        returned = exchange(models)
        base = place_early(scalars, near, base, returned, rows)
        if iteration < ITERS - 1:
            base, picked = place_late_and_pick(scalars, far, base, returned, pieces)
    cleaned = place_late(scalars, far, base, returned, residuals.shape)
    return (cleaned, score.reshape(sched_dev, SRC_GROUP))


def solution(mesh):
    in_specs = (
        P("tm", None, "sky"),
        P("tm"),
        P("tm", "sky", None),
        P(("tm", "sky"), None),
        P(("tm", "sky"), None),
        P(),
    )
    out_specs = (P("tm", None, "sky"), P(("tm", "sky"), None))
    return jax.shard_map(
        on_device, mesh=mesh, in_specs=in_specs, out_specs=out_specs, check_vma=False
    )
```

```python
import functools

import jax
import jax.numpy as jnp
from jax import lax
from jax.experimental import pallas as pl
from jax.experimental.pallas import tpu as pltpu
from jax.sharding import PartitionSpec as P

SRC_GROUP = 128
ITERS = 2
STREAMS = 4
LATE_STREAMS = 2
STEP = 16
BETA = 2.0
ROUND = 1.5 * 2.0 ** 23
RIDGE = 1.0
MIB = 1024 * 1024
BASIS_VMEM = 8 * MIB
FIT_VMEM = 22 * MIB
EARLY_VMEM = 20 * MIB
PICK_VMEM = 12 * MIB
LATE_PICK_VMEM = 18 * MIB
LATE_VMEM = 12 * MIB
BASIS_CALLS = (1, 2, 3, 2)
UNROLL = 32
PICK_UNROLL = 16
SUB = 8
HBM_SPARE = 32
COST_US = 10 ** 9

COS_POLY = (1.0, -19.73920440673828, 64.9391098022461, -85.4500503540039, 60.16689682006836,
            -25.96480369567871, 6.52468729019165)
SIN_POLY = (6.283185005187988, -41.34158706665039, 81.59986114501953, -76.61351013183594,
            41.33811950683594, -12.463061332702637)

VMEM = pl.BlockSpec(memory_space=pltpu.VMEM)
HBM = pl.BlockSpec(memory_space=pltpu.HBM)
ANY = pl.BlockSpec(memory_space=pl.ANY)
SMEM = pl.BlockSpec(memory_space=pltpu.SMEM)


def horner(poly, v):
    acc = jnp.full_like(v, poly[-1])
    for term in poly[-2::-1]:
        acc = acc * v + term
    return acc


def basis_kernel(after, time_ref, period_ref, inverse_ref, *refs):
    basis_ref, norm_ref = refs[after:]
    obs = time_ref.shape[0]
    nper = period_ref.shape[1]
    rows = 64
    for chunk in range(nper // 128):
        lanes = pl.ds(chunk * 128, 128)
        sines = pl.ds(nper + chunk * 128, 128)
        period = period_ref[:, lanes]
        inverse = inverse_ref[:, lanes]

        def step(index, sums):
            at = pl.ds(pl.multiple_of(index * rows, rows), rows)
            time = time_ref[at, :]
            turns = (time * inverse + ROUND) - ROUND
            part = (time - turns * period) * inverse
            square = part * part
            cosine = horner(COS_POLY, square).astype(jnp.bfloat16)
            sine = (horner(SIN_POLY, square) * part).astype(jnp.bfloat16)
            basis_ref[0, at, lanes] = cosine
            basis_ref[0, at, sines] = sine
            cosine = cosine.astype(jnp.float32)
            sine = sine.astype(jnp.float32)
            return (
                sums[0] + jnp.sum((cosine * cosine).reshape(rows // 8, 8, 128), axis=0),
                sums[1] + jnp.sum((sine * sine).reshape(rows // 8, 8, 128), axis=0),
            )

        zero = jnp.zeros((8, 128), jnp.float32)
        total_c, total_s = lax.fori_loop(0, obs // rows, step, (zero, zero))
        norm_ref[0, :, lanes] = 1.0 / (jnp.sum(total_c, axis=0, keepdims=True) + RIDGE)
        norm_ref[0, :, sines] = 1.0 / (jnp.sum(total_s, axis=0, keepdims=True) + RIDGE)


def make_basis(times, periods, after):
    sched_dev, obs = times.shape
    nper = periods.shape[0]
    wide = jnp.broadcast_to(
        times.astype(jnp.float32).reshape(-1, 1), (sched_dev * obs, SRC_GROUP)
    )
    period = periods.astype(jnp.float32)[None, :]
    return pl.pallas_call(
        functools.partial(basis_kernel, len(after)),
        grid=(sched_dev,),
        in_specs=[
            pl.BlockSpec((obs, SRC_GROUP), lambda j: (j, 0)),
            pl.BlockSpec((1, nper), lambda j: (0, 0)),
            pl.BlockSpec((1, nper), lambda j: (0, 0)),
        ] + [ANY] * len(after),
        out_specs=[
            pl.BlockSpec((1, obs, 2 * nper), lambda j: (j, 0, 0)),
            pl.BlockSpec((1, 1, 2 * nper), lambda j: (j, 0, 0)),
        ],
        out_shape=[
            jax.ShapeDtypeStruct((sched_dev, obs, 2 * nper), jnp.bfloat16),
            jax.ShapeDtypeStruct((sched_dev, 1, 2 * nper), jnp.float32),
        ],
        compiler_params=pltpu.CompilerParams(vmem_limit_bytes=BASIS_VMEM),
        cost_estimate=pl.CostEstimate(
            flops=sched_dev * obs * nper * 2500, bytes_accessed=sched_dev * obs * nper * 4, transcendentals=0
        ),
    )(wide, period, 1.0 / period, *after)


def fit_kernel(order, src_ref, dst_ref, *refs):
    refs = list(refs)

    def take(count):
        taken = refs[:count]
        del refs[:count]
        return taken

    tm_count = len(order)
    arrived = dict(zip(order, take(tm_count)))
    parts = take(len(BASIS_CALLS))
    (norm_ref,) = take(1)
    outs = take(tm_count)
    score_ref, basis_ref, sems, rows_ref, back_ref = take(5)
    slots = [take(4), take(4)]
    plans, obs, twice = basis_ref.shape
    nper = twice // 2
    capacity, width = arrived[0].shape
    spaced = capacity + STEP
    steps = src_ref.shape[1]
    held = [(part, plan) for part, count in zip(parts, BASIS_CALLS) for plan in range(count)]

    def basis_copy(plan):
        part, index = held[plan]
        return pltpu.make_async_copy(part.at[index], basis_ref.at[plan], sems.at[plan])

    for plan in range(plans):
        basis_copy(plan).start()
    for owner in range(tm_count):
        rows_ref[pl.ds(owner * spaced, capacity), :] = own_half(arrived, owner, capacity)[...].astype(jnp.float32)

    def correlate(plan, obs_ref, corr_ref):
        for step in range(steps):
            obs_ref[pl.ds(dst_ref[plan, step], STEP), :] = rows_ref[pl.ds(src_ref[plan, step], STEP), :]
        corr_ref[...] = lax.dot_general(
            obs_ref[:obs, :].astype(jnp.bfloat16), basis_ref[plan], (((0,), (0,)), ((), ())),
            preferred_element_type=jnp.float32,
        )

    def finish(plan, corr_ref, coeff_ref, model_ref):
        group = 16
        for start in range(0, width, group):
            at = pl.ds(start, group)
            power = []
            for chunk in range(nper // 128):
                lanes = pl.ds(chunk * 128, 128)
                sines = pl.ds(nper + chunk * 128, 128)
                cosine = corr_ref[at, lanes]
                sine = corr_ref[at, sines]
                power.append(
                    cosine * (cosine * norm_ref[plan, :, lanes]) + sine * (sine * norm_ref[plan, :, sines])
                )
            highest = functools.reduce(jnp.maximum, power)
            highest = jnp.max(highest, axis=1, keepdims=True)
            expo = [jnp.exp(BETA * (value - highest)) for value in power]
            total = jnp.sum(functools.reduce(jnp.add, expo), axis=1, keepdims=True)
            scale = 1.0 / total
            for chunk in range(nper // 128):
                lanes = pl.ds(chunk * 128, 128)
                sines = pl.ds(nper + chunk * 128, 128)
                share = expo[chunk] * scale
                coeff_ref[at, lanes] = (share * (corr_ref[at, lanes] * norm_ref[plan, :, lanes])).astype(jnp.bfloat16)
                coeff_ref[at, sines] = (share * (corr_ref[at, sines] * norm_ref[plan, :, sines])).astype(jnp.bfloat16)
            score_ref[plan, at, :] = BETA * highest + jnp.log(total)
        model_ref[:obs, :] = lax.dot_general(
            basis_ref[plan], coeff_ref[...], (((1,), (1,)), ((), ())), preferred_element_type=jnp.float32
        )
        for step in range(steps):
            back_ref[pl.ds(src_ref[plan, step], STEP), :] = model_ref[pl.ds(dst_ref[plan, step], STEP), :]

    basis_copy(0).wait()
    correlate(0, slots[0][0], slots[0][1])

    def pair(index, carry):
        plan = index * 2
        for ahead in (1, 2):
            for known in range(ahead, plans, 2):
                pl.when(plan + ahead == known)(basis_copy(known).wait)
        correlate(plan + 1, slots[1][0], slots[1][1])
        finish(plan, *slots[0][1:])
        correlate(jnp.minimum(plan + 2, plans - 1), slots[0][0], slots[0][1])
        finish(plan + 1, *slots[1][1:])
        return carry

    lax.fori_loop(0, plans // 2, pair, 0)
    for owner in range(tm_count):
        outs[owner][...] = back_ref[pl.ds(owner * spaced, capacity), :].astype(jnp.bfloat16)


def fit_plans(tables, arrived, parts, norms):
    tm_count = len(arrived)
    order = [0] + ask_order(tm_count)
    _, obs, twice = parts[0].shape
    sched_dev = norms.shape[0]
    capacity, width = arrived[0].shape
    work = sched_dev * obs * twice * width
    spaced = tm_count * (capacity + STEP) + STEP
    slot = [
        pltpu.VMEM((obs + STEP, width), jnp.float32),
        pltpu.VMEM((width, twice), jnp.float32),
        pltpu.VMEM((width, twice), jnp.bfloat16),
        pltpu.VMEM((obs + STEP, width), jnp.float32),
    ]
    *models, score = pl.pallas_call(
        functools.partial(fit_kernel, order),
        in_specs=[SMEM, SMEM] + [VMEM] * tm_count + [ANY] * len(parts) + [VMEM],
        out_specs=[VMEM] * (tm_count + 1),
        out_shape=[jax.ShapeDtypeStruct((capacity, width), jnp.bfloat16)] * tm_count
        + [jax.ShapeDtypeStruct((sched_dev, width, 1), jnp.float32)],
        scratch_shapes=[
            pltpu.VMEM((sched_dev, obs, twice), jnp.bfloat16),
            pltpu.SemaphoreType.DMA((sched_dev,)),
            pltpu.VMEM((spaced, width), jnp.float32),
            pltpu.VMEM((spaced, width), jnp.float32),
        ] + slot + slot,
        compiler_params=pltpu.CompilerParams(vmem_limit_bytes=FIT_VMEM),
        cost_estimate=pl.CostEstimate(flops=20 * work, bytes_accessed=sched_dev * obs * twice * 2, transcendentals=0),
    )(*tables, *[arrived[owner] for owner in order], *parts, norms)
    return models, score


def load_attitude(sky, own_ref, passed, whole_ref, sems):
    rows = own_ref.shape[1]
    count = len(passed) // 2 + 1
    copies = [(None, sky, own_ref)]
    for hop in range(1, count):
        copies.append((sky >= hop, sky - hop, passed[2 * hop - 2]))
        copies.append((sky + hop < count, sky + hop, passed[2 * hop - 1]))

    def each(act):
        for index, (valid, quarter, ref) in enumerate(copies):
            def run(index=index, quarter=quarter, ref=ref):
                at = pl.ds(pl.multiple_of(quarter * rows, rows), rows)
                act(pltpu.make_async_copy(ref, whole_ref.at[:, at, :], sems.at[index]))

            if valid is None:
                run()
            else:
                pl.when(valid)(run)

    each(lambda copy: copy.start())
    return lambda: each(lambda copy: copy.wait())


def whiten_and_pick(me, asked_ref, cnt_ref, count_ref, whole_ref, wait, load, picked, white_ref, gather_ref):
    segs, slots, _ = whole_ref.shape
    capacity, width = picked[0].shape
    picked = by_step(picked)
    picked[3] = picked[2]
    blocks = white_ref.shape[0] // (segs * slots)
    row = lax.broadcasted_iota(jnp.int32, (slots, width * blocks), 0)
    wait()
    for seg in range(segs):
        masked = jnp.where(row < count_ref[seg], load(seg).astype(jnp.float32), 0.0).astype(jnp.bfloat16)
        white = jnp.dot(whole_ref[seg], masked, preferred_element_type=jnp.float32)
        for block in range(blocks):
            white_ref[pl.ds((block * segs + seg) * slots, slots), :] = white[:, block * width:(block + 1) * width]
    for owner in range(len(picked)):
        asker = owner ^ me

        def step(index, carry):
            first = index * PICK_UNROLL
            for lane in range(PICK_UNROLL):
                gather_ref[pl.ds(owner * capacity + first + lane, 1), :] = white_ref[
                    pl.ds(asked_ref[asker * capacity + first + lane], 1), :
                ]
            return carry

        lax.fori_loop(0, (cnt_ref[asker] + PICK_UNROLL - 1) // PICK_UNROLL, step, 0)
        block = gather_ref[pl.ds(owner * capacity, capacity), :]
        own_half(picked, owner, capacity)[...] = block.astype(jnp.bfloat16)


def add_rows(me, asked_ref, cnt_ref, owners, returned, rows_ref, sums, tiled):
    returned = dict(zip(owners, returned))
    capacity = asked_ref.shape[0] // cnt_ref.shape[0]
    streams = len(sums)
    for total in sums:
        total[...] = jnp.zeros_like(total)
    for number, owner in enumerate(owners):
        tiles = capacity // SUB
        block = returned[owner][...].astype(jnp.float32)
        if tiled:
            rows_ref[pl.ds(number * tiles, tiles)] = block.reshape(tiles, SUB, -1)
        else:
            rows_ref[pl.ds(number * capacity, capacity), :] = block
        asker = owner ^ me

        def row_at(index, lane):
            if tiled:
                return rows_ref[number * tiles + index * (UNROLL // SUB) + lane // SUB, pl.ds(lane % SUB, 1), :]
            return rows_ref[pl.ds(number * capacity + index * UNROLL + lane, 1), :]

        def step(index, carry):
            first = asker * capacity + index * UNROLL
            for start in range(0, UNROLL, streams):
                lanes = [start + lane for lane in range(streams)]
                places = [asked_ref[first + lane] for lane in lanes]
                values = [
                    total[pl.ds(place, 1), :] + row_at(index, lane)
                    for total, place, lane in zip(sums, places, lanes)
                ]
                for total, place, value in zip(sums, places, values):
                    total[pl.ds(place, 1), :] = value
            return carry

        lax.fori_loop(0, (cnt_ref[asker] + UNROLL - 1) // UNROLL, step, 0)


def placed_at(sums, at):
    return functools.reduce(jnp.add, [total[at, :] for total in sums])


def early_kernel(owners, table_base, asked_ref, cnt_ref, where_ref, base_ref, *refs):
    refs = list(refs)
    returned = [refs.pop(0) for _ in owners]
    out_ref, rows_ref = refs.pop(0), refs.pop(0)
    if table_base:
        held_ref, sem = refs.pop(0), refs.pop(0)
        copy = pltpu.make_async_copy(base_ref.at[pl.ds(0, held_ref.shape[0]), :], held_ref, sem)
        copy.start()
    add_rows(where_ref[0], asked_ref, cnt_ref, owners, returned, rows_ref, refs, True)
    if table_base:
        copy.wait()
        out_ref[...] = held_ref[...] - placed_at(refs, pl.ds(0, out_ref.shape[0]))
        return
    segs, slots, total_width = base_ref.shape
    width = out_ref.shape[1]
    for block in range(total_width // width):
        for seg in range(segs):
            at = pl.ds((block * segs + seg) * slots, slots)
            base = base_ref[seg, :, block * width:(block + 1) * width].astype(jnp.float32)
            out_ref[at, :] = base - placed_at(refs, at)


def place_early(scalars, owners, base, returned, rows):
    asked, cnt, _, where = scalars
    table_base = base.ndim == 2
    capacity = returned[0].shape[0]
    sums = [pltpu.VMEM((rows + 8, SRC_GROUP), jnp.float32)] * STREAMS
    held = [pltpu.VMEM((rows, SRC_GROUP), jnp.float32), pltpu.SemaphoreType.DMA(())] if table_base else []
    return pl.pallas_call(
        functools.partial(early_kernel, owners, table_base),
        in_specs=[SMEM] * 3 + [HBM if table_base else VMEM] + [VMEM] * len(owners),
        out_specs=VMEM,
        out_shape=jax.ShapeDtypeStruct((rows, SRC_GROUP), jnp.float32),
        scratch_shapes=[pltpu.VMEM((len(owners) * capacity // SUB, SUB, SRC_GROUP), jnp.float32)] + held + sums,
        compiler_params=pltpu.CompilerParams(vmem_limit_bytes=EARLY_VMEM),
        cost_estimate=pl.CostEstimate(flops=6 * COST_US, bytes_accessed=1 << 20, transcendentals=0),
    )(asked, cnt, where, base, *[returned[owner] for owner in owners])


def pick_kernel(tm_count, passed_count, asked_ref, cnt_ref, count_ref, where_ref, base_ref, own_ref, *refs):
    refs = list(refs)
    passed = [refs.pop(0) for _ in range(passed_count)]
    picked = [refs.pop(0) for _ in range(tm_count - 1)]
    whole_ref, sems, white_ref, gather_ref = refs
    wait = load_attitude(where_ref[1], own_ref, passed, whole_ref, sems)
    whiten_and_pick(
        where_ref[0], asked_ref, cnt_ref, count_ref, whole_ref, wait, lambda seg: base_ref[seg], picked, white_ref,
        gather_ref,
    )


def pick_rows(scalars, base, attitude, rows):
    asked, cnt, seg_counts, where = scalars
    tm_count, = cnt.shape
    seg_dev, slots, _ = base.shape
    capacity = asked.shape[0] // tm_count
    return by_step(pl.pallas_call(
        functools.partial(pick_kernel, tm_count, len(attitude) - 1),
        in_specs=[SMEM] * 4 + [VMEM] + [ANY] * len(attitude),
        out_specs=[VMEM] * (tm_count - 1),
        out_shape=block_shapes(tm_count, capacity),
        scratch_shapes=[
            pltpu.VMEM((seg_dev, slots, slots), jnp.bfloat16),
            pltpu.SemaphoreType.DMA((len(attitude),)),
            pltpu.VMEM((rows + 8, SRC_GROUP), jnp.float32),
            pltpu.VMEM((tm_count * capacity, SRC_GROUP), jnp.float32),
        ],
        compiler_params=pltpu.CompilerParams(vmem_limit_bytes=PICK_VMEM),
        cost_estimate=pl.CostEstimate(flops=5 * COST_US, bytes_accessed=1 << 20, transcendentals=0),
    )(asked, cnt, seg_counts, where, base, *attitude))


def late_pick_kernel(tm_count, passed_count, owners, asked_ref, cnt_ref, count_ref, where_ref, part_ref, own_ref,
                     *refs):
    refs = list(refs)

    def take(count):
        taken = refs[:count]
        del refs[:count]
        return taken

    passed = take(passed_count)
    returned = take(len(owners))
    (out_ref,) = take(1)
    picked = take(tm_count - 1)
    whole_ref, sems, white_ref, gather_ref, table_ref, sem = take(6)
    segs, slots, _ = whole_ref.shape
    blocks = table_ref.shape[0] // (segs * slots)
    wait = load_attitude(where_ref[1], own_ref, passed, whole_ref, sems)
    add_rows(where_ref[0], asked_ref, cnt_ref, owners, returned, gather_ref, refs, False)
    table_ref[...] = part_ref[...] - placed_at(refs, pl.ds(0, table_ref.shape[0]))
    copy = pltpu.make_async_copy(table_ref, out_ref.at[pl.ds(0, table_ref.shape[0]), :], sem)
    copy.start()

    def load(seg):
        return jnp.concatenate(
            [table_ref[pl.ds((block * segs + seg) * slots, slots), :] for block in range(blocks)], axis=1
        )

    whiten_and_pick(
        where_ref[0], asked_ref, cnt_ref, count_ref, whole_ref, wait, load, picked, white_ref, gather_ref
    )
    copy.wait()


def place_late_and_pick(scalars, owners, part, returned, attitude):
    asked, cnt, seg_counts, where = scalars
    tm_count, = cnt.shape
    seg_dev = seg_counts.shape[0]
    slots = attitude[0].shape[2]
    capacity = asked.shape[0] // tm_count
    rows = part.shape[0]
    table = pltpu.VMEM((rows + 8, SRC_GROUP), jnp.float32)
    out = pl.pallas_call(
        functools.partial(late_pick_kernel, tm_count, len(attitude) - 1, owners),
        in_specs=[SMEM] * 4 + [VMEM] + [ANY] * len(attitude) + [VMEM] * len(owners),
        out_specs=[HBM] + [VMEM] * (tm_count - 1),
        out_shape=[jax.ShapeDtypeStruct((HBM_SPARE * rows, SRC_GROUP), jnp.float32)]
        + block_shapes(tm_count, capacity),
        scratch_shapes=[
            pltpu.VMEM((seg_dev, slots, slots), jnp.bfloat16),
            pltpu.SemaphoreType.DMA((len(attitude),)),
            table,
            pltpu.VMEM((tm_count * capacity, SRC_GROUP), jnp.float32),
            pltpu.VMEM((rows, SRC_GROUP), jnp.float32),
            pltpu.SemaphoreType.DMA(()),
        ] + [table] * LATE_STREAMS,
        compiler_params=pltpu.CompilerParams(vmem_limit_bytes=LATE_PICK_VMEM),
        cost_estimate=pl.CostEstimate(flops=7 * COST_US, bytes_accessed=1 << 20, transcendentals=0),
    )(asked, cnt, seg_counts, where, part, *attitude, *[returned[owner] for owner in owners])
    return out[0], by_step(out[1:])


def late_kernel(owners, asked_ref, cnt_ref, where_ref, part_ref, *refs):
    refs = list(refs)
    returned = [refs.pop(0) for _ in owners]
    out_ref, rows_ref, held_ref, sems = refs[:4]
    sums = refs[4:]
    segs, slots, total_width = out_ref.shape
    width = part_ref.shape[1]
    add_rows(where_ref[0], asked_ref, cnt_ref, owners, returned, rows_ref, sums, False)
    copies = []
    for seg in range(segs):
        for block in range(total_width // width):
            at = pl.ds((block * segs + seg) * slots, slots)
            held_ref[seg, :, block * width:(block + 1) * width] = part_ref[at, :] - placed_at(sums, at)
        copies.append(pltpu.make_async_copy(held_ref.at[seg], out_ref.at[seg], sems.at[seg]))
        copies[-1].start()
    for copy in copies:
        copy.wait()


def place_late(scalars, owners, part, returned, shape):
    asked, cnt, _, where = scalars
    capacity = returned[0].shape[0]
    return pl.pallas_call(
        functools.partial(late_kernel, owners),
        in_specs=[SMEM] * 3 + [VMEM] * (1 + len(owners)),
        out_specs=HBM,
        out_shape=jax.ShapeDtypeStruct(shape, jnp.float32),
        scratch_shapes=[
            pltpu.VMEM((len(owners) * capacity, SRC_GROUP), jnp.float32),
            pltpu.VMEM(shape, jnp.float32),
            pltpu.SemaphoreType.DMA((shape[0],)),
        ] + [pltpu.VMEM((part.shape[0] + 8, SRC_GROUP), jnp.float32)] * LATE_STREAMS,
        compiler_params=pltpu.CompilerParams(vmem_limit_bytes=LATE_VMEM),
        cost_estimate=pl.CostEstimate(flops=4 * COST_US, bytes_accessed=1 << 20, transcendentals=0),
    )(asked, cnt, where, part, *[returned[owner] for owner in owners])


def make_lists(sched_seg, sched_slot, seg_dev, slots, column_blocks, tm_count, capacity):
    sched_dev, obs = sched_seg.shape
    me = lax.axis_index("tm")
    owner = sched_seg // seg_dev
    partner = owner ^ me
    block_of = (jnp.arange(sched_dev, dtype=jnp.int32) % column_blocks)[:, None]
    local_row = (block_of * seg_dev + sched_seg % seg_dev) * slots + sched_slot
    hot = (partner[:, :, None] == jnp.arange(tm_count, dtype=jnp.int32)).astype(jnp.int32)
    cnt = jnp.sum(hot, axis=1)
    plans = jnp.arange(sched_dev)
    before = (plans[None, :] < plans[:, None]).astype(jnp.int32)
    src = jnp.sum(before[:, :, None] * cnt[None, :, :], axis=1)
    owners = jnp.arange(tm_count)
    ahead = (owners[None, :] < owners[:, None]).astype(jnp.int32)
    dst = jnp.sum(ahead[None, :, :] * cnt[:, None, :], axis=2)
    entry = jnp.arange(obs)
    rank = jnp.sum(
        ((partner[:, None, :] == partner[:, :, None]) & (entry[None, :] < entry[:, None])).astype(jnp.int32),
        axis=2,
    )
    place = owner * capacity + jnp.sum(hot * src[:, None, :], axis=2) + rank
    order = jnp.sum(hot * dst[:, None, :], axis=2) + rank
    time = sched_seg * slots + sched_slot
    times = jnp.sum(jnp.where(order[:, None, :] == entry[None, :, None], time[:, None, :], 0), axis=2)
    rows = seg_dev * slots * column_blocks
    wanted = rows + jnp.sum(
        jnp.where(
            place.reshape(1, -1) == jnp.arange(tm_count * capacity, dtype=jnp.int32)[:, None],
            local_row.reshape(1, -1) - rows,
            0,
        ),
        axis=1,
    )
    step_count = (cnt + STEP - 1) // STEP
    step_first = jnp.sum(ahead[None, :, :] * step_count[:, None, :], axis=2)
    step = jnp.arange(obs // STEP + tm_count)[None, :, None] - step_first[:, None, :]
    inside = (step >= 0) & (step < step_count[:, None, :])
    spaced = capacity + STEP
    end = tm_count * spaced
    step_src = end + jnp.sum(
        jnp.where(inside, owners * spaced - end + src[:, None, :] + step * STEP, 0), axis=2
    )
    step_dst = obs + jnp.sum(jnp.where(inside, dst[:, None, :] + step * STEP - obs, 0), axis=2)
    return (step_src, step_dst), times, wanted


def send_order(count):
    return sorted(range(1, count), key=lambda step: (bin(step // 2).count("1"), step % 2, -step))


def ask_order(count):
    first = [1, 2, count // 2]
    rest = (step for step in range(4, count) if step not in first)
    return first + sorted(rest, key=lambda step: -bin(step // 2).count("1")) + [3]


def block_shapes(count, capacity):
    return [
        jax.ShapeDtypeStruct((2 * capacity if step == 2 else capacity, SRC_GROUP), jnp.bfloat16)
        for step in range(count)
        if step != 3
    ]


def own_half(refs, step, capacity):
    if step == 3:
        return refs[step].at[pl.ds(capacity, capacity), :]
    return refs[step].at[pl.ds(0, capacity), :]


def by_step(blocks):
    return dict(zip([step for step in range(len(blocks) + 1) if step != 3], blocks))


def send_on(block, step):
    return lax.ppermute(block, "tm", [(i, i ^ step) for i in range(lax.axis_size("tm"))])


def ask_exchange(blocks):
    out = {step: send_on(block, step) if step else block for step, block in blocks.items()}
    both, *_ = lax.optimization_barrier([out[step] for step in out if step > 1])
    out[3] = send_on(both, 1)
    return out, both


def exchange(blocks):
    return [send_on(block, step) if step else block for step, block in enumerate(blocks)]


def pass_along(attitude, beside):
    count = lax.axis_size("sky")
    right = left = attitude
    pieces = [attitude]
    for hop in range(1, count):
        right = lax.ppermute(right, "sky", [(i, i + 1) for i in range(hop - 1, count - 1)])
        left = lax.ppermute(left, "sky", [(i, i - 1) for i in range(1, count - hop + 1)])
        if hop in beside:
            right, left = beside[hop](right, left)
        pieces += [right, left]
    return pieces


def on_device(residuals, seg_counts, attitude, sched_seg, sched_slot, periods):
    tm_count = lax.axis_size("tm")
    sched_dev, obs = sched_seg.shape
    seg_dev, slots, width = residuals.shape
    column_blocks = width // SRC_GROUP
    capacity = 2 * sched_dev * obs // tm_count
    tables, times, wanted = make_lists(
        sched_seg, sched_slot, seg_dev, slots, column_blocks, tm_count, capacity
    )
    wanted = wanted.reshape(tm_count, capacity)
    made = []
    asked = None

    def basis_part(after):
        first, count = sum(BASIS_CALLS[:len(made)]), BASIS_CALLS[len(made)]
        made.append(make_basis(times[first:first + count], periods, after))

    def first_hop(right, left):
        nonlocal asked
        held, right, left = lax.optimization_barrier((wanted, right, left))
        basis_part([right, left])
        held, _ = lax.optimization_barrier((held, made[0][1]))
        asked = lax.all_to_all(held, "tm", split_axis=0, concat_axis=0, tiled=True)
        basis_part([made[0][1]])
        return right, left

    def second_hop(right, left):
        basis_part([right, left])
        return right, left

    pieces = pass_along(attitude, {1: first_hop, 2: second_hop})
    cnt = jnp.sum((asked < seg_dev * slots * column_blocks).astype(jnp.int32), axis=1)
    where = jnp.stack([lax.axis_index("tm"), lax.axis_index("sky")])
    where, _ = lax.optimization_barrier((where, made[-1][1]))
    scalars = (asked.reshape(-1), cnt, seg_counts, where)
    rows = seg_dev * slots * column_blocks
    order = [0] + send_order(tm_count)
    near, far = order[:3 * tm_count // 4], order[3 * tm_count // 4:]

    base = residuals
    picked = pick_rows(scalars, base, pieces, rows)
    for iteration in range(ITERS):
        arrived, both = ask_exchange(picked)
        if iteration == 0:
            basis_part([both])
            parts, norms = zip(*made)
            norms = jnp.concatenate(norms)
        models, score = fit_plans(tables, arrived, parts, norms)
        returned = exchange(models)
        base = place_early(scalars, near, base, returned, rows)
        if iteration < ITERS - 1:
            base, picked = place_late_and_pick(scalars, far, base, returned, pieces)
    cleaned = place_late(scalars, far, base, returned, residuals.shape)
    return (cleaned, score.reshape(sched_dev, SRC_GROUP))


def solution(mesh):
    in_specs = (
        P("tm", None, "sky"),
        P("tm"),
        P("tm", "sky", None),
        P(("tm", "sky"), None),
        P(("tm", "sky"), None),
        P(),
    )
    out_specs = (P("tm", None, "sky"), P(("tm", "sky"), None))
    return jax.shard_map(
        on_device, mesh=mesh, in_specs=in_specs, out_specs=out_specs, check_vma=False
    )
```

```python
import functools

import jax
import jax.numpy as jnp
from jax import lax
from jax.experimental import pallas as pl
from jax.experimental.pallas import tpu as pltpu
from jax.sharding import PartitionSpec as P

SRC_GROUP = 128
ITERS = 2
STREAMS = 4
LATE_STREAMS = 2
STEP = 16
BETA = 2.0
ROUND = 1.5 * 2.0 ** 23
RIDGE = 1.0
MIB = 1024 * 1024
BASIS_VMEM = 8 * MIB
FIT_VMEM = 22 * MIB
EARLY_VMEM = 20 * MIB
PICK_VMEM = 12 * MIB
LATE_PICK_VMEM = 18 * MIB
LATE_VMEM = 12 * MIB
BASIS_CALLS = (1, 2, 3, 2)
UNROLL = 32
PICK_UNROLL = 16
SUB = 8
HBM_SPARE = 32
COST_US = 10 ** 9

COS_POLY = (1.0, -19.73920440673828, 64.9391098022461, -85.4500503540039, 60.16689682006836,
            -25.96480369567871, 6.52468729019165)
SIN_POLY = (6.283185005187988, -41.34158706665039, 81.59986114501953, -76.61351013183594,
            41.33811950683594, -12.463061332702637)

VMEM = pl.BlockSpec(memory_space=pltpu.VMEM)
HBM = pl.BlockSpec(memory_space=pltpu.HBM)
ANY = pl.BlockSpec(memory_space=pl.ANY)
SMEM = pl.BlockSpec(memory_space=pltpu.SMEM)


def horner(poly, v):
    acc = jnp.full_like(v, poly[-1])
    for term in poly[-2::-1]:
        acc = acc * v + term
    return acc


def basis_kernel(after, time_ref, period_ref, inverse_ref, *refs):
    basis_ref, norm_ref = refs[after:]
    obs = time_ref.shape[0]
    nper = period_ref.shape[1]
    rows = 64
    for chunk in range(nper // 128):
        lanes = pl.ds(chunk * 128, 128)
        sines = pl.ds(nper + chunk * 128, 128)
        period = period_ref[:, lanes]
        inverse = inverse_ref[:, lanes]

        def step(index, sums):
            at = pl.ds(pl.multiple_of(index * rows, rows), rows)
            time = time_ref[at, :]
            turns = (time * inverse + ROUND) - ROUND
            part = (time - turns * period) * inverse
            square = part * part
            cosine = horner(COS_POLY, square).astype(jnp.bfloat16)
            sine = (horner(SIN_POLY, square) * part).astype(jnp.bfloat16)
            basis_ref[0, at, lanes] = cosine
            basis_ref[0, at, sines] = sine
            cosine = cosine.astype(jnp.float32)
            sine = sine.astype(jnp.float32)
            return (
                sums[0] + jnp.sum((cosine * cosine).reshape(rows // 8, 8, 128), axis=0),
                sums[1] + jnp.sum((sine * sine).reshape(rows // 8, 8, 128), axis=0),
            )

        zero = jnp.zeros((8, 128), jnp.float32)
        total_c, total_s = lax.fori_loop(0, obs // rows, step, (zero, zero))
        norm_ref[0, :, lanes] = 1.0 / (jnp.sum(total_c, axis=0, keepdims=True) + RIDGE)
        norm_ref[0, :, sines] = 1.0 / (jnp.sum(total_s, axis=0, keepdims=True) + RIDGE)


def make_basis(times, periods, after):
    sched_dev, obs = times.shape
    nper = periods.shape[0]
    wide = jnp.broadcast_to(
        times.astype(jnp.float32).reshape(-1, 1), (sched_dev * obs, SRC_GROUP)
    )
    period = periods.astype(jnp.float32)[None, :]
    return pl.pallas_call(
        functools.partial(basis_kernel, len(after)),
        grid=(sched_dev,),
        in_specs=[
            pl.BlockSpec((obs, SRC_GROUP), lambda j: (j, 0)),
            pl.BlockSpec((1, nper), lambda j: (0, 0)),
            pl.BlockSpec((1, nper), lambda j: (0, 0)),
        ] + [ANY] * len(after),
        out_specs=[
            pl.BlockSpec((1, obs, 2 * nper), lambda j: (j, 0, 0)),
            pl.BlockSpec((1, 1, 2 * nper), lambda j: (j, 0, 0)),
        ],
        out_shape=[
            jax.ShapeDtypeStruct((sched_dev, obs, 2 * nper), jnp.bfloat16),
            jax.ShapeDtypeStruct((sched_dev, 1, 2 * nper), jnp.float32),
        ],
        compiler_params=pltpu.CompilerParams(vmem_limit_bytes=BASIS_VMEM),
        cost_estimate=pl.CostEstimate(
            flops=sched_dev * obs * nper * 8000, bytes_accessed=sched_dev * obs * nper * 4, transcendentals=0
        ),
    )(wide, period, 1.0 / period, *after)


def fit_kernel(order, src_ref, dst_ref, *refs):
    refs = list(refs)

    def take(count):
        taken = refs[:count]
        del refs[:count]
        return taken

    tm_count = len(order)
    arrived = dict(zip(order, take(tm_count)))
    parts = take(len(BASIS_CALLS))
    (norm_ref,) = take(1)
    outs = take(tm_count)
    score_ref, basis_ref, sems, rows_ref, back_ref = take(5)
    slots = [take(4), take(4)]
    plans, obs, twice = basis_ref.shape
    nper = twice // 2
    capacity, width = arrived[0].shape
    spaced = capacity + STEP
    steps = src_ref.shape[1]
    held = [(part, plan) for part, count in zip(parts, BASIS_CALLS) for plan in range(count)]

    def basis_copy(plan):
        part, index = held[plan]
        return pltpu.make_async_copy(part.at[index], basis_ref.at[plan], sems.at[plan])

    for plan in range(plans):
        basis_copy(plan).start()
    for owner in range(tm_count):
        rows_ref[pl.ds(owner * spaced, capacity), :] = arrived[owner][...].astype(jnp.float32)

    def correlate(plan, obs_ref, corr_ref):
        for step in range(steps):
            obs_ref[pl.ds(dst_ref[plan, step], STEP), :] = rows_ref[pl.ds(src_ref[plan, step], STEP), :]
        corr_ref[...] = lax.dot_general(
            obs_ref[:obs, :].astype(jnp.bfloat16), basis_ref[plan], (((0,), (0,)), ((), ())),
            preferred_element_type=jnp.float32,
        )

    def finish(plan, corr_ref, coeff_ref, model_ref):
        group = 16
        for start in range(0, width, group):
            at = pl.ds(start, group)
            power = []
            for chunk in range(nper // 128):
                lanes = pl.ds(chunk * 128, 128)
                sines = pl.ds(nper + chunk * 128, 128)
                cosine = corr_ref[at, lanes]
                sine = corr_ref[at, sines]
                power.append(
                    cosine * (cosine * norm_ref[plan, :, lanes]) + sine * (sine * norm_ref[plan, :, sines])
                )
            highest = functools.reduce(jnp.maximum, power)
            highest = jnp.max(highest, axis=1, keepdims=True)
            expo = [jnp.exp(BETA * (value - highest)) for value in power]
            total = jnp.sum(functools.reduce(jnp.add, expo), axis=1, keepdims=True)
            scale = 1.0 / total
            for chunk in range(nper // 128):
                lanes = pl.ds(chunk * 128, 128)
                sines = pl.ds(nper + chunk * 128, 128)
                share = expo[chunk] * scale
                coeff_ref[at, lanes] = (share * (corr_ref[at, lanes] * norm_ref[plan, :, lanes])).astype(jnp.bfloat16)
                coeff_ref[at, sines] = (share * (corr_ref[at, sines] * norm_ref[plan, :, sines])).astype(jnp.bfloat16)
            score_ref[plan, at, :] = BETA * highest + jnp.log(total)
        model_ref[:obs, :] = lax.dot_general(
            basis_ref[plan], coeff_ref[...], (((1,), (1,)), ((), ())), preferred_element_type=jnp.float32
        )
        for step in range(steps):
            back_ref[pl.ds(src_ref[plan, step], STEP), :] = model_ref[pl.ds(dst_ref[plan, step], STEP), :]

    basis_copy(0).wait()
    correlate(0, slots[0][0], slots[0][1])

    def pair(index, carry):
        plan = index * 2
        for ahead in (1, 2):
            for known in range(ahead, plans, 2):
                pl.when(plan + ahead == known)(basis_copy(known).wait)
        correlate(plan + 1, slots[1][0], slots[1][1])
        finish(plan, *slots[0][1:])
        correlate(jnp.minimum(plan + 2, plans - 1), slots[0][0], slots[0][1])
        finish(plan + 1, *slots[1][1:])
        return carry

    lax.fori_loop(0, plans // 2, pair, 0)
    for owner in range(tm_count):
        outs[owner][...] = back_ref[pl.ds(owner * spaced, capacity), :].astype(jnp.bfloat16)


def fit_plans(tables, arrived, parts, norms):
    tm_count = len(arrived)
    order = [0] + send_order(tm_count)
    _, obs, twice = parts[0].shape
    sched_dev = norms.shape[0]
    capacity, width = arrived[0].shape
    work = sched_dev * obs * twice * width
    spaced = tm_count * (capacity + STEP) + STEP
    slot = [
        pltpu.VMEM((obs + STEP, width), jnp.float32),
        pltpu.VMEM((width, twice), jnp.float32),
        pltpu.VMEM((width, twice), jnp.bfloat16),
        pltpu.VMEM((obs + STEP, width), jnp.float32),
    ]
    *models, score = pl.pallas_call(
        functools.partial(fit_kernel, order),
        in_specs=[SMEM, SMEM] + [VMEM] * tm_count + [ANY] * len(parts) + [VMEM],
        out_specs=[VMEM] * (tm_count + 1),
        out_shape=[jax.ShapeDtypeStruct((capacity, width), jnp.bfloat16)] * tm_count
        + [jax.ShapeDtypeStruct((sched_dev, width, 1), jnp.float32)],
        scratch_shapes=[
            pltpu.VMEM((sched_dev, obs, twice), jnp.bfloat16),
            pltpu.SemaphoreType.DMA((sched_dev,)),
            pltpu.VMEM((spaced, width), jnp.float32),
            pltpu.VMEM((spaced, width), jnp.float32),
        ] + slot + slot,
        compiler_params=pltpu.CompilerParams(vmem_limit_bytes=FIT_VMEM),
        cost_estimate=pl.CostEstimate(flops=20 * work, bytes_accessed=sched_dev * obs * twice * 2, transcendentals=0),
    )(*tables, *[arrived[owner] for owner in order], *parts, norms)
    return models, score


def load_attitude(sky, own_ref, passed, whole_ref, sems):
    rows = own_ref.shape[1]
    count = len(passed) // 2 + 1
    copies = [(None, sky, own_ref)]
    for hop in range(1, count):
        copies.append((sky >= hop, sky - hop, passed[2 * hop - 2]))
        copies.append((sky + hop < count, sky + hop, passed[2 * hop - 1]))

    def each(act):
        for index, (valid, quarter, ref) in enumerate(copies):
            def run(index=index, quarter=quarter, ref=ref):
                at = pl.ds(pl.multiple_of(quarter * rows, rows), rows)
                act(pltpu.make_async_copy(ref, whole_ref.at[:, at, :], sems.at[index]))

            if valid is None:
                run()
            else:
                pl.when(valid)(run)

    each(lambda copy: copy.start())
    return lambda: each(lambda copy: copy.wait())


def whiten_and_pick(me, asked_ref, cnt_ref, count_ref, whole_ref, wait, load, picked, white_ref, gather_ref):
    segs, slots, _ = whole_ref.shape
    capacity, width = picked[0].shape
    blocks = white_ref.shape[0] // (segs * slots)
    row = lax.broadcasted_iota(jnp.int32, (slots, width * blocks), 0)
    wait()
    for seg in range(segs):
        masked = jnp.where(row < count_ref[seg], load(seg).astype(jnp.float32), 0.0).astype(jnp.bfloat16)
        white = jnp.dot(whole_ref[seg], masked, preferred_element_type=jnp.float32)
        for block in range(blocks):
            white_ref[pl.ds((block * segs + seg) * slots, slots), :] = white[:, block * width:(block + 1) * width]
    for owner, out_ref in enumerate(picked):
        asker = owner ^ me

        def step(index, carry):
            first = index * PICK_UNROLL
            for lane in range(PICK_UNROLL):
                gather_ref[pl.ds(owner * capacity + first + lane, 1), :] = white_ref[
                    pl.ds(asked_ref[asker * capacity + first + lane], 1), :
                ]
            return carry

        lax.fori_loop(0, (cnt_ref[asker] + PICK_UNROLL - 1) // PICK_UNROLL, step, 0)
        out_ref[...] = gather_ref[pl.ds(owner * capacity, capacity), :].astype(jnp.bfloat16)


def add_rows(me, asked_ref, cnt_ref, owners, returned, rows_ref, sums, tiled):
    capacity = returned[0].shape[0]
    streams = len(sums)
    for total in sums:
        total[...] = jnp.zeros_like(total)
    for number, (owner, ref) in enumerate(zip(owners, returned)):
        tiles = capacity // SUB
        block = ref[...].astype(jnp.float32)
        if tiled:
            rows_ref[pl.ds(number * tiles, tiles)] = block.reshape(tiles, SUB, -1)
        else:
            rows_ref[pl.ds(number * capacity, capacity), :] = block
        asker = owner ^ me

        def row_at(index, lane):
            if tiled:
                return rows_ref[number * tiles + index * (UNROLL // SUB) + lane // SUB, pl.ds(lane % SUB, 1), :]
            return rows_ref[pl.ds(number * capacity + index * UNROLL + lane, 1), :]

        def step(index, carry):
            first = asker * capacity + index * UNROLL
            for start in range(0, UNROLL, streams):
                lanes = [start + lane for lane in range(streams)]
                places = [asked_ref[first + lane] for lane in lanes]
                values = [
                    total[pl.ds(place, 1), :] + row_at(index, lane)
                    for total, place, lane in zip(sums, places, lanes)
                ]
                for total, place, value in zip(sums, places, values):
                    total[pl.ds(place, 1), :] = value
            return carry

        lax.fori_loop(0, (cnt_ref[asker] + UNROLL - 1) // UNROLL, step, 0)


def placed_at(sums, at):
    return functools.reduce(jnp.add, [total[at, :] for total in sums])


def early_kernel(owners, table_base, asked_ref, cnt_ref, where_ref, base_ref, *refs):
    refs = list(refs)
    returned = [refs.pop(0) for _ in owners]
    out_ref, rows_ref = refs.pop(0), refs.pop(0)
    if table_base:
        held_ref, sem = refs.pop(0), refs.pop(0)
        copy = pltpu.make_async_copy(base_ref.at[pl.ds(0, held_ref.shape[0]), :], held_ref, sem)
        copy.start()
    add_rows(where_ref[0], asked_ref, cnt_ref, owners, returned, rows_ref, refs, True)
    if table_base:
        copy.wait()
        out_ref[...] = held_ref[...] - placed_at(refs, pl.ds(0, out_ref.shape[0]))
        return
    segs, slots, total_width = base_ref.shape
    width = out_ref.shape[1]
    for block in range(total_width // width):
        for seg in range(segs):
            at = pl.ds((block * segs + seg) * slots, slots)
            base = base_ref[seg, :, block * width:(block + 1) * width].astype(jnp.float32)
            out_ref[at, :] = base - placed_at(refs, at)


def place_early(scalars, owners, base, returned, rows):
    asked, cnt, _, where = scalars
    table_base = base.ndim == 2
    capacity = returned[0].shape[0]
    sums = [pltpu.VMEM((rows + 8, SRC_GROUP), jnp.float32)] * STREAMS
    held = [pltpu.VMEM((rows, SRC_GROUP), jnp.float32), pltpu.SemaphoreType.DMA(())] if table_base else []
    return pl.pallas_call(
        functools.partial(early_kernel, owners, table_base),
        in_specs=[SMEM] * 3 + [HBM if table_base else VMEM] + [VMEM] * len(owners),
        out_specs=VMEM,
        out_shape=jax.ShapeDtypeStruct((rows, SRC_GROUP), jnp.float32),
        scratch_shapes=[pltpu.VMEM((len(owners) * capacity // SUB, SUB, SRC_GROUP), jnp.float32)] + held + sums,
        compiler_params=pltpu.CompilerParams(vmem_limit_bytes=EARLY_VMEM),
        cost_estimate=pl.CostEstimate(flops=6 * COST_US, bytes_accessed=1 << 20, transcendentals=0),
    )(asked, cnt, where, base, *[returned[owner] for owner in owners])


def pick_kernel(tm_count, passed_count, asked_ref, cnt_ref, count_ref, where_ref, base_ref, own_ref, *refs):
    refs = list(refs)
    passed = [refs.pop(0) for _ in range(passed_count)]
    picked = [refs.pop(0) for _ in range(tm_count)]
    whole_ref, sems, white_ref, gather_ref = refs
    wait = load_attitude(where_ref[1], own_ref, passed, whole_ref, sems)
    whiten_and_pick(
        where_ref[0], asked_ref, cnt_ref, count_ref, whole_ref, wait, lambda seg: base_ref[seg], picked, white_ref,
        gather_ref,
    )


def pick_rows(scalars, base, attitude, rows):
    asked, cnt, seg_counts, where = scalars
    tm_count, = cnt.shape
    seg_dev, slots, _ = base.shape
    capacity = asked.shape[0] // tm_count
    return pl.pallas_call(
        functools.partial(pick_kernel, tm_count, len(attitude) - 1),
        in_specs=[SMEM] * 4 + [VMEM] + [ANY] * len(attitude),
        out_specs=[VMEM] * tm_count,
        out_shape=[jax.ShapeDtypeStruct((capacity, SRC_GROUP), jnp.bfloat16)] * tm_count,
        scratch_shapes=[
            pltpu.VMEM((seg_dev, slots, slots), jnp.bfloat16),
            pltpu.SemaphoreType.DMA((len(attitude),)),
            pltpu.VMEM((rows + 8, SRC_GROUP), jnp.float32),
            pltpu.VMEM((tm_count * capacity, SRC_GROUP), jnp.float32),
        ],
        compiler_params=pltpu.CompilerParams(vmem_limit_bytes=PICK_VMEM),
        cost_estimate=pl.CostEstimate(flops=5 * COST_US, bytes_accessed=1 << 20, transcendentals=0),
    )(asked, cnt, seg_counts, where, base, *attitude)


def late_pick_kernel(tm_count, passed_count, owners, asked_ref, cnt_ref, count_ref, where_ref, part_ref, own_ref,
                     *refs):
    refs = list(refs)

    def take(count):
        taken = refs[:count]
        del refs[:count]
        return taken

    passed = take(passed_count)
    returned = take(len(owners))
    (out_ref,) = take(1)
    picked = take(tm_count)
    whole_ref, sems, white_ref, gather_ref, table_ref, sem = take(6)
    segs, slots, _ = whole_ref.shape
    blocks = table_ref.shape[0] // (segs * slots)
    wait = load_attitude(where_ref[1], own_ref, passed, whole_ref, sems)
    add_rows(where_ref[0], asked_ref, cnt_ref, owners, returned, gather_ref, refs, False)
    table_ref[...] = part_ref[...] - placed_at(refs, pl.ds(0, table_ref.shape[0]))
    copy = pltpu.make_async_copy(table_ref, out_ref.at[pl.ds(0, table_ref.shape[0]), :], sem)
    copy.start()

    def load(seg):
        return jnp.concatenate(
            [table_ref[pl.ds((block * segs + seg) * slots, slots), :] for block in range(blocks)], axis=1
        )

    whiten_and_pick(
        where_ref[0], asked_ref, cnt_ref, count_ref, whole_ref, wait, load, picked, white_ref, gather_ref
    )
    copy.wait()


def place_late_and_pick(scalars, owners, part, returned, attitude):
    asked, cnt, seg_counts, where = scalars
    tm_count, = cnt.shape
    seg_dev = seg_counts.shape[0]
    slots = attitude[0].shape[2]
    capacity = asked.shape[0] // tm_count
    rows = part.shape[0]
    table = pltpu.VMEM((rows + 8, SRC_GROUP), jnp.float32)
    out = pl.pallas_call(
        functools.partial(late_pick_kernel, tm_count, len(attitude) - 1, owners),
        in_specs=[SMEM] * 4 + [VMEM] + [ANY] * len(attitude) + [VMEM] * len(owners),
        out_specs=[HBM] + [VMEM] * tm_count,
        out_shape=[jax.ShapeDtypeStruct((HBM_SPARE * rows, SRC_GROUP), jnp.float32)]
        + [jax.ShapeDtypeStruct((capacity, SRC_GROUP), jnp.bfloat16)] * tm_count,
        scratch_shapes=[
            pltpu.VMEM((seg_dev, slots, slots), jnp.bfloat16),
            pltpu.SemaphoreType.DMA((len(attitude),)),
            table,
            pltpu.VMEM((tm_count * capacity, SRC_GROUP), jnp.float32),
            pltpu.VMEM((rows, SRC_GROUP), jnp.float32),
            pltpu.SemaphoreType.DMA(()),
        ] + [table] * LATE_STREAMS,
        compiler_params=pltpu.CompilerParams(vmem_limit_bytes=LATE_PICK_VMEM),
        cost_estimate=pl.CostEstimate(flops=7 * COST_US, bytes_accessed=1 << 20, transcendentals=0),
    )(asked, cnt, seg_counts, where, part, *attitude, *[returned[owner] for owner in owners])
    return out[0], list(out[1:])


def late_kernel(owners, asked_ref, cnt_ref, where_ref, part_ref, *refs):
    refs = list(refs)
    returned = [refs.pop(0) for _ in owners]
    out_ref, rows_ref, held_ref, sems = refs[:4]
    sums = refs[4:]
    segs, slots, total_width = out_ref.shape
    width = part_ref.shape[1]
    add_rows(where_ref[0], asked_ref, cnt_ref, owners, returned, rows_ref, sums, False)
    copies = []
    for seg in range(segs):
        for block in range(total_width // width):
            at = pl.ds((block * segs + seg) * slots, slots)
            held_ref[seg, :, block * width:(block + 1) * width] = part_ref[at, :] - placed_at(sums, at)
        copies.append(pltpu.make_async_copy(held_ref.at[seg], out_ref.at[seg], sems.at[seg]))
        copies[-1].start()
    for copy in copies:
        copy.wait()


def place_late(scalars, owners, part, returned, shape):
    asked, cnt, _, where = scalars
    capacity = returned[0].shape[0]
    return pl.pallas_call(
        functools.partial(late_kernel, owners),
        in_specs=[SMEM] * 3 + [VMEM] * (1 + len(owners)),
        out_specs=HBM,
        out_shape=jax.ShapeDtypeStruct(shape, jnp.float32),
        scratch_shapes=[
            pltpu.VMEM((len(owners) * capacity, SRC_GROUP), jnp.float32),
            pltpu.VMEM(shape, jnp.float32),
            pltpu.SemaphoreType.DMA((shape[0],)),
        ] + [pltpu.VMEM((part.shape[0] + 8, SRC_GROUP), jnp.float32)] * LATE_STREAMS,
        compiler_params=pltpu.CompilerParams(vmem_limit_bytes=LATE_VMEM),
        cost_estimate=pl.CostEstimate(flops=4 * COST_US, bytes_accessed=1 << 20, transcendentals=0),
    )(asked, cnt, where, part, *[returned[owner] for owner in owners])


def make_lists(sched_seg, sched_slot, seg_dev, slots, column_blocks, tm_count, capacity):
    sched_dev, obs = sched_seg.shape
    me = lax.axis_index("tm")
    owner = sched_seg // seg_dev
    partner = owner ^ me
    block_of = (jnp.arange(sched_dev, dtype=jnp.int32) % column_blocks)[:, None]
    local_row = (block_of * seg_dev + sched_seg % seg_dev) * slots + sched_slot
    hot = (partner[:, :, None] == jnp.arange(tm_count, dtype=jnp.int32)).astype(jnp.int32)
    cnt = jnp.sum(hot, axis=1)
    plans = jnp.arange(sched_dev)
    before = (plans[None, :] < plans[:, None]).astype(jnp.int32)
    src = jnp.sum(before[:, :, None] * cnt[None, :, :], axis=1)
    owners = jnp.arange(tm_count)
    ahead = (owners[None, :] < owners[:, None]).astype(jnp.int32)
    dst = jnp.sum(ahead[None, :, :] * cnt[:, None, :], axis=2)
    entry = jnp.arange(obs)
    rank = jnp.sum(
        ((partner[:, None, :] == partner[:, :, None]) & (entry[None, :] < entry[:, None])).astype(jnp.int32),
        axis=2,
    )
    place = owner * capacity + jnp.sum(hot * src[:, None, :], axis=2) + rank
    order = jnp.sum(hot * dst[:, None, :], axis=2) + rank
    time = sched_seg * slots + sched_slot
    times = jnp.sum(jnp.where(order[:, None, :] == entry[None, :, None], time[:, None, :], 0), axis=2)
    rows = seg_dev * slots * column_blocks
    wanted = rows + jnp.sum(
        jnp.where(
            place.reshape(1, -1) == jnp.arange(tm_count * capacity, dtype=jnp.int32)[:, None],
            local_row.reshape(1, -1) - rows,
            0,
        ),
        axis=1,
    )
    step_count = (cnt + STEP - 1) // STEP
    step_first = jnp.sum(ahead[None, :, :] * step_count[:, None, :], axis=2)
    step = jnp.arange(obs // STEP + tm_count)[None, :, None] - step_first[:, None, :]
    inside = (step >= 0) & (step < step_count[:, None, :])
    spaced = capacity + STEP
    end = tm_count * spaced
    step_src = end + jnp.sum(
        jnp.where(inside, owners * spaced - end + src[:, None, :] + step * STEP, 0), axis=2
    )
    step_dst = obs + jnp.sum(jnp.where(inside, dst[:, None, :] + step * STEP - obs, 0), axis=2)
    return (step_src, step_dst), times, wanted


def send_order(count):
    return sorted(range(1, count), key=lambda step: (bin(step // 2).count("1"), step % 2, -step))


def exchange(blocks):
    count = len(blocks)
    out = list(blocks)
    for step in range(1, count):
        out[step] = lax.ppermute(blocks[step], "tm", [(i, i ^ step) for i in range(count)])
    return out


def pass_along(attitude, beside):
    count = lax.axis_size("sky")
    right = left = attitude
    pieces = [attitude]
    for hop in range(1, count):
        right = lax.ppermute(right, "sky", [(i, i + 1) for i in range(hop - 1, count - 1)])
        left = lax.ppermute(left, "sky", [(i, i - 1) for i in range(1, count - hop + 1)])
        if hop in beside:
            right, left = beside[hop](right, left)
        pieces += [right, left]
    return pieces


def on_device(residuals, seg_counts, attitude, sched_seg, sched_slot, periods):
    tm_count = lax.axis_size("tm")
    sched_dev, obs = sched_seg.shape
    seg_dev, slots, width = residuals.shape
    column_blocks = width // SRC_GROUP
    capacity = 2 * sched_dev * obs // tm_count
    tables, times, wanted = make_lists(
        sched_seg, sched_slot, seg_dev, slots, column_blocks, tm_count, capacity
    )
    wanted = wanted.reshape(tm_count, capacity)
    made = []
    asked = None

    def basis_part(after):
        first, count = sum(BASIS_CALLS[:len(made)]), BASIS_CALLS[len(made)]
        made.append(make_basis(times[first:first + count], periods, after))

    def first_hop(right, left):
        nonlocal asked
        basis_part([right, left])
        held, _ = lax.optimization_barrier((wanted, made[0][1]))
        asked = lax.all_to_all(held, "tm", split_axis=0, concat_axis=0, tiled=True)
        return right, left

    def second_hop(right, left):
        basis_part([right, left])
        basis_part([right, left])
        return right, left

    pieces = pass_along(attitude, {1: first_hop, 2: second_hop})
    cnt = jnp.sum((asked < seg_dev * slots * column_blocks).astype(jnp.int32), axis=1)
    where = jnp.stack([lax.axis_index("tm"), lax.axis_index("sky")])
    scalars = (asked.reshape(-1), cnt, seg_counts, where)
    rows = seg_dev * slots * column_blocks
    order = [0] + send_order(tm_count)
    near, far = order[:3 * tm_count // 4], order[3 * tm_count // 4:]

    base = residuals
    picked = pick_rows(scalars, base, pieces, rows)
    basis_part([picked[0]])
    parts, norms = zip(*made)
    norms = jnp.concatenate(norms)
    for iteration in range(ITERS):
        models, score = fit_plans(tables, exchange(picked), parts, norms)
        returned = exchange(models)
        base = place_early(scalars, near, base, returned, rows)
        if iteration < ITERS - 1:
            base, picked = place_late_and_pick(scalars, far, base, returned, pieces)
    cleaned = place_late(scalars, far, base, returned, residuals.shape)
    return (cleaned, score.reshape(sched_dev, SRC_GROUP))


def solution(mesh):
    in_specs = (
        P("tm", None, "sky"),
        P("tm"),
        P("tm", "sky", None),
        P(("tm", "sky"), None),
        P(("tm", "sky"), None),
        P(),
    )
    out_specs = (P("tm", None, "sky"), P(("tm", "sky"), None))
    return jax.shard_map(
        on_device, mesh=mesh, in_specs=in_specs, out_specs=out_specs, check_vma=False
    )
```

```python
import functools

import jax
import jax.numpy as jnp
from jax import lax
from jax.experimental import pallas as pl
from jax.experimental.pallas import tpu as pltpu
from jax.sharding import PartitionSpec as P

SRC_GROUP = 128
ITERS = 2
STREAMS = 4
LATE_STREAMS = 2
STEP = 16
BETA = 2.0
ROUND = 1.5 * 2.0 ** 23
RIDGE = 1.0
MIB = 1024 * 1024
BASIS_VMEM = 8 * MIB
FIT_VMEM = 22 * MIB
EARLY_VMEM = 20 * MIB
PICK_VMEM = 12 * MIB
LATE_PICK_VMEM = 18 * MIB
LATE_VMEM = 12 * MIB
BASIS_CALLS = (1, 2, 3, 2)
UNROLL = 32
PICK_UNROLL = 16
SUB = 8
HBM_SPARE = 32
COST_US = 10 ** 9

COS_POLY = (1.0, -19.73920440673828, 64.9391098022461, -85.4500503540039, 60.16689682006836,
            -25.96480369567871, 6.52468729019165)
SIN_POLY = (6.283185005187988, -41.34158706665039, 81.59986114501953, -76.61351013183594,
            41.33811950683594, -12.463061332702637)

VMEM = pl.BlockSpec(memory_space=pltpu.VMEM)
HBM = pl.BlockSpec(memory_space=pltpu.HBM)
ANY = pl.BlockSpec(memory_space=pl.ANY)
SMEM = pl.BlockSpec(memory_space=pltpu.SMEM)


def horner(poly, v):
    acc = jnp.full_like(v, poly[-1])
    for term in poly[-2::-1]:
        acc = acc * v + term
    return acc


def basis_kernel(after, time_ref, period_ref, inverse_ref, *refs):
    basis_ref, norm_ref = refs[after:]
    obs = time_ref.shape[0]
    nper = period_ref.shape[1]
    rows = 64
    for chunk in range(nper // 128):
        lanes = pl.ds(chunk * 128, 128)
        sines = pl.ds(nper + chunk * 128, 128)
        period = period_ref[:, lanes]
        inverse = inverse_ref[:, lanes]

        def step(index, sums):
            at = pl.ds(pl.multiple_of(index * rows, rows), rows)
            time = time_ref[at, :]
            turns = (time * inverse + ROUND) - ROUND
            part = (time - turns * period) * inverse
            square = part * part
            cosine = horner(COS_POLY, square).astype(jnp.bfloat16)
            sine = (horner(SIN_POLY, square) * part).astype(jnp.bfloat16)
            basis_ref[0, at, lanes] = cosine
            basis_ref[0, at, sines] = sine
            cosine = cosine.astype(jnp.float32)
            sine = sine.astype(jnp.float32)
            return (
                sums[0] + jnp.sum((cosine * cosine).reshape(rows // 8, 8, 128), axis=0),
                sums[1] + jnp.sum((sine * sine).reshape(rows // 8, 8, 128), axis=0),
            )

        zero = jnp.zeros((8, 128), jnp.float32)
        total_c, total_s = lax.fori_loop(0, obs // rows, step, (zero, zero))
        norm_ref[0, :, lanes] = 1.0 / (jnp.sum(total_c, axis=0, keepdims=True) + RIDGE)
        norm_ref[0, :, sines] = 1.0 / (jnp.sum(total_s, axis=0, keepdims=True) + RIDGE)


def make_basis(times, periods, after):
    sched_dev, obs = times.shape
    nper = periods.shape[0]
    wide = jnp.broadcast_to(
        times.astype(jnp.float32).reshape(-1, 1), (sched_dev * obs, SRC_GROUP)
    )
    period = periods.astype(jnp.float32)[None, :]
    return pl.pallas_call(
        functools.partial(basis_kernel, len(after)),
        grid=(sched_dev,),
        in_specs=[
            pl.BlockSpec((obs, SRC_GROUP), lambda j: (j, 0)),
            pl.BlockSpec((1, nper), lambda j: (0, 0)),
            pl.BlockSpec((1, nper), lambda j: (0, 0)),
        ] + [ANY] * len(after),
        out_specs=[
            pl.BlockSpec((1, obs, 2 * nper), lambda j: (j, 0, 0)),
            pl.BlockSpec((1, 1, 2 * nper), lambda j: (j, 0, 0)),
        ],
        out_shape=[
            jax.ShapeDtypeStruct((sched_dev, obs, 2 * nper), jnp.bfloat16),
            jax.ShapeDtypeStruct((sched_dev, 1, 2 * nper), jnp.float32),
        ],
        compiler_params=pltpu.CompilerParams(vmem_limit_bytes=BASIS_VMEM),
        cost_estimate=pl.CostEstimate(
            flops=sched_dev * obs * nper * 8000, bytes_accessed=sched_dev * obs * nper * 4, transcendentals=0
        ),
    )(wide, period, 1.0 / period, *after)


def fit_kernel(order, src_ref, dst_ref, *refs):
    refs = list(refs)

    def take(count):
        taken = refs[:count]
        del refs[:count]
        return taken

    tm_count = len(order)
    arrived = dict(zip(order, take(tm_count)))
    parts = take(len(BASIS_CALLS))
    (norm_ref,) = take(1)
    outs = take(tm_count)
    score_ref, basis_ref, sems, rows_ref, back_ref = take(5)
    slots = [take(4), take(4)]
    plans, obs, twice = basis_ref.shape
    nper = twice // 2
    capacity, width = arrived[0].shape
    spaced = capacity + STEP
    steps = src_ref.shape[1]
    held = [(part, plan) for part, count in zip(parts, BASIS_CALLS) for plan in range(count)]

    def basis_copy(plan):
        part, index = held[plan]
        return pltpu.make_async_copy(part.at[index], basis_ref.at[plan], sems.at[plan])

    for plan in range(plans):
        basis_copy(plan).start()
    for owner in range(tm_count):
        rows_ref[pl.ds(owner * spaced, capacity), :] = arrived[owner][...].astype(jnp.float32)

    def correlate(plan, obs_ref, corr_ref):
        for step in range(steps):
            obs_ref[pl.ds(dst_ref[plan, step], STEP), :] = rows_ref[pl.ds(src_ref[plan, step], STEP), :]
        corr_ref[...] = lax.dot_general(
            obs_ref[:obs, :].astype(jnp.bfloat16), basis_ref[plan], (((0,), (0,)), ((), ())),
            preferred_element_type=jnp.float32,
        )

    def finish(plan, corr_ref, coeff_ref, model_ref):
        group = 16
        for start in range(0, width, group):
            at = pl.ds(start, group)
            power = []
            for chunk in range(nper // 128):
                lanes = pl.ds(chunk * 128, 128)
                sines = pl.ds(nper + chunk * 128, 128)
                cosine = corr_ref[at, lanes]
                sine = corr_ref[at, sines]
                power.append(
                    cosine * (cosine * norm_ref[plan, :, lanes]) + sine * (sine * norm_ref[plan, :, sines])
                )
            highest = functools.reduce(jnp.maximum, power)
            highest = jnp.max(highest, axis=1, keepdims=True)
            expo = [jnp.exp(BETA * (value - highest)) for value in power]
            total = jnp.sum(functools.reduce(jnp.add, expo), axis=1, keepdims=True)
            scale = 1.0 / total
            for chunk in range(nper // 128):
                lanes = pl.ds(chunk * 128, 128)
                sines = pl.ds(nper + chunk * 128, 128)
                share = expo[chunk] * scale
                coeff_ref[at, lanes] = (share * (corr_ref[at, lanes] * norm_ref[plan, :, lanes])).astype(jnp.bfloat16)
                coeff_ref[at, sines] = (share * (corr_ref[at, sines] * norm_ref[plan, :, sines])).astype(jnp.bfloat16)
            score_ref[plan, at, :] = BETA * highest + jnp.log(total)
            model_ref[:obs, :] = lax.dot_general(
            coeff_ref[...], basis_ref[plan], (((1,), (1,)), ((), ())), preferred_element_type=jnp.float32
        ).T
        for step in range(steps):
            back_ref[pl.ds(src_ref[plan, step], STEP), :] = model_ref[pl.ds(dst_ref[plan, step], STEP), :]

    basis_copy(0).wait()
    correlate(0, slots[0][0], slots[0][1])

    def pair(index, carry):
        plan = index * 2
        for ahead in (1, 2):
            for known in range(ahead, plans, 2):
                pl.when(plan + ahead == known)(basis_copy(known).wait)
        correlate(plan + 1, slots[1][0], slots[1][1])
        finish(plan, *slots[0][1:])
        correlate(jnp.minimum(plan + 2, plans - 1), slots[0][0], slots[0][1])
        finish(plan + 1, *slots[1][1:])
        return carry

    lax.fori_loop(0, plans // 2, pair, 0)
    for owner in range(tm_count):
        outs[owner][...] = back_ref[pl.ds(owner * spaced, capacity), :].astype(jnp.bfloat16)


def fit_plans(tables, arrived, parts, norms):
    tm_count = len(arrived)
    order = [0] + send_order(tm_count)
    _, obs, twice = parts[0].shape
    sched_dev = norms.shape[0]
    capacity, width = arrived[0].shape
    work = sched_dev * obs * twice * width
    spaced = tm_count * (capacity + STEP) + STEP
    slot = [
        pltpu.VMEM((obs + STEP, width), jnp.float32),
        pltpu.VMEM((width, twice), jnp.float32),
        pltpu.VMEM((width, twice), jnp.bfloat16),
        pltpu.VMEM((obs + STEP, width), jnp.float32),
    ]
    *models, score = pl.pallas_call(
        functools.partial(fit_kernel, order),
        in_specs=[SMEM, SMEM] + [VMEM] * tm_count + [ANY] * len(parts) + [VMEM],
        out_specs=[VMEM] * (tm_count + 1),
        out_shape=[jax.ShapeDtypeStruct((capacity, width), jnp.bfloat16)] * tm_count
        + [jax.ShapeDtypeStruct((sched_dev, width, 1), jnp.float32)],
        scratch_shapes=[
            pltpu.VMEM((sched_dev, obs, twice), jnp.bfloat16),
            pltpu.SemaphoreType.DMA((sched_dev,)),
            pltpu.VMEM((spaced, width), jnp.float32),
            pltpu.VMEM((spaced, width), jnp.float32),
        ] + slot + slot,
        compiler_params=pltpu.CompilerParams(vmem_limit_bytes=FIT_VMEM),
        cost_estimate=pl.CostEstimate(flops=20 * work, bytes_accessed=sched_dev * obs * twice * 2, transcendentals=0),
    )(*tables, *[arrived[owner] for owner in order], *parts, norms)
    return models, score


def load_attitude(sky, own_ref, passed, whole_ref, sems):
    rows = own_ref.shape[1]
    count = whole_ref.shape[1] // rows
    copies = [(None, sky, own_ref)]
    for hop in range(1, 2 if count == 4 else count):
        copies.append((sky >= hop, sky - hop, passed[2 * hop - 2]))
        copies.append((sky + hop < count, sky + hop, passed[2 * hop - 1]))
    if count == 4:
        copies.append((None, sky ^ 2, passed[2]))
        copies.append(((sky == 0) | (sky == 3), 3 - sky, passed[3]))

    def each(act):
        for index, (valid, quarter, ref) in enumerate(copies):
            def run(index=index, quarter=quarter, ref=ref):
                at = pl.ds(pl.multiple_of(quarter * rows, rows), rows)
                act(pltpu.make_async_copy(ref, whole_ref.at[:, at, :], sems.at[index]))

            if valid is None:
                run()
            else:
                pl.when(valid)(run)

    each(lambda copy: copy.start())
    return lambda: each(lambda copy: copy.wait())


def whiten_and_pick(me, asked_ref, cnt_ref, count_ref, whole_ref, wait, load, picked, white_ref, gather_ref):
    segs, slots, _ = whole_ref.shape
    capacity, width = picked[0].shape
    blocks = white_ref.shape[0] // (segs * slots)
    row = lax.broadcasted_iota(jnp.int32, (slots, width * blocks), 0)
    wait()
    for seg in range(segs):
        masked = jnp.where(row < count_ref[seg], load(seg).astype(jnp.float32), 0.0).astype(jnp.bfloat16)
        white = jnp.dot(whole_ref[seg], masked, preferred_element_type=jnp.float32)
        for block in range(blocks):
            white_ref[pl.ds((block * segs + seg) * slots, slots), :] = white[:, block * width:(block + 1) * width]
    for owner, out_ref in enumerate(picked):
        asker = owner ^ me

        def step(index, carry):
            first = index * PICK_UNROLL
            for lane in range(PICK_UNROLL):
                gather_ref[pl.ds(owner * capacity + first + lane, 1), :] = white_ref[
                    pl.ds(asked_ref[asker * capacity + first + lane], 1), :
                ]
            return carry

        lax.fori_loop(0, (cnt_ref[asker] + PICK_UNROLL - 1) // PICK_UNROLL, step, 0)
        out_ref[...] = gather_ref[pl.ds(owner * capacity, capacity), :].astype(jnp.bfloat16)


def add_rows(me, asked_ref, cnt_ref, owners, returned, rows_ref, sums, tiled):
    capacity = returned[0].shape[0]
    streams = len(sums)
    for total in sums:
        total[...] = jnp.zeros_like(total)
    for number, (owner, ref) in enumerate(zip(owners, returned)):
        tiles = capacity // SUB
        block = ref[...].astype(jnp.float32)
        if tiled:
            rows_ref[pl.ds(number * tiles, tiles)] = block.reshape(tiles, SUB, -1)
        else:
            rows_ref[pl.ds(number * capacity, capacity), :] = block
        asker = owner ^ me

        def row_at(index, lane):
            if tiled:
                return rows_ref[number * tiles + index * (UNROLL // SUB) + lane // SUB, pl.ds(lane % SUB, 1), :]
            return rows_ref[pl.ds(number * capacity + index * UNROLL + lane, 1), :]

        def step(index, carry):
            first = asker * capacity + index * UNROLL
            for start in range(0, UNROLL, streams):
                lanes = [start + lane for lane in range(streams)]
                places = [asked_ref[first + lane] for lane in lanes]
                values = [
                    total[pl.ds(place, 1), :] + row_at(index, lane)
                    for total, place, lane in zip(sums, places, lanes)
                ]
                for total, place, value in zip(sums, places, values):
                    total[pl.ds(place, 1), :] = value
            return carry

        lax.fori_loop(0, (cnt_ref[asker] + UNROLL - 1) // UNROLL, step, 0)


def placed_at(sums, at):
    return functools.reduce(jnp.add, [total[at, :] for total in sums])


def early_kernel(owners, table_base, asked_ref, cnt_ref, where_ref, base_ref, *refs):
    refs = list(refs)
    returned = [refs.pop(0) for _ in owners]
    out_ref, rows_ref = refs.pop(0), refs.pop(0)
    if table_base:
        held_ref, sem = refs.pop(0), refs.pop(0)
        copy = pltpu.make_async_copy(base_ref.at[pl.ds(0, held_ref.shape[0]), :], held_ref, sem)
        copy.start()
    add_rows(where_ref[0], asked_ref, cnt_ref, owners, returned, rows_ref, refs, True)
    if table_base:
        copy.wait()
        out_ref[...] = held_ref[...] - placed_at(refs, pl.ds(0, out_ref.shape[0]))
        return
    segs, slots, total_width = base_ref.shape
    width = out_ref.shape[1]
    for block in range(total_width // width):
        for seg in range(segs):
            at = pl.ds((block * segs + seg) * slots, slots)
            base = base_ref[seg, :, block * width:(block + 1) * width].astype(jnp.float32)
            out_ref[at, :] = base - placed_at(refs, at)


def place_early(scalars, owners, base, returned, rows):
    asked, cnt, _, where = scalars
    table_base = base.ndim == 2
    capacity = returned[0].shape[0]
    sums = [pltpu.VMEM((rows + 8, SRC_GROUP), jnp.float32)] * STREAMS
    held = [pltpu.VMEM((rows, SRC_GROUP), jnp.float32), pltpu.SemaphoreType.DMA(())] if table_base else []
    return pl.pallas_call(
        functools.partial(early_kernel, owners, table_base),
        in_specs=[SMEM] * 3 + [HBM if table_base else VMEM] + [VMEM] * len(owners),
        out_specs=VMEM,
        out_shape=jax.ShapeDtypeStruct((rows, SRC_GROUP), jnp.float32),
        scratch_shapes=[pltpu.VMEM((len(owners) * capacity // SUB, SUB, SRC_GROUP), jnp.float32)] + held + sums,
        compiler_params=pltpu.CompilerParams(vmem_limit_bytes=EARLY_VMEM),
        cost_estimate=pl.CostEstimate(flops=6 * COST_US, bytes_accessed=1 << 20, transcendentals=0),
    )(asked, cnt, where, base, *[returned[owner] for owner in owners])


def pick_kernel(tm_count, passed_count, asked_ref, cnt_ref, count_ref, where_ref, base_ref, own_ref, *refs):
    refs = list(refs)
    passed = [refs.pop(0) for _ in range(passed_count)]
    picked = [refs.pop(0) for _ in range(tm_count)]
    whole_ref, sems, white_ref, gather_ref = refs
    wait = load_attitude(where_ref[1], own_ref, passed, whole_ref, sems)
    whiten_and_pick(
        where_ref[0], asked_ref, cnt_ref, count_ref, whole_ref, wait, lambda seg: base_ref[seg], picked, white_ref,
        gather_ref,
    )


def pick_rows(scalars, base, attitude, rows):
    asked, cnt, seg_counts, where = scalars
    tm_count, = cnt.shape
    seg_dev, slots, _ = base.shape
    capacity = asked.shape[0] // tm_count
    return pl.pallas_call(
        functools.partial(pick_kernel, tm_count, len(attitude) - 1),
        in_specs=[SMEM] * 4 + [VMEM] + [ANY] * len(attitude),
        out_specs=[VMEM] * tm_count,
        out_shape=[jax.ShapeDtypeStruct((capacity, SRC_GROUP), jnp.bfloat16)] * tm_count,
        scratch_shapes=[
            pltpu.VMEM((seg_dev, slots, slots), jnp.bfloat16),
            pltpu.SemaphoreType.DMA((len(attitude),)),
            pltpu.VMEM((rows + 8, SRC_GROUP), jnp.float32),
            pltpu.VMEM((tm_count * capacity, SRC_GROUP), jnp.float32),
        ],
        compiler_params=pltpu.CompilerParams(vmem_limit_bytes=PICK_VMEM),
        cost_estimate=pl.CostEstimate(flops=5 * COST_US, bytes_accessed=1 << 20, transcendentals=0),
    )(asked, cnt, seg_counts, where, base, *attitude)


def late_pick_kernel(tm_count, passed_count, owners, asked_ref, cnt_ref, count_ref, where_ref, part_ref, own_ref,
                     *refs):
    refs = list(refs)

    def take(count):
        taken = refs[:count]
        del refs[:count]
        return taken

    passed = take(passed_count)
    returned = take(len(owners))
    (out_ref,) = take(1)
    picked = take(tm_count)
    whole_ref, sems, white_ref, gather_ref, table_ref, sem = take(6)
    segs, slots, _ = whole_ref.shape
    blocks = table_ref.shape[0] // (segs * slots)
    wait = load_attitude(where_ref[1], own_ref, passed, whole_ref, sems)
    add_rows(where_ref[0], asked_ref, cnt_ref, owners, returned, gather_ref, refs, False)
    table_ref[...] = part_ref[...] - placed_at(refs, pl.ds(0, table_ref.shape[0]))
    copy = pltpu.make_async_copy(table_ref, out_ref.at[pl.ds(0, table_ref.shape[0]), :], sem)
    copy.start()

    def load(seg):
        return jnp.concatenate(
            [table_ref[pl.ds((block * segs + seg) * slots, slots), :] for block in range(blocks)], axis=1
        )

    whiten_and_pick(
        where_ref[0], asked_ref, cnt_ref, count_ref, whole_ref, wait, load, picked, white_ref, gather_ref
    )
    copy.wait()


def place_late_and_pick(scalars, owners, part, returned, attitude):
    asked, cnt, seg_counts, where = scalars
    tm_count, = cnt.shape
    seg_dev = seg_counts.shape[0]
    slots = attitude[0].shape[2]
    capacity = asked.shape[0] // tm_count
    rows = part.shape[0]
    table = pltpu.VMEM((rows + 8, SRC_GROUP), jnp.float32)
    out = pl.pallas_call(
        functools.partial(late_pick_kernel, tm_count, len(attitude) - 1, owners),
        in_specs=[SMEM] * 4 + [VMEM] + [ANY] * len(attitude) + [VMEM] * len(owners),
        out_specs=[HBM] + [VMEM] * tm_count,
        out_shape=[jax.ShapeDtypeStruct((HBM_SPARE * rows, SRC_GROUP), jnp.float32)]
        + [jax.ShapeDtypeStruct((capacity, SRC_GROUP), jnp.bfloat16)] * tm_count,
        scratch_shapes=[
            pltpu.VMEM((seg_dev, slots, slots), jnp.bfloat16),
            pltpu.SemaphoreType.DMA((len(attitude),)),
            table,
            pltpu.VMEM((tm_count * capacity, SRC_GROUP), jnp.float32),
            pltpu.VMEM((rows, SRC_GROUP), jnp.float32),
            pltpu.SemaphoreType.DMA(()),
        ] + [table] * LATE_STREAMS,
        compiler_params=pltpu.CompilerParams(vmem_limit_bytes=LATE_PICK_VMEM),
        cost_estimate=pl.CostEstimate(flops=7 * COST_US, bytes_accessed=1 << 20, transcendentals=0),
    )(asked, cnt, seg_counts, where, part, *attitude, *[returned[owner] for owner in owners])
    return out[0], list(out[1:])


def late_kernel(owners, asked_ref, cnt_ref, where_ref, part_ref, *refs):
    refs = list(refs)
    returned = [refs.pop(0) for _ in owners]
    out_ref, rows_ref, held_ref, sems = refs[:4]
    sums = refs[4:]
    segs, slots, total_width = out_ref.shape
    width = part_ref.shape[1]
    add_rows(where_ref[0], asked_ref, cnt_ref, owners, returned, rows_ref, sums, False)
    copies = []
    for seg in range(segs):
        for block in range(total_width // width):
            at = pl.ds((block * segs + seg) * slots, slots)
            held_ref[seg, :, block * width:(block + 1) * width] = part_ref[at, :] - placed_at(sums, at)
        copies.append(pltpu.make_async_copy(held_ref.at[seg], out_ref.at[seg], sems.at[seg]))
        copies[-1].start()
    for copy in copies:
        copy.wait()


def place_late(scalars, owners, part, returned, shape):
    asked, cnt, _, where = scalars
    capacity = returned[0].shape[0]
    return pl.pallas_call(
        functools.partial(late_kernel, owners),
        in_specs=[SMEM] * 3 + [VMEM] * (1 + len(owners)),
        out_specs=HBM,
        out_shape=jax.ShapeDtypeStruct(shape, jnp.float32),
        scratch_shapes=[
            pltpu.VMEM((len(owners) * capacity, SRC_GROUP), jnp.float32),
            pltpu.VMEM(shape, jnp.float32),
            pltpu.SemaphoreType.DMA((shape[0],)),
        ] + [pltpu.VMEM((part.shape[0] + 8, SRC_GROUP), jnp.float32)] * LATE_STREAMS,
        compiler_params=pltpu.CompilerParams(vmem_limit_bytes=LATE_VMEM),
        cost_estimate=pl.CostEstimate(flops=4 * COST_US, bytes_accessed=1 << 20, transcendentals=0),
    )(asked, cnt, where, part, *[returned[owner] for owner in owners])


def make_lists(sched_seg, sched_slot, seg_dev, slots, column_blocks, tm_count, capacity):
    sched_dev, obs = sched_seg.shape
    me = lax.axis_index("tm")
    owner = sched_seg // seg_dev
    partner = owner ^ me
    block_of = (jnp.arange(sched_dev, dtype=jnp.int32) % column_blocks)[:, None]
    local_row = (block_of * seg_dev + sched_seg % seg_dev) * slots + sched_slot
    hot = (partner[:, :, None] == jnp.arange(tm_count, dtype=jnp.int32)).astype(jnp.int32)
    cnt = jnp.sum(hot, axis=1)
    plans = jnp.arange(sched_dev)
    before = (plans[None, :] < plans[:, None]).astype(jnp.int32)
    src = jnp.sum(before[:, :, None] * cnt[None, :, :], axis=1)
    owners = jnp.arange(tm_count)
    ahead = (owners[None, :] < owners[:, None]).astype(jnp.int32)
    dst = jnp.sum(ahead[None, :, :] * cnt[:, None, :], axis=2)
    entry = jnp.arange(obs)
    rank = jnp.sum(
        ((partner[:, None, :] == partner[:, :, None]) & (entry[None, :] < entry[:, None])).astype(jnp.int32),
        axis=2,
    )
    place = owner * capacity + jnp.sum(hot * src[:, None, :], axis=2) + rank
    order = jnp.sum(hot * dst[:, None, :], axis=2) + rank
    time = sched_seg * slots + sched_slot
    times = jnp.sum(jnp.where(order[:, None, :] == entry[None, :, None], time[:, None, :], 0), axis=2)
    rows = seg_dev * slots * column_blocks
    wanted = rows + jnp.sum(
        jnp.where(
            place.reshape(1, -1) == jnp.arange(tm_count * capacity, dtype=jnp.int32)[:, None],
            local_row.reshape(1, -1) - rows,
            0,
        ),
        axis=1,
    )
    step_count = (cnt + STEP - 1) // STEP
    step_first = jnp.sum(ahead[None, :, :] * step_count[:, None, :], axis=2)
    step = jnp.arange(obs // STEP + tm_count)[None, :, None] - step_first[:, None, :]
    inside = (step >= 0) & (step < step_count[:, None, :])
    spaced = capacity + STEP
    end = tm_count * spaced
    step_src = end + jnp.sum(
        jnp.where(inside, owners * spaced - end + src[:, None, :] + step * STEP, 0), axis=2
    )
    step_dst = obs + jnp.sum(jnp.where(inside, dst[:, None, :] + step * STEP - obs, 0), axis=2)
    return (step_src, step_dst), times, wanted


def send_order(count):
    return sorted(range(1, count), key=lambda step: (bin(step // 2).count("1"), step % 2, -step))


def exchange(blocks):
    count = len(blocks)
    out = list(blocks)
    for step in range(1, count):
        out[step] = lax.ppermute(blocks[step], "tm", [(i, i ^ step) for i in range(count)])
    return out


def pass_along(attitude, beside):
    count = lax.axis_size("sky")
    if count == 4:
        right = lax.ppermute(attitude, "sky", [(0, 1), (1, 2), (2, 3)])
        left = lax.ppermute(attitude, "sky", [(1, 0), (2, 1), (3, 2)])
        across = lax.ppermute(attitude, "sky", [(0, 2), (1, 3), (2, 0), (3, 1)])
        across, _ = beside[1](across, across)
        last = lax.ppermute(across, "sky", [(2, 3), (1, 0)])
        across, _ = beside[2](across, across)
        return [attitude, right, left, across, last]
    right = left = attitude
    pieces = [attitude]
    for hop in range(1, count):
        right = lax.ppermute(right, "sky", [(i, i + 1) for i in range(hop - 1, count - 1)])
        left = lax.ppermute(left, "sky", [(i, i - 1) for i in range(1, count - hop + 1)])
        if hop in beside:
            right, left = beside[hop](right, left)
        pieces += [right, left]
    return pieces


def on_device(residuals, seg_counts, attitude, sched_seg, sched_slot, periods):
    tm_count = lax.axis_size("tm")
    sched_dev, obs = sched_seg.shape
    seg_dev, slots, width = residuals.shape
    column_blocks = width // SRC_GROUP
    capacity = 2 * sched_dev * obs // tm_count
    tables, times, wanted = make_lists(
        sched_seg, sched_slot, seg_dev, slots, column_blocks, tm_count, capacity
    )
    wanted = wanted.reshape(tm_count, capacity)
    made = []
    asked = None

    def basis_part(after):
        first, count = sum(BASIS_CALLS[:len(made)]), BASIS_CALLS[len(made)]
        made.append(make_basis(times[first:first + count], periods, after))

    def first_hop(right, left):
        nonlocal asked
        asked = lax.all_to_all(wanted, "tm", split_axis=0, concat_axis=0, tiled=True)
        basis_part([])
        right, left, *_ = lax.optimization_barrier((right, left, asked, made[0][1]))
        return right, left

    def second_hop(right, left):
        basis_part([right, left])
        basis_part([right, left])
        return right, left

    pieces = pass_along(attitude, {1: first_hop, 2: second_hop})
    cnt = jnp.sum((asked < seg_dev * slots * column_blocks).astype(jnp.int32), axis=1)
    where = jnp.stack([lax.axis_index("tm"), lax.axis_index("sky")])
    where, _ = lax.optimization_barrier((where, made[-1][1]))
    scalars = (asked.reshape(-1), cnt, seg_counts, where)
    rows = seg_dev * slots * column_blocks
    order = [0] + send_order(tm_count)
    near, far = order[:3 * tm_count // 4], order[3 * tm_count // 4:]

    base = residuals
    picked = pick_rows(scalars, base, pieces, rows)
    basis_part([picked[0]])
    parts, norms = zip(*made)
    norms = jnp.concatenate(norms)
    for iteration in range(ITERS):
        models, score = fit_plans(tables, exchange(picked), parts, norms)
        returned = exchange(models)
        base = place_early(scalars, near, base, returned, rows)
        if iteration < ITERS - 1:
            base, picked = place_late_and_pick(scalars, far, base, returned, pieces)
    cleaned = place_late(scalars, far, base, returned, residuals.shape)
    return (cleaned, score.reshape(sched_dev, SRC_GROUP))


def solution(mesh):
    in_specs = (
        P("tm", None, "sky"),
        P("tm"),
        P("tm", "sky", None),
        P(("tm", "sky"), None),
        P(("tm", "sky"), None),
        P(),
    )
    out_specs = (P("tm", None, "sky"), P(("tm", "sky"), None))
    return jax.shard_map(
        on_device, mesh=mesh, in_specs=in_specs, out_specs=out_specs, check_vma=False
    )
```

```python
import functools

import jax
import jax.numpy as jnp
from jax import lax
from jax.experimental import pallas as pl
from jax.experimental.pallas import tpu as pltpu
from jax.sharding import PartitionSpec as P

SRC_GROUP = 128
ITERS = 2
STREAMS = 4
LATE_STREAMS = 2
STEP = 16
BETA = 2.0
LOG2_E = 1.4426950408889634
ROUND = 1.5 * 2.0 ** 23
RIDGE = 1.0
MIB = 1024 * 1024
BASIS_VMEM = 8 * MIB
FIT_VMEM = 22 * MIB
EARLY_VMEM = 20 * MIB
PICK_VMEM = 12 * MIB
LATE_PICK_VMEM = 18 * MIB
LATE_VMEM = 12 * MIB
BASIS_CALLS = (1, 2, 3, 2)
UNROLL = 32
PICK_UNROLL = 32
SUB = 8
HBM_SPARE = 32
COST_US = 10 ** 9

COS_POLY = (1.0, -19.73920440673828, 64.9391098022461, -85.4500503540039, 60.16689682006836,
            -25.96480369567871, 6.52468729019165)
SIN_POLY = (6.283185005187988, -41.34158706665039, 81.59986114501953, -76.61351013183594,
            41.33811950683594, -12.463061332702637)

VMEM = pl.BlockSpec(memory_space=pltpu.VMEM)
HBM = pl.BlockSpec(memory_space=pltpu.HBM)
ANY = pl.BlockSpec(memory_space=pl.ANY)
SMEM = pl.BlockSpec(memory_space=pltpu.SMEM)


def horner(poly, v):
    acc = jnp.full_like(v, poly[-1])
    for term in poly[-2::-1]:
        acc = acc * v + term
    return acc


def basis_kernel(after, time_ref, period_ref, inverse_ref, *refs):
    basis_ref, norm_ref = refs[after:]
    obs = time_ref.shape[0]
    nper = period_ref.shape[1]
    rows = 64
    for chunk in range(nper // 128):
        lanes = pl.ds(chunk * 128, 128)
        sines = pl.ds(nper + chunk * 128, 128)
        period = period_ref[:, lanes]
        inverse = inverse_ref[:, lanes]

        def step(index, sums):
            at = pl.ds(pl.multiple_of(index * rows, rows), rows)
            time = time_ref[at, :]
            turns = (time * inverse + ROUND) - ROUND
            part = (time - turns * period) * inverse
            square = part * part
            cosine = horner(COS_POLY, square).astype(jnp.bfloat16)
            sine = (horner(SIN_POLY, square) * part).astype(jnp.bfloat16)
            basis_ref[0, at, lanes] = cosine
            basis_ref[0, at, sines] = sine
            cosine = cosine.astype(jnp.float32)
            sine = sine.astype(jnp.float32)
            return (
                sums[0] + jnp.sum((cosine * cosine).reshape(rows // 8, 8, 128), axis=0),
                sums[1] + jnp.sum((sine * sine).reshape(rows // 8, 8, 128), axis=0),
            )

        zero = jnp.zeros((8, 128), jnp.float32)
        total_c, total_s = lax.fori_loop(0, obs // rows, step, (zero, zero))
        norm_ref[0, :, lanes] = 1.0 / (jnp.sum(total_c, axis=0, keepdims=True) + RIDGE)
        norm_ref[0, :, sines] = 1.0 / (jnp.sum(total_s, axis=0, keepdims=True) + RIDGE)


def make_basis(times, periods, after):
    sched_dev, obs = times.shape
    nper = periods.shape[0]
    wide = jnp.broadcast_to(
        times.astype(jnp.float32).reshape(-1, 1), (sched_dev * obs, SRC_GROUP)
    )
    period = periods.astype(jnp.float32)[None, :]
    return pl.pallas_call(
        functools.partial(basis_kernel, len(after)),
        grid=(sched_dev,),
        in_specs=[
            pl.BlockSpec((obs, SRC_GROUP), lambda j: (j, 0)),
            pl.BlockSpec((1, nper), lambda j: (0, 0)),
            pl.BlockSpec((1, nper), lambda j: (0, 0)),
        ] + [ANY] * len(after),
        out_specs=[
            pl.BlockSpec((1, obs, 2 * nper), lambda j: (j, 0, 0)),
            pl.BlockSpec((1, 1, 2 * nper), lambda j: (j, 0, 0)),
        ],
        out_shape=[
            jax.ShapeDtypeStruct((sched_dev, obs, 2 * nper), jnp.bfloat16),
            jax.ShapeDtypeStruct((sched_dev, 1, 2 * nper), jnp.float32),
        ],
        compiler_params=pltpu.CompilerParams(vmem_limit_bytes=BASIS_VMEM),
        cost_estimate=pl.CostEstimate(
            flops=sched_dev * obs * nper * 8000, bytes_accessed=sched_dev * obs * nper * 4, transcendentals=0
        ),
    )(wide, period, 1.0 / period, *after)


def fit_kernel(order, src_ref, dst_ref, *refs):
    refs = list(refs)

    def take(count):
        taken = refs[:count]
        del refs[:count]
        return taken

    tm_count = len(order)
    arrived = dict(zip(order, take(tm_count)))
    parts = take(len(BASIS_CALLS))
    (norm_ref,) = take(1)
    outs = take(tm_count)
    score_ref, basis_ref, sems, rows_ref, back_ref = take(5)
    slots = [take(4), take(4)]
    plans, obs, twice = basis_ref.shape
    nper = twice // 2
    capacity, width = arrived[0].shape
    spaced = capacity + STEP
    steps = src_ref.shape[1]
    held = [(part, plan) for part, count in zip(parts, BASIS_CALLS) for plan in range(count)]

    def basis_copy(plan):
        part, index = held[plan]
        return pltpu.make_async_copy(part.at[index], basis_ref.at[plan], sems.at[plan])

    for plan in range(plans):
        basis_copy(plan).start()
    for owner in range(tm_count):
        rows_ref[pl.ds(owner * spaced, capacity), :] = arrived[owner][...].astype(jnp.float32)

    def correlate(plan, obs_ref, corr_ref):
        for step in range(steps):
            obs_ref[pl.ds(dst_ref[plan, step], STEP), :] = rows_ref[pl.ds(src_ref[plan, step], STEP), :]
        corr_ref[...] = lax.dot_general(
            obs_ref[:obs, :].astype(jnp.bfloat16), basis_ref[plan], (((0,), (0,)), ((), ())),
            preferred_element_type=jnp.float32,
        )

    def finish(plan, corr_ref, coeff_ref, model_ref):
        group = 16
        for start in range(0, width, group):
            at = pl.ds(start, group)
            power = []
            for chunk in range(nper // 128):
                lanes = pl.ds(chunk * 128, 128)
                sines = pl.ds(nper + chunk * 128, 128)
                cosine = corr_ref[at, lanes]
                sine = corr_ref[at, sines]
                power.append(
                    cosine * (cosine * norm_ref[plan, :, lanes]) + sine * (sine * norm_ref[plan, :, sines])
                )
            highest = functools.reduce(jnp.maximum, power)
            highest = jnp.max(highest, axis=1, keepdims=True)
            expo = [jnp.exp2((value - highest) * (BETA * LOG2_E)) for value in power]
            total = jnp.sum(functools.reduce(jnp.add, expo), axis=1, keepdims=True)
            scale = 1.0 / total
            for chunk in range(nper // 128):
                lanes = pl.ds(chunk * 128, 128)
                sines = pl.ds(nper + chunk * 128, 128)
                share = expo[chunk] * scale
                coeff_ref[at, lanes] = (share * (corr_ref[at, lanes] * norm_ref[plan, :, lanes])).astype(jnp.bfloat16)
                coeff_ref[at, sines] = (share * (corr_ref[at, sines] * norm_ref[plan, :, sines])).astype(jnp.bfloat16)
            score_ref[plan, at, :] = BETA * highest + jnp.log(total)
        model_ref[:obs, :] = lax.dot_general(
            basis_ref[plan], coeff_ref[...], (((1,), (1,)), ((), ())), preferred_element_type=jnp.float32
        )
        for step in range(steps):
            back_ref[pl.ds(src_ref[plan, step], STEP), :] = model_ref[pl.ds(dst_ref[plan, step], STEP), :]

    basis_copy(0).wait()
    correlate(0, slots[0][0], slots[0][1])

    def pair(index, carry):
        plan = index * 2
        for ahead in (1, 2):
            for known in range(ahead, plans, 2):
                pl.when(plan + ahead == known)(basis_copy(known).wait)
        correlate(plan + 1, slots[1][0], slots[1][1])
        finish(plan, *slots[0][1:])
        correlate(jnp.minimum(plan + 2, plans - 1), slots[0][0], slots[0][1])
        finish(plan + 1, *slots[1][1:])
        return carry

    lax.fori_loop(0, plans // 2, pair, 0)
    for owner in range(tm_count):
        outs[owner][...] = back_ref[pl.ds(owner * spaced, capacity), :].astype(jnp.bfloat16)


def fit_plans(tables, arrived, parts, norms):
    tm_count = len(arrived)
    order = [0] + send_order(tm_count)
    _, obs, twice = parts[0].shape
    sched_dev = norms.shape[0]
    capacity, width = arrived[0].shape
    work = sched_dev * obs * twice * width
    spaced = tm_count * (capacity + STEP) + STEP
    slot = [
        pltpu.VMEM((obs + STEP, width), jnp.float32),
        pltpu.VMEM((width, twice), jnp.float32),
        pltpu.VMEM((width, twice), jnp.bfloat16),
        pltpu.VMEM((obs + STEP, width), jnp.float32),
    ]
    *models, score = pl.pallas_call(
        functools.partial(fit_kernel, order),
        in_specs=[SMEM, SMEM] + [VMEM] * tm_count + [ANY] * len(parts) + [VMEM],
        out_specs=[VMEM] * (tm_count + 1),
        out_shape=[jax.ShapeDtypeStruct((capacity, width), jnp.bfloat16)] * tm_count
        + [jax.ShapeDtypeStruct((sched_dev, width, 1), jnp.float32)],
        scratch_shapes=[
            pltpu.VMEM((sched_dev, obs, twice), jnp.bfloat16),
            pltpu.SemaphoreType.DMA((sched_dev,)),
            pltpu.VMEM((spaced, width), jnp.float32),
            pltpu.VMEM((spaced, width), jnp.float32),
        ] + slot + slot,
        compiler_params=pltpu.CompilerParams(vmem_limit_bytes=FIT_VMEM),
        cost_estimate=pl.CostEstimate(flops=20 * work, bytes_accessed=sched_dev * obs * twice * 2, transcendentals=0),
    )(*tables, *[arrived[owner] for owner in order], *parts, norms)
    return models, score


def load_attitude(sky, own_ref, passed, whole_ref, sems):
    rows = own_ref.shape[1]
    count = len(passed) // 2 + 1
    copies = [(None, sky, own_ref)]
    for hop in range(1, count):
        copies.append((sky >= hop, sky - hop, passed[2 * hop - 2]))
        copies.append((sky + hop < count, sky + hop, passed[2 * hop - 1]))

    def each(act):
        for index, (valid, quarter, ref) in enumerate(copies):
            def run(index=index, quarter=quarter, ref=ref):
                at = pl.ds(pl.multiple_of(quarter * rows, rows), rows)
                act(pltpu.make_async_copy(ref, whole_ref.at[:, at, :], sems.at[index]))

            if valid is None:
                run()
            else:
                pl.when(valid)(run)

    each(lambda copy: copy.start())
    return lambda: each(lambda copy: copy.wait())


def whiten_and_pick(me, asked_ref, cnt_ref, count_ref, whole_ref, wait, load, picked, white_ref, gather_ref):
    segs, slots, _ = whole_ref.shape
    capacity, width = picked[0].shape
    blocks = white_ref.shape[0] // (segs * slots)
    row = lax.broadcasted_iota(jnp.int32, (slots, width * blocks), 0)
    wait()
    for seg in range(segs):
        masked = jnp.where(row < count_ref[seg], load(seg).astype(jnp.float32), 0.0).astype(jnp.bfloat16)
        white = jnp.dot(whole_ref[seg], masked, preferred_element_type=jnp.float32)
        for block in range(blocks):
            white_ref[pl.ds((block * segs + seg) * slots, slots), :] = white[:, block * width:(block + 1) * width]
    for owner, out_ref in enumerate(picked):
        asker = owner ^ me

        def step(index, carry):
            first = index * PICK_UNROLL
            for lane in range(PICK_UNROLL):
                gather_ref[pl.ds(owner * capacity + first + lane, 1), :] = white_ref[
                    pl.ds(asked_ref[asker * capacity + first + lane], 1), :
                ]
            return carry

        lax.fori_loop(0, (cnt_ref[asker] + PICK_UNROLL - 1) // PICK_UNROLL, step, 0)
        out_ref[...] = gather_ref[pl.ds(owner * capacity, capacity), :].astype(jnp.bfloat16)


def add_rows(me, asked_ref, cnt_ref, owners, returned, rows_ref, sums, tiled):
    capacity = returned[0].shape[0]
    streams = len(sums)
    for total in sums:
        total[...] = jnp.zeros_like(total)
    for number, (owner, ref) in enumerate(zip(owners, returned)):
        tiles = capacity // SUB
        block = ref[...].astype(jnp.float32)
        if tiled:
            rows_ref[pl.ds(number * tiles, tiles)] = block.reshape(tiles, SUB, -1)
        else:
            rows_ref[pl.ds(number * capacity, capacity), :] = block
        asker = owner ^ me

        def row_at(index, lane):
            if tiled:
                return rows_ref[number * tiles + index * (UNROLL // SUB) + lane // SUB, pl.ds(lane % SUB, 1), :]
            return rows_ref[pl.ds(number * capacity + index * UNROLL + lane, 1), :]

        def step(index, carry):
            first = asker * capacity + index * UNROLL
            for start in range(0, UNROLL, streams):
                lanes = [start + lane for lane in range(streams)]
                places = [asked_ref[first + lane] for lane in lanes]
                values = [
                    total[pl.ds(place, 1), :] + row_at(index, lane)
                    for total, place, lane in zip(sums, places, lanes)
                ]
                for total, place, value in zip(sums, places, values):
                    total[pl.ds(place, 1), :] = value
            return carry

        lax.fori_loop(0, (cnt_ref[asker] + UNROLL - 1) // UNROLL, step, 0)


def placed_at(sums, at):
    return functools.reduce(jnp.add, [total[at, :] for total in sums])


def early_kernel(owners, table_base, asked_ref, cnt_ref, where_ref, base_ref, *refs):
    refs = list(refs)
    returned = [refs.pop(0) for _ in owners]
    out_ref, rows_ref = refs.pop(0), refs.pop(0)
    if table_base:
        held_ref, sem = refs.pop(0), refs.pop(0)
        copy = pltpu.make_async_copy(base_ref.at[pl.ds(0, held_ref.shape[0]), :], held_ref, sem)
        copy.start()
    add_rows(where_ref[0], asked_ref, cnt_ref, owners, returned, rows_ref, refs, True)
    if table_base:
        copy.wait()
        out_ref[...] = held_ref[...] - placed_at(refs, pl.ds(0, out_ref.shape[0]))
        return
    segs, slots, total_width = base_ref.shape
    width = out_ref.shape[1]
    for block in range(total_width // width):
        for seg in range(segs):
            at = pl.ds((block * segs + seg) * slots, slots)
            base = base_ref[seg, :, block * width:(block + 1) * width].astype(jnp.float32)
            out_ref[at, :] = base - placed_at(refs, at)


def place_early(scalars, owners, base, returned, rows):
    asked, cnt, _, where = scalars
    table_base = base.ndim == 2
    capacity = returned[0].shape[0]
    sums = [pltpu.VMEM((rows + 8, SRC_GROUP), jnp.float32)] * STREAMS
    held = [pltpu.VMEM((rows, SRC_GROUP), jnp.float32), pltpu.SemaphoreType.DMA(())] if table_base else []
    return pl.pallas_call(
        functools.partial(early_kernel, owners, table_base),
        in_specs=[SMEM] * 3 + [HBM if table_base else VMEM] + [VMEM] * len(owners),
        out_specs=VMEM,
        out_shape=jax.ShapeDtypeStruct((rows, SRC_GROUP), jnp.float32),
        scratch_shapes=[pltpu.VMEM((len(owners) * capacity // SUB, SUB, SRC_GROUP), jnp.float32)] + held + sums,
        compiler_params=pltpu.CompilerParams(vmem_limit_bytes=EARLY_VMEM),
        cost_estimate=pl.CostEstimate(flops=6 * COST_US, bytes_accessed=1 << 20, transcendentals=0),
    )(asked, cnt, where, base, *[returned[owner] for owner in owners])


def pick_kernel(tm_count, passed_count, asked_ref, cnt_ref, count_ref, where_ref, base_ref, own_ref, *refs):
    refs = list(refs)
    passed = [refs.pop(0) for _ in range(passed_count)]
    picked = [refs.pop(0) for _ in range(tm_count)]
    whole_ref, sems, white_ref, gather_ref = refs
    wait = load_attitude(where_ref[1], own_ref, passed, whole_ref, sems)
    whiten_and_pick(
        where_ref[0], asked_ref, cnt_ref, count_ref, whole_ref, wait, lambda seg: base_ref[seg], picked, white_ref,
        gather_ref,
    )


def pick_rows(scalars, base, attitude, rows):
    asked, cnt, seg_counts, where = scalars
    tm_count, = cnt.shape
    seg_dev, slots, _ = base.shape
    capacity = asked.shape[0] // tm_count
    return pl.pallas_call(
        functools.partial(pick_kernel, tm_count, len(attitude) - 1),
        in_specs=[SMEM] * 4 + [VMEM] + [ANY] * len(attitude),
        out_specs=[VMEM] * tm_count,
        out_shape=[jax.ShapeDtypeStruct((capacity, SRC_GROUP), jnp.bfloat16)] * tm_count,
        scratch_shapes=[
            pltpu.VMEM((seg_dev, slots, slots), jnp.bfloat16),
            pltpu.SemaphoreType.DMA((len(attitude),)),
            pltpu.VMEM((rows + 8, SRC_GROUP), jnp.float32),
            pltpu.VMEM((tm_count * capacity, SRC_GROUP), jnp.float32),
        ],
        compiler_params=pltpu.CompilerParams(vmem_limit_bytes=PICK_VMEM),
        cost_estimate=pl.CostEstimate(flops=5 * COST_US, bytes_accessed=1 << 20, transcendentals=0),
    )(asked, cnt, seg_counts, where, base, *attitude)


def late_pick_kernel(tm_count, passed_count, owners, asked_ref, cnt_ref, count_ref, where_ref, part_ref, own_ref,
                     *refs):
    refs = list(refs)

    def take(count):
        taken = refs[:count]
        del refs[:count]
        return taken

    passed = take(passed_count)
    returned = take(len(owners))
    (out_ref,) = take(1)
    picked = take(tm_count)
    whole_ref, sems, white_ref, gather_ref, table_ref, sem = take(6)
    segs, slots, _ = whole_ref.shape
    blocks = table_ref.shape[0] // (segs * slots)
    wait = load_attitude(where_ref[1], own_ref, passed, whole_ref, sems)
    add_rows(where_ref[0], asked_ref, cnt_ref, owners, returned, gather_ref, refs, False)
    table_ref[...] = part_ref[...] - placed_at(refs, pl.ds(0, table_ref.shape[0]))
    copy = pltpu.make_async_copy(table_ref, out_ref.at[pl.ds(0, table_ref.shape[0]), :], sem)
    copy.start()

    def load(seg):
        return jnp.concatenate(
            [table_ref[pl.ds((block * segs + seg) * slots, slots), :] for block in range(blocks)], axis=1
        )

    whiten_and_pick(
        where_ref[0], asked_ref, cnt_ref, count_ref, whole_ref, wait, load, picked, white_ref, gather_ref
    )
    copy.wait()


def place_late_and_pick(scalars, owners, part, returned, attitude):
    asked, cnt, seg_counts, where = scalars
    tm_count, = cnt.shape
    seg_dev = seg_counts.shape[0]
    slots = attitude[0].shape[2]
    capacity = asked.shape[0] // tm_count
    rows = part.shape[0]
    table = pltpu.VMEM((rows + 8, SRC_GROUP), jnp.float32)
    out = pl.pallas_call(
        functools.partial(late_pick_kernel, tm_count, len(attitude) - 1, owners),
        in_specs=[SMEM] * 4 + [VMEM] + [ANY] * len(attitude) + [VMEM] * len(owners),
        out_specs=[HBM] + [VMEM] * tm_count,
        out_shape=[jax.ShapeDtypeStruct((HBM_SPARE * rows, SRC_GROUP), jnp.float32)]
        + [jax.ShapeDtypeStruct((capacity, SRC_GROUP), jnp.bfloat16)] * tm_count,
        scratch_shapes=[
            pltpu.VMEM((seg_dev, slots, slots), jnp.bfloat16),
            pltpu.SemaphoreType.DMA((len(attitude),)),
            table,
            pltpu.VMEM((tm_count * capacity, SRC_GROUP), jnp.float32),
            pltpu.VMEM((rows, SRC_GROUP), jnp.float32),
            pltpu.SemaphoreType.DMA(()),
        ] + [table] * LATE_STREAMS,
        compiler_params=pltpu.CompilerParams(vmem_limit_bytes=LATE_PICK_VMEM),
        cost_estimate=pl.CostEstimate(flops=7 * COST_US, bytes_accessed=1 << 20, transcendentals=0),
    )(asked, cnt, seg_counts, where, part, *attitude, *[returned[owner] for owner in owners])
    return out[0], list(out[1:])


def late_kernel(owners, asked_ref, cnt_ref, where_ref, part_ref, *refs):
    refs = list(refs)
    returned = [refs.pop(0) for _ in owners]
    out_ref, rows_ref, held_ref, sems = refs[:4]
    sums = refs[4:]
    segs, slots, total_width = out_ref.shape
    width = part_ref.shape[1]
    add_rows(where_ref[0], asked_ref, cnt_ref, owners, returned, rows_ref, sums, False)
    copies = []
    for seg in range(segs):
        for block in range(total_width // width):
            at = pl.ds((block * segs + seg) * slots, slots)
            held_ref[seg, :, block * width:(block + 1) * width] = part_ref[at, :] - placed_at(sums, at)
        copies.append(pltpu.make_async_copy(held_ref.at[seg], out_ref.at[seg], sems.at[seg]))
        copies[-1].start()
    for copy in copies:
        copy.wait()


def place_late(scalars, owners, part, returned, shape):
    asked, cnt, _, where = scalars
    capacity = returned[0].shape[0]
    return pl.pallas_call(
        functools.partial(late_kernel, owners),
        in_specs=[SMEM] * 3 + [VMEM] * (1 + len(owners)),
        out_specs=HBM,
        out_shape=jax.ShapeDtypeStruct(shape, jnp.float32),
        scratch_shapes=[
            pltpu.VMEM((len(owners) * capacity, SRC_GROUP), jnp.float32),
            pltpu.VMEM(shape, jnp.float32),
            pltpu.SemaphoreType.DMA((shape[0],)),
        ] + [pltpu.VMEM((part.shape[0] + 8, SRC_GROUP), jnp.float32)] * LATE_STREAMS,
        compiler_params=pltpu.CompilerParams(vmem_limit_bytes=LATE_VMEM),
        cost_estimate=pl.CostEstimate(flops=4 * COST_US, bytes_accessed=1 << 20, transcendentals=0),
    )(asked, cnt, where, part, *[returned[owner] for owner in owners])


def make_lists(sched_seg, sched_slot, seg_dev, slots, column_blocks, tm_count, capacity):
    sched_dev, obs = sched_seg.shape
    me = lax.axis_index("tm")
    owner = sched_seg // seg_dev
    partner = owner ^ me
    block_of = (jnp.arange(sched_dev, dtype=jnp.int32) % column_blocks)[:, None]
    local_row = (block_of * seg_dev + sched_seg % seg_dev) * slots + sched_slot
    hot = (partner[:, :, None] == jnp.arange(tm_count, dtype=jnp.int32)).astype(jnp.int32)
    cnt = jnp.sum(hot, axis=1)
    plans = jnp.arange(sched_dev)
    before = (plans[None, :] < plans[:, None]).astype(jnp.int32)
    src = jnp.sum(before[:, :, None] * cnt[None, :, :], axis=1)
    owners = jnp.arange(tm_count)
    ahead = (owners[None, :] < owners[:, None]).astype(jnp.int32)
    dst = jnp.sum(ahead[None, :, :] * cnt[:, None, :], axis=2)
    entry = jnp.arange(obs)
    rank = jnp.sum(
        ((partner[:, None, :] == partner[:, :, None]) & (entry[None, :] < entry[:, None])).astype(jnp.int32),
        axis=2,
    )
    place = owner * capacity + jnp.sum(hot * src[:, None, :], axis=2) + rank
    order = jnp.sum(hot * dst[:, None, :], axis=2) + rank
    time = sched_seg * slots + sched_slot
    times = jnp.sum(jnp.where(order[:, None, :] == entry[None, :, None], time[:, None, :], 0), axis=2)
    rows = seg_dev * slots * column_blocks
    wanted = rows + jnp.sum(
        jnp.where(
            place.reshape(1, -1) == jnp.arange(tm_count * capacity, dtype=jnp.int32)[:, None],
            local_row.reshape(1, -1) - rows,
            0,
        ),
        axis=1,
    )
    step_count = (cnt + STEP - 1) // STEP
    step_first = jnp.sum(ahead[None, :, :] * step_count[:, None, :], axis=2)
    step = jnp.arange(obs // STEP + tm_count)[None, :, None] - step_first[:, None, :]
    inside = (step >= 0) & (step < step_count[:, None, :])
    spaced = capacity + STEP
    end = tm_count * spaced
    step_src = end + jnp.sum(
        jnp.where(inside, owners * spaced - end + src[:, None, :] + step * STEP, 0), axis=2
    )
    step_dst = obs + jnp.sum(jnp.where(inside, dst[:, None, :] + step * STEP - obs, 0), axis=2)
    return (step_src, step_dst), times, wanted


def send_order(count):
    return sorted(range(1, count), key=lambda step: (bin(step // 2).count("1"), step % 2, -step))


def exchange(blocks):
    count = len(blocks)
    out = list(blocks)
    for step in range(1, count):
        out[step] = lax.ppermute(blocks[step], "tm", [(i, i ^ step) for i in range(count)])
    return out


def pass_along(attitude, beside):
    count = lax.axis_size("sky")
    right = left = attitude
    pieces = [attitude]
    for hop in range(1, count):
        right = lax.ppermute(right, "sky", [(i, i + 1) for i in range(hop - 1, count - 1)])
        left = lax.ppermute(left, "sky", [(i, i - 1) for i in range(1, count - hop + 1)])
        if hop in beside:
            right, left = beside[hop](right, left)
        pieces += [right, left]
    return pieces


def on_device(residuals, seg_counts, attitude, sched_seg, sched_slot, periods):
    tm_count = lax.axis_size("tm")
    sched_dev, obs = sched_seg.shape
    seg_dev, slots, width = residuals.shape
    column_blocks = width // SRC_GROUP
    capacity = 2 * sched_dev * obs // tm_count
    tables, times, wanted = make_lists(
        sched_seg, sched_slot, seg_dev, slots, column_blocks, tm_count, capacity
    )
    wanted = wanted.reshape(tm_count, capacity)
    made = []
    asked = None

    def basis_part(after):
        first, count = sum(BASIS_CALLS[:len(made)]), BASIS_CALLS[len(made)]
        made.append(make_basis(times[first:first + count], periods, after))

    def first_hop(right, left):
        nonlocal asked
        basis_part([right, left])
        held, _ = lax.optimization_barrier((wanted, made[0][1]))
        asked = lax.all_to_all(held, "tm", split_axis=0, concat_axis=0, tiled=True)
        return right, left

    def second_hop(right, left):
        basis_part([right, left])
        basis_part([right, left])
        return right, left

    pieces = pass_along(attitude, {1: first_hop, 2: second_hop})
    cnt = jnp.sum((asked < seg_dev * slots * column_blocks).astype(jnp.int32), axis=1)
    where = jnp.stack([lax.axis_index("tm"), lax.axis_index("sky")])
    scalars = (asked.reshape(-1), cnt, seg_counts, where)
    rows = seg_dev * slots * column_blocks
    order = [0] + send_order(tm_count)
    near, far = order[:3 * tm_count // 4], order[3 * tm_count // 4:]

    base = residuals
    picked = pick_rows(scalars, base, pieces, rows)
    basis_part([picked[0]])
    parts, norms = zip(*made)
    norms = jnp.concatenate(norms)
    for iteration in range(ITERS):
        models, score = fit_plans(tables, exchange(picked), parts, norms)
        returned = exchange(models)
        base = place_early(scalars, near, base, returned, rows)
        if iteration < ITERS - 1:
            base, picked = place_late_and_pick(scalars, far, base, returned, pieces)
    cleaned = place_late(scalars, far, base, returned, residuals.shape)
    return (cleaned, score.reshape(sched_dev, SRC_GROUP))


def solution(mesh):
    in_specs = (
        P("tm", None, "sky"),
        P("tm"),
        P("tm", "sky", None),
        P(("tm", "sky"), None),
        P(("tm", "sky"), None),
        P(),
    )
    out_specs = (P("tm", None, "sky"), P(("tm", "sky"), None))
    return jax.shard_map(
        on_device, mesh=mesh, in_specs=in_specs, out_specs=out_specs, check_vma=False
    )
```

```python
import functools

import jax
import jax.numpy as jnp
from jax import lax
from jax.experimental import pallas as pl
from jax.experimental.pallas import tpu as pltpu
from jax.sharding import PartitionSpec as P

SRC_GROUP = 128
ITERS = 2
STREAMS = 4
LATE_STREAMS = 2
STEP = 16
BETA = 2.0
LOG2_E = 1.4426950408889634
ROUND = 1.5 * 2.0 ** 23
RIDGE = 1.0
MIB = 1024 * 1024
BASIS_VMEM = 8 * MIB
FIT_VMEM = 22 * MIB
EARLY_VMEM = 20 * MIB
PICK_VMEM = 12 * MIB
LATE_PICK_VMEM = 18 * MIB
LATE_VMEM = 12 * MIB
BASIS_CALLS = (1, 2, 3, 2)
UNROLL = 32
PICK_UNROLL = 32
SUB = 8
HBM_SPARE = 32
COST_US = 10 ** 9

COS_POLY = (1.0, -19.73920440673828, 64.9391098022461, -85.4500503540039, 60.16689682006836,
            -25.96480369567871, 6.52468729019165)
SIN_POLY = (6.283185005187988, -41.34158706665039, 81.59986114501953, -76.61351013183594,
            41.33811950683594, -12.463061332702637)

VMEM = pl.BlockSpec(memory_space=pltpu.VMEM)
HBM = pl.BlockSpec(memory_space=pltpu.HBM)
ANY = pl.BlockSpec(memory_space=pl.ANY)
SMEM = pl.BlockSpec(memory_space=pltpu.SMEM)


def horner(poly, v):
    acc = jnp.full_like(v, poly[-1])
    for term in poly[-2::-1]:
        acc = acc * v + term
    return acc


def basis_kernel(after, time_ref, period_ref, inverse_ref, *refs):
    basis_ref, norm_ref = refs[after:]
    obs = time_ref.shape[0]
    nper = period_ref.shape[1]
    rows = 64
    for chunk in range(nper // 128):
        lanes = pl.ds(chunk * 128, 128)
        sines = pl.ds(nper + chunk * 128, 128)
        period = period_ref[:, lanes]
        inverse = inverse_ref[:, lanes]

        def step(index, sums):
            at = pl.ds(pl.multiple_of(index * rows, rows), rows)
            time = time_ref[at, :]
            turns = (time * inverse + ROUND) - ROUND
            part = (time - turns * period) * inverse
            square = part * part
            cosine = horner(COS_POLY, square).astype(jnp.bfloat16)
            sine = (horner(SIN_POLY, square) * part).astype(jnp.bfloat16)
            basis_ref[0, at, lanes] = cosine
            basis_ref[0, at, sines] = sine
            cosine = cosine.astype(jnp.float32)
            sine = sine.astype(jnp.float32)
            return (
                sums[0] + jnp.sum((cosine * cosine).reshape(rows // 8, 8, 128), axis=0),
                sums[1] + jnp.sum((sine * sine).reshape(rows // 8, 8, 128), axis=0),
            )

        zero = jnp.zeros((8, 128), jnp.float32)
        total_c, total_s = lax.fori_loop(0, obs // rows, step, (zero, zero))
        norm_ref[0, :, lanes] = 1.0 / (jnp.sum(total_c, axis=0, keepdims=True) + RIDGE)
        norm_ref[0, :, sines] = 1.0 / (jnp.sum(total_s, axis=0, keepdims=True) + RIDGE)


def make_basis(times, periods, after):
    sched_dev, obs = times.shape
    nper = periods.shape[0]
    wide = jnp.broadcast_to(
        times.astype(jnp.float32).reshape(-1, 1), (sched_dev * obs, SRC_GROUP)
    )
    period = periods.astype(jnp.float32)[None, :]
    return pl.pallas_call(
        functools.partial(basis_kernel, len(after)),
        grid=(sched_dev,),
        in_specs=[
            pl.BlockSpec((obs, SRC_GROUP), lambda j: (j, 0)),
            pl.BlockSpec((1, nper), lambda j: (0, 0)),
            pl.BlockSpec((1, nper), lambda j: (0, 0)),
        ] + [ANY] * len(after),
        out_specs=[
            pl.BlockSpec((1, obs, 2 * nper), lambda j: (j, 0, 0)),
            pl.BlockSpec((1, 1, 2 * nper), lambda j: (j, 0, 0)),
        ],
        out_shape=[
            jax.ShapeDtypeStruct((sched_dev, obs, 2 * nper), jnp.bfloat16),
            jax.ShapeDtypeStruct((sched_dev, 1, 2 * nper), jnp.float32),
        ],
        compiler_params=pltpu.CompilerParams(vmem_limit_bytes=BASIS_VMEM),
        cost_estimate=pl.CostEstimate(
            flops=sched_dev * obs * nper * 8000, bytes_accessed=sched_dev * obs * nper * 4, transcendentals=0
        ),
    )(wide, period, 1.0 / period, *after)


def fit_kernel(order, src_ref, dst_ref, *refs):
    refs = list(refs)

    def take(count):
        taken = refs[:count]
        del refs[:count]
        return taken

    tm_count = len(order)
    arrived = dict(zip(order, take(tm_count)))
    parts = take(len(BASIS_CALLS))
    (norm_ref,) = take(1)
    outs = take(tm_count)
    score_ref, basis_ref, sems, rows_ref, back_ref = take(5)
    slots = [take(4), take(4)]
    plans, obs, twice = basis_ref.shape
    nper = twice // 2
    capacity, width = arrived[0].shape
    spaced = capacity + STEP
    steps = src_ref.shape[1]
    held = [(part, plan) for part, count in zip(parts, BASIS_CALLS) for plan in range(count)]

    def basis_copy(plan):
        part, index = held[plan]
        return pltpu.make_async_copy(part.at[index], basis_ref.at[plan], sems.at[plan])

    for plan in range(plans):
        basis_copy(plan).start()
    for owner in range(tm_count):
        rows_ref[pl.ds(owner * spaced, capacity), :] = arrived[owner][...].astype(jnp.float32)

    def correlate(plan, obs_ref, corr_ref):
        for step in range(steps):
            obs_ref[pl.ds(dst_ref[plan, step], STEP), :] = rows_ref[pl.ds(src_ref[plan, step], STEP), :]
        corr_ref[...] = lax.dot_general(
            obs_ref[:obs, :].astype(jnp.bfloat16), basis_ref[plan], (((0,), (0,)), ((), ())),
            preferred_element_type=jnp.float32,
        )

    def finish(plan, corr_ref, coeff_ref, model_ref):
        group = 16
        for start in range(0, width, group):
            at = pl.ds(start, group)
            power = []
            for chunk in range(nper // 128):
                lanes = pl.ds(chunk * 128, 128)
                sines = pl.ds(nper + chunk * 128, 128)
                cosine = corr_ref[at, lanes]
                sine = corr_ref[at, sines]
                power.append(
                    cosine * (cosine * norm_ref[plan, :, lanes]) + sine * (sine * norm_ref[plan, :, sines])
                )
            highest = functools.reduce(jnp.maximum, power)
            highest = jnp.max(highest, axis=1, keepdims=True)
            expo = [jnp.exp2((value - highest) * (BETA * LOG2_E)) for value in power]
            total = jnp.sum(functools.reduce(jnp.add, expo), axis=1, keepdims=True)
            scale = 1.0 / total
            for chunk in range(nper // 128):
                lanes = pl.ds(chunk * 128, 128)
                sines = pl.ds(nper + chunk * 128, 128)
                share = expo[chunk] * scale
                coeff_ref[at, lanes] = (share * (corr_ref[at, lanes] * norm_ref[plan, :, lanes])).astype(jnp.bfloat16)
                coeff_ref[at, sines] = (share * (corr_ref[at, sines] * norm_ref[plan, :, sines])).astype(jnp.bfloat16)
            score_ref[plan, at, :] = BETA * highest + jnp.log(total)
        model_ref[:obs, :] = lax.dot_general(
            basis_ref[plan], coeff_ref[...], (((1,), (1,)), ((), ())), preferred_element_type=jnp.float32
        )
        for step in range(steps):
            back_ref[pl.ds(src_ref[plan, step], STEP), :] = model_ref[pl.ds(dst_ref[plan, step], STEP), :]

    basis_copy(0).wait()
    correlate(0, slots[0][0], slots[0][1])

    def pair(index, carry):
        plan = index * 2
        for ahead in (1, 2):
            for known in range(ahead, plans, 2):
                pl.when(plan + ahead == known)(basis_copy(known).wait)
        correlate(plan + 1, slots[1][0], slots[1][1])
        finish(plan, *slots[0][1:])
        correlate(jnp.minimum(plan + 2, plans - 1), slots[0][0], slots[0][1])
        finish(plan + 1, *slots[1][1:])
        return carry

    lax.fori_loop(0, plans // 2, pair, 0)
    for owner in range(tm_count):
        outs[owner][...] = back_ref[pl.ds(owner * spaced, capacity), :].astype(jnp.bfloat16)


def fit_plans(tables, arrived, parts, norms):
    tm_count = len(arrived)
    order = [0] + send_order(tm_count)[1:] + [1]
    _, obs, twice = parts[0].shape
    sched_dev = norms.shape[0]
    capacity, width = arrived[0].shape
    work = sched_dev * obs * twice * width
    spaced = tm_count * (capacity + STEP) + STEP
    slot = [
        pltpu.VMEM((obs + STEP, width), jnp.float32),
        pltpu.VMEM((width, twice), jnp.float32),
        pltpu.VMEM((width, twice), jnp.bfloat16),
        pltpu.VMEM((obs + STEP, width), jnp.float32),
    ]
    *models, score = pl.pallas_call(
        functools.partial(fit_kernel, order),
        in_specs=[SMEM, SMEM] + [VMEM] * tm_count + [ANY] * len(parts) + [VMEM],
        out_specs=[VMEM] * (tm_count + 1),
        out_shape=[jax.ShapeDtypeStruct((capacity, width), jnp.bfloat16)] * tm_count
        + [jax.ShapeDtypeStruct((sched_dev, width, 1), jnp.float32)],
        scratch_shapes=[
            pltpu.VMEM((sched_dev, obs, twice), jnp.bfloat16),
            pltpu.SemaphoreType.DMA((sched_dev,)),
            pltpu.VMEM((spaced, width), jnp.float32),
            pltpu.VMEM((spaced, width), jnp.float32),
        ] + slot + slot,
        compiler_params=pltpu.CompilerParams(vmem_limit_bytes=FIT_VMEM),
        cost_estimate=pl.CostEstimate(flops=20 * work, bytes_accessed=sched_dev * obs * twice * 2, transcendentals=0),
    )(*tables, *[arrived[owner] for owner in order], *parts, norms)
    return models, score


def load_attitude(sky, own_ref, passed, whole_ref, sems):
    rows = own_ref.shape[1]
    count = len(passed) // 2 + 1
    copies = [(None, sky, own_ref)]
    for hop in range(1, count):
        copies.append((sky >= hop, sky - hop, passed[2 * hop - 2]))
        copies.append((sky + hop < count, sky + hop, passed[2 * hop - 1]))

    def each(act):
        for index, (valid, quarter, ref) in enumerate(copies):
            def run(index=index, quarter=quarter, ref=ref):
                at = pl.ds(pl.multiple_of(quarter * rows, rows), rows)
                act(pltpu.make_async_copy(ref, whole_ref.at[:, at, :], sems.at[index]))

            if valid is None:
                run()
            else:
                pl.when(valid)(run)

    each(lambda copy: copy.start())
    return lambda: each(lambda copy: copy.wait())


def whiten_and_pick(me, asked_ref, cnt_ref, count_ref, whole_ref, wait, load, picked, white_ref, gather_ref):
    segs, slots, _ = whole_ref.shape
    capacity, width = picked[0].shape
    blocks = white_ref.shape[0] // (segs * slots)
    row = lax.broadcasted_iota(jnp.int32, (slots, width * blocks), 0)
    wait()
    for seg in range(segs):
        masked = jnp.where(row < count_ref[seg], load(seg).astype(jnp.float32), 0.0).astype(jnp.bfloat16)
        white = jnp.dot(whole_ref[seg], masked, preferred_element_type=jnp.float32)
        for block in range(blocks):
            white_ref[pl.ds((block * segs + seg) * slots, slots), :] = white[:, block * width:(block + 1) * width]
    for owner, out_ref in enumerate(picked):
        asker = owner ^ me

        def step(index, carry):
            first = index * PICK_UNROLL
            for lane in range(PICK_UNROLL):
                gather_ref[pl.ds(owner * capacity + first + lane, 1), :] = white_ref[
                    pl.ds(asked_ref[asker * capacity + first + lane], 1), :
                ]
            return carry

        lax.fori_loop(0, (cnt_ref[asker] + PICK_UNROLL - 1) // PICK_UNROLL, step, 0)
        out_ref[...] = gather_ref[pl.ds(owner * capacity, capacity), :].astype(jnp.bfloat16)


def add_rows(me, asked_ref, cnt_ref, owners, returned, rows_ref, sums, tiled):
    capacity = returned[0].shape[0]
    streams = len(sums)
    for total in sums:
        total[...] = jnp.zeros_like(total)
    for number, (owner, ref) in enumerate(zip(owners, returned)):
        tiles = capacity // SUB
        block = ref[...].astype(jnp.float32)
        if tiled:
            rows_ref[pl.ds(number * tiles, tiles)] = block.reshape(tiles, SUB, -1)
        else:
            rows_ref[pl.ds(number * capacity, capacity), :] = block
        asker = owner ^ me

        def row_at(index, lane):
            if tiled:
                return rows_ref[number * tiles + index * (UNROLL // SUB) + lane // SUB, pl.ds(lane % SUB, 1), :]
            return rows_ref[pl.ds(number * capacity + index * UNROLL + lane, 1), :]

        def step(index, carry):
            first = asker * capacity + index * UNROLL
            for start in range(0, UNROLL, streams):
                lanes = [start + lane for lane in range(streams)]
                places = [asked_ref[first + lane] for lane in lanes]
                values = [
                    total[pl.ds(place, 1), :] + row_at(index, lane)
                    for total, place, lane in zip(sums, places, lanes)
                ]
                for total, place, value in zip(sums, places, values):
                    total[pl.ds(place, 1), :] = value
            return carry

        lax.fori_loop(0, (cnt_ref[asker] + UNROLL - 1) // UNROLL, step, 0)


def placed_at(sums, at):
    return functools.reduce(jnp.add, [total[at, :] for total in sums])


def early_kernel(owners, table_base, asked_ref, cnt_ref, where_ref, base_ref, *refs):
    refs = list(refs)
    returned = [refs.pop(0) for _ in owners]
    out_ref, rows_ref = refs.pop(0), refs.pop(0)
    if table_base:
        held_ref, sem = refs.pop(0), refs.pop(0)
        copy = pltpu.make_async_copy(base_ref.at[pl.ds(0, held_ref.shape[0]), :], held_ref, sem)
        copy.start()
    add_rows(where_ref[0], asked_ref, cnt_ref, owners, returned, rows_ref, refs, True)
    if table_base:
        copy.wait()
        out_ref[...] = held_ref[...] - placed_at(refs, pl.ds(0, out_ref.shape[0]))
        return
    segs, slots, total_width = base_ref.shape
    width = out_ref.shape[1]
    for block in range(total_width // width):
        for seg in range(segs):
            at = pl.ds((block * segs + seg) * slots, slots)
            base = base_ref[seg, :, block * width:(block + 1) * width].astype(jnp.float32)
            out_ref[at, :] = base - placed_at(refs, at)


def place_early(scalars, owners, base, returned, rows):
    asked, cnt, _, where = scalars
    table_base = base.ndim == 2
    capacity = returned[0].shape[0]
    sums = [pltpu.VMEM((rows + 8, SRC_GROUP), jnp.float32)] * STREAMS
    held = [pltpu.VMEM((rows, SRC_GROUP), jnp.float32), pltpu.SemaphoreType.DMA(())] if table_base else []
    return pl.pallas_call(
        functools.partial(early_kernel, owners, table_base),
        in_specs=[SMEM] * 3 + [HBM if table_base else VMEM] + [VMEM] * len(owners),
        out_specs=VMEM,
        out_shape=jax.ShapeDtypeStruct((rows, SRC_GROUP), jnp.float32),
        scratch_shapes=[pltpu.VMEM((len(owners) * capacity // SUB, SUB, SRC_GROUP), jnp.float32)] + held + sums,
        compiler_params=pltpu.CompilerParams(vmem_limit_bytes=EARLY_VMEM),
        cost_estimate=pl.CostEstimate(flops=6 * COST_US, bytes_accessed=1 << 20, transcendentals=0),
    )(asked, cnt, where, base, *[returned[owner] for owner in owners])


def pick_kernel(tm_count, passed_count, asked_ref, cnt_ref, count_ref, where_ref, base_ref, own_ref, *refs):
    refs = list(refs)
    passed = [refs.pop(0) for _ in range(passed_count)]
    picked = [refs.pop(0) for _ in range(tm_count)]
    whole_ref, sems, white_ref, gather_ref = refs
    wait = load_attitude(where_ref[1], own_ref, passed, whole_ref, sems)
    whiten_and_pick(
        where_ref[0], asked_ref, cnt_ref, count_ref, whole_ref, wait, lambda seg: base_ref[seg], picked, white_ref,
        gather_ref,
    )


def pick_rows(scalars, base, attitude, rows):
    asked, cnt, seg_counts, where = scalars
    tm_count, = cnt.shape
    seg_dev, slots, _ = base.shape
    capacity = asked.shape[0] // tm_count
    return pl.pallas_call(
        functools.partial(pick_kernel, tm_count, len(attitude) - 1),
        in_specs=[SMEM] * 4 + [VMEM] + [ANY] * len(attitude),
        out_specs=[VMEM] * tm_count,
        out_shape=[jax.ShapeDtypeStruct((capacity, SRC_GROUP), jnp.bfloat16)] * tm_count,
        scratch_shapes=[
            pltpu.VMEM((seg_dev, slots, slots), jnp.bfloat16),
            pltpu.SemaphoreType.DMA((len(attitude),)),
            pltpu.VMEM((rows + 8, SRC_GROUP), jnp.float32),
            pltpu.VMEM((tm_count * capacity, SRC_GROUP), jnp.float32),
        ],
        compiler_params=pltpu.CompilerParams(vmem_limit_bytes=PICK_VMEM),
        cost_estimate=pl.CostEstimate(flops=5 * COST_US, bytes_accessed=1 << 20, transcendentals=0),
    )(asked, cnt, seg_counts, where, base, *attitude)


def late_pick_kernel(tm_count, passed_count, owners, asked_ref, cnt_ref, count_ref, where_ref, part_ref, own_ref,
                     *refs):
    refs = list(refs)

    def take(count):
        taken = refs[:count]
        del refs[:count]
        return taken

    passed = take(passed_count)
    returned = take(len(owners))
    (out_ref,) = take(1)
    picked = take(tm_count)
    whole_ref, sems, white_ref, gather_ref, table_ref, sem = take(6)
    segs, slots, _ = whole_ref.shape
    blocks = table_ref.shape[0] // (segs * slots)
    wait = load_attitude(where_ref[1], own_ref, passed, whole_ref, sems)
    add_rows(where_ref[0], asked_ref, cnt_ref, owners, returned, gather_ref, refs, False)
    table_ref[...] = part_ref[...] - placed_at(refs, pl.ds(0, table_ref.shape[0]))
    copy = pltpu.make_async_copy(table_ref, out_ref.at[pl.ds(0, table_ref.shape[0]), :], sem)
    copy.start()

    def load(seg):
        return jnp.concatenate(
            [table_ref[pl.ds((block * segs + seg) * slots, slots), :] for block in range(blocks)], axis=1
        )

    whiten_and_pick(
        where_ref[0], asked_ref, cnt_ref, count_ref, whole_ref, wait, load, picked, white_ref, gather_ref
    )
    copy.wait()


def place_late_and_pick(scalars, owners, part, returned, attitude):
    asked, cnt, seg_counts, where = scalars
    tm_count, = cnt.shape
    seg_dev = seg_counts.shape[0]
    slots = attitude[0].shape[2]
    capacity = asked.shape[0] // tm_count
    rows = part.shape[0]
    table = pltpu.VMEM((rows + 8, SRC_GROUP), jnp.float32)
    out = pl.pallas_call(
        functools.partial(late_pick_kernel, tm_count, len(attitude) - 1, owners),
        in_specs=[SMEM] * 4 + [VMEM] + [ANY] * len(attitude) + [VMEM] * len(owners),
        out_specs=[HBM] + [VMEM] * tm_count,
        out_shape=[jax.ShapeDtypeStruct((HBM_SPARE * rows, SRC_GROUP), jnp.float32)]
        + [jax.ShapeDtypeStruct((capacity, SRC_GROUP), jnp.bfloat16)] * tm_count,
        scratch_shapes=[
            pltpu.VMEM((seg_dev, slots, slots), jnp.bfloat16),
            pltpu.SemaphoreType.DMA((len(attitude),)),
            table,
            pltpu.VMEM((tm_count * capacity, SRC_GROUP), jnp.float32),
            pltpu.VMEM((rows, SRC_GROUP), jnp.float32),
            pltpu.SemaphoreType.DMA(()),
        ] + [table] * LATE_STREAMS,
        compiler_params=pltpu.CompilerParams(vmem_limit_bytes=LATE_PICK_VMEM),
        cost_estimate=pl.CostEstimate(flops=7 * COST_US, bytes_accessed=1 << 20, transcendentals=0),
    )(asked, cnt, seg_counts, where, part, *attitude, *[returned[owner] for owner in owners])
    return out[0], list(out[1:])


def late_kernel(owners, asked_ref, cnt_ref, where_ref, part_ref, *refs):
    refs = list(refs)
    returned = [refs.pop(0) for _ in owners]
    out_ref, rows_ref, held_ref, sems = refs[:4]
    sums = refs[4:]
    segs, slots, total_width = out_ref.shape
    width = part_ref.shape[1]
    add_rows(where_ref[0], asked_ref, cnt_ref, owners, returned, rows_ref, sums, False)
    copies = []
    for seg in range(segs):
        for block in range(total_width // width):
            at = pl.ds((block * segs + seg) * slots, slots)
            held_ref[seg, :, block * width:(block + 1) * width] = part_ref[at, :] - placed_at(sums, at)
        copies.append(pltpu.make_async_copy(held_ref.at[seg], out_ref.at[seg], sems.at[seg]))
        copies[-1].start()
    for copy in copies:
        copy.wait()


def place_late(scalars, owners, part, returned, shape):
    asked, cnt, _, where = scalars
    capacity = returned[0].shape[0]
    return pl.pallas_call(
        functools.partial(late_kernel, owners),
        in_specs=[SMEM] * 3 + [VMEM] * (1 + len(owners)),
        out_specs=HBM,
        out_shape=jax.ShapeDtypeStruct(shape, jnp.float32),
        scratch_shapes=[
            pltpu.VMEM((len(owners) * capacity, SRC_GROUP), jnp.float32),
            pltpu.VMEM(shape, jnp.float32),
            pltpu.SemaphoreType.DMA((shape[0],)),
        ] + [pltpu.VMEM((part.shape[0] + 8, SRC_GROUP), jnp.float32)] * LATE_STREAMS,
        compiler_params=pltpu.CompilerParams(vmem_limit_bytes=LATE_VMEM),
        cost_estimate=pl.CostEstimate(flops=4 * COST_US, bytes_accessed=1 << 20, transcendentals=0),
    )(asked, cnt, where, part, *[returned[owner] for owner in owners])


def make_lists(sched_seg, sched_slot, seg_dev, slots, column_blocks, tm_count, capacity):
    sched_dev, obs = sched_seg.shape
    me = lax.axis_index("tm")
    owner = sched_seg // seg_dev
    partner = owner ^ me
    block_of = (jnp.arange(sched_dev, dtype=jnp.int32) % column_blocks)[:, None]
    local_row = (block_of * seg_dev + sched_seg % seg_dev) * slots + sched_slot
    hot = (partner[:, :, None] == jnp.arange(tm_count, dtype=jnp.int32)).astype(jnp.int32)
    cnt = jnp.sum(hot, axis=1)
    plans = jnp.arange(sched_dev)
    before = (plans[None, :] < plans[:, None]).astype(jnp.int32)
    src = jnp.sum(before[:, :, None] * cnt[None, :, :], axis=1)
    owners = jnp.arange(tm_count)
    ahead = (owners[None, :] < owners[:, None]).astype(jnp.int32)
    dst = jnp.sum(ahead[None, :, :] * cnt[:, None, :], axis=2)
    entry = jnp.arange(obs)
    rank = jnp.sum(
        ((partner[:, None, :] == partner[:, :, None]) & (entry[None, :] < entry[:, None])).astype(jnp.int32),
        axis=2,
    )
    place = owner * capacity + jnp.sum(hot * src[:, None, :], axis=2) + rank
    order = jnp.sum(hot * dst[:, None, :], axis=2) + rank
    time = sched_seg * slots + sched_slot
    times = jnp.sum(jnp.where(order[:, None, :] == entry[None, :, None], time[:, None, :], 0), axis=2)
    rows = seg_dev * slots * column_blocks
    wanted = rows + jnp.sum(
        jnp.where(
            place.reshape(1, -1) == jnp.arange(tm_count * capacity, dtype=jnp.int32)[:, None],
            local_row.reshape(1, -1) - rows,
            0,
        ),
        axis=1,
    )
    step_count = (cnt + STEP - 1) // STEP
    step_first = jnp.sum(ahead[None, :, :] * step_count[:, None, :], axis=2)
    step = jnp.arange(obs // STEP + tm_count)[None, :, None] - step_first[:, None, :]
    inside = (step >= 0) & (step < step_count[:, None, :])
    spaced = capacity + STEP
    end = tm_count * spaced
    step_src = end + jnp.sum(
        jnp.where(inside, owners * spaced - end + src[:, None, :] + step * STEP, 0), axis=2
    )
    step_dst = obs + jnp.sum(jnp.where(inside, dst[:, None, :] + step * STEP - obs, 0), axis=2)
    return (step_src, step_dst), times, wanted


def send_order(count):
    return sorted(range(1, count), key=lambda step: (bin(step // 2).count("1"), step % 2, -step))


def exchange(blocks):
    count = len(blocks)
    out = list(blocks)
    for step in range(1, count):
        out[step] = lax.ppermute(blocks[step], "tm", [(i, i ^ step) for i in range(count)])
    return out


def pass_along(attitude, beside):
    count = lax.axis_size("sky")
    right = left = attitude
    pieces = [attitude]
    for hop in range(1, count):
        right = lax.ppermute(right, "sky", [(i, i + 1) for i in range(hop - 1, count - 1)])
        left = lax.ppermute(left, "sky", [(i, i - 1) for i in range(1, count - hop + 1)])
        if hop in beside:
            right, left = beside[hop](right, left)
        pieces += [right, left]
    return pieces


def on_device(residuals, seg_counts, attitude, sched_seg, sched_slot, periods):
    tm_count = lax.axis_size("tm")
    sched_dev, obs = sched_seg.shape
    seg_dev, slots, width = residuals.shape
    column_blocks = width // SRC_GROUP
    capacity = 2 * sched_dev * obs // tm_count
    tables, times, wanted = make_lists(
        sched_seg, sched_slot, seg_dev, slots, column_blocks, tm_count, capacity
    )
    wanted = wanted.reshape(tm_count, capacity)
    made = []
    asked = None

    def basis_part(after):
        first, count = sum(BASIS_CALLS[:len(made)]), BASIS_CALLS[len(made)]
        made.append(make_basis(times[first:first + count], periods, after))

    def first_hop(right, left):
        nonlocal asked
        basis_part([right, left])
        held, _ = lax.optimization_barrier((wanted, made[0][1]))
        asked = lax.all_to_all(held, "tm", split_axis=0, concat_axis=0, tiled=True)
        return right, left

    def second_hop(right, left):
        basis_part([right, left])
        basis_part([right, left])
        return right, left

    pieces = pass_along(attitude, {1: first_hop, 2: second_hop})
    cnt = jnp.sum((asked < seg_dev * slots * column_blocks).astype(jnp.int32), axis=1)
    where = jnp.stack([lax.axis_index("tm"), lax.axis_index("sky")])
    scalars = (asked.reshape(-1), cnt, seg_counts, where)
    rows = seg_dev * slots * column_blocks
    order = [0] + send_order(tm_count)
    near, far = order[:3 * tm_count // 4], order[3 * tm_count // 4:]

    base = residuals
    picked = pick_rows(scalars, base, pieces, rows)
    basis_part([picked[0]])
    parts, norms = zip(*made)
    norms = jnp.concatenate(norms)
    for iteration in range(ITERS):
        models, score = fit_plans(tables, exchange(picked), parts, norms)
        returned = exchange(models)
        base = place_early(scalars, near, base, returned, rows)
        if iteration < ITERS - 1:
            base, picked = place_late_and_pick(scalars, far, base, returned, pieces)
    cleaned = place_late(scalars, far, base, returned, residuals.shape)
    return (cleaned, score.reshape(sched_dev, SRC_GROUP))


def solution(mesh):
    in_specs = (
        P("tm", None, "sky"),
        P("tm"),
        P("tm", "sky", None),
        P(("tm", "sky"), None),
        P(("tm", "sky"), None),
        P(),
    )
    out_specs = (P("tm", None, "sky"), P(("tm", "sky"), None))
    return jax.shard_map(
        on_device, mesh=mesh, in_specs=in_specs, out_specs=out_specs, check_vma=False
    )
```

```python
import functools

import jax
import jax.numpy as jnp
from jax import lax
from jax.experimental import pallas as pl
from jax.experimental.pallas import tpu as pltpu
from jax.sharding import PartitionSpec as P

SRC_GROUP = 128
ITERS = 2
STREAMS = 4
LATE_STREAMS = 2
STEP = 16
BETA = 2.0
LOG2_E = 1.4426950408889634
ROUND = 1.5 * 2.0 ** 23
RIDGE = 1.0
MIB = 1024 * 1024
BASIS_VMEM = 8 * MIB
FIT_VMEM = 22 * MIB
EARLY_VMEM = 20 * MIB
PICK_VMEM = 12 * MIB
LATE_PICK_VMEM = 18 * MIB
LATE_VMEM = 12 * MIB
BASIS_CALLS = (1, 2, 3, 2)
UNROLL = 32
PICK_UNROLL = 32
SUB = 8
HBM_SPARE = 32
COST_US = 10 ** 9

COS_POLY = (1.0, -19.73920440673828, 64.9391098022461, -85.4500503540039, 60.16689682006836,
            -25.96480369567871, 6.52468729019165)
SIN_POLY = (6.283185005187988, -41.34158706665039, 81.59986114501953, -76.61351013183594,
            41.33811950683594, -12.463061332702637)

VMEM = pl.BlockSpec(memory_space=pltpu.VMEM)
HBM = pl.BlockSpec(memory_space=pltpu.HBM)
ANY = pl.BlockSpec(memory_space=pl.ANY)
SMEM = pl.BlockSpec(memory_space=pltpu.SMEM)


def horner(poly, v):
    acc = jnp.full_like(v, poly[-1])
    for term in poly[-2::-1]:
        acc = acc * v + term
    return acc


def basis_kernel(after, time_ref, period_ref, inverse_ref, *refs):
    basis_ref, norm_ref = refs[after:]
    obs = time_ref.shape[0]
    nper = period_ref.shape[1]
    rows = 64
    for chunk in range(nper // 128):
        lanes = pl.ds(chunk * 128, 128)
        sines = pl.ds(nper + chunk * 128, 128)
        period = period_ref[:, lanes]
        inverse = inverse_ref[:, lanes]

        def step(index, sums):
            at = pl.ds(pl.multiple_of(index * rows, rows), rows)
            time = time_ref[at, :]
            turns = (time * inverse + ROUND) - ROUND
            part = (time - turns * period) * inverse
            square = part * part
            cosine = horner(COS_POLY, square).astype(jnp.bfloat16)
            sine = (horner(SIN_POLY, square) * part).astype(jnp.bfloat16)
            basis_ref[0, at, lanes] = cosine
            basis_ref[0, at, sines] = sine
            cosine = cosine.astype(jnp.float32)
            sine = sine.astype(jnp.float32)
            return (
                sums[0] + jnp.sum((cosine * cosine).reshape(rows // 8, 8, 128), axis=0),
                sums[1] + jnp.sum((sine * sine).reshape(rows // 8, 8, 128), axis=0),
            )

        zero = jnp.zeros((8, 128), jnp.float32)
        total_c, total_s = lax.fori_loop(0, obs // rows, step, (zero, zero))
        norm_ref[0, :, lanes] = 1.0 / (jnp.sum(total_c, axis=0, keepdims=True) + RIDGE)
        norm_ref[0, :, sines] = 1.0 / (jnp.sum(total_s, axis=0, keepdims=True) + RIDGE)


def make_basis(times, periods, after):
    sched_dev, obs = times.shape
    nper = periods.shape[0]
    wide = jnp.broadcast_to(
        times.astype(jnp.float32).reshape(-1, 1), (sched_dev * obs, SRC_GROUP)
    )
    period = periods.astype(jnp.float32)[None, :]
    return pl.pallas_call(
        functools.partial(basis_kernel, len(after)),
        grid=(sched_dev,),
        in_specs=[
            pl.BlockSpec((obs, SRC_GROUP), lambda j: (j, 0)),
            pl.BlockSpec((1, nper), lambda j: (0, 0)),
            pl.BlockSpec((1, nper), lambda j: (0, 0)),
        ] + [ANY] * len(after),
        out_specs=[
            pl.BlockSpec((1, obs, 2 * nper), lambda j: (j, 0, 0)),
            pl.BlockSpec((1, 1, 2 * nper), lambda j: (j, 0, 0)),
        ],
        out_shape=[
            jax.ShapeDtypeStruct((sched_dev, obs, 2 * nper), jnp.bfloat16),
            jax.ShapeDtypeStruct((sched_dev, 1, 2 * nper), jnp.float32),
        ],
        compiler_params=pltpu.CompilerParams(vmem_limit_bytes=BASIS_VMEM),
        cost_estimate=pl.CostEstimate(
            flops=sched_dev * obs * nper * 8000, bytes_accessed=sched_dev * obs * nper * 4, transcendentals=0
        ),
    )(wide, period, 1.0 / period, *after)


def fit_kernel(order, src_ref, dst_ref, *refs):
    refs = list(refs)

    def take(count):
        taken = refs[:count]
        del refs[:count]
        return taken

    tm_count = len(order)
    arrived = dict(zip(order, take(tm_count)))
    parts = take(len(BASIS_CALLS))
    (norm_ref,) = take(1)
    outs = take(tm_count)
    score_ref, basis_ref, sems, rows_ref, back_ref = take(5)
    slots = [take(4), take(4)]
    plans, obs, twice = basis_ref.shape
    nper = twice // 2
    capacity, width = arrived[0].shape
    spaced = capacity + STEP
    steps = src_ref.shape[1]
    held = [(part, plan) for part, count in zip(parts, BASIS_CALLS) for plan in range(count)]

    def basis_copy(plan):
        part, index = held[plan]
        return pltpu.make_async_copy(part.at[index], basis_ref.at[plan], sems.at[plan])

    for plan in range(plans):
        basis_copy(plan).start()
    for owner in range(tm_count):
        rows_ref[pl.ds(owner * spaced, capacity), :] = arrived[owner][...].astype(jnp.float32)

    def correlate(plan, obs_ref, corr_ref):
        for step in range(steps):
            obs_ref[pl.ds(dst_ref[plan, step], STEP), :] = rows_ref[pl.ds(src_ref[plan, step], STEP), :]
        corr_ref[...] = lax.dot_general(
            obs_ref[:obs, :].astype(jnp.bfloat16), basis_ref[plan], (((0,), (0,)), ((), ())),
            preferred_element_type=jnp.float32,
        )

    def finish(plan, corr_ref, coeff_ref, model_ref):
        group = 16
        for start in range(0, width, group):
            at = pl.ds(start, group)
            power = []
            for chunk in range(nper // 128):
                lanes = pl.ds(chunk * 128, 128)
                sines = pl.ds(nper + chunk * 128, 128)
                cosine = corr_ref[at, lanes]
                sine = corr_ref[at, sines]
                power.append(
                    cosine * (cosine * norm_ref[plan, :, lanes]) + sine * (sine * norm_ref[plan, :, sines])
                )
            highest = functools.reduce(jnp.maximum, power)
            highest = jnp.max(highest, axis=1, keepdims=True)
            expo = [jnp.exp2((value - highest) * (BETA * LOG2_E)) for value in power]
            total = jnp.sum(functools.reduce(jnp.add, expo), axis=1, keepdims=True)
            scale = 1.0 / total
            for chunk in range(nper // 128):
                lanes = pl.ds(chunk * 128, 128)
                sines = pl.ds(nper + chunk * 128, 128)
                share = expo[chunk] * scale
                coeff_ref[at, lanes] = (share * (corr_ref[at, lanes] * norm_ref[plan, :, lanes])).astype(jnp.bfloat16)
                coeff_ref[at, sines] = (share * (corr_ref[at, sines] * norm_ref[plan, :, sines])).astype(jnp.bfloat16)
            score_ref[plan, at, :] = BETA * highest + jnp.log(total)
        model_ref[:obs, :] = lax.dot_general(
            basis_ref[plan], coeff_ref[...], (((1,), (1,)), ((), ())), preferred_element_type=jnp.float32
        )
        for step in range(steps):
            back_ref[pl.ds(src_ref[plan, step], STEP), :] = model_ref[pl.ds(dst_ref[plan, step], STEP), :]

    basis_copy(0).wait()
    correlate(0, slots[0][0], slots[0][1])

    def pair(index, carry):
        plan = index * 2
        for ahead in (1, 2):
            for known in range(ahead, plans, 2):
                pl.when(plan + ahead == known)(basis_copy(known).wait)
        correlate(plan + 1, slots[1][0], slots[1][1])
        finish(plan, *slots[0][1:])
        correlate(plan + 2, slots[0][0], slots[0][1])
        finish(plan + 1, *slots[1][1:])
        return carry

    lax.fori_loop(0, plans // 2 - 1, pair, 0)
    basis_copy(plans - 1).wait()
    correlate(plans - 1, slots[1][0], slots[1][1])
    finish(plans - 2, *slots[0][1:])
    finish(plans - 1, *slots[1][1:])
    for owner in range(tm_count):
        outs[owner][...] = back_ref[pl.ds(owner * spaced, capacity), :].astype(jnp.bfloat16)


def fit_plans(tables, arrived, parts, norms):
    tm_count = len(arrived)
    order = [0] + send_order(tm_count)[1:] + [1]
    _, obs, twice = parts[0].shape
    sched_dev = norms.shape[0]
    capacity, width = arrived[0].shape
    work = sched_dev * obs * twice * width
    spaced = tm_count * (capacity + STEP) + STEP
    slot = [
        pltpu.VMEM((obs + STEP, width), jnp.float32),
        pltpu.VMEM((width, twice), jnp.float32),
        pltpu.VMEM((width, twice), jnp.bfloat16),
        pltpu.VMEM((obs + STEP, width), jnp.float32),
    ]
    *models, score = pl.pallas_call(
        functools.partial(fit_kernel, order),
        in_specs=[SMEM, SMEM] + [VMEM] * tm_count + [ANY] * len(parts) + [VMEM],
        out_specs=[VMEM] * (tm_count + 1),
        out_shape=[jax.ShapeDtypeStruct((capacity, width), jnp.bfloat16)] * tm_count
        + [jax.ShapeDtypeStruct((sched_dev, width, 1), jnp.float32)],
        scratch_shapes=[
            pltpu.VMEM((sched_dev, obs, twice), jnp.bfloat16),
            pltpu.SemaphoreType.DMA((sched_dev,)),
            pltpu.VMEM((spaced, width), jnp.float32),
            pltpu.VMEM((spaced, width), jnp.float32),
        ] + slot + slot,
        compiler_params=pltpu.CompilerParams(vmem_limit_bytes=FIT_VMEM),
        cost_estimate=pl.CostEstimate(flops=20 * work, bytes_accessed=sched_dev * obs * twice * 2, transcendentals=0),
    )(*tables, *[arrived[owner] for owner in order], *parts, norms)
    return models, score


def load_attitude(sky, own_ref, passed, whole_ref, sems):
    rows = own_ref.shape[1]
    count = len(passed) // 2 + 1
    copies = [(None, sky, own_ref)]
    for hop in range(1, count):
        copies.append((sky >= hop, sky - hop, passed[2 * hop - 2]))
        copies.append((sky + hop < count, sky + hop, passed[2 * hop - 1]))

    def each(act):
        for index, (valid, quarter, ref) in enumerate(copies):
            def run(index=index, quarter=quarter, ref=ref):
                at = pl.ds(pl.multiple_of(quarter * rows, rows), rows)
                act(pltpu.make_async_copy(ref, whole_ref.at[:, at, :], sems.at[index]))

            if valid is None:
                run()
            else:
                pl.when(valid)(run)

    each(lambda copy: copy.start())
    return lambda: each(lambda copy: copy.wait())


def whiten_and_pick(me, asked_ref, cnt_ref, count_ref, whole_ref, wait, load, picked, white_ref, gather_ref):
    segs, slots, _ = whole_ref.shape
    capacity, width = picked[0].shape
    blocks = white_ref.shape[0] // (segs * slots)
    row = lax.broadcasted_iota(jnp.int32, (slots, width * blocks), 0)
    wait()
    for seg in range(segs):
        masked = jnp.where(row < count_ref[seg], load(seg).astype(jnp.float32), 0.0).astype(jnp.bfloat16)
        white = jnp.dot(whole_ref[seg], masked, preferred_element_type=jnp.float32)
        for block in range(blocks):
            white_ref[pl.ds((block * segs + seg) * slots, slots), :] = white[:, block * width:(block + 1) * width]
    for owner, out_ref in enumerate(picked):
        asker = owner ^ me

        def step(index, carry):
            first = index * PICK_UNROLL
            for lane in range(PICK_UNROLL):
                gather_ref[pl.ds(owner * capacity + first + lane, 1), :] = white_ref[
                    pl.ds(asked_ref[asker * capacity + first + lane], 1), :
                ]
            return carry

        lax.fori_loop(0, (cnt_ref[asker] + PICK_UNROLL - 1) // PICK_UNROLL, step, 0)
        out_ref[...] = gather_ref[pl.ds(owner * capacity, capacity), :].astype(jnp.bfloat16)


def add_rows(me, asked_ref, cnt_ref, owners, returned, rows_ref, sums, tiled):
    capacity = returned[0].shape[0]
    streams = len(sums)
    for total in sums:
        total[...] = jnp.zeros_like(total)
    for number, (owner, ref) in enumerate(zip(owners, returned)):
        tiles = capacity // SUB
        block = ref[...].astype(jnp.float32)
        if tiled:
            rows_ref[pl.ds(number * tiles, tiles)] = block.reshape(tiles, SUB, -1)
        else:
            rows_ref[pl.ds(number * capacity, capacity), :] = block
        asker = owner ^ me

        def row_at(index, lane):
            if tiled:
                return rows_ref[number * tiles + index * (UNROLL // SUB) + lane // SUB, pl.ds(lane % SUB, 1), :]
            return rows_ref[pl.ds(number * capacity + index * UNROLL + lane, 1), :]

        def step(index, carry):
            first = asker * capacity + index * UNROLL
            for start in range(0, UNROLL, streams):
                lanes = [start + lane for lane in range(streams)]
                places = [asked_ref[first + lane] for lane in lanes]
                values = [
                    total[pl.ds(place, 1), :] + row_at(index, lane)
                    for total, place, lane in zip(sums, places, lanes)
                ]
                for total, place, value in zip(sums, places, values):
                    total[pl.ds(place, 1), :] = value
            return carry

        lax.fori_loop(0, (cnt_ref[asker] + UNROLL - 1) // UNROLL, step, 0)


def placed_at(sums, at):
    return functools.reduce(jnp.add, [total[at, :] for total in sums])


def early_kernel(owners, table_base, asked_ref, cnt_ref, where_ref, base_ref, *refs):
    refs = list(refs)
    returned = [refs.pop(0) for _ in owners]
    out_ref, rows_ref = refs.pop(0), refs.pop(0)
    if table_base:
        held_ref, sem = refs.pop(0), refs.pop(0)
        copy = pltpu.make_async_copy(base_ref.at[pl.ds(0, held_ref.shape[0]), :], held_ref, sem)
        copy.start()
    add_rows(where_ref[0], asked_ref, cnt_ref, owners, returned, rows_ref, refs, True)
    if table_base:
        copy.wait()
        out_ref[...] = held_ref[...] - placed_at(refs, pl.ds(0, out_ref.shape[0]))
        return
    segs, slots, total_width = base_ref.shape
    width = out_ref.shape[1]
    for block in range(total_width // width):
        for seg in range(segs):
            at = pl.ds((block * segs + seg) * slots, slots)
            base = base_ref[seg, :, block * width:(block + 1) * width].astype(jnp.float32)
            out_ref[at, :] = base - placed_at(refs, at)


def place_early(scalars, owners, base, returned, rows):
    asked, cnt, _, where = scalars
    table_base = base.ndim == 2
    capacity = returned[0].shape[0]
    sums = [pltpu.VMEM((rows + 8, SRC_GROUP), jnp.float32)] * STREAMS
    held = [pltpu.VMEM((rows, SRC_GROUP), jnp.float32), pltpu.SemaphoreType.DMA(())] if table_base else []
    return pl.pallas_call(
        functools.partial(early_kernel, owners, table_base),
        in_specs=[SMEM] * 3 + [HBM if table_base else VMEM] + [VMEM] * len(owners),
        out_specs=VMEM,
        out_shape=jax.ShapeDtypeStruct((rows, SRC_GROUP), jnp.float32),
        scratch_shapes=[pltpu.VMEM((len(owners) * capacity // SUB, SUB, SRC_GROUP), jnp.float32)] + held + sums,
        compiler_params=pltpu.CompilerParams(vmem_limit_bytes=EARLY_VMEM),
        cost_estimate=pl.CostEstimate(flops=6 * COST_US, bytes_accessed=1 << 20, transcendentals=0),
    )(asked, cnt, where, base, *[returned[owner] for owner in owners])


def pick_kernel(tm_count, passed_count, asked_ref, cnt_ref, count_ref, where_ref, base_ref, own_ref, *refs):
    refs = list(refs)
    passed = [refs.pop(0) for _ in range(passed_count)]
    picked = [refs.pop(0) for _ in range(tm_count)]
    whole_ref, sems, white_ref, gather_ref = refs
    wait = load_attitude(where_ref[1], own_ref, passed, whole_ref, sems)
    whiten_and_pick(
        where_ref[0], asked_ref, cnt_ref, count_ref, whole_ref, wait, lambda seg: base_ref[seg], picked, white_ref,
        gather_ref,
    )


def pick_rows(scalars, base, attitude, rows):
    asked, cnt, seg_counts, where = scalars
    tm_count, = cnt.shape
    seg_dev, slots, _ = base.shape
    capacity = asked.shape[0] // tm_count
    return pl.pallas_call(
        functools.partial(pick_kernel, tm_count, len(attitude) - 1),
        in_specs=[SMEM] * 4 + [VMEM] + [ANY] * len(attitude),
        out_specs=[VMEM] * tm_count,
        out_shape=[jax.ShapeDtypeStruct((capacity, SRC_GROUP), jnp.bfloat16)] * tm_count,
        scratch_shapes=[
            pltpu.VMEM((seg_dev, slots, slots), jnp.bfloat16),
            pltpu.SemaphoreType.DMA((len(attitude),)),
            pltpu.VMEM((rows + 8, SRC_GROUP), jnp.float32),
            pltpu.VMEM((tm_count * capacity, SRC_GROUP), jnp.float32),
        ],
        compiler_params=pltpu.CompilerParams(vmem_limit_bytes=PICK_VMEM),
        cost_estimate=pl.CostEstimate(flops=5 * COST_US, bytes_accessed=1 << 20, transcendentals=0),
    )(asked, cnt, seg_counts, where, base, *attitude)


def late_pick_kernel(tm_count, passed_count, owners, asked_ref, cnt_ref, count_ref, where_ref, part_ref, own_ref,
                     *refs):
    refs = list(refs)

    def take(count):
        taken = refs[:count]
        del refs[:count]
        return taken

    passed = take(passed_count)
    returned = take(len(owners))
    (out_ref,) = take(1)
    picked = take(tm_count)
    whole_ref, sems, white_ref, gather_ref, table_ref, sem = take(6)
    segs, slots, _ = whole_ref.shape
    blocks = table_ref.shape[0] // (segs * slots)
    wait = load_attitude(where_ref[1], own_ref, passed, whole_ref, sems)
    add_rows(where_ref[0], asked_ref, cnt_ref, owners, returned, gather_ref, refs, False)
    table_ref[...] = part_ref[...] - placed_at(refs, pl.ds(0, table_ref.shape[0]))
    copy = pltpu.make_async_copy(table_ref, out_ref.at[pl.ds(0, table_ref.shape[0]), :], sem)
    copy.start()

    def load(seg):
        return jnp.concatenate(
            [table_ref[pl.ds((block * segs + seg) * slots, slots), :] for block in range(blocks)], axis=1
        )

    whiten_and_pick(
        where_ref[0], asked_ref, cnt_ref, count_ref, whole_ref, wait, load, picked, white_ref, gather_ref
    )
    copy.wait()


def place_late_and_pick(scalars, owners, part, returned, attitude):
    asked, cnt, seg_counts, where = scalars
    tm_count, = cnt.shape
    seg_dev = seg_counts.shape[0]
    slots = attitude[0].shape[2]
    capacity = asked.shape[0] // tm_count
    rows = part.shape[0]
    table = pltpu.VMEM((rows + 8, SRC_GROUP), jnp.float32)
    out = pl.pallas_call(
        functools.partial(late_pick_kernel, tm_count, len(attitude) - 1, owners),
        in_specs=[SMEM] * 4 + [VMEM] + [ANY] * len(attitude) + [VMEM] * len(owners),
        out_specs=[HBM] + [VMEM] * tm_count,
        out_shape=[jax.ShapeDtypeStruct((HBM_SPARE * rows, SRC_GROUP), jnp.float32)]
        + [jax.ShapeDtypeStruct((capacity, SRC_GROUP), jnp.bfloat16)] * tm_count,
        scratch_shapes=[
            pltpu.VMEM((seg_dev, slots, slots), jnp.bfloat16),
            pltpu.SemaphoreType.DMA((len(attitude),)),
            table,
            pltpu.VMEM((tm_count * capacity, SRC_GROUP), jnp.float32),
            pltpu.VMEM((rows, SRC_GROUP), jnp.float32),
            pltpu.SemaphoreType.DMA(()),
        ] + [table] * LATE_STREAMS,
        compiler_params=pltpu.CompilerParams(vmem_limit_bytes=LATE_PICK_VMEM),
        cost_estimate=pl.CostEstimate(flops=7 * COST_US, bytes_accessed=1 << 20, transcendentals=0),
    )(asked, cnt, seg_counts, where, part, *attitude, *[returned[owner] for owner in owners])
    return out[0], list(out[1:])


def late_kernel(owners, asked_ref, cnt_ref, where_ref, part_ref, *refs):
    refs = list(refs)
    returned = [refs.pop(0) for _ in owners]
    out_ref, rows_ref, held_ref, sems = refs[:4]
    sums = refs[4:]
    segs, slots, total_width = out_ref.shape
    width = part_ref.shape[1]
    add_rows(where_ref[0], asked_ref, cnt_ref, owners, returned, rows_ref, sums, False)
    copies = []
    for seg in range(segs):
        for block in range(total_width // width):
            at = pl.ds((block * segs + seg) * slots, slots)
            held_ref[seg, :, block * width:(block + 1) * width] = part_ref[at, :] - placed_at(sums, at)
        copies.append(pltpu.make_async_copy(held_ref.at[seg], out_ref.at[seg], sems.at[seg]))
        copies[-1].start()
    for copy in copies:
        copy.wait()


def place_late(scalars, owners, part, returned, shape):
    asked, cnt, _, where = scalars
    capacity = returned[0].shape[0]
    return pl.pallas_call(
        functools.partial(late_kernel, owners),
        in_specs=[SMEM] * 3 + [VMEM] * (1 + len(owners)),
        out_specs=HBM,
        out_shape=jax.ShapeDtypeStruct(shape, jnp.float32),
        scratch_shapes=[
            pltpu.VMEM((len(owners) * capacity, SRC_GROUP), jnp.float32),
            pltpu.VMEM(shape, jnp.float32),
            pltpu.SemaphoreType.DMA((shape[0],)),
        ] + [pltpu.VMEM((part.shape[0] + 8, SRC_GROUP), jnp.float32)] * LATE_STREAMS,
        compiler_params=pltpu.CompilerParams(vmem_limit_bytes=LATE_VMEM),
        cost_estimate=pl.CostEstimate(flops=4 * COST_US, bytes_accessed=1 << 20, transcendentals=0),
    )(asked, cnt, where, part, *[returned[owner] for owner in owners])


def make_lists(sched_seg, sched_slot, seg_dev, slots, column_blocks, tm_count, capacity):
    sched_dev, obs = sched_seg.shape
    me = lax.axis_index("tm")
    owner = sched_seg // seg_dev
    partner = owner ^ me
    block_of = (jnp.arange(sched_dev, dtype=jnp.int32) % column_blocks)[:, None]
    local_row = (block_of * seg_dev + sched_seg % seg_dev) * slots + sched_slot
    hot = (partner[:, :, None] == jnp.arange(tm_count, dtype=jnp.int32)).astype(jnp.int32)
    cnt = jnp.sum(hot, axis=1)
    plans = jnp.arange(sched_dev)
    before = (plans[None, :] < plans[:, None]).astype(jnp.int32)
    src = jnp.sum(before[:, :, None] * cnt[None, :, :], axis=1)
    owners = jnp.arange(tm_count)
    ahead = (owners[None, :] < owners[:, None]).astype(jnp.int32)
    dst = jnp.sum(ahead[None, :, :] * cnt[:, None, :], axis=2)
    entry = jnp.arange(obs)
    rank = jnp.sum(
        ((partner[:, None, :] == partner[:, :, None]) & (entry[None, :] < entry[:, None])).astype(jnp.int32),
        axis=2,
    )
    place = owner * capacity + jnp.sum(hot * src[:, None, :], axis=2) + rank
    order = jnp.sum(hot * dst[:, None, :], axis=2) + rank
    time = sched_seg * slots + sched_slot
    times = jnp.sum(jnp.where(order[:, None, :] == entry[None, :, None], time[:, None, :], 0), axis=2)
    rows = seg_dev * slots * column_blocks
    wanted = rows + jnp.sum(
        jnp.where(
            place.reshape(1, -1) == jnp.arange(tm_count * capacity, dtype=jnp.int32)[:, None],
            local_row.reshape(1, -1) - rows,
            0,
        ),
        axis=1,
    )
    step_count = (cnt + STEP - 1) // STEP
    step_first = jnp.sum(ahead[None, :, :] * step_count[:, None, :], axis=2)
    step = jnp.arange(obs // STEP + tm_count)[None, :, None] - step_first[:, None, :]
    inside = (step >= 0) & (step < step_count[:, None, :])
    spaced = capacity + STEP
    end = tm_count * spaced
    step_src = end + jnp.sum(
        jnp.where(inside, owners * spaced - end + src[:, None, :] + step * STEP, 0), axis=2
    )
    step_dst = obs + jnp.sum(jnp.where(inside, dst[:, None, :] + step * STEP - obs, 0), axis=2)
    return (step_src, step_dst), times, wanted


def send_order(count):
    return sorted(range(1, count), key=lambda step: (bin(step // 2).count("1"), step % 2, -step))


def exchange(blocks):
    count = len(blocks)
    out = list(blocks)
    for step in range(1, count):
        out[step] = lax.ppermute(blocks[step], "tm", [(i, i ^ step) for i in range(count)])
    return out


def pass_along(attitude, beside):
    count = lax.axis_size("sky")
    right = left = attitude
    pieces = [attitude]
    for hop in range(1, count):
        right = lax.ppermute(right, "sky", [(i, i + 1) for i in range(hop - 1, count - 1)])
        left = lax.ppermute(left, "sky", [(i, i - 1) for i in range(1, count - hop + 1)])
        if hop in beside:
            right, left = beside[hop](right, left)
        pieces += [right, left]
    return pieces


def on_device(residuals, seg_counts, attitude, sched_seg, sched_slot, periods):
    tm_count = lax.axis_size("tm")
    sched_dev, obs = sched_seg.shape
    seg_dev, slots, width = residuals.shape
    column_blocks = width // SRC_GROUP
    capacity = 2 * sched_dev * obs // tm_count
    tables, times, wanted = make_lists(
        sched_seg, sched_slot, seg_dev, slots, column_blocks, tm_count, capacity
    )
    wanted = wanted.reshape(tm_count, capacity)
    made = []
    asked = None

    def basis_part(after):
        first, count = sum(BASIS_CALLS[:len(made)]), BASIS_CALLS[len(made)]
        made.append(make_basis(times[first:first + count], periods, after))

    def first_hop(right, left):
        nonlocal asked
        basis_part([right, left])
        held, _ = lax.optimization_barrier((wanted, made[0][1]))
        asked = lax.all_to_all(held, "tm", split_axis=0, concat_axis=0, tiled=True)
        return right, left

    def second_hop(right, left):
        basis_part([right, left])
        basis_part([right, left])
        return right, left

    pieces = pass_along(attitude, {1: first_hop, 2: second_hop})
    cnt = jnp.sum((asked < seg_dev * slots * column_blocks).astype(jnp.int32), axis=1)
    where = jnp.stack([lax.axis_index("tm"), lax.axis_index("sky")])
    scalars = (asked.reshape(-1), cnt, seg_counts, where)
    rows = seg_dev * slots * column_blocks
    order = [0] + send_order(tm_count)
    near, far = order[:3 * tm_count // 4], order[3 * tm_count // 4:]

    base = residuals
    picked = pick_rows(scalars, base, pieces, rows)
    basis_part([picked[0]])
    parts, norms = zip(*made)
    norms = jnp.concatenate(norms)
    for iteration in range(ITERS):
        models, score = fit_plans(tables, exchange(picked), parts, norms)
        returned = exchange(models)
        base = place_early(scalars, near, base, returned, rows)
        if iteration < ITERS - 1:
            base, picked = place_late_and_pick(scalars, far, base, returned, pieces)
    cleaned = place_late(scalars, far, base, returned, residuals.shape)
    return (cleaned, score.reshape(sched_dev, SRC_GROUP))


def solution(mesh):
    in_specs = (
        P("tm", None, "sky"),
        P("tm"),
        P("tm", "sky", None),
        P(("tm", "sky"), None),
        P(("tm", "sky"), None),
        P(),
    )
    out_specs = (P("tm", None, "sky"), P(("tm", "sky"), None))
    return jax.shard_map(
        on_device, mesh=mesh, in_specs=in_specs, out_specs=out_specs, check_vma=False
    )
```
